32 devices in a mesh: dp: 4 (over y, x), fsdp: 8 (over z, core).
Axes of the slice: x: 2, y: 2, z: 4, core: 2. Of those that a mesh axis runs over, the one named last changes fastest.
Arguments:
- images: bfloat16 [1280, 16, 256], P(('dp', 'fsdp'))
- partner: int32 [1280], P(('dp', 'fsdp')), may hold values from 0 to 39
- mix_pair: int32 [1280, 2], P(('dp', 'fsdp')), may hold values from 1 to 8
- labels: int32 [1280], P(('dp', 'fsdp')), may hold values from 0 to 999
- step: int32 [1], replicated, may hold values from 2 to 20
- layer_mats: float32 [3, 512, 1536], P(None, 'fsdp')
- layer_side: float32 [3, 142, 1536], P(None, None, 'fsdp')
- layer_vecs: float32 [3, 576], P(None, 'fsdp')
- head_mat: float32 [1280, 1258], P('fsdp')
- fc_bias: float32 [1000], replicated, may hold values from -3 to 3
- mats_first: float32 [3, 512, 1536], P(None, 'fsdp')
- mats_second: float32 [3, 512, 1536], P(None, 'fsdp'), as said below
- side_first: float32 [3, 142, 1536], P(None, None, 'fsdp')
- side_second: float32 [3, 142, 1536], P(None, None, 'fsdp'), as said below
- vecs_first: float32 [3, 576], P(None, 'fsdp')
- vecs_second: float32 [3, 576], P(None, 'fsdp'), as said below
- head_first: float32 [1280, 1258], P('fsdp')
- head_second: float32 [1280, 1258], P('fsdp'), as said below
- bias_first: float32 [1000], replicated
- bias_second: float32 [1000], replicated, as said below
Outputs:
- loss: float32 [], replicated
- mats_new: float32 [3, 512, 1536], P(None, 'fsdp')
- mats_moment: float32 [3, 512, 1536], P(None, 'fsdp')
- mats_square: float32 [3, 512, 1536], P(None, 'fsdp')
- side_new: float32 [3, 142, 1536], P(None, None, 'fsdp')
- side_moment: float32 [3, 142, 1536], P(None, None, 'fsdp')
- side_square: float32 [3, 142, 1536], P(None, None, 'fsdp')
- vecs_new: float32 [3, 576], P(None, 'fsdp')
- vecs_moment: float32 [3, 576], P(None, 'fsdp')
- vecs_square: float32 [3, 576], P(None, 'fsdp')
- head_new: float32 [1280, 1258], P('fsdp')
- head_moment: float32 [1280, 1258], P('fsdp')
- head_square: float32 [1280, 1258], P('fsdp')
- bias_new: float32 [1000], replicated
- bias_moment: float32 [1000], replicated
- bias_square: float32 [1000], replicated
- norms: float32 [2, 17], replicated
The draws below stay inside these ranges and needn't reach their ends.
Inputs may be any that keep to these rules, and one draw needn't show every extreme that they name: partner[i] indexes an image within the block of 40 consecutive images that holds image i. `mats_second`: entries are positive. `side_second`: entries are positive. `vecs_second`: entries are positive. `head_second`: entries are positive. `bias_second`: entries are positive.
All inputs are finite; a program needn't handle non-finite values.
Results may differ from the reference program's by a relative error of at most 0.01.
Values may be sent and summed in bfloat16 or wider, within the bound.
No kernel may reach another device: no remote copies, remote signals or barrier semaphores. Data moves between devices by JAX's collectives and lax.ppermute only.
A program may use at most 256 MiB of HBM per device.

```python
import jax
import jax.numpy as jnp
from jax import lax

WIDTH = 256
EXPAND = 1536
SQUEEZE = 64
HEAD = 1280
CLASSES = 1000
EDGE = 4
LAYERS = 3
IMG_DEV = 40
MAP = 16
IMAGES = 1280
SIDE = 142
VECS = 576
HEADCOLS = 1258


def noise(key, shape):
    return jax.random.normal(key, shape, jnp.float32)


def ramp(length):
    return jnp.exp(jnp.log(3.0) * jnp.arange(length, dtype=jnp.float32) / max(length - 1, 1))


def grad_scale():
    return 1.0 / IMAGES ** 0.5


def moment_pair(key, scale_map):
    key_one, key_two = jax.random.split(key)
    first_part = 0.1 / 0.9 * scale_map * jax.random.normal(key_one, scale_map.shape, jnp.float32)
    second_part = 0.001001 * scale_map * scale_map * jnp.exp(jax.random.uniform(key_two, scale_map.shape, jnp.float32, 0.0, 1.386))
    return (first_part, second_part)


def mats_scale():
    return 0.1 * grad_scale() * jnp.ones((LAYERS, 2 * WIDTH, EXPAND), jnp.float32)


def side_scale():
    row_ids = jnp.arange(SIDE)[None, :, None]
    factor = jnp.where(row_ids < 9, 0.3, jnp.where(row_ids < 9 + 2 * SQUEEZE, 0.1, 0.3))
    return grad_scale() * factor * jnp.ones((LAYERS, SIDE, EXPAND), jnp.float32)


def vecs_scale():
    return 0.3 * grad_scale() * jnp.ones((LAYERS, VECS), jnp.float32)


def head_scale():
    col_ids = jnp.arange(HEADCOLS)[None, :]
    factor = jnp.where(col_ids < WIDTH, 0.1, jnp.where(col_ids < WIDTH + CLASSES, 0.02, 0.3))
    return grad_scale() * factor * jnp.ones((HEAD, HEADCOLS), jnp.float32)


def bias_scale():
    return 0.03 * grad_scale() * jnp.ones((CLASSES,), jnp.float32)


def draw_images(key, part):
    key_one, key_two = jax.random.split(key)
    base = noise(key_one, (IMAGES, MAP, WIDTH))
    channel = jnp.exp(jax.random.uniform(key_two, (WIDTH,), jnp.float32, -1.15, 1.15))
    value = 0.6 * base * channel[None, None, :] * ramp(IMAGES)[:, None, None]
    return value.astype(jnp.bfloat16)


def draw_layer_mats(key, part):
    row_ids = jnp.arange(2 * WIDTH)[None, :, None]
    scale = jnp.where(row_ids < WIDTH, WIDTH ** (-0.5), EXPAND ** (-0.5)) * ramp(2 * WIDTH)[None, :, None]
    return scale * noise(key, (LAYERS, 2 * WIDTH, EXPAND))


def draw_layer_side(key, part):
    row_ids = jnp.arange(SIDE)[None, :, None]
    bias_row = 9 + 2 * SQUEEZE
    scale = jnp.where(row_ids < 9, 1.0 / 3.0, jnp.where(row_ids < 9 + SQUEEZE, EXPAND ** (-0.5), jnp.where(row_ids < bias_row, 2.0 * SQUEEZE ** (-0.5), jnp.where(row_ids == bias_row, 0.5, jnp.where((row_ids - bias_row) % 2 == 1, 0.1, 0.2)))))
    stretch = jnp.where(row_ids < bias_row, ramp(EXPAND)[None, None, :], 1.0)
    offset = jnp.where((row_ids > bias_row) & ((row_ids - bias_row) % 2 == 1), 1.0, 0.0)
    return offset + scale * stretch * noise(key, (LAYERS, SIDE, EXPAND))


def draw_layer_vecs(key, part):
    col_ids = jnp.arange(VECS)[None, :]
    scale = jnp.where(col_ids < SQUEEZE, 0.5, jnp.where(col_ids < SQUEEZE + WIDTH, 0.1, 0.2))
    offset = jnp.where((col_ids >= SQUEEZE) & (col_ids < SQUEEZE + WIDTH), 1.0, 0.0)
    return offset + scale * noise(key, (LAYERS, VECS))


def draw_head_mat(key, part):
    col_ids = jnp.arange(HEADCOLS)[None, :]
    stretch = ramp(HEAD)[:, None]
    scale = jnp.where(col_ids < WIDTH, WIDTH ** (-0.5) * stretch, jnp.where(col_ids < WIDTH + CLASSES, 2.5 * HEAD ** (-0.5) * stretch, jnp.where(col_ids == WIDTH + CLASSES, 0.1, 0.2)))
    offset = jnp.where(col_ids == WIDTH + CLASSES, 1.0, 0.0)
    return offset + scale * noise(key, (HEAD, HEADCOLS))


def draw_mats_first(key, part):
    return moment_pair(jax.random.fold_in(key, 11), mats_scale())[0]


def draw_mats_second(key, part):
    return moment_pair(jax.random.fold_in(key, 12), mats_scale())[1]


def draw_side_first(key, part):
    return moment_pair(jax.random.fold_in(key, 21), side_scale())[0]


def draw_side_second(key, part):
    return moment_pair(jax.random.fold_in(key, 22), side_scale())[1]


def draw_vecs_first(key, part):
    return moment_pair(jax.random.fold_in(key, 31), vecs_scale())[0]


def draw_vecs_second(key, part):
    return moment_pair(jax.random.fold_in(key, 32), vecs_scale())[1]


def draw_head_first(key, part):
    return moment_pair(jax.random.fold_in(key, 41), head_scale())[0]


def draw_head_second(key, part):
    return moment_pair(jax.random.fold_in(key, 42), head_scale())[1]


def draw_bias_first(key, part):
    return moment_pair(jax.random.fold_in(key, 51), bias_scale())[0]


def draw_bias_second(key, part):
    return moment_pair(jax.random.fold_in(key, 52), bias_scale())[1]


def touch_ends(drawn, stream_key, low, top_value):
    longest = drawn.shape.index(max(drawn.shape))
    spots = []
    for shift in (0, 1):
        where = [jax.random.randint(jax.random.fold_in(stream_key, axis), (), 0, length) for axis, length in enumerate(drawn.shape)]
        where[longest] = (where[longest] + shift) % drawn.shape[longest]
        spots.append(tuple(where))
    return drawn.at[spots[0]].set(low).at[spots[1]].set(top_value)


def normal_values(key, extent, deviation, most, kind=jnp.bfloat16):
    drawn = jax.random.normal(key, extent, jnp.float32) * deviation
    return jnp.minimum(jnp.maximum(drawn, -most), most).astype(kind)


def setup_inputs(seed: int = 0) -> dict:
    splits = jax.random.split(jax.random.key(seed), 21)
    images = draw_images(jax.random.fold_in(splits[20], 71), 0)
    partner = touch_ends(jax.random.randint(splits[1], (IMAGES,), 0, IMG_DEV), jax.random.fold_in(splits[1], 1), 0, IMG_DEV - 1).astype(jnp.int32)
    mix_pair = touch_ends(jax.random.randint(splits[2], (IMAGES, 2), 1, 9), jax.random.fold_in(splits[2], 1), 1, 8).astype(jnp.int32)
    labels = touch_ends(jax.random.randint(splits[3], (IMAGES,), 0, CLASSES), jax.random.fold_in(splits[3], 1), 0, CLASSES - 1).astype(jnp.int32)
    step = jax.random.randint(splits[4], (1,), 2, 21).astype(jnp.int32)
    layer_mats = draw_layer_mats(jax.random.fold_in(splits[20], 71), 0)
    layer_side = draw_layer_side(jax.random.fold_in(splits[20], 71), 0)
    layer_vecs = draw_layer_vecs(jax.random.fold_in(splits[20], 71), 0)
    head_mat = draw_head_mat(jax.random.fold_in(splits[20], 71), 0)
    fc_bias = normal_values(splits[9], (CLASSES,), 0.5, 3.0, jnp.float32)
    mats_first = draw_mats_first(jax.random.fold_in(splits[20], 71), 0)
    mats_second = draw_mats_second(jax.random.fold_in(splits[20], 71), 0)
    side_first = draw_side_first(jax.random.fold_in(splits[20], 71), 0)
    side_second = draw_side_second(jax.random.fold_in(splits[20], 71), 0)
    vecs_first = draw_vecs_first(jax.random.fold_in(splits[20], 71), 0)
    vecs_second = draw_vecs_second(jax.random.fold_in(splits[20], 71), 0)
    head_first = draw_head_first(jax.random.fold_in(splits[20], 71), 0)
    head_second = draw_head_second(jax.random.fold_in(splits[20], 71), 0)
    bias_first = draw_bias_first(jax.random.fold_in(splits[20], 71), 0)
    bias_second = draw_bias_second(jax.random.fold_in(splits[20], 71), 0)
    return dict(images=images, partner=partner, mix_pair=mix_pair, labels=labels, step=step, layer_mats=layer_mats, layer_side=layer_side, layer_vecs=layer_vecs, head_mat=head_mat, fc_bias=fc_bias, mats_first=mats_first, mats_second=mats_second, side_first=side_first, side_second=side_second, vecs_first=vecs_first, vecs_second=vecs_second, head_first=head_first, head_second=head_second, bias_first=bias_first, bias_second=bias_second)


EPS_BN = 0.001
BETA_ONE = 0.9
BETA_TWO = 0.999
EPS_ADAM = 1e-06
DECAY_RATE = 0.01
RATE_MATRIX = 0.5
RATE_VECTOR = 0.25
HIGHEST = lax.Precision.HIGHEST

@jax.custom_vjp
def low(v):
    return lax.optimization_barrier(v.astype(jnp.bfloat16)).astype(jnp.float32)

@jax.custom_vjp
def low_back(v):
    return v

def low_keep(v):
    return (low(v), None)

def low_pass(kept, grad):
    return (grad,)

def back_keep(v):
    return (v, None)

def back_low(kept, grad):
    return (low(grad),)
low.defvjp(low_keep, low_pass)
low_back.defvjp(back_keep, back_low)

def batch_norm(hidden, norm_gain, norm_bias):
    center = lax.optimization_barrier(jnp.mean(hidden, axis=0))
    spread = lax.optimization_barrier(jnp.mean(hidden * hidden, axis=0)) - center * center
    return (hidden - center) * lax.rsqrt(spread + EPS_BN) * norm_gain + norm_bias

def depthwise(values, kernel):
    padded = jnp.pad(values, ((0, 0), (1, 1), (1, 1), (0, 0)))
    edge_len = values.shape[1]
    output = jnp.zeros_like(values)
    for row_shift in range(3):
        for col_shift in range(3):
            output = output + padded[:, row_shift:row_shift + edge_len, col_shift:col_shift + edge_len, :] * kernel[3 * row_shift + col_shift]
    return output

def block(stream, matrices, side_params, vectors):
    matrices = low(matrices)
    side_params = low(side_params)
    vectors = low(vectors)
    image_count = stream.shape[0] // MAP
    bias_row = 9 + 2 * SQUEEZE
    hidden_one = low_back(jnp.dot(low(stream), matrices[:WIDTH], precision=HIGHEST))
    active_one = jax.nn.silu(batch_norm(hidden_one, side_params[bias_row + 1], side_params[bias_row + 2]))
    spatial = depthwise(active_one.reshape(image_count, EDGE, EDGE, EXPAND), side_params[:9]).reshape(hidden_one.shape)
    active_two = jax.nn.silu(batch_norm(spatial, side_params[bias_row + 3], side_params[bias_row + 4])).reshape(image_count, MAP, EXPAND)
    pooled = lax.optimization_barrier(jnp.mean(active_two, axis=1))
    squeezed = jax.nn.silu(jnp.dot(pooled, side_params[9:9 + SQUEEZE].T, precision=HIGHEST) + vectors[:SQUEEZE])
    excite = jax.nn.sigmoid(jnp.dot(squeezed, side_params[9 + SQUEEZE:bias_row], precision=HIGHEST) + side_params[bias_row])
    scaled = low((active_two * excite[:, None, :]).reshape(hidden_one.shape))
    projected = low_back(jnp.dot(scaled, matrices[WIDTH:].T, precision=HIGHEST))
    return stream + batch_norm(projected, vectors[SQUEEZE:SQUEEZE + WIDTH], vectors[SQUEEZE + WIDTH:])

def head_logits(stream, head_params, class_bias):
    head_low = low(head_params)
    image_count = stream.shape[0] // MAP
    hidden = low_back(jnp.dot(low(stream), head_low[:, :WIDTH].T, precision=HIGHEST))
    active = jax.nn.silu(batch_norm(hidden, head_low[:, WIDTH + CLASSES], head_low[:, WIDTH + CLASSES + 1]))
    features = lax.optimization_barrier(jnp.mean(active.reshape(image_count, MAP, HEAD), axis=1))
    return low_back(jnp.dot(low(features), head_low[:, WIDTH:WIDTH + CLASSES], precision=HIGHEST)) + class_bias

def lamb_moments(weight, moment_one, moment_two, gradient, decay_mask, step_float):
    first_new = BETA_ONE * moment_one + (1.0 - BETA_ONE) * gradient
    second_new = BETA_TWO * moment_two + (1.0 - BETA_TWO) * gradient * gradient
    corrected = first_new / (1.0 - BETA_ONE ** step_float) / (jnp.sqrt(second_new / (1.0 - BETA_TWO ** step_float)) + EPS_ADAM)
    return (first_new, second_new, corrected + DECAY_RATE * decay_mask * weight)

def group_sums(mats_rows, side_rows, head_cols):
    per_layer = jnp.stack([lax.optimization_barrier(jnp.sum(mats_rows[:, :WIDTH], axis=1)), lax.optimization_barrier(jnp.sum(mats_rows[:, WIDTH:], axis=1)), lax.optimization_barrier(jnp.sum(side_rows[:, :9], axis=1)), lax.optimization_barrier(jnp.sum(side_rows[:, 9:9 + SQUEEZE], axis=1)), lax.optimization_barrier(jnp.sum(side_rows[:, 9 + SQUEEZE:9 + 2 * SQUEEZE], axis=1))], axis=1)
    tail = jnp.stack([jnp.sum(head_cols[:WIDTH]), jnp.sum(head_cols[WIDTH:WIDTH + CLASSES])])
    return jnp.concatenate([per_layer.reshape(-1), tail])

def rate_maps(trust_ratio):
    groups = trust_ratio[:5 * LAYERS].reshape(LAYERS, 5)
    row_ids = jnp.arange(2 * WIDTH)[None, :]
    mats_rate = RATE_MATRIX * jnp.where(row_ids < WIDTH, groups[:, 0:1], groups[:, 1:2])
    side_ids = jnp.arange(SIDE)[None, :]
    side_rate = jnp.where(side_ids < 9, RATE_MATRIX * groups[:, 2:3], jnp.where(side_ids < 9 + SQUEEZE, RATE_MATRIX * groups[:, 3:4], jnp.where(side_ids < 9 + 2 * SQUEEZE, RATE_MATRIX * groups[:, 4:5], RATE_VECTOR)))
    col_ids = jnp.arange(HEADCOLS)
    head_rate = jnp.where(col_ids < WIDTH, RATE_MATRIX * trust_ratio[5 * LAYERS], jnp.where(col_ids < WIDTH + CLASSES, RATE_MATRIX * trust_ratio[5 * LAYERS + 1], RATE_VECTOR))
    return (mats_rate, side_rate, head_rate)

def reference(images, partner, mix_pair, labels, step, layer_mats, layer_side, layer_vecs, head_mat, fc_bias, mats_first, mats_second, side_first, side_second, vecs_first, vecs_second, head_first, head_second, bias_first, bias_second):
    total_images = images.shape[0]
    block_start = jnp.arange(total_images, dtype=jnp.int32) // IMG_DEV * IMG_DEV
    partner_index = (block_start + partner).astype(jnp.int32)
    pair_float = mix_pair.astype(jnp.float32)
    mixing = pair_float[:, 0] / (pair_float[:, 0] + pair_float[:, 1])
    pixels = images.astype(jnp.float32)
    mixed = mixing[:, None, None] * pixels + (1.0 - mixing)[:, None, None] * pixels[partner_index]
    partner_label = labels[partner_index]

    def objective(matrices, side_params, vectors, head_params, class_bias):
        stream = mixed.reshape(total_images * MAP, WIDTH)
        for layer_index in range(LAYERS):
            stream = jax.checkpoint(block)(stream, matrices[layer_index], side_params[layer_index], vectors[layer_index])
        logits = head_logits(stream, head_params, class_bias)
        row_max = lax.optimization_barrier(jnp.max(logits, axis=1, keepdims=True))
        log_total = row_max[:, 0] + jnp.log(lax.optimization_barrier(jnp.sum(jnp.exp(logits - row_max), axis=1)))
        own_logit = jnp.take_along_axis(logits, labels[:, None], axis=1)[:, 0]
        other_logit = jnp.take_along_axis(logits, partner_label[:, None], axis=1)[:, 0]
        return jnp.mean(mixing * (log_total - own_logit) + (1.0 - mixing) * (log_total - other_logit))
    loss_value, pullback = jax.vjp(objective, layer_mats, layer_side, layer_vecs, head_mat, fc_bias)
    grad_mats, grad_side, grad_vecs, grad_head, grad_bias = pullback(jnp.ones((), jnp.float32))
    step_float = step[0].astype(jnp.float32)
    side_decay = (jnp.arange(SIDE) < 9 + 2 * SQUEEZE).astype(jnp.float32)[None, :, None]
    head_decay = (jnp.arange(HEADCOLS) < WIDTH + CLASSES).astype(jnp.float32)[None, :]
    mats_moment, mats_square, mats_dir = lamb_moments(layer_mats, mats_first, mats_second, grad_mats, 1.0, step_float)
    side_moment, side_square, side_dir = lamb_moments(layer_side, side_first, side_second, grad_side, side_decay, step_float)
    vecs_moment, vecs_square, vecs_dir = lamb_moments(layer_vecs, vecs_first, vecs_second, grad_vecs, 0.0, step_float)
    head_moment, head_square, head_dir = lamb_moments(head_mat, head_first, head_second, grad_head, head_decay, step_float)
    bias_moment, bias_square, bias_dir = lamb_moments(fc_bias, bias_first, bias_second, grad_bias, 0.0, step_float)
    weight_squares = group_sums(lax.optimization_barrier(jnp.sum(layer_mats * layer_mats, axis=2)), lax.optimization_barrier(jnp.sum(layer_side * layer_side, axis=2)), lax.optimization_barrier(jnp.sum(head_mat * head_mat, axis=0)))
    update_squares = group_sums(lax.optimization_barrier(jnp.sum(mats_dir * mats_dir, axis=2)), lax.optimization_barrier(jnp.sum(side_dir * side_dir, axis=2)), lax.optimization_barrier(jnp.sum(head_dir * head_dir, axis=0)))
    weight_norm = jnp.sqrt(weight_squares)
    update_norm = jnp.sqrt(update_squares)
    mats_rate, side_rate, head_rate = rate_maps(weight_norm / update_norm)
    mats_new = layer_mats - mats_rate[:, :, None] * mats_dir
    side_new = layer_side - side_rate[:, :, None] * side_dir
    vecs_new = layer_vecs - RATE_VECTOR * vecs_dir
    head_new = head_mat - head_rate[None, :] * head_dir
    bias_new = fc_bias - RATE_VECTOR * bias_dir
    norms = jnp.stack([weight_norm, update_norm])
    return (loss_value, mats_new, mats_moment, mats_square, side_new, side_moment, side_square, vecs_new, vecs_moment, vecs_square, head_new, head_moment, head_square, bias_new, bias_moment, bias_square, norms)
```

```python
import functools

import jax
import jax.numpy as jnp
from jax import lax
from jax.experimental import pallas as pl
from jax.experimental.pallas import tpu as pltpu
from jax.sharding import PartitionSpec as P

WIDTH = 256
EXPAND = 1536
SQUEEZE = 64
HEAD = 1280
CLASSES = 1000
LOGITS = 1024
EDGE = 4
LAYERS = 3
MAP = 16
SIDE = 142
SIDE_PAD = 144
VECS = 576
HEADCOLS = 1258
HEADPAD = 1280

EPS_BN = 0.001
BETA_ONE = 0.9
BETA_TWO = 0.999
EPS_ADAM = 1e-06
DECAY_RATE = 0.01
RATE_MATRIX = 0.5
RATE_VECTOR = 0.25

BOTH = ("dp", "fsdp")
F32 = jnp.float32
BF16 = jnp.bfloat16
HIGHEST = lax.Precision.HIGHEST
LANE = 128
TILE = 8
ROWS = MAP * TILE
CHUNK = 256
VMEM_BYTES = 44 * 1024 * 1024

NT = (((1,), (1,)), ((), ()))
TN = (((0,), (0,)), ((), ()))


def call(kernel, outs, ins, scratch=()):
    return pl.pallas_call(
        kernel,
        out_shape=outs,
        in_specs=[pl.BlockSpec(memory_space=pltpu.VMEM)] * len(ins),
        out_specs=[pl.BlockSpec(memory_space=pltpu.VMEM)] * len(outs),
        scratch_shapes=list(scratch),
        compiler_params=pltpu.CompilerParams(vmem_limit_bytes=VMEM_BYTES),
    )(*ins)


def shape(dims, dtype=F32):
    return jax.ShapeDtypeStruct(dims, dtype)


def dot(left, right):
    return jnp.dot(left, right, preferred_element_type=F32)


def dot_nt(left, right):
    return lax.dot_general(left, right, NT, preferred_element_type=F32)


def dot_tn(left, right):
    return lax.dot_general(left, right, TN, preferred_element_type=F32)


def halves(value):
    high = value.astype(BF16)
    return high, (value - high.astype(F32)).astype(BF16)


def sigmoid(value):
    return 0.5 * jnp.tanh(0.5 * value) + 0.5


def chunk_at(index, size=CHUNK):
    return pl.ds(pl.multiple_of(index * size, size), size)


def spread(rows, first, count):
    return jnp.concatenate([rows[first + k : first + k + 1, :] for k in range(count)], axis=1)


def fold(vectors, rows):
    pieces = [
        vector[:, k * LANE : (k + 1) * LANE]
        for vector in vectors
        for k in range(vector.shape[1] // LANE)
    ]
    if rows > len(pieces):
        pieces.append(jnp.zeros((rows - len(pieces), LANE), F32))
    return jnp.concatenate(pieces, axis=0)


def padded(rows):
    return -(-rows // 8) * 8


def moment_rows(columns):
    return padded(3 * columns // LANE)


def pack_moments(total, squares, count):
    mean = total / count
    spread_sum = jnp.maximum(squares - total * mean, 0.0)
    high = mean.astype(BF16).astype(F32)
    return fold([high, mean - high, spread_sum], moment_rows(total.shape[1])).astype(BF16)


def read_moments(recv_ref, columns, count):
    groups = columns // LANE
    devices = recv_ref.shape[0]
    parts = recv_ref[...].astype(F32)
    means = parts[:, :groups] + parts[:, groups : 2 * groups]
    mean = jnp.sum(means, axis=0) / devices
    apart = means - mean[None]
    spread_sum = jnp.sum(parts[:, 2 * groups : 3 * groups], axis=0) / count
    variance = (spread_sum + jnp.sum(apart * apart, axis=0)) / devices
    return spread(mean, 0, groups), lax.rsqrt(spread(variance, 0, groups) + EPS_BN)


def read_sums(recv_ref):
    return jnp.sum(recv_ref[...].astype(F32), axis=0)


def share(payload):
    devices = lax.axis_size("dp") * lax.axis_size("fsdp")
    copies = jnp.broadcast_to(payload[None], (devices, *payload.shape))
    return lax.all_to_all(copies, BOTH, 0, 0)


def as_tile(block):
    return block.reshape(MAP, TILE, LANE)


def sum_columns(x_ref, w_ref, transposed, h_scr, stat_scr):
    columns = stat_scr.shape[1]

    def step(index, carry):
        at = chunk_at(index)
        if transposed:
            h_scr[...] = dot_nt(x_ref[...], w_ref[at, :WIDTH])
        else:
            h_scr[...] = dot(x_ref[...], w_ref[:WIDTH, at])
        hidden = h_scr[...]
        stat_scr[0:1, at] = jnp.sum(hidden, axis=0, keepdims=True)
        stat_scr[1:2, at] = jnp.sum(hidden * hidden, axis=0, keepdims=True)
        return carry

    lax.fori_loop(0, columns // CHUNK, step, 0)


def enter_kernel(images_ref, partner_ref, mix_ref, mats_ref, x_ref, pay_ref, xb_scr, h_scr, stat_scr):
    count = images_ref.shape[0]
    pixels = images_ref[...]
    row = lax.broadcasted_iota(jnp.int32, (ROWS, count), 0)
    column = lax.broadcasted_iota(jnp.int32, (ROWS, count), 1)
    place = lax.shift_right_logical(row, 3)
    inside = jnp.bitwise_and(row, 7)
    pair = mix_ref[...].astype(F32)
    mixing = pair[:, 0:1] / (pair[:, 0:1] + pair[:, 1:2])
    for tile in range(count // ROWS):
        near = slice(tile * TILE, (tile + 1) * TILE)
        other = jnp.concatenate([partner_ref[near, :]] * MAP, axis=0)
        weight = jnp.concatenate([mixing[near, :]] * MAP, axis=0)
        own_hot = jnp.where(column == (tile * TILE + inside) * MAP + place, 1.0, 0.0).astype(BF16)
        other_hot = jnp.where(column == other * MAP + place, 1.0, 0.0).astype(BF16)
        mixed = weight * dot(own_hot, pixels) + (1.0 - weight) * dot(other_hot, pixels)
        x_ref[tile * ROWS : (tile + 1) * ROWS, :] = mixed
    xb_scr[...] = x_ref[...].astype(BF16)
    sum_columns(xb_scr, mats_ref, False, h_scr, stat_scr)
    pay_ref[...] = pack_moments(stat_scr[0:1, :], stat_scr[1:2, :], count)


def enter(images, partner, mix_pair, mats):
    count = images.shape[0]
    return call(
        enter_kernel,
        [shape((count, WIDTH)), shape((moment_rows(EXPAND), LANE), BF16)],
        [images, partner, mix_pair, mats],
        [pltpu.VMEM((count, WIDTH), BF16), pltpu.VMEM((count, CHUNK), F32), pltpu.VMEM((8, EXPAND), F32)],
    )


def tap_terms():
    for row in range(EDGE):
        for col in range(EDGE):
            for row_shift in range(3):
                for col_shift in range(3):
                    from_row, from_col = row + row_shift - 1, col + col_shift - 1
                    if 0 <= from_row < EDGE and 0 <= from_col < EDGE:
                        yield EDGE * row + col, 3 * row_shift + col_shift, EDGE * from_row + from_col


TERMS = list(tap_terms())


def spatial_kernel(x_ref, mats_ref, side_ref, recv_ref, d_ref, pay_ref, norm_ref, xb_scr, h_scr, row_scr, stat_scr):
    count = x_ref.shape[0]
    xb_scr[...] = x_ref[...].astype(BF16)
    rows = side_ref[2 * SQUEEZE : SIDE_PAD, :].astype(F32)
    mean, inverse = read_moments(recv_ref, EXPAND, count)
    norm_ref[0:1, :] = mean
    norm_ref[1:2, :] = inverse
    scale = inverse * rows[10:11, :]
    row_scr[0:9, :] = rows[0:9, :]
    row_scr[9:10, :] = scale
    row_scr[10:11, :] = rows[11:12, :] - mean * scale

    def step(index, carry):
        h_scr[...] = dot(xb_scr[...], mats_ref[:WIDTH, chunk_at(index)])
        for part in range(CHUNK // LANE):
            lanes = chunk_at(index * (CHUNK // LANE) + part, LANE)
            taps = [jnp.broadcast_to(row_scr[k : k + 1, lanes], (TILE, LANE)) for k in range(9)]
            scale_row = row_scr[9:10, lanes]
            shift_row = row_scr[10:11, lanes]

            def tile_step(tile, sums):
                at = chunk_at(tile, ROWS)
                pre = h_scr[at, part * LANE : (part + 1) * LANE] * scale_row + shift_row
                active = as_tile(pre * sigmoid(pre))
                result = [None] * MAP
                for target, tap, source in TERMS:
                    term = active[source] * taps[tap]
                    result[target] = term if result[target] is None else result[target] + term
                total, squares = sums
                for value in result:
                    total = total + value
                    squares = squares + value * value
                d_ref[at, lanes] = jnp.concatenate(result, axis=0).astype(BF16)
                return total, squares

            zero = jnp.zeros((TILE, LANE), F32)
            total, squares = lax.fori_loop(0, count // ROWS, tile_step, (zero, zero))
            stat_scr[0:1, lanes] = jnp.sum(total, axis=0, keepdims=True)
            stat_scr[1:2, lanes] = jnp.sum(squares, axis=0, keepdims=True)
        return carry

    lax.fori_loop(0, EXPAND // CHUNK, step, 0)
    pay_ref[...] = pack_moments(stat_scr[0:1, :], stat_scr[1:2, :], count)


def spatial(x, mats, side, recv):
    count = x.shape[0]
    return call(
        spatial_kernel,
        [shape((count, EXPAND), BF16), shape((moment_rows(EXPAND), LANE), BF16), shape((8, EXPAND))],
        [x, mats, side, recv],
        [
            pltpu.VMEM((count, WIDTH), BF16),
            pltpu.VMEM((count, CHUNK), F32),
            pltpu.VMEM((16, EXPAND), F32),
            pltpu.VMEM((8, EXPAND), F32),
        ],
    )


def project_kernel(
    d_ref, mats_ref, side_ref, vec_ref, recv_ref,
    p_ref, pay_ref, norm_ref, pooled_ref, excite_ref, squeeze_ref,
    a_scr, y_scr, row_scr,
):
    count = d_ref.shape[0]
    tiles = count // ROWS
    rows = side_ref[2 * SQUEEZE : SIDE_PAD, :].astype(F32)
    mean, inverse = read_moments(recv_ref, EXPAND, count)
    norm_ref[0:1, :] = mean
    norm_ref[1:2, :] = inverse
    scale = inverse * rows[12:13, :]
    row_scr[0:1, :] = scale
    row_scr[1:2, :] = rows[13:14, :] - mean * scale

    def activate(index, carry):
        lanes = chunk_at(index, LANE)
        scale_row = row_scr[0:1, lanes]
        shift_row = row_scr[1:2, lanes]
        for tile in range(tiles):
            at = slice(tile * ROWS, (tile + 1) * ROWS)
            pre = d_ref[at, lanes].astype(F32) * scale_row + shift_row
            active = pre * sigmoid(pre)
            a_scr[at, lanes] = active
            pooled_ref[tile * TILE : (tile + 1) * TILE, lanes] = jnp.sum(as_tile(active), axis=0) / MAP
        return carry

    lax.fori_loop(0, EXPAND // LANE, activate, 0)
    reduce_mat = side_ref[0:SQUEEZE, :]
    excite_mat = side_ref[SQUEEZE : 2 * SQUEEZE, :]
    high, low = halves(pooled_ref[...])
    before = dot_nt(high, reduce_mat) + dot_nt(low, reduce_mat) + vec_ref[2:3, :SQUEEZE]
    squeeze_ref[...] = before
    high, low = halves(before * sigmoid(before))
    excite_ref[...] = sigmoid(dot(high, excite_mat) + dot(low, excite_mat) + rows[9:10, :])

    def gate(index, carry):
        lanes = chunk_at(index, LANE)
        for tile in range(tiles):
            at = slice(tile * ROWS, (tile + 1) * ROWS)
            factor = excite_ref[tile * TILE : (tile + 1) * TILE, lanes]
            scaled = as_tile(a_scr[at, lanes]) * factor[None]
            y_scr[at, lanes] = scaled.reshape(ROWS, LANE).astype(BF16)
        return carry

    lax.fori_loop(0, EXPAND // LANE, gate, 0)
    projected = dot_nt(y_scr[...], mats_ref[WIDTH:, :])
    p_ref[...] = projected
    total = jnp.sum(projected, axis=0, keepdims=True)
    squares = jnp.sum(projected * projected, axis=0, keepdims=True)
    pay_ref[...] = pack_moments(total, squares, count)


def project(d, mats, side, vec, recv):
    count = d.shape[0]
    images = count // MAP
    return call(
        project_kernel,
        [
            shape((count, WIDTH)),
            shape((moment_rows(WIDTH), LANE), BF16),
            shape((8, EXPAND)),
            shape((images, EXPAND)),
            shape((images, EXPAND)),
            shape((images, SQUEEZE)),
        ],
        [d, mats, side, vec, recv],
        [
            pltpu.VMEM((count, EXPAND), F32),
            pltpu.VMEM((count, EXPAND), BF16),
            pltpu.VMEM((8, EXPAND), F32),
        ],
    )


def residual_kernel(transposed, x_ref, p_ref, vec_ref, recv_ref, w_ref, out_ref, pay_ref, norm_ref, cross_ref, xb_scr, h_scr, stat_scr):
    count = x_ref.shape[0]
    mean, inverse = read_moments(recv_ref, WIDTH, count)
    norm_ref[0:1, :] = mean
    norm_ref[1:2, :] = inverse
    normed = (p_ref[...] - mean) * inverse
    result = x_ref[...] + (normed * vec_ref[0:1, :] + vec_ref[1:2, :])
    out_ref[...] = result
    xb_scr[...] = result.astype(BF16)
    high, low = halves(normed)
    cross_ref[...] = dot_tn(high, xb_scr[...]) + dot_tn(low, xb_scr[...])
    sum_columns(xb_scr, w_ref, transposed, h_scr, stat_scr)
    pay_ref[...] = pack_moments(stat_scr[0:1, :], stat_scr[1:2, :], count)


def residual(x, p, vec, recv, weights, transposed):
    count = x.shape[0]
    columns = HEAD if transposed else EXPAND
    return call(
        functools.partial(residual_kernel, transposed),
        [
            shape((count, WIDTH)),
            shape((moment_rows(columns), LANE), BF16),
            shape((8, WIDTH)),
            shape((WIDTH, WIDTH)),
        ],
        [x, p, vec, recv, weights],
        [pltpu.VMEM((count, WIDTH), BF16), pltpu.VMEM((count, CHUNK), F32), pltpu.VMEM((8, columns), F32)],
    )


def head_rows(head_ref):
    pick_row = lax.broadcasted_iota(jnp.int32, (TILE, LANE), 0)
    pick_col = lax.broadcasted_iota(jnp.int32, (TILE, LANE), 1)
    first = WIDTH + CLASSES - (HEADPAD - LANE)
    pick = jnp.where((pick_col == pick_row + first) & (pick_row < 2), 1.0, 0.0).astype(BF16)
    return dot_nt(pick, head_ref[:, HEADPAD - LANE :])


def head_kernel(
    image_count, x_ref, head_ref, bias_ref, label_col_ref, label_row_ref, partner_ref, mix_ref,
    p_ref, norm3_ref, recv_ref,
    dz_ref, pay_ref, norm_ref, grad_fc_ref,
    xb_scr, h_scr, f_scr, g_scr, q_scr, row_scr, stat_scr,
):
    count = x_ref.shape[0]
    tiles = count // ROWS
    images = count // MAP
    xb_scr[...] = x_ref[...].astype(BF16)
    mean, inverse = read_moments(recv_ref, HEAD, count)
    gain_bias = head_rows(head_ref)
    norm_ref[0:1, :] = mean
    norm_ref[1:2, :] = inverse
    scale = inverse * gain_bias[0:1, :]
    norm_ref[2:3, :] = gain_bias[0:1, :]
    row_scr[0:1, :] = scale
    row_scr[1:2, :] = gain_bias[1:2, :] - mean * scale
    row_scr[2:3, :] = mean

    def features(index, carry):
        at_chunk = chunk_at(index)
        h_scr[:, at_chunk] = dot_nt(xb_scr[...], head_ref[at_chunk, :WIDTH])
        for part in range(CHUNK // LANE):
            lanes = chunk_at(index * (CHUNK // LANE) + part, LANE)
            scale_row = row_scr[0:1, lanes]
            shift_row = row_scr[1:2, lanes]
            for tile in range(tiles):
                pre = h_scr[tile * ROWS : (tile + 1) * ROWS, lanes] * scale_row + shift_row
                active = as_tile(pre * sigmoid(pre))
                f_scr[tile * TILE : (tile + 1) * TILE, lanes] = jnp.sum(active, axis=0) / MAP
        return carry

    lax.fori_loop(0, HEAD // CHUNK, features, 0)
    features_low = f_scr[...].astype(BF16)
    classifier = head_ref[:, WIDTH:]
    ids = lax.broadcasted_iota(jnp.int32, (images, LOGITS), 1)
    logits = dot(features_low, classifier) + bias_ref[...]
    logits = jnp.where(ids < CLASSES, logits, -1e30)
    row_max = jnp.max(logits, axis=1, keepdims=True)
    log_total = row_max + jnp.log(jnp.sum(jnp.exp(logits - row_max), axis=1, keepdims=True))
    pair = mix_ref[...].astype(F32)
    mixing = pair[:, 0:1] / (pair[:, 0:1] + pair[:, 1:2])
    people = lax.broadcasted_iota(jnp.int32, (images, images), 1)
    label_row = jnp.broadcast_to(label_row_ref[...].astype(F32), (images, images))
    partner_label = jnp.sum(
        jnp.where(people == partner_ref[...], label_row, 0.0), axis=1, keepdims=True
    ).astype(jnp.int32)
    own_hot = jnp.where(ids == label_col_ref[...], 1.0, 0.0)
    other_hot = jnp.where(ids == partner_label, 1.0, 0.0)
    own_logit = jnp.sum(own_hot * logits, axis=1, keepdims=True)
    other_logit = jnp.sum(other_hot * logits, axis=1, keepdims=True)
    loss = mixing * (log_total - own_logit) + (1.0 - mixing) * (log_total - other_logit)
    loss = jnp.sum(loss, axis=0, keepdims=True)
    grad_logits = (
        jnp.exp(logits - log_total) - mixing * own_hot - (1.0 - mixing) * other_hot
    ) / image_count
    grad_low = grad_logits.astype(BF16)
    grad_fc_ref[...] = dot_tn(features_low, grad_low).astype(BF16)
    g_scr[...] = dot_nt(grad_low, classifier) / MAP
    bias_sum = jnp.sum(grad_logits, axis=0, keepdims=True)
    bias_ids = lax.broadcasted_iota(jnp.int32, (1, LOGITS), 1)
    loss_high = loss.astype(BF16).astype(F32)
    bias_sum = jnp.where(bias_ids == CLASSES, loss_high, bias_sum)
    bias_sum = jnp.where(bias_ids == CLASSES + 1, loss - loss_high, bias_sum)

    def back(index, carry):
        lanes = chunk_at(index, LANE)
        scale_row = row_scr[0:1, lanes]
        shift_row = row_scr[1:2, lanes]
        mean_row = row_scr[2:3, lanes]
        total = jnp.zeros((TILE, LANE), F32)
        weighted = jnp.zeros((TILE, LANE), F32)
        for tile in range(tiles):
            at = slice(tile * ROWS, (tile + 1) * ROWS)
            hidden = h_scr[at, lanes]
            pre = hidden * scale_row + shift_row
            gate = sigmoid(pre)
            slope = as_tile(gate * (1.0 + pre * (1.0 - gate)))
            grad = slope * g_scr[tile * TILE : (tile + 1) * TILE, lanes][None]
            total = total + jnp.sum(grad, axis=0)
            weighted = weighted + jnp.sum(grad * as_tile(hidden - mean_row), axis=0)
            flat = grad.reshape(ROWS, LANE)
            dz_ref[at, lanes] = flat.astype(BF16)
            q_scr[at, lanes] = (flat * scale_row).astype(BF16)
        stat_scr[0:1, lanes] = jnp.sum(total, axis=0, keepdims=True)
        stat_scr[1:2, lanes] = jnp.sum(weighted, axis=0, keepdims=True)
        return carry

    lax.fori_loop(0, HEAD // LANE, back, 0)
    below = dot(q_scr[...], head_ref[:, :WIDTH])
    normed = (p_ref[...] - norm3_ref[0:1, :]) * norm3_ref[1:2, :]
    below_sum = jnp.sum(below, axis=0, keepdims=True)
    below_gain = jnp.sum(below * normed, axis=0, keepdims=True)
    pay_ref[...] = fold(
        [stat_scr[0:1, :], stat_scr[1:2, :] * inverse, below_sum, below_gain, bias_sum], 32
    ).astype(BF16)


def head(x, head_full, bias, label_col, label_row, partner, mix_pair, p, norm3, recv, image_count):
    count = x.shape[0]
    images = count // MAP
    return call(
        functools.partial(head_kernel, image_count),
        [
            shape((count, HEAD), BF16),
            shape((32, LANE), BF16),
            shape((8, HEAD)),
            shape((HEAD, LOGITS), BF16),
        ],
        [x, head_full, bias, label_col, label_row, partner, mix_pair, p, norm3, recv],
        [
            pltpu.VMEM((count, WIDTH), BF16),
            pltpu.VMEM((count, HEAD), F32),
            pltpu.VMEM((images, HEAD), F32),
            pltpu.VMEM((images, HEAD), F32),
            pltpu.VMEM((count, HEAD), BF16),
            pltpu.VMEM((8, HEAD), F32),
            pltpu.VMEM((8, HEAD), F32),
        ],
    )


def upper_back(
    is_head, row_count, x_ref, w_ref, dz_ref, norm_ref, gain, sums, columns,
    xb_scr, xt_scr, h_scr, row_scr, dh_scr, grad_w_ref, glob_ref,
):
    groups = columns // LANE
    sum_bias = spread(sums, 0, groups)
    sum_gain = spread(sums, groups, groups)
    glob_ref[0:1, :] = sum_gain
    glob_ref[1:2, :] = sum_bias
    mean = norm_ref[0:1, :]
    inverse = norm_ref[1:2, :]
    scale = inverse * gain
    slant = scale * inverse * (sum_gain / row_count)
    row_scr[0:1, :columns] = scale
    row_scr[1:2, :columns] = slant
    row_scr[2:3, :columns] = mean * slant - scale * (sum_bias / row_count)
    xb_scr[...] = x_ref[...].astype(BF16)
    xt_scr[...] = xb_scr[...].T

    def step(index, carry):
        at = chunk_at(index)
        if is_head:
            h_scr[...] = dot_nt(xb_scr[...], w_ref[at, :WIDTH])
        else:
            h_scr[...] = dot(xb_scr[...], w_ref[:WIDTH, at])
        grad = (
            dz_ref[:, at].astype(F32) * row_scr[0:1, at]
            - h_scr[...] * row_scr[1:2, at]
            + row_scr[2:3, at]
        )
        low = grad.astype(BF16)
        dh_scr[:, at] = low
        if is_head:
            grad_w_ref[at, :] = dot_tn(low, xb_scr[...]).astype(BF16)
        else:
            grad_w_ref[:, at] = dot(xt_scr[...], low).astype(BF16)
        return carry

    lax.fori_loop(0, columns // CHUNK, step, 0)
    return scale * sum_bias, slant * row_count


def gate_kernel(
    is_head, row_count,
    recv_ref, x_ref, w_ref, dz_ref, norm_ref, upside_ref, cross_ref, stream_ref,
    p_ref, norm3_ref, vec_ref, mats_ref, d_ref, norm2_ref, side_ref, pooled_ref, excite_ref, squeeze_ref,
    dz2_ref, pay_ref, stream_out_ref, grad_w_ref, grad_p_ref, grad_side_ref, grad_sb_ref, glob_ref, glob3_ref,
    xb_scr, xt_scr, h_scr, row_scr, dh_scr, u_scr, slope_scr, y_scr, gp_scr, gt_scr, ge_scr, pool_scr, stat_scr,
):
    columns = HEAD if is_head else EXPAND
    groups = columns // LANE
    count = x_ref.shape[0]
    tiles = count // ROWS
    sums = read_sums(recv_ref)
    if is_head:
        gain = norm_ref[2:3, :]
    else:
        gain = upside_ref[2 * SQUEEZE : SIDE_PAD, :].astype(F32)[10:11, :]
    bias_pull, slant = upper_back(
        is_head, row_count, x_ref, w_ref, dz_ref, norm_ref, gain, sums, columns,
        xb_scr, xt_scr, h_scr, row_scr, dh_scr, grad_w_ref, glob_ref,
    )
    if is_head:
        weights_t = w_ref[:, :WIDTH]
        slanted = weights_t.astype(F32) * jnp.broadcast_to(slant, (TILE, columns)).T[:, 0:1]
        high, low = halves(slanted)
        spread_mat = dot_tn(high, weights_t) + dot_tn(low, weights_t)
        pull = jnp.dot(jnp.broadcast_to(bias_pull, (TILE, columns)), weights_t.astype(F32),
                       preferred_element_type=F32, precision=HIGHEST)[0:1, :]
        stream = dot(dh_scr[:, :columns], weights_t)
    else:
        weights = w_ref[:WIDTH, :]
        high, low = halves(weights.astype(F32) * slant)
        spread_mat = dot_nt(high, weights) + dot_nt(low, weights)
        pull = lax.dot_general(jnp.broadcast_to(bias_pull, (TILE, columns)), weights.astype(F32), NT,
                               preferred_element_type=F32, precision=HIGHEST)[0:1, :]
        stream = stream_ref[...] + dot_nt(dh_scr[:, :columns], weights)
    stream_out_ref[...] = stream
    sum_bias = spread(sums, 2 * groups, WIDTH // LANE) - pull
    corrected = jnp.sum(cross_ref[...].T * spread_mat, axis=0, keepdims=True) / row_count
    sum_gain = spread(sums, 2 * groups + WIDTH // LANE, WIDTH // LANE) - corrected
    glob3_ref[0:1, :] = sum_gain
    glob3_ref[1:2, :] = sum_bias
    if is_head:
        glob3_ref[2:6, :] = jnp.concatenate(
            [spread(sums, 2 * groups + 4 + 2 * k, 2) for k in range(LOGITS // WIDTH)], axis=0
        )
    inverse3 = norm3_ref[1:2, :]
    normed = (p_ref[...] - norm3_ref[0:1, :]) * inverse3
    grad_p = (inverse3 * vec_ref[0:1, :]) * (
        stream - sum_bias / row_count - normed * (sum_gain / row_count)
    )
    gp_scr[...] = grad_p.astype(BF16)
    gt_scr[...] = gp_scr[...].T

    rows = side_ref[2 * SQUEEZE : SIDE_PAD, :].astype(F32)
    mean2 = norm2_ref[0:1, :]
    scale2 = norm2_ref[1:2, :] * rows[12:13, :]
    row_scr[0:1, :EXPAND] = scale2
    row_scr[1:2, :EXPAND] = rows[13:14, :] - mean2 * scale2
    row_scr[2:3, :EXPAND] = mean2

    def first(index, carry):
        at_chunk = chunk_at(index)
        h_scr[...] = dot(gp_scr[...], mats_ref[WIDTH:, at_chunk])
        for part in range(CHUNK // LANE):
            lanes = chunk_at(index * (CHUNK // LANE) + part, LANE)
            scale_row = row_scr[0:1, lanes]
            shift_row = row_scr[1:2, lanes]
            for tile in range(tiles):
                at = slice(tile * ROWS, (tile + 1) * ROWS)
                near = slice(tile * TILE, (tile + 1) * TILE)
                pre = d_ref[at, lanes].astype(F32) * scale_row + shift_row
                gate = sigmoid(pre)
                active = pre * gate
                slope = gate + active - active * gate
                grad = h_scr[at, part * LANE : (part + 1) * LANE]
                factor = excite_ref[near, lanes]
                ge_scr[near, lanes] = jnp.sum(as_tile(grad * active), axis=0)
                y_scr[at, lanes] = (as_tile(active) * factor[None]).reshape(ROWS, LANE).astype(BF16)
                slope_scr[at, lanes] = slope
                u_scr[at, lanes] = (as_tile(grad * slope) * factor[None]).reshape(ROWS, LANE)
        grad_p_ref[:, at_chunk] = dot(gt_scr[...], y_scr[:, at_chunk]).astype(BF16)
        return carry

    lax.fori_loop(0, EXPAND // CHUNK, first, 0)
    excite = excite_ref[...]
    grad_gate = ge_scr[...] * excite * (1.0 - excite)
    before = squeeze_ref[...]
    opened = sigmoid(before)
    squeezed = before * opened
    reduce_mat = side_ref[0:SQUEEZE, :]
    excite_mat = side_ref[SQUEEZE : 2 * SQUEEZE, :]
    high, low = halves(grad_gate)
    grad_squeezed = dot_nt(high, excite_mat) + dot_nt(low, excite_mat)
    grad_pre = grad_squeezed * (opened * (1.0 + before * (1.0 - opened)))
    squeezed_high, squeezed_low = halves(squeezed)
    grad_excite = dot_tn(squeezed_high, high) + dot_tn(squeezed_low, high) + dot_tn(squeezed_high, low)
    pre_high, pre_low = halves(grad_pre)
    pooled_high, pooled_low = halves(pooled_ref[...])
    grad_reduce = (
        dot_tn(pre_high, pooled_high) + dot_tn(pre_low, pooled_high) + dot_tn(pre_high, pooled_low)
    )
    grad_side_ref[0:SQUEEZE, :] = grad_reduce.astype(BF16)
    grad_side_ref[SQUEEZE : 2 * SQUEEZE, :] = grad_excite.astype(BF16)
    grad_sb_ref[0:1, :] = jnp.sum(grad_gate, axis=0, keepdims=True)
    grad_sb_ref[1:2, :SQUEEZE] = jnp.sum(grad_pre, axis=0, keepdims=True)
    grad_sb_ref[1:2, SQUEEZE:] = jnp.zeros((1, EXPAND - SQUEEZE), F32)
    pool_scr[...] = (dot(pre_high, reduce_mat) + dot(pre_low, reduce_mat)) / MAP

    def second(index, carry):
        lanes = chunk_at(index, LANE)
        mean_row = row_scr[2:3, lanes]
        total = jnp.zeros((TILE, LANE), F32)
        weighted = jnp.zeros((TILE, LANE), F32)
        for tile in range(tiles):
            at = slice(tile * ROWS, (tile + 1) * ROWS)
            pool = pool_scr[tile * TILE : (tile + 1) * TILE, lanes]
            grad = as_tile(u_scr[at, lanes]) + as_tile(slope_scr[at, lanes]) * pool[None]
            total = total + jnp.sum(grad, axis=0)
            weighted = weighted + jnp.sum(
                grad * as_tile(d_ref[at, lanes].astype(F32) - mean_row), axis=0
            )
            dz2_ref[at, lanes] = grad.reshape(ROWS, LANE).astype(BF16)
        stat_scr[0:1, lanes] = jnp.sum(total, axis=0, keepdims=True)
        stat_scr[1:2, lanes] = jnp.sum(weighted, axis=0, keepdims=True)
        return carry

    lax.fori_loop(0, EXPAND // LANE, second, 0)
    pay_ref[...] = fold(
        [stat_scr[0:1, :], stat_scr[1:2, :] * norm2_ref[1:2, :]], 24
    ).astype(BF16)


def gate_back(is_head, row_count, recv, upper, cross, stream, lower):
    count = upper["x"].shape[0]
    images = count // MAP
    columns = HEAD if is_head else EXPAND
    grad_w = (HEAD, WIDTH) if is_head else (WIDTH, EXPAND)
    return call(
        functools.partial(gate_kernel, is_head, row_count),
        [
            shape((count, EXPAND), BF16),
            shape((24, LANE), BF16),
            shape((count, WIDTH)),
            shape(grad_w, BF16),
            shape((WIDTH, EXPAND), BF16),
            shape((2 * SQUEEZE, EXPAND), BF16),
            shape((8, EXPAND)),
            shape((8, columns)),
            shape((8, WIDTH)),
        ],
        [
            recv, upper["x"], upper["weights"], upper["dz"], upper["norm"], upper["side"], cross, stream,
            lower["p"], lower["norm3"], lower["vec"], lower["mats"], lower["d"], lower["norm2"],
            lower["side"], lower["pooled"], lower["excite"], lower["squeeze"],
        ],
        [
            pltpu.VMEM((count, WIDTH), BF16),
            pltpu.VMEM((WIDTH, count), BF16),
            pltpu.VMEM((count, CHUNK), F32),
            pltpu.VMEM((8, EXPAND), F32),
            pltpu.VMEM((count, EXPAND), BF16),
            pltpu.VMEM((count, EXPAND), F32),
            pltpu.VMEM((count, EXPAND), F32),
            pltpu.VMEM((count, EXPAND), BF16),
            pltpu.VMEM((count, WIDTH), BF16),
            pltpu.VMEM((WIDTH, count), BF16),
            pltpu.VMEM((images, EXPAND), F32),
            pltpu.VMEM((images, EXPAND), F32),
            pltpu.VMEM((8, EXPAND), F32),
        ],
    )


def tap_kernel(
    is_first, row_count,
    recv_ref, dz2_ref, d_ref, norm2_ref, x_ref, mats_ref, norm1_ref, side_ref, stream_ref, p_ref, norm3_ref,
    dz_ref, pay_ref, taps_ref, glob_ref,
    xb_scr, h_scr, row_scr, q_scr, stat_scr,
):
    count = x_ref.shape[0]
    groups = EXPAND // LANE
    sums = read_sums(recv_ref)
    sum_bias = spread(sums, 0, groups)
    sum_gain = spread(sums, groups, groups)
    glob_ref[0:1, :] = sum_gain
    glob_ref[1:2, :] = sum_bias
    rows = side_ref[2 * SQUEEZE : SIDE_PAD, :].astype(F32)
    mean2 = norm2_ref[0:1, :]
    inverse2 = norm2_ref[1:2, :]
    scale2 = inverse2 * rows[12:13, :]
    slant2 = scale2 * inverse2 * (sum_gain / row_count)
    mean1 = norm1_ref[0:1, :]
    scale1 = norm1_ref[1:2, :] * rows[10:11, :]
    row_scr[0:9, :] = rows[0:9, :]
    row_scr[9:10, :] = scale2
    row_scr[10:11, :] = slant2
    row_scr[11:12, :] = mean2 * slant2 - scale2 * (sum_bias / row_count)
    row_scr[12:13, :] = scale1
    row_scr[13:14, :] = rows[11:12, :] - mean1 * scale1
    row_scr[14:15, :] = mean1
    xb_scr[...] = x_ref[...].astype(BF16)

    def step(index, carry):
        h_scr[...] = dot(xb_scr[...], mats_ref[:WIDTH, chunk_at(index)])
        for part in range(CHUNK // LANE):
            lanes = chunk_at(index * (CHUNK // LANE) + part, LANE)
            near = slice(part * LANE, (part + 1) * LANE)
            taps = [jnp.broadcast_to(row_scr[k : k + 1, lanes], (TILE, LANE)) for k in range(9)]

            def tile_step(tile, sums_in):
                at = chunk_at(tile, ROWS)
                grad_d = as_tile(
                    dz2_ref[at, lanes].astype(F32) * row_scr[9:10, lanes]
                    - d_ref[at, lanes].astype(F32) * row_scr[10:11, lanes]
                    + row_scr[11:12, lanes]
                )
                hidden = h_scr[at, near]
                pre = hidden * row_scr[12:13, lanes] + row_scr[13:14, lanes]
                gate = sigmoid(pre)
                flat = pre * gate
                active = as_tile(flat)
                slope = as_tile(gate + flat - flat * gate)
                apart = as_tile(hidden - row_scr[14:15, lanes])
                grad_a = [None] * MAP
                tap_sums = [None] * 9
                for target, tap, source in TERMS:
                    term = grad_d[target] * taps[tap]
                    grad_a[source] = term if grad_a[source] is None else grad_a[source] + term
                    term = grad_d[target] * active[source]
                    tap_sums[tap] = term if tap_sums[tap] is None else tap_sums[tap] + term
                total, weighted = sums_in[9], sums_in[10]
                grads = []
                for place in range(MAP):
                    grad = grad_a[place] * slope[place]
                    total = total + grad
                    weighted = weighted + grad * apart[place]
                    grads.append(grad)
                grad = jnp.concatenate(grads, axis=0)
                dz_ref[at, lanes] = grad.astype(BF16)
                if not is_first:
                    q_scr[at, lanes] = (grad * row_scr[12:13, lanes]).astype(BF16)
                return (*[sums_in[k] + tap_sums[k] for k in range(9)], total, weighted)

            zero = jnp.zeros((TILE, LANE), F32)
            result = lax.fori_loop(0, count // ROWS, tile_step, (zero,) * 11)
            for k in range(9):
                taps_ref[k : k + 1, lanes] = jnp.sum(result[k], axis=0, keepdims=True)
            stat_scr[0:1, lanes] = jnp.sum(result[9], axis=0, keepdims=True)
            stat_scr[1:2, lanes] = jnp.sum(result[10], axis=0, keepdims=True)
        return carry

    lax.fori_loop(0, EXPAND // CHUNK, step, 0)
    vectors = [stat_scr[0:1, :], stat_scr[1:2, :] * norm1_ref[1:2, :]]
    if not is_first:
        below = stream_ref[...] + dot_nt(q_scr[...], mats_ref[:WIDTH, :])
        normed = (p_ref[...] - norm3_ref[0:1, :]) * norm3_ref[1:2, :]
        vectors.append(jnp.sum(below, axis=0, keepdims=True))
        vectors.append(jnp.sum(below * normed, axis=0, keepdims=True))
    pay_ref[...] = fold(vectors, pay_ref.shape[0]).astype(BF16)


def tap_back(is_first, row_count, recv, dz2, layer, stream, below):
    count = dz2.shape[0]
    return call(
        functools.partial(tap_kernel, is_first, row_count),
        [
            shape((count, EXPAND), BF16),
            shape((24 if is_first else 32, LANE), BF16),
            shape((16, EXPAND)),
            shape((8, EXPAND)),
        ],
        [
            recv, dz2, layer["d"], layer["norm2"], layer["x"], layer["mats"], layer["norm1"], layer["side"],
            stream, below["p"], below["norm3"],
        ],
        [
            pltpu.VMEM((count, WIDTH), BF16),
            pltpu.VMEM((count, CHUNK), F32),
            pltpu.VMEM((16, EXPAND), F32),
            pltpu.VMEM((count, EXPAND), BF16),
            pltpu.VMEM((8, EXPAND), F32),
        ],
    )


def last_kernel(
    row_count, recv_ref, x_ref, w_ref, dz_ref, norm_ref, side_ref,
    grad_w_ref, glob_ref, xb_scr, xt_scr, h_scr, row_scr, dh_scr,
):
    gain = side_ref[2 * SQUEEZE : SIDE_PAD, :].astype(F32)[10:11, :]
    upper_back(
        False, row_count, x_ref, w_ref, dz_ref, norm_ref, gain, read_sums(recv_ref), EXPAND,
        xb_scr, xt_scr, h_scr, row_scr, dh_scr, grad_w_ref, glob_ref,
    )


def last_back(row_count, recv, layer, dz):
    count = dz.shape[0]
    return call(
        functools.partial(last_kernel, row_count),
        [shape((WIDTH, EXPAND), BF16), shape((8, EXPAND))],
        [recv, layer["x"], layer["mats"], dz, layer["norm1"], layer["side"]],
        [
            pltpu.VMEM((count, WIDTH), BF16),
            pltpu.VMEM((WIDTH, count), BF16),
            pltpu.VMEM((count, CHUNK), F32),
            pltpu.VMEM((8, EXPAND), F32),
            pltpu.VMEM((count, EXPAND), BF16),
        ],
    )


def lamb_moments(weight, moment_one, moment_two, gradient, decay_mask, step_float):
    first_new = BETA_ONE * moment_one + (1.0 - BETA_ONE) * gradient
    second_new = BETA_TWO * moment_two + (1.0 - BETA_TWO) * gradient * gradient
    corrected = (
        first_new
        / (1.0 - BETA_ONE**step_float)
        / (jnp.sqrt(second_new / (1.0 - BETA_TWO**step_float)) + EPS_ADAM)
    )
    return (first_new, second_new, corrected + DECAY_RATE * decay_mask * weight)


def group_sums(mats, side, head, row_ids):
    rows = jnp.sum(mats * mats, axis=2)
    is_expand = (row_ids < WIDTH)[None, :]
    side_rows = jnp.sum(side * side, axis=2)
    head_cols = jnp.sum(head * head, axis=0)
    per_layer = jnp.stack(
        [
            jnp.sum(jnp.where(is_expand, rows, 0.0), axis=1),
            jnp.sum(jnp.where(is_expand, 0.0, rows), axis=1),
            jnp.sum(side_rows[:, :9], axis=1),
            jnp.sum(side_rows[:, 9 : 9 + SQUEEZE], axis=1),
            jnp.sum(side_rows[:, 9 + SQUEEZE : 9 + 2 * SQUEEZE], axis=1),
        ],
        axis=1,
    )
    tail = jnp.stack([jnp.sum(head_cols[:WIDTH]), jnp.sum(head_cols[WIDTH : WIDTH + CLASSES])])
    return jnp.concatenate([per_layer.reshape(-1), tail])


def rate_maps(trust_ratio, row_ids):
    groups = trust_ratio[: 5 * LAYERS].reshape(LAYERS, 5)
    mats_rate = RATE_MATRIX * jnp.where(row_ids[None, :] < WIDTH, groups[:, 0:1], groups[:, 1:2])
    side_ids = jnp.arange(SIDE)[None, :]
    side_rate = jnp.where(
        side_ids < 9,
        RATE_MATRIX * groups[:, 2:3],
        jnp.where(
            side_ids < 9 + SQUEEZE,
            RATE_MATRIX * groups[:, 3:4],
            jnp.where(side_ids < 9 + 2 * SQUEEZE, RATE_MATRIX * groups[:, 4:5], RATE_VECTOR),
        ),
    )
    col_ids = jnp.arange(HEADCOLS)
    head_rate = jnp.where(
        col_ids < WIDTH,
        RATE_MATRIX * trust_ratio[5 * LAYERS],
        jnp.where(
            col_ids < WIDTH + CLASSES, RATE_MATRIX * trust_ratio[5 * LAYERS + 1], RATE_VECTOR
        ),
    )
    return (mats_rate, side_rate, head_rate)


def body(
    images, partner, mix_pair, labels, step,
    layer_mats, layer_side, layer_vecs, head_mat, fc_bias,
    mats_first, mats_second, side_first, side_second, vecs_first, vecs_second,
    head_first, head_second, bias_first, bias_second,
):
    local_images = images.shape[0]
    owners = lax.axis_size("fsdp")
    replicas = lax.axis_size("dp") * owners
    image_count = float(local_images * replicas)
    count = local_images * MAP
    row_count = float(count * replicas)
    mine = lax.axis_index("fsdp")
    side_width = layer_side.shape[2]
    vec_width = layer_vecs.shape[1]
    rows_dev = layer_mats.shape[1]

    side_low = jnp.concatenate(
        [
            layer_side[:, 9 : 9 + 2 * SQUEEZE],
            layer_side[:, :9],
            layer_side[:, 9 + 2 * SQUEEZE :],
            jnp.pad(layer_vecs, ((0, 0), (0, side_width - vec_width)))[:, None, :],
            jnp.zeros((LAYERS, 1, side_width), F32),
        ],
        axis=1,
    ).astype(BF16)
    mats_all = [
        lax.all_gather(layer_mats[k].astype(BF16), "fsdp", axis=0, tiled=True) for k in range(LAYERS)
    ]
    side_all = lax.all_gather(side_low, "fsdp", axis=2, tiled=True)
    head_full = lax.all_gather(
        jnp.pad(head_mat, ((0, 0), (0, HEADPAD - HEADCOLS))).astype(BF16), "fsdp", axis=0, tiled=True
    )
    vecs_all = side_all[:, SIDE, :].reshape(LAYERS, owners, side_width)[:, :, :vec_width]
    vecs_all = vecs_all.reshape(LAYERS, VECS).astype(F32)
    vecs_all = jnp.stack(
        [
            vecs_all[:, SQUEEZE : SQUEEZE + WIDTH],
            vecs_all[:, SQUEEZE + WIDTH :],
            jnp.pad(vecs_all[:, :SQUEEZE], ((0, 0), (0, WIDTH - SQUEEZE))),
        ],
        axis=1,
    )
    vecs_all = jnp.pad(vecs_all, ((0, 0), (0, 5), (0, 0)))

    partner_col = partner[:, None]
    layers = []
    crosses = []
    x, pay = enter(images.reshape(count, WIDTH), partner_col, mix_pair, mats_all[0])
    for k in range(LAYERS):
        mats, side, vec = mats_all[k], side_all[k], vecs_all[k]
        d, pay, norm1 = spatial(x, mats, side, share(pay))
        p, pay, norm2, pooled, excite, squeeze = project(d, mats, side, vec, share(pay))
        last = k == LAYERS - 1
        above, pay, norm3, cross = residual(
            x, p, vec, share(pay), head_full if last else mats_all[k + 1], last
        )
        crosses.append(lax.psum(cross, BOTH))
        layers.append(
            dict(
                x=x, d=d, norm1=norm1, p=p, norm2=norm2, pooled=pooled, excite=excite, squeeze=squeeze,
                norm3=norm3, mats=mats, weights=mats, side=side, vec=vec,
            )
        )
        x = above
    top = layers[-1]
    dz, pay, head_norm, grad_fc = head(
        x, head_full, jnp.pad(fc_bias, (0, LOGITS - CLASSES))[None], labels[:, None], labels[None, :],
        partner_col, mix_pair, top["p"], top["norm3"], share(pay), image_count,
    )
    upper = dict(x=x, weights=head_full, dz=dz, norm=head_norm, side=top["side"])
    stream = x
    mats_grads = [None] * LAYERS
    side_grads = [None] * LAYERS
    globs = [None] * LAYERS
    for k in reversed(range(LAYERS)):
        layer = layers[k]
        is_head = k == LAYERS - 1
        dz2, pay, stream, grad_w, grad_p, grad_side, grad_sb, glob, glob3 = gate_back(
            is_head, row_count, share(pay), upper, crosses[k], stream, layer
        )
        if is_head:
            head_glob, head_glob3, grad_head = glob, glob3, grad_w
        else:
            globs[k + 1]["one"] = glob
            mats_grads[k + 1] = (grad_w, mats_grads[k + 1])
        mats_grads[k] = grad_p
        dz, pay, taps, glob2 = tap_back(
            k == 0, row_count, share(pay), dz2, layer, stream, layers[max(k - 1, 0)]
        )
        globs[k] = dict(two=glob2, three=glob3)
        sb_row = jnp.pad(
            jnp.pad(grad_sb[1, :SQUEEZE], (0, VECS - SQUEEZE)).reshape(owners, vec_width),
            ((0, 0), (0, side_width - vec_width)),
        ).reshape(1, EXPAND)
        side_grads[k] = jnp.concatenate(
            [taps[:9].astype(BF16), grad_side, grad_sb[0:1].astype(BF16), sb_row.astype(BF16)], axis=0
        )
        upper = dict(x=layer["x"], weights=layer["mats"], dz=dz, norm=layer["norm1"], side=layer["side"])
    grad_w, globs[0]["one"] = last_back(row_count, share(pay), layers[0], dz)
    mats_grads[0] = (grad_w, mats_grads[0])

    def to_owner(array, dim):
        return lax.psum_scatter(array, "fsdp", scatter_dimension=dim, tiled=True)

    shard_mats = jnp.stack([to_owner(jnp.concatenate(pair, axis=0), 0) for pair in mats_grads])
    shard_side = jnp.stack([to_owner(array, 1) for array in side_grads])
    shard_head = to_owner(jnp.concatenate([grad_head, grad_fc], axis=1), 0)
    shard_mats, shard_side, shard_head = lax.psum((shard_mats, shard_side, shard_head), "dp")
    shard_mats = shard_mats.astype(F32)
    shard_side = shard_side.astype(F32)
    shard_head = shard_head.astype(F32)

    def own_columns(vector, width):
        return lax.dynamic_slice_in_dim(vector, mine * width, width, axis=-1)

    side_tail = jnp.stack(
        [
            own_columns(jnp.concatenate([g["one"][0:2], g["two"][0:2]], axis=0), side_width)
            for g in globs
        ]
    )
    vec_tail = jnp.stack(
        [
            own_columns(
                jnp.concatenate([jnp.zeros((SQUEEZE,), F32), g["three"][0], g["three"][1]]), vec_width
            )
            for g in globs
        ]
    )
    vec_ids = mine * vec_width + jnp.arange(vec_width)
    grad_vecs = jnp.where(
        vec_ids[None, :] < SQUEEZE, shard_side[:, SIDE - 4, :vec_width], vec_tail
    )
    grad_side = jnp.concatenate([shard_side[:, : SIDE - 4], side_tail], axis=1)
    head_tail = own_columns(head_glob[0:2], head_mat.shape[0]).T
    grad_head = jnp.concatenate([shard_head[:, : WIDTH + CLASSES], head_tail], axis=1)
    bias_loss = head_glob3[2:6].reshape(LOGITS)
    grad_bias = bias_loss[:CLASSES]
    loss_value = (bias_loss[CLASSES] + bias_loss[CLASSES + 1]) / image_count

    step_float = step[0].astype(F32)
    side_decay = (jnp.arange(SIDE) < 9 + 2 * SQUEEZE).astype(F32)[None, :, None]
    head_decay = (jnp.arange(HEADCOLS) < WIDTH + CLASSES).astype(F32)[None, :]
    mats_moment, mats_square, mats_dir = lamb_moments(
        layer_mats, mats_first, mats_second, shard_mats, 1.0, step_float
    )
    side_moment, side_square, side_dir = lamb_moments(
        layer_side, side_first, side_second, grad_side, side_decay, step_float
    )
    vecs_moment, vecs_square, vecs_dir = lamb_moments(
        layer_vecs, vecs_first, vecs_second, grad_vecs, 0.0, step_float
    )
    head_moment, head_square, head_dir = lamb_moments(
        head_mat, head_first, head_second, grad_head, head_decay, step_float
    )
    bias_moment, bias_square, bias_dir = lamb_moments(
        fc_bias, bias_first, bias_second, grad_bias, 0.0, step_float
    )
    row_ids = mine * rows_dev + jnp.arange(rows_dev)
    squares = jnp.stack(
        [
            group_sums(layer_mats, layer_side, head_mat, row_ids),
            group_sums(mats_dir, side_dir, head_dir, row_ids),
        ]
    )
    squares = jnp.broadcast_to(squares[None], (owners, *squares.shape))
    norms = jnp.sqrt(jnp.sum(lax.all_to_all(squares, "fsdp", 0, 0), axis=0))
    mats_rate, side_rate, head_rate = rate_maps(norms[0] / norms[1], row_ids)
    mats_new = layer_mats - mats_rate[:, :, None] * mats_dir
    side_new = layer_side - side_rate[:, :, None] * side_dir
    vecs_new = layer_vecs - RATE_VECTOR * vecs_dir
    head_new = head_mat - head_rate[None, :] * head_dir
    bias_new = fc_bias - RATE_VECTOR * bias_dir
    return (
        loss_value,
        mats_new, mats_moment, mats_square,
        side_new, side_moment, side_square,
        vecs_new, vecs_moment, vecs_square,
        head_new, head_moment, head_square,
        bias_new, bias_moment, bias_square,
        norms,
    )


def solution(mesh):
    rows, columns = P(None, "fsdp", None), P(None, None, "fsdp")
    vecs, heads = P(None, "fsdp"), P("fsdp", None)
    return jax.shard_map(
        body,
        mesh=mesh,
        in_specs=(
            P(BOTH, None, None), P(BOTH), P(BOTH, None), P(BOTH), P(),
            rows, columns, vecs, heads, P(),
            rows, rows, columns, columns, vecs, vecs, heads, heads, P(), P(),
        ),
        out_specs=(
            P(),
            rows, rows, rows,
            columns, columns, columns,
            vecs, vecs, vecs,
            heads, heads, heads,
            P(), P(), P(), P(),
        ),
        check_vma=False,
    )
```

```python
import functools

import jax
import jax.numpy as jnp
from jax import lax
from jax.experimental import pallas as pl
from jax.experimental.pallas import tpu as pltpu
from jax.sharding import PartitionSpec as P

WIDTH = 256
EXPAND = 1536
SQUEEZE = 64
HEAD = 1280
CLASSES = 1000
LOGITS = 1024
EDGE = 4
LAYERS = 3
MAP = 16
SIDE = 142
SIDE_PAD = 144
VECS = 576
HEADCOLS = 1258
HEADPAD = 1280

EPS_BN = 0.001
BETA_ONE = 0.9
BETA_TWO = 0.999
EPS_ADAM = 1e-06
DECAY_RATE = 0.01
RATE_MATRIX = 0.5
RATE_VECTOR = 0.25

BOTH = ("dp", "fsdp")
F32 = jnp.float32
BF16 = jnp.bfloat16
LANE = 128
TILE = 8
ROWS = MAP * TILE
CHUNK = 256
PARTS = CHUNK // LANE
VMEM_BYTES = 48 * 1024 * 1024

NT = (((1,), (1,)), ((), ()))
TN = (((0,), (0,)), ((), ()))


class Refs:
    def __init__(self, names, refs, loads, stores):
        for name, ref in zip(names, refs):
            setattr(self, name, ref)
        self.loads = loads
        self.stores = stores
        self.pending = {}

    def start(self):
        for index, (name, where) in enumerate(self.loads):
            source = getattr(self, name + "_far")
            if where is not None:
                source = source.at[where]
            copy = pltpu.make_async_copy(source, getattr(self, name), self.load_sem.at[index])
            copy.start()
            self.pending[name] = copy

    def wait(self, *names):
        for name in names:
            self.pending.pop(name).wait()

    def send(self, *names):
        for name in names:
            copy = pltpu.make_async_copy(
                getattr(self, name), getattr(self, name + "_far"), self.store_sem.at[self.stores.index(name)]
            )
            copy.start()
            self.pending["out " + name] = copy

    def finish(self):
        for name in list(self.pending):
            self.pending.pop(name).wait()


def shape(dims, dtype=F32):
    return jax.ShapeDtypeStruct(dims, dtype)


def call(kernel, ins, outs, scratch):
    near, far = pl.BlockSpec(memory_space=pltpu.VMEM), pl.BlockSpec(memory_space=pltpu.HBM)
    names, arrays, in_specs, loads, stores, extra = [], [], [], [], [], {}
    for name, (array, place) in ins.items():
        arrays.append(array)
        if isinstance(place, str) and place == "near":
            names.append(name)
            in_specs.append(near)
            continue
        names.append(name + "_far")
        in_specs.append(far)
        where = None if isinstance(place, str) else place
        dims = array.shape
        if where is not None:
            dims = tuple(
                len(range(*part.indices(size))) for part, size in zip(where, array.shape)
            )
            where = tuple(
                pl.ds(part.indices(size)[0], dim) for part, size, dim in zip(where, array.shape, dims)
            )
        loads.append((name, where))
        extra[name] = pltpu.VMEM(dims, array.dtype)
    out_shapes, out_specs, out_names = [], [], []
    for name, (struct, place) in outs.items():
        if place in ("near", "both"):
            names.append(name)
            out_names.append(name)
            out_shapes.append(struct)
            out_specs.append(near)
        if place in ("far", "both"):
            names.append(name + "_far")
            out_names.append(name + "_far" if place == "both" else name)
            out_shapes.append(struct)
            out_specs.append(far)
            stores.append(name)
            if place == "far":
                extra[name] = pltpu.VMEM(struct.shape, struct.dtype)
    extra.update(scratch)
    extra["load_sem"] = pltpu.SemaphoreType.DMA((max(len(loads), 1),))
    extra["store_sem"] = pltpu.SemaphoreType.DMA((max(len(stores), 1),))

    def flat(*refs):
        kernel(Refs(names + list(extra), refs, loads, stores))

    results = pl.pallas_call(
        flat,
        out_shape=out_shapes,
        in_specs=in_specs,
        out_specs=out_specs,
        scratch_shapes=list(extra.values()),
        compiler_params=pltpu.CompilerParams(vmem_limit_bytes=VMEM_BYTES),
    )(*arrays)
    return dict(zip(out_names, results))


def dot(left, right):
    return jnp.dot(left, right, preferred_element_type=F32)


def dot_nt(left, right):
    return lax.dot_general(left, right, NT, preferred_element_type=F32)


def dot_tn(left, right):
    return lax.dot_general(left, right, TN, preferred_element_type=F32)


def halves(value):
    high = value.astype(BF16)
    return high, (value - high.astype(F32)).astype(BF16)


def stacked(value):
    return jnp.concatenate(halves(value), axis=0)


def folded(value):
    count = value.shape[0] // 2
    return value[:count] + value[count:]


def sigmoid(value):
    return 0.5 * jnp.tanh(0.5 * value) + 0.5


def chunk_at(index, size=CHUNK):
    return pl.ds(pl.multiple_of(index * size, size), size)


def tile_rows(tile):
    return slice(tile * ROWS, (tile + 1) * ROWS)


def tile_images(tile):
    return slice(tile * TILE, (tile + 1) * TILE)


def as_tile(block):
    return block.reshape(MAP, TILE, LANE)


def spread(rows, first, count):
    return jnp.concatenate([rows[first + k : first + k + 1, :] for k in range(count)], axis=1)


def fold(vectors, rows):
    pieces = [
        vector[:, k * LANE : (k + 1) * LANE]
        for vector in vectors
        for k in range(vector.shape[1] // LANE)
    ]
    if rows > len(pieces):
        pieces.append(jnp.zeros((rows - len(pieces), LANE), F32))
    return jnp.concatenate(pieces, axis=0)


def column_sum(value):
    return jnp.sum(value, axis=0, keepdims=True)


def slice_rows(devices):
    return max(1, WIDTH // devices)


def write_alike(pay_ref, rows):
    pay_ref[...] = jnp.broadcast_to(rows.astype(BF16)[None], pay_ref.shape)


def write_with_slices(pay_ref, rows, matrix):
    devices = pay_ref.shape[0]
    part = slice_rows(devices)
    first = rows.shape[0]
    low = rows.astype(BF16)
    for device in range(devices):
        own = matrix[device * part : (device + 1) * part, :]
        block = jnp.concatenate([own[:, :LANE], own[:, LANE:]], axis=0)
        if 2 * part < 16:
            block = jnp.concatenate([block, jnp.zeros((16 - 2 * part, LANE), F32)], axis=0)
        pay_ref[device, 0:first, :] = low
        pay_ref[device, first : first + 16, :] = block.astype(BF16)


def read_matrix(recv_ref, first):
    devices, rows = recv_ref.shape[:2]
    part = slice_rows(devices)
    if part == TILE:
        values = recv_ref[...].astype(F32)
        left = values[:, first : first + part].reshape(WIDTH, LANE)
        right = values[:, first + part : first + 2 * part].reshape(WIDTH, LANE)
        return jnp.concatenate([left, right], axis=1)
    flat = recv_ref[...].reshape(devices * rows, LANE)
    row = lax.broadcasted_iota(jnp.int32, (WIDTH, devices * rows), 0)
    column = lax.broadcasted_iota(jnp.int32, (WIDTH, devices * rows), 1)
    source = row // part * rows + first + row % part
    left = dot(jnp.where(column == source, 1.0, 0.0).astype(BF16), flat)
    right = dot(jnp.where(column == source + part, 1.0, 0.0).astype(BF16), flat)
    return jnp.concatenate([left, right], axis=1)


def moment_rows(columns):
    return -(-3 * columns // LANE // 8) * 8


def centred(total, squares, count):
    return jnp.maximum(squares - total * total / count, 0.0)


def pack_moments(total, squares, count):
    mean = total / count
    high = mean.astype(BF16).astype(F32)
    return fold([high, mean - high, centred(total, squares, count)], moment_rows(total.shape[1]))


def read_moments(recv_ref, columns, count):
    groups = columns // LANE
    devices = recv_ref.shape[0]
    parts = recv_ref[...].astype(F32)
    means = parts[:, :groups] + parts[:, groups : 2 * groups]
    mean = jnp.sum(means, axis=0) / devices
    apart = means - mean[None]
    spread_sum = jnp.sum(parts[:, 2 * groups : 3 * groups], axis=0) / count
    variance = (spread_sum + jnp.sum(apart * apart, axis=0)) / devices
    return spread(mean, 0, groups), lax.rsqrt(spread(variance, 0, groups) + EPS_BN)


def pack_product_moments(x_ref, total, squares, count):
    sums = column_sum(x_ref[...].astype(F32))
    high = sums.astype(BF16).astype(F32)
    return fold([high, sums - high, centred(total, squares, count)], 16)


def read_product_moments(recv_ref, weights, transposed, columns, count):
    devices, rows = recv_ref.shape[:2]
    values = recv_ref[...]
    flat = values.reshape(devices * rows, LANE)
    row = lax.broadcasted_iota(jnp.int32, (devices, devices * rows), 0)
    column = lax.broadcasted_iota(jnp.int32, (devices, devices * rows), 1) - row * rows
    left = dot(jnp.where((column == 0) | (column == 2), 1.0, 0.0).astype(BF16), flat)
    right = dot(jnp.where((column == 1) | (column == 3), 1.0, 0.0).astype(BF16), flat)
    sums = stacked(jnp.concatenate([left, right], axis=1) / count)
    means = folded(dot_nt(sums, weights) if transposed else dot(sums, weights))
    mean = column_sum(means) / devices
    apart = means - mean
    squares = jnp.sum(values.astype(F32), axis=0)
    variance = (spread(squares, 4, columns // LANE) / count + column_sum(apart * apart)) / devices
    return mean, lax.rsqrt(variance + EPS_BN)


def read_sums(recv_ref):
    return jnp.sum(recv_ref[...].astype(F32), axis=0)


def keep_norm(norm_ref, mean, inverse, gain, bias):
    scale = inverse * gain
    norm_ref[0:1, :] = mean
    norm_ref[1:2, :] = inverse
    norm_ref[2:3, :] = scale
    norm_ref[3:4, :] = bias - mean * scale
    norm_ref[4:8, :] = jnp.zeros((4, norm_ref.shape[1]), F32)


def product_sums(x_ref, w_ref, transposed, h_ref, stat_ref):
    def step(index, carry):
        at = chunk_at(index)
        if transposed:
            h_ref[...] = dot_nt(x_ref[...], w_ref[at, :])
        else:
            h_ref[...] = dot(x_ref[...], w_ref[:, at])
        hidden = h_ref[...]
        stat_ref[0:1, at] = column_sum(hidden)
        stat_ref[1:2, at] = column_sum(hidden * hidden)
        return carry

    lax.fori_loop(0, stat_ref.shape[1] // CHUNK, step, 0)


def mix_kernel(r):
    count = r.images.shape[0]
    pixels = r.images[...]
    row = lax.broadcasted_iota(jnp.int32, (ROWS, count), 0)
    column = lax.broadcasted_iota(jnp.int32, (ROWS, count), 1)
    place = lax.shift_right_logical(row, 3)
    inside = jnp.bitwise_and(row, 7)
    pair = r.mix[...].astype(F32)
    mixing = pair[:, 0:1] / (pair[:, 0:1] + pair[:, 1:2])
    for tile in range(count // ROWS):
        near = tile_images(tile)
        other = jnp.concatenate([r.partner[near, :]] * MAP, axis=0)
        weight = jnp.concatenate([mixing[near, :]] * MAP, axis=0)
        own_hot = jnp.where(column == (tile * TILE + inside) * MAP + place, 1.0, 0.0).astype(BF16)
        other_hot = jnp.where(column == other * MAP + place, 1.0, 0.0).astype(BF16)
        mixed = weight * dot(own_hot, pixels) + (1.0 - weight) * dot(other_hot, pixels)
        r.x[tile_rows(tile), :] = mixed
    r.xb[...] = r.x[...].astype(BF16)
    r.send("x", "xb")
    r.finish()


def mix(images, partner, mix_pair):
    dims = images.shape
    return call(
        mix_kernel,
        dict(images=(images, "near"), partner=(partner, "near"), mix=(mix_pair, "near")),
        dict(x=(shape(dims), "far"), xb=(shape(dims, BF16), "both")),
        {},
    )


def first_kernel(r):
    count = r.xb.shape[0]
    r.start()
    r.wait("w")
    product_sums(r.xb, r.w, False, r.h, r.stat)
    write_alike(r.pay, pack_product_moments(r.xb, r.stat[0:1, :], r.stat[1:2, :], count))


def first(xb, mats, devices):
    count = xb.shape[0]
    return call(
        first_kernel,
        dict(xb=(xb, "near"), w=(mats, (slice(0, WIDTH), slice(None)))),
        dict(pay=(shape((devices, 16, LANE), BF16), "near")),
        dict(h=pltpu.VMEM((count, CHUNK), F32), stat=pltpu.VMEM((8, EXPAND), F32)),
    )


def tap_terms():
    for row in range(EDGE):
        for col in range(EDGE):
            for row_shift in range(3):
                for col_shift in range(3):
                    from_row, from_col = row + row_shift - 1, col + col_shift - 1
                    if 0 <= from_row < EDGE and 0 <= from_col < EDGE:
                        yield EDGE * row + col, 3 * row_shift + col_shift, EDGE * from_row + from_col


TERMS = list(tap_terms())


def spatial_kernel(r):
    count = r.xb.shape[0]
    r.start()
    r.wait("side", "w")
    rows = r.side[...].astype(F32)
    r.taps[0:9, :] = rows[0:9, :]
    mean, inverse = read_product_moments(r.recv, r.w[...], False, EXPAND, count)
    keep_norm(r.norm, mean, inverse, rows[10:11, :], rows[11:12, :])
    r.send("norm")
    if r.recv.shape[1] > 16:
        r.cross[...] = jnp.sum(r.recv[...].astype(F32)[:, 16:32], axis=0)

    def step(index, carry):
        at_chunk = chunk_at(index)
        r.h[...] = dot(r.xb[...], r.w[:, at_chunk])
        for part in range(PARTS):
            lanes = chunk_at(index * PARTS + part, LANE)
            taps = [jnp.broadcast_to(r.taps[k : k + 1, lanes], (TILE, LANE)) for k in range(9)]
            scale_row = r.norm[2:3, lanes]
            shift_row = r.norm[3:4, lanes]

            def tile_step(tile, sums):
                at = chunk_at(tile, ROWS)
                pre = r.h[at, part * LANE : (part + 1) * LANE] * scale_row + shift_row
                active = as_tile(pre * sigmoid(pre))
                result = [None] * MAP
                for target, tap, source in TERMS:
                    term = active[source] * taps[tap]
                    result[target] = term if result[target] is None else result[target] + term
                total, squares = sums
                for value in result:
                    total = total + value
                    squares = squares + value * value
                r.d[at, lanes] = jnp.concatenate(result, axis=0).astype(BF16)
                return total, squares

            zero = jnp.zeros((TILE, LANE), F32)
            total, squares = lax.fori_loop(0, count // ROWS, tile_step, (zero, zero))
            r.stat[0:1, lanes] = column_sum(total)
            r.stat[1:2, lanes] = column_sum(squares)
        pltpu.make_async_copy(r.d.at[:, at_chunk], r.d_far.at[:, at_chunk], r.part_sem.at[index]).start()
        return carry

    lax.fori_loop(0, EXPAND // CHUNK, step, 0)
    write_alike(r.pay, pack_moments(r.stat[0:1, :], r.stat[1:2, :], count))
    for index in range(EXPAND // CHUNK):
        at_chunk = pl.ds(index * CHUNK, CHUNK)
        pltpu.make_async_copy(r.d.at[:, at_chunk], r.d_far.at[:, at_chunk], r.part_sem.at[index]).wait()
    r.finish()


def spatial(xb, mats, side, recv):
    count = xb.shape[0]
    devices = recv.shape[0]
    outs = dict(
        d=(shape((count, EXPAND), BF16), "both"),
        pay=(shape((devices, moment_rows(EXPAND), LANE), BF16), "near"),
        norm=(shape((8, EXPAND)), "far"),
    )
    if recv.shape[1] > 16:
        outs["cross"] = (shape((16, LANE)), "near")
    return call(
        spatial_kernel,
        dict(
            recv=(recv, "near"),
            xb=(xb, "near"),
            side=(side, (slice(2 * SQUEEZE, SIDE_PAD), slice(None))),
            w=(mats, (slice(0, WIDTH), slice(None))),
        ),
        outs,
        dict(
            h=pltpu.VMEM((count, CHUNK), F32),
            taps=pltpu.VMEM((16, EXPAND), F32),
            stat=pltpu.VMEM((8, EXPAND), F32),
            part_sem=pltpu.SemaphoreType.DMA((EXPAND // CHUNK,)),
        ),
    )


def project_kernel(with_cross, r):
    count = r.d.shape[0]
    tiles = count // ROWS
    r.start()
    mean, inverse = read_moments(r.recv, EXPAND, count)
    r.wait("side")
    rows = r.side[2 * SQUEEZE : SIDE_PAD, :].astype(F32)
    keep_norm(r.norm, mean, inverse, rows[12:13, :], rows[13:14, :])
    r.send("norm")

    def activate(index, carry):
        lanes = chunk_at(index, LANE)
        scale_row = r.norm[2:3, lanes]
        shift_row = r.norm[3:4, lanes]
        for tile in range(tiles):
            at = tile_rows(tile)
            pre = r.d[at, lanes].astype(F32) * scale_row + shift_row
            active = pre * sigmoid(pre)
            r.a[at, lanes] = active
            r.pooled[tile_images(tile), lanes] = jnp.sum(as_tile(active), axis=0) / MAP
        return carry

    lax.fori_loop(0, EXPAND // LANE, activate, 0)
    r.send("pooled")
    before = folded(dot_nt(stacked(r.pooled[...]), r.side[0:SQUEEZE, :])) + r.vec[2:3, :SQUEEZE]
    r.squeeze[...] = before
    r.send("squeeze")
    opened = folded(dot(stacked(before * sigmoid(before)), r.side[SQUEEZE : 2 * SQUEEZE, :]))
    r.excite[...] = sigmoid(opened + rows[9:10, :])
    r.send("excite")

    def gate(index, carry):
        lanes = chunk_at(index, LANE)
        for tile in range(tiles):
            at = tile_rows(tile)
            scaled = as_tile(r.a[at, lanes]) * r.excite[tile_images(tile), lanes][None]
            r.y[at, lanes] = scaled.reshape(ROWS, LANE).astype(BF16)
        return carry

    lax.fori_loop(0, EXPAND // LANE, gate, 0)
    r.wait("w")
    projected = dot_nt(r.y[...], r.w[...])
    r.p[...] = projected
    moments = pack_moments(column_sum(projected), column_sum(projected * projected), count)
    if with_cross:
        moments = jnp.concatenate([moments, r.cross[...]], axis=0)
    write_alike(r.pay, moments)
    r.finish()


def project(d, mats, side, vec, recv, cross):
    count = d.shape[0]
    images = count // MAP
    devices = recv.shape[0]
    ins = dict(
        recv=(recv, "near"),
        d=(d, "near"),
        vec=(vec, "near"),
        side=(side, "far"),
        w=(mats, (slice(WIDTH, 2 * WIDTH), slice(None))),
    )
    rows = moment_rows(WIDTH)
    if cross is not None:
        ins["cross"] = (cross, "near")
        rows += 16
    return call(
        functools.partial(project_kernel, cross is not None),
        ins,
        dict(
            p=(shape((count, WIDTH)), "near"),
            pay=(shape((devices, rows, LANE), BF16), "near"),
            norm=(shape((8, EXPAND)), "far"),
            pooled=(shape((images, EXPAND)), "far"),
            excite=(shape((images, EXPAND)), "far"),
            squeeze=(shape((images, SQUEEZE)), "far"),
        ),
        dict(a=pltpu.VMEM((count, EXPAND), F32), y=pltpu.VMEM((count, EXPAND), BF16)),
    )


def residual_kernel(transposed, with_cross, r):
    count = r.p.shape[0]
    r.start()
    mean, inverse = read_moments(r.recv, WIDTH, count)
    keep_norm(r.norm, mean, inverse, r.vec[0:1, :], r.vec[1:2, :])
    if with_cross:
        r.cross[...] = read_matrix(r.recv, moment_rows(WIDTH))
        r.send("cross")
    normed = (r.p[...] - mean) * inverse
    r.normed[...] = normed
    r.wait("before")
    result = r.before[...] + (normed * r.vec[0:1, :] + r.vec[1:2, :])
    r.x[...] = result
    r.xb[...] = result.astype(BF16)
    r.send("norm", "normed", "x", "xb")
    cross = dot_tn(normed.astype(BF16), r.xb[...])
    r.wait("w")
    product_sums(r.xb, r.w, transposed, r.h, r.stat)
    moments = pack_product_moments(r.xb, r.stat[0:1, :], r.stat[1:2, :], count)
    write_with_slices(r.pay, moments, cross)
    r.finish()


def residual(x, p, vec, recv, weights, transposed):
    count = x.shape[0]
    devices = recv.shape[0]
    with_cross = recv.shape[1] > moment_rows(WIDTH)
    columns = HEAD if transposed else EXPAND
    where = (slice(0, HEAD), slice(0, WIDTH)) if transposed else (slice(0, WIDTH), slice(None))
    outs = dict(
        x=(shape((count, WIDTH)), "far"),
        xb=(shape((count, WIDTH), BF16), "both"),
        normed=(shape((count, WIDTH)), "far"),
        pay=(shape((devices, 32, LANE), BF16), "near"),
        norm=(shape((8, WIDTH)), "far"),
    )
    if with_cross:
        outs["cross"] = (shape((WIDTH, WIDTH)), "far")
    return call(
        functools.partial(residual_kernel, transposed, with_cross),
        dict(
            recv=(recv, "near"), p=(p, "near"), vec=(vec, "near"), before=(x, "far"), w=(weights, where)
        ),
        outs,
        dict(h=pltpu.VMEM((count, CHUNK), F32), stat=pltpu.VMEM((8, columns), F32)),
    )


def head_rows(last_columns):
    pick_row = lax.broadcasted_iota(jnp.int32, (TILE, LANE), 0)
    pick_col = lax.broadcasted_iota(jnp.int32, (TILE, LANE), 1)
    first_col = WIDTH + CLASSES - (HEADPAD - LANE)
    pick = jnp.where((pick_col == pick_row + first_col) & (pick_row < 2), 1.0, 0.0).astype(BF16)
    return dot_nt(pick, last_columns)


def head_kernel(image_count, r):
    count = r.xb.shape[0]
    tiles = count // ROWS
    images = count // MAP
    r.start()
    r.wait("w")
    mean, inverse = read_product_moments(r.recv, r.w[...], True, HEAD, count)
    cross = jnp.sum(r.recv[...].astype(F32)[:, 16:32], axis=0)
    r.wait("classifier")
    gain_bias = head_rows(r.classifier[:, LOGITS - LANE :])
    keep_norm(r.norm, mean, inverse, gain_bias[0:1, :], gain_bias[1:2, :])
    r.send("norm")

    def features(index, carry):
        at_chunk = chunk_at(index)
        r.h[:, at_chunk] = dot_nt(r.xb[...], r.w[at_chunk, :])
        for part in range(PARTS):
            lanes = chunk_at(index * PARTS + part, LANE)
            scale_row = r.norm[2:3, lanes]
            shift_row = r.norm[3:4, lanes]
            for tile in range(tiles):
                pre = r.h[tile_rows(tile), lanes] * scale_row + shift_row
                active = as_tile(pre * sigmoid(pre))
                r.f[tile_images(tile), lanes] = jnp.sum(active, axis=0) / MAP
        return carry

    lax.fori_loop(0, HEAD // CHUNK, features, 0)
    features_low = r.f[...].astype(BF16)
    classifier = r.classifier[...]
    ids = lax.broadcasted_iota(jnp.int32, (images, LOGITS), 1)
    logits = dot(features_low, classifier) + r.bias[...]
    logits = jnp.where(ids < CLASSES, logits, -1e30)
    row_max = jnp.max(logits, axis=1, keepdims=True)
    log_total = row_max + jnp.log(jnp.sum(jnp.exp(logits - row_max), axis=1, keepdims=True))
    pair = r.mix[...].astype(F32)
    mixing = pair[:, 0:1] / (pair[:, 0:1] + pair[:, 1:2])
    people = lax.broadcasted_iota(jnp.int32, (images, images), 1)
    label_row = jnp.broadcast_to(r.label_row[...].astype(F32), (images, images))
    partner_label = jnp.sum(
        jnp.where(people == r.partner[...], label_row, 0.0), axis=1, keepdims=True
    ).astype(jnp.int32)
    own_hot = jnp.where(ids == r.label_col[...], 1.0, 0.0)
    other_hot = jnp.where(ids == partner_label, 1.0, 0.0)
    own_logit = jnp.sum(own_hot * logits, axis=1, keepdims=True)
    other_logit = jnp.sum(other_hot * logits, axis=1, keepdims=True)
    loss = column_sum(mixing * (log_total - own_logit) + (1.0 - mixing) * (log_total - other_logit))
    grad_logits = (
        jnp.exp(logits - log_total) - mixing * own_hot - (1.0 - mixing) * other_hot
    ) / image_count
    grad_low = grad_logits.astype(BF16)
    r.grad_fc[...] = dot_tn(features_low, grad_low).astype(BF16)
    r.send("grad_fc")
    r.f[...] = dot_nt(grad_low, classifier) / MAP
    bias_sum = column_sum(grad_logits)
    bias_ids = lax.broadcasted_iota(jnp.int32, (1, LOGITS), 1)
    loss_high = loss.astype(BF16).astype(F32)
    bias_sum = jnp.where(bias_ids == CLASSES, loss_high, bias_sum)
    bias_sum = jnp.where(bias_ids == CLASSES + 1, loss - loss_high, bias_sum)

    def back(index, carry):
        lanes = chunk_at(index, LANE)
        scale_row = r.norm[2:3, lanes]
        shift_row = r.norm[3:4, lanes]
        mean_row = r.norm[0:1, lanes]
        total = jnp.zeros((TILE, LANE), F32)
        weighted = jnp.zeros((TILE, LANE), F32)
        for tile in range(tiles):
            at = tile_rows(tile)
            hidden = r.h[at, lanes]
            pre = hidden * scale_row + shift_row
            gate = sigmoid(pre)
            slope = as_tile(gate * (1.0 + pre * (1.0 - gate)))
            grad = slope * r.f[tile_images(tile), lanes][None]
            total = total + jnp.sum(grad, axis=0)
            weighted = weighted + jnp.sum(grad * as_tile(hidden - mean_row), axis=0)
            flat = grad.reshape(ROWS, LANE)
            r.dz[at, lanes] = flat.astype(BF16)
            r.q[at, lanes] = (flat * scale_row).astype(BF16)
        r.stat[0:1, lanes] = column_sum(total)
        r.stat[1:2, lanes] = column_sum(weighted)
        return carry

    lax.fori_loop(0, HEAD // LANE, back, 0)
    below = dot(r.q[...], r.w[...])
    r.wait("normed")
    rows = fold(
        [
            r.stat[0:1, :], r.stat[1:2, :] * inverse,
            column_sum(below), column_sum(below * r.normed[...]), bias_sum,
        ],
        32,
    )
    write_alike(r.pay, jnp.concatenate([rows, cross], axis=0))
    r.finish()


def head(xb, head_full, bias, label_col, label_row, partner, mix_pair, normed, recv, image_count):
    count = xb.shape[0]
    images = count // MAP
    devices = recv.shape[0]
    return call(
        functools.partial(head_kernel, image_count),
        dict(
            recv=(recv, "near"),
            xb=(xb, "near"),
            bias=(bias, "near"),
            label_col=(label_col, "near"),
            label_row=(label_row, "near"),
            partner=(partner, "near"),
            mix=(mix_pair, "near"),
            w=(head_full, (slice(0, HEAD), slice(0, WIDTH))),
            classifier=(head_full, (slice(0, HEAD), slice(WIDTH, HEADPAD))),
            normed=(normed, "far"),
        ),
        dict(
            dz=(shape((count, HEAD), BF16), "near"),
            pay=(shape((devices, 48, LANE), BF16), "near"),
            norm=(shape((8, HEAD)), "far"),
            grad_fc=(shape((HEAD, LOGITS), BF16), "far"),
        ),
        dict(
            h=pltpu.VMEM((count, HEAD), F32),
            f=pltpu.VMEM((images, HEAD), F32),
            q=pltpu.VMEM((count, HEAD), BF16),
            stat=pltpu.VMEM((8, HEAD), F32),
        ),
    )


def product_back(is_head, row_count, sums, columns, r):
    groups = columns // LANE
    sum_bias = spread(sums, 0, groups)
    sum_gain = spread(sums, groups, groups)
    r.glob[0:1, :] = sum_gain
    r.glob[1:2, :] = sum_bias
    r.glob[2:8, :] = jnp.zeros((6, columns), F32)
    r.send("glob")
    r.wait("unorm", "xb", "w")
    mean = r.unorm[0:1, :]
    scale = r.unorm[2:3, :]
    slant = scale * r.unorm[1:2, :] * (sum_gain / row_count)
    r.coef[0:1, :columns] = slant
    r.coef[1:2, :columns] = mean * slant - scale * (sum_bias / row_count)
    r.xt[...] = r.xb[...].T
    count = r.xb.shape[0]

    def step(index, carry):
        at = chunk_at(index)
        if is_head:
            r.h[...] = dot_nt(r.xb[...], r.w[at, :])
        else:
            r.h[...] = dot(r.xb[...], r.w[:, at])
        grad = r.dz[:, at].astype(F32) * r.unorm[2:3, at] - r.h[...] * r.coef[0:1, at] + r.coef[1:2, at]
        low = grad.astype(BF16)
        r.dh[0:count, at] = low
        if is_head:
            r.grad_w[at, :] = dot_tn(low, r.xb[...]).astype(r.grad_w.dtype)
        else:
            r.grad_w[:, at] = dot(r.xt[...], low).astype(r.grad_w.dtype)
        return carry

    lax.fori_loop(0, columns // CHUNK, step, 0)
    return scale * sum_bias, slant


def owner_blocks(r, owners, row_of_owner, taps):
    rows_dev = 2 * WIDTH // owners
    width = EXPAND // owners
    vec_width = VECS // owners
    chunks = EXPAND // CHUNK
    squeeze_sums = jnp.concatenate([r.squeeze_sum[...], jnp.zeros((1, VECS - LANE), F32)], axis=1)
    for owner in range(owners):
        at = slice(owner * width, (owner + 1) * width)
        squeeze_row = squeeze_sums[:, owner * vec_width : (owner + 1) * vec_width]
        squeeze_row = jnp.concatenate([squeeze_row, jnp.zeros((1, width - vec_width), F32)], axis=1)
        pieces = [r.excite_sum[:, at], squeeze_row]
        pieces.append(taps[0:9, at] if taps is not None else jnp.zeros((9, width), F32))
        pieces.append(jnp.zeros((5, width), F32))
        first_row = chunks * rows_dev
        r.grads[owner, first_row : first_row + 2 * SQUEEZE, 0:width] = r.rx[:, at].astype(BF16)
        last_row = first_row + 2 * SQUEEZE
        r.grads[owner, last_row : last_row + 16, 0:width] = jnp.concatenate(pieces, axis=0).astype(BF16)


def gate_kernel(is_head, row_count, owners, r):
    columns = HEAD if is_head else EXPAND
    groups = columns // LANE
    count = r.xb.shape[0]
    tiles = count // ROWS
    rows_dev = 2 * WIDTH // owners
    r.start()
    sums = read_sums(r.recv)
    bias_pull, slant = product_back(is_head, row_count, sums, columns, r)
    if is_head:
        r.send("grad_w")
        weights = r.w[...].astype(F32)
        column = lax.broadcasted_iota(jnp.int32, (1, WIDTH), 1)
        high, low = halves(jnp.broadcast_to(bias_pull, (TILE, columns)))
        pull = column_sum(dot(high, r.w[...]) + dot(low, r.w[...])) / TILE
        turned = jnp.broadcast_to(slant, (LANE, columns)).T
        slanted = (weights * jnp.concatenate([turned, turned], axis=1)).astype(BF16)
        square = dot_tn(slanted, r.w[...])
        stream = dot(r.dh[0:count, :columns], r.w[...])
        cross = read_matrix(r.recv, 32)
    else:
        r.dh[count : count + WIDTH, :] = (r.w[...].astype(F32) * slant).astype(BF16)
        high, low = halves(bias_pull)
        r.dh[count + WIDTH :, :] = jnp.concatenate(
            [high.astype(F32), low.astype(F32), jnp.zeros((14, columns), F32)], axis=0
        ).astype(BF16)
        product = dot_nt(r.dh[...], r.w[...])
        square = product[count : count + WIDTH]
        pull = column_sum(product[count + WIDTH : count + WIDTH + 2])
        stream = r.stream_in[...] + product[0:count]
        r.wait("cross")
        cross = r.cross[...]
    r.stream[...] = stream
    sum_bias = spread(sums, 2 * groups, WIDTH // LANE) - pull
    corrected = column_sum(cross.T * square)
    sum_gain = spread(sums, 2 * groups + WIDTH // LANE, WIDTH // LANE) - corrected
    r.glob3[0:1, :] = sum_gain
    r.glob3[1:2, :] = sum_bias
    if is_head:
        first_row = 2 * groups + 2 * WIDTH // LANE
        r.glob3[2:6, :] = jnp.concatenate(
            [spread(sums, first_row + PARTS * k, PARTS) for k in range(LOGITS // WIDTH)], axis=0
        )
    else:
        r.glob3[2:6, :] = jnp.zeros((4, WIDTH), F32)
    r.glob3[6:8, :] = jnp.zeros((2, WIDTH), F32)
    r.send("glob3")
    r.wait("norm3", "normed")
    grad_p = r.norm3[2:3, :] * (
        stream - sum_bias / row_count - r.normed[...] * (sum_gain / row_count)
    )
    r.gp[...] = grad_p.astype(BF16)
    r.gt[...] = r.gp[...].T
    r.wait("wp", "d", "norm2", "excite")
    half = owners // 2

    def first(index, carry):
        at_chunk = chunk_at(index)
        r.h[...] = dot(r.gp[...], r.wp[:, at_chunk])
        for part in range(PARTS):
            lanes = chunk_at(index * PARTS + part, LANE)
            scale_row = r.norm2[2:3, lanes]
            shift_row = r.norm2[3:4, lanes]
            for tile in range(tiles):
                at = tile_rows(tile)
                near = tile_images(tile)
                pre = r.d[at, lanes].astype(F32) * scale_row + shift_row
                gate = sigmoid(pre)
                active = pre * gate
                slope = gate + active - active * gate
                grad = r.h[at, part * LANE : (part + 1) * LANE]
                factor = r.excite[near, lanes]
                r.ge[near, lanes] = jnp.sum(as_tile(grad * active), axis=0)
                r.y[at, lanes] = (as_tile(active) * factor[None]).reshape(ROWS, LANE).astype(BF16)
                r.slope[at, lanes] = slope
                r.u[at, lanes] = (as_tile(grad * slope) * factor[None]).reshape(ROWS, LANE)
        grad_p_chunk = dot(r.gt[...], r.y[:, at_chunk])
        place = pl.ds(pl.multiple_of(index * rows_dev, rows_dev), rows_dev)
        for owner in range(half):
            cut = slice(owner * rows_dev, (owner + 1) * rows_dev)
            r.grads[half + owner, place, :] = grad_p_chunk[cut, :].astype(BF16)
            if is_head:
                r.grads[owner, place, :] = jnp.zeros((rows_dev, CHUNK), BF16)
            else:
                r.grads[owner, place, :] = r.grad_w[cut, at_chunk]
        return carry

    lax.fori_loop(0, EXPAND // CHUNK, first, 0)
    r.wait("pooled", "squeeze", "side")
    excite = r.excite[...]
    grad_gate = r.ge[...] * excite * (1.0 - excite)
    before = r.squeeze[...]
    opened = sigmoid(before)
    squeezed = before * opened
    reduce_mat = r.side[0:SQUEEZE, :]
    excite_mat = r.side[SQUEEZE:, :]
    gate_high, gate_low = halves(grad_gate)
    grad_squeezed = folded(dot_nt(jnp.concatenate([gate_high, gate_low], axis=0), excite_mat))
    grad_pre = grad_squeezed * (opened * (1.0 + before * (1.0 - opened)))
    r.pool[...] = folded(dot(stacked(grad_pre), reduce_mat)) / MAP

    def second(index, carry):
        lanes = chunk_at(index, LANE)
        mean_row = r.norm2[0:1, lanes]
        total = jnp.zeros((TILE, LANE), F32)
        weighted = jnp.zeros((TILE, LANE), F32)
        for tile in range(tiles):
            at = tile_rows(tile)
            pool = r.pool[tile_images(tile), lanes]
            grad = as_tile(r.u[at, lanes]) + as_tile(r.slope[at, lanes]) * pool[None]
            total = total + jnp.sum(grad, axis=0)
            weighted = weighted + jnp.sum(
                grad * as_tile(r.d[at, lanes].astype(F32) - mean_row), axis=0
            )
            r.dz2[at, lanes] = grad.reshape(ROWS, LANE).astype(BF16)
        r.stat[0:1, lanes] = column_sum(total)
        r.stat[1:2, lanes] = column_sum(weighted)
        return carry

    lax.fori_loop(0, EXPAND // LANE, second, 0)
    write_alike(r.pay, fold([r.stat[0:1, :], r.stat[1:2, :] * r.norm2[1:2, :]], 24))
    squeezed_high, squeezed_low = halves(squeezed)
    pre_high, pre_low = halves(grad_pre)
    pooled_high, pooled_low = halves(r.pooled[...])
    r.rx[SQUEEZE:, :] = dot_tn(
        jnp.concatenate([squeezed_high, squeezed_low, squeezed_high], axis=0),
        jnp.concatenate([gate_high, gate_high, gate_low], axis=0),
    )
    r.rx[0:SQUEEZE, :] = dot_tn(
        jnp.concatenate([pre_high, pre_low, pre_high], axis=0),
        jnp.concatenate([pooled_high, pooled_high, pooled_low], axis=0),
    )
    r.excite_sum[...] = column_sum(grad_gate)
    r.squeeze_sum[...] = jnp.concatenate(
        [column_sum(grad_pre), jnp.zeros((1, LANE - SQUEEZE), F32)], axis=1
    )
    taps = None
    if not is_head:
        r.wait("taps")
        taps = r.taps[...]
    owner_blocks(r, owners, half, taps)
    r.send("grads")
    r.finish()


def gate_back(is_head, row_count, owners, recv, upper, cross, stream, lower):
    count = upper["xb_far"].shape[0]
    images = count // MAP
    devices = recv.shape[0]
    columns = HEAD if is_head else EXPAND
    block = EXPAND // CHUNK * (2 * WIDTH // owners) + 2 * SQUEEZE + 16
    where = (slice(0, HEAD), slice(0, WIDTH)) if is_head else (slice(0, WIDTH), slice(None))
    ins = dict(
        recv=(recv, "near"),
        dz=(upper["dz"], "near"),
        unorm=(upper["norm"], "far"),
        xb=(upper["xb_far"], "far"),
        w=(upper["weights"], where),
        norm3=(lower["norm3"], "far"),
        normed=(lower["normed"], "far"),
        norm2=(lower["norm2"], "far"),
        wp=(lower["mats"], (slice(WIDTH, 2 * WIDTH), slice(None))),
        d=(lower["d_far"], "far"),
        excite=(lower["excite"], "far"),
        pooled=(lower["pooled"], "far"),
        squeeze=(lower["squeeze"], "far"),
        side=(lower["side"], (slice(0, 2 * SQUEEZE), slice(None))),
    )
    outs = dict(
        dz2=(shape((count, EXPAND), BF16), "near"),
        pay=(shape((devices, 24, LANE), BF16), "near"),
        stream=(shape((count, WIDTH)), "near"),
        grads=(shape((owners, block, CHUNK), BF16), "far"),
        glob=(shape((8, columns)), "far"),
        glob3=(shape((8, WIDTH)), "far"),
    )
    scratch = dict(
        xt=pltpu.VMEM((WIDTH, count), BF16),
        h=pltpu.VMEM((count, CHUNK), F32),
        coef=pltpu.VMEM((8, EXPAND), F32),
        dh=pltpu.VMEM((count + WIDTH + 16, columns), BF16),
        u=pltpu.VMEM((count, EXPAND), F32),
        slope=pltpu.VMEM((count, EXPAND), F32),
        y=pltpu.VMEM((count, EXPAND), BF16),
        gp=pltpu.VMEM((count, WIDTH), BF16),
        gt=pltpu.VMEM((WIDTH, count), BF16),
        ge=pltpu.VMEM((images, EXPAND), F32),
        pool=pltpu.VMEM((images, EXPAND), F32),
        rx=pltpu.VMEM((2 * SQUEEZE, EXPAND), F32),
        excite_sum=pltpu.VMEM((1, EXPAND), F32),
        squeeze_sum=pltpu.VMEM((1, LANE), F32),
        stat=pltpu.VMEM((8, EXPAND), F32),
    )
    if is_head:
        outs["grad_w"] = (shape((HEAD, WIDTH), BF16), "far")
    else:
        ins["cross"] = (cross, "far")
        ins["stream_in"] = (stream, "near")
        ins["taps"] = (upper["taps"], "far")
        scratch["grad_w"] = pltpu.VMEM((WIDTH, EXPAND), BF16)
    return call(functools.partial(gate_kernel, is_head, row_count, owners), ins, outs, scratch)


def tap_kernel(is_first, row_count, r):
    count = r.dz2.shape[0]
    groups = EXPAND // LANE
    r.start()
    sums = read_sums(r.recv)
    sum_bias = spread(sums, 0, groups)
    sum_gain = spread(sums, groups, groups)
    r.glob[0:1, :] = sum_gain
    r.glob[1:2, :] = sum_bias
    r.glob[2:8, :] = jnp.zeros((6, EXPAND), F32)
    r.send("glob")
    r.wait("side", "norm2")
    scale2 = r.norm2[2:3, :]
    slant2 = scale2 * r.norm2[1:2, :] * (sum_gain / row_count)
    r.coef[0:9, :] = r.side[...].astype(F32)[0:9, :]
    r.coef[9:10, :] = slant2
    r.coef[10:11, :] = r.norm2[0:1, :] * slant2 - scale2 * (sum_bias / row_count)
    r.wait("norm1", "xb", "w", "d")

    def step(index, carry):
        at_chunk = chunk_at(index)
        r.h[...] = dot(r.xb[...], r.w[:, at_chunk])
        for part in range(PARTS):
            lanes = chunk_at(index * PARTS + part, LANE)
            near = slice(part * LANE, (part + 1) * LANE)
            taps = [jnp.broadcast_to(r.coef[k : k + 1, lanes], (TILE, LANE)) for k in range(9)]

            def tile_step(tile, sums_in):
                at = chunk_at(tile, ROWS)
                grad_d = as_tile(
                    r.dz2[at, lanes].astype(F32) * r.norm2[2:3, lanes]
                    - r.d[at, lanes].astype(F32) * r.coef[9:10, lanes]
                    + r.coef[10:11, lanes]
                )
                hidden = r.h[at, near]
                pre = hidden * r.norm1[2:3, lanes] + r.norm1[3:4, lanes]
                gate = sigmoid(pre)
                flat = pre * gate
                active = as_tile(flat)
                slope = as_tile(gate + flat - flat * gate)
                apart = as_tile(hidden - r.norm1[0:1, lanes])
                grad_a = [None] * MAP
                tap_sums = [None] * 9
                for target, tap, source in TERMS:
                    term = grad_d[target] * taps[tap]
                    grad_a[source] = term if grad_a[source] is None else grad_a[source] + term
                    term = grad_d[target] * active[source]
                    tap_sums[tap] = term if tap_sums[tap] is None else tap_sums[tap] + term
                total, weighted = sums_in[9], sums_in[10]
                grads = []
                for place in range(MAP):
                    grad = grad_a[place] * slope[place]
                    total = total + grad
                    weighted = weighted + grad * apart[place]
                    grads.append(grad)
                grad = jnp.concatenate(grads, axis=0)
                r.dz[at, lanes] = grad.astype(BF16)
                if not is_first:
                    r.q[at, lanes] = (grad * r.norm1[2:3, lanes]).astype(BF16)
                return (*[sums_in[k] + tap_sums[k] for k in range(9)], total, weighted)

            zero = jnp.zeros((TILE, LANE), F32)
            result = lax.fori_loop(0, count // ROWS, tile_step, (zero,) * 11)
            for k in range(9):
                r.taps[k : k + 1, lanes] = column_sum(result[k])
            r.stat[0:1, lanes] = column_sum(result[9])
            r.stat[1:2, lanes] = column_sum(result[10])
        return carry

    lax.fori_loop(0, EXPAND // CHUNK, step, 0)
    r.taps[9:16, :] = jnp.zeros((7, EXPAND), F32)
    r.send("taps")
    vectors = [r.stat[0:1, :], r.stat[1:2, :] * r.norm1[1:2, :]]
    if not is_first:
        below = r.stream[...] + dot_nt(r.q[...], r.w[...])
        r.wait("normed")
        vectors.append(column_sum(below))
        vectors.append(column_sum(below * r.normed[...]))
    write_alike(r.pay, fold(vectors, r.pay.shape[1]))
    r.finish()


def tap_back(is_first, row_count, recv, dz2, layer, stream, below):
    count = dz2.shape[0]
    devices = recv.shape[0]
    ins = dict(
        recv=(recv, "near"),
        dz2=(dz2, "near"),
        side=(layer["side"], (slice(2 * SQUEEZE, SIDE_PAD), slice(None))),
        norm2=(layer["norm2"], "far"),
        norm1=(layer["norm1"], "far"),
        xb=(layer["xb_far"], "far"),
        w=(layer["mats"], (slice(0, WIDTH), slice(None))),
        d=(layer["d_far"], "far"),
    )
    scratch = dict(
        h=pltpu.VMEM((count, CHUNK), F32),
        coef=pltpu.VMEM((16, EXPAND), F32),
        stat=pltpu.VMEM((8, EXPAND), F32),
    )
    if not is_first:
        ins["stream"] = (stream, "near")
        ins["normed"] = (below["normed"], "far")
        scratch["q"] = pltpu.VMEM((count, EXPAND), BF16)
    return call(
        functools.partial(tap_kernel, is_first, row_count),
        ins,
        dict(
            dz=(shape((count, EXPAND), BF16), "near"),
            pay=(shape((devices, 24 if is_first else 32, LANE), BF16), "near"),
            taps=(shape((16, EXPAND)), "far"),
            glob=(shape((8, EXPAND)), "far"),
        ),
        scratch,
    )


def last_kernel(row_count, replicas, owners, r):
    r.start()
    product_back(False, row_count, read_sums(r.recv), EXPAND, r)
    half = owners // 2
    part = slice_rows(replicas * owners)
    rows_dev = 2 * WIDTH // owners
    chunks = EXPAND // CHUNK
    pad = r.grads.shape[1] - chunks * part
    for replica in range(replicas):
        for owner in range(owners):
            first_row = rows_dev * (owner % half) + (2 * replica + owner // half) * part
            own = r.grad_w[first_row : first_row + part, :]
            block = jnp.concatenate(
                [own[:, k * CHUNK : (k + 1) * CHUNK] for k in range(chunks)]
                + ([jnp.zeros((pad, CHUNK), F32)] if pad else []),
                axis=0,
            )
            r.grads[replica * owners + owner, :, :] = block.astype(BF16)
    r.finish()


def last_back(row_count, replicas, owners, recv, layer, dz):
    count = dz.shape[0]
    devices = recv.shape[0]
    block = -(-EXPAND // CHUNK * slice_rows(devices) // 16) * 16
    return call(
        functools.partial(last_kernel, row_count, replicas, owners),
        dict(
            recv=(recv, "near"),
            dz=(dz, "near"),
            unorm=(layer["norm1"], "far"),
            xb=(layer["xb_far"], "far"),
            w=(layer["mats"], (slice(0, WIDTH), slice(None))),
        ),
        dict(
            grads=(shape((devices, block, CHUNK), BF16), "near"),
            glob=(shape((8, EXPAND)), "far"),
        ),
        dict(
            xt=pltpu.VMEM((WIDTH, count), BF16),
            h=pltpu.VMEM((count, CHUNK), F32),
            coef=pltpu.VMEM((8, EXPAND), F32),
            dh=pltpu.VMEM((count, EXPAND), BF16),
            grad_w=pltpu.VMEM((WIDTH, EXPAND), F32),
        ),
    )


def lamb_moments(weight, moment_one, moment_two, gradient, decay_mask, step_float):
    first_new = BETA_ONE * moment_one + (1.0 - BETA_ONE) * gradient
    second_new = BETA_TWO * moment_two + (1.0 - BETA_TWO) * gradient * gradient
    corrected = (
        first_new
        / (1.0 - BETA_ONE**step_float)
        / (jnp.sqrt(second_new / (1.0 - BETA_TWO**step_float)) + EPS_ADAM)
    )
    return (first_new, second_new, corrected + DECAY_RATE * decay_mask * weight)


def group_sums(mats, side, head_shard, row_ids):
    rows = jnp.sum(mats * mats, axis=2)
    is_expand = (row_ids < WIDTH)[None, :]
    side_rows = jnp.sum(side * side, axis=2)
    head_cols = jnp.sum(head_shard * head_shard, axis=0)
    per_layer = jnp.stack(
        [
            jnp.sum(jnp.where(is_expand, rows, 0.0), axis=1),
            jnp.sum(jnp.where(is_expand, 0.0, rows), axis=1),
            jnp.sum(side_rows[:, :9], axis=1),
            jnp.sum(side_rows[:, 9 : 9 + SQUEEZE], axis=1),
            jnp.sum(side_rows[:, 9 + SQUEEZE : 9 + 2 * SQUEEZE], axis=1),
        ],
        axis=1,
    )
    tail = jnp.stack([jnp.sum(head_cols[:WIDTH]), jnp.sum(head_cols[WIDTH : WIDTH + CLASSES])])
    return jnp.concatenate([per_layer.reshape(-1), tail])


def rate_maps(trust_ratio, row_ids):
    groups = trust_ratio[: 5 * LAYERS].reshape(LAYERS, 5)
    mats_rate = RATE_MATRIX * jnp.where(row_ids[None, :] < WIDTH, groups[:, 0:1], groups[:, 1:2])
    side_ids = jnp.arange(SIDE)[None, :]
    side_rate = jnp.where(
        side_ids < 9,
        RATE_MATRIX * groups[:, 2:3],
        jnp.where(
            side_ids < 9 + SQUEEZE,
            RATE_MATRIX * groups[:, 3:4],
            jnp.where(side_ids < 9 + 2 * SQUEEZE, RATE_MATRIX * groups[:, 4:5], RATE_VECTOR),
        ),
    )
    col_ids = jnp.arange(HEADCOLS)
    head_rate = jnp.where(
        col_ids < WIDTH,
        RATE_MATRIX * trust_ratio[5 * LAYERS],
        jnp.where(
            col_ids < WIDTH + CLASSES, RATE_MATRIX * trust_ratio[5 * LAYERS + 1], RATE_VECTOR
        ),
    )
    return (mats_rate, side_rate, head_rate)


def exchange(payload):
    return lax.all_to_all(payload, BOTH, 0, 0)


def spread_over(array, axis):
    copies = jnp.broadcast_to(array[None], (lax.axis_size(axis), *array.shape))
    return lax.all_to_all(copies, axis, 0, 0)


def replica_sum(array):
    return jnp.sum(spread_over(array, "dp").astype(F32), axis=0)


def body(
    images, partner, mix_pair, labels, step,
    layer_mats, layer_side, layer_vecs, head_mat, fc_bias,
    mats_first, mats_second, side_first, side_second, vecs_first, vecs_second,
    head_first, head_second, bias_first, bias_second,
):
    local_images = images.shape[0]
    owners = lax.axis_size("fsdp")
    replicas = lax.axis_size("dp")
    devices = owners * replicas
    image_count = float(local_images * devices)
    count = local_images * MAP
    row_count = float(count * devices)
    mine = lax.axis_index("fsdp")
    side_width = layer_side.shape[2]
    vec_width = layer_vecs.shape[1]
    rows_dev = layer_mats.shape[1]
    half = owners // 2

    side_low = jnp.concatenate(
        [
            layer_side[:, 9 : 9 + 2 * SQUEEZE],
            layer_side[:, :9],
            layer_side[:, 9 + 2 * SQUEEZE :],
            jnp.pad(layer_vecs, ((0, 0), (0, side_width - vec_width)))[:, None, :],
            jnp.zeros((LAYERS, 1, side_width), F32),
        ],
        axis=1,
    ).astype(BF16)
    mats_all = [
        lax.all_gather(layer_mats[k].astype(BF16), "fsdp", axis=0, tiled=True) for k in range(LAYERS)
    ]
    side_zero = lax.all_gather(side_low[0], "fsdp", axis=1, tiled=True)
    side_room = -(-side_width // CHUNK) * CHUNK
    side_rest = lax.all_gather(
        jnp.pad(side_low[1:], ((0, 0), (0, 0), (0, side_room - side_width))), "fsdp", axis=0
    )
    side_rest = jnp.moveaxis(side_rest[..., :side_width], 0, 2).reshape(LAYERS - 1, SIDE_PAD, EXPAND)
    side_all = [side_zero, side_rest[0], side_rest[1]]
    head_full = lax.all_gather(
        jnp.pad(head_mat, ((0, 0), (0, HEADPAD - HEADCOLS))).astype(BF16), "fsdp", axis=0, tiled=True
    )

    def vec_rows(side):
        vec = side[SIDE].reshape(owners, side_width)[:, :vec_width].reshape(VECS).astype(F32)
        squeeze_bias = jnp.pad(vec[:SQUEEZE], (0, WIDTH - SQUEEZE))
        rows = jnp.stack([vec[SQUEEZE : SQUEEZE + WIDTH], vec[SQUEEZE + WIDTH :], squeeze_bias])
        return jnp.pad(rows, ((0, 5), (0, 0)))

    vecs_all = [vec_rows(side) for side in side_all]

    partner_col = partner[:, None]
    layers = []
    crosses = []
    entry = mix(images.reshape(count, WIDTH), partner_col, mix_pair)
    x, xb, xb_far = entry["x"], entry["xb"], entry["xb_far"]
    pay = first(xb, mats_all[0], devices)["pay"]
    for k in range(LAYERS):
        mats, side, vec = mats_all[k], side_all[k], vecs_all[k]
        one = spatial(xb, mats, side, exchange(pay))
        two = project(one["d"], mats, side, vec, exchange(one["pay"]), one.get("cross"))
        last = k == LAYERS - 1
        three = residual(
            x, two["p"], vec, exchange(two["pay"]), head_full if last else mats_all[k + 1], last
        )
        if "cross" in three:
            crosses.append(three["cross"])
        layers.append(
            dict(
                xb_far=xb_far, d_far=one["d_far"], norm1=one["norm"], norm2=two["norm"],
                pooled=two["pooled"], excite=two["excite"], squeeze=two["squeeze"],
                norm3=three["norm"], normed=three["normed"], mats=mats, weights=mats, side=side,
            )
        )
        x, xb, xb_far, pay = three["x"], three["xb"], three["xb_far"], three["pay"]
    top = head(
        xb, head_full, jnp.pad(fc_bias, (0, LOGITS - CLASSES))[None], labels[:, None], labels[None, :],
        partner_col, mix_pair, layers[-1]["normed"], exchange(pay), image_count,
    )

    def to_owner(blocks):
        rows = blocks.shape[0] * blocks.shape[1]
        return lax.psum_scatter(
            blocks.reshape(rows, blocks.shape[2]), "fsdp", scatter_dimension=0, tiled=True
        )

    upper = dict(xb_far=xb_far, weights=head_full, dz=top["dz"], norm=top["norm"])
    pay = top["pay"]
    stream = None
    globs = [{} for _ in range(LAYERS)]
    blocks = [None] * LAYERS
    for k in reversed(range(LAYERS)):
        layer = layers[k]
        is_head = k == LAYERS - 1
        gate = gate_back(
            is_head, row_count, owners, exchange(pay), upper,
            None if is_head else crosses[k], stream, layer,
        )
        stream = gate["stream"]
        globs[k]["three"] = gate["glob3"]
        blocks[k] = gate["grads"]
        if is_head:
            head_glob, bias_loss = gate["glob"], gate["glob3"][2:6].reshape(LOGITS)
            grad_head = jnp.concatenate([gate["grad_w"], top["grad_fc"]], axis=1)
            shard_head = to_owner(grad_head.reshape(owners, -1, HEADPAD))
        else:
            globs[k + 1]["one"] = gate["glob"]
        tap = tap_back(
            k == 0, row_count, exchange(gate["pay"]), gate["dz2"], layer, stream, layers[max(k - 1, 0)]
        )
        globs[k]["two"] = tap["glob"]
        pay = tap["pay"]
        upper = dict(
            xb_far=layer["xb_far"], weights=layer["mats"], dz=tap["dz"], norm=layer["norm1"], taps=tap["taps"]
        )
    late_taps = jnp.moveaxis(tap["taps"][:9].astype(BF16).reshape(9, owners, side_width), 1, 0)
    late_taps = jnp.broadcast_to(late_taps[None], (replicas, *late_taps.shape))
    late_taps = exchange(late_taps.reshape(devices, 9, side_width))
    final = last_back(row_count, replicas, owners, exchange(pay), layers[0], tap["dz"])
    globs[0]["one"] = final["glob"]
    late_taps = jnp.sum(late_taps.astype(F32), axis=0)

    shards = [None] * LAYERS
    room = blocks[0].shape[1]
    pair = replica_sum(to_owner(jnp.concatenate([blocks[2], blocks[1]], axis=1)))
    shards[2], shards[1] = pair[:room], pair[room:]
    shards[0] = replica_sum(to_owner(blocks[0]))
    shard_head = replica_sum(shard_head)

    part = slice_rows(devices)
    chunks = EXPAND // CHUNK
    late = jnp.sum(exchange(final["grads"]).astype(F32), axis=0).astype(BF16)
    other = lax.ppermute(late, "fsdp", [(half + k, k) for k in range(half)])
    late = spread_over(jnp.stack([late, other]), "dp")[:, :, : chunks * part]
    late = jnp.moveaxis(late.reshape(replicas, 2, chunks, part, CHUNK), 2, 3)
    late = late.reshape(rows_dev, EXPAND).astype(F32)

    def mats_of(shard):
        rows = shard[: chunks * rows_dev].reshape(chunks, rows_dev, CHUNK)
        return jnp.moveaxis(rows, 0, 1).reshape(rows_dev, EXPAND)

    from_mats = [late] + [mats_of(shard) for shard in shards]
    owns_expand = mine < half
    grad_mats = jnp.stack(
        [jnp.where(owns_expand, from_mats[k], from_mats[k + 1]) for k in range(LAYERS)]
    )

    def own_columns(vector, width):
        return lax.dynamic_slice_in_dim(vector, mine * width, width, axis=-1)

    first_row = chunks * rows_dev
    last_row = first_row + 2 * SQUEEZE
    vec_ids = mine * vec_width + jnp.arange(vec_width)
    side_list, vec_list = [], []
    for k in range(LAYERS):
        shard = shards[k][:, :side_width]
        taps = late_taps if k == 0 else shards[k - 1][last_row + 2 : last_row + 11, :side_width]
        norms_part = own_columns(
            jnp.concatenate([globs[k]["one"][0:2], globs[k]["two"][0:2]], axis=0), side_width
        )
        side_list.append(
            jnp.concatenate([taps, shard[first_row : last_row + 1], norms_part], axis=0)
        )
        outer = globs[k]["three"]
        outer = own_columns(
            jnp.concatenate([jnp.zeros((SQUEEZE,), F32), outer[0], outer[1]]), vec_width
        )
        vec_list.append(jnp.where(vec_ids < SQUEEZE, shard[last_row + 1, :vec_width], outer))
    grad_side = jnp.stack(side_list)
    grad_vecs = jnp.stack(vec_list)
    head_tail = own_columns(head_glob[0:2], head_mat.shape[0]).T
    grad_head = jnp.concatenate([shard_head[:, : WIDTH + CLASSES], head_tail], axis=1)
    grad_bias = bias_loss[:CLASSES]
    loss_value = (bias_loss[CLASSES] + bias_loss[CLASSES + 1]) / image_count

    step_float = step[0].astype(F32)
    side_decay = (jnp.arange(SIDE) < 9 + 2 * SQUEEZE).astype(F32)[None, :, None]
    head_decay = (jnp.arange(HEADCOLS) < WIDTH + CLASSES).astype(F32)[None, :]
    mats_moment, mats_square, mats_dir = lamb_moments(
        layer_mats, mats_first, mats_second, grad_mats, 1.0, step_float
    )
    side_moment, side_square, side_dir = lamb_moments(
        layer_side, side_first, side_second, grad_side, side_decay, step_float
    )
    vecs_moment, vecs_square, vecs_dir = lamb_moments(
        layer_vecs, vecs_first, vecs_second, grad_vecs, 0.0, step_float
    )
    head_moment, head_square, head_dir = lamb_moments(
        head_mat, head_first, head_second, grad_head, head_decay, step_float
    )
    bias_moment, bias_square, bias_dir = lamb_moments(
        fc_bias, bias_first, bias_second, grad_bias, 0.0, step_float
    )
    row_ids = mine * rows_dev + jnp.arange(rows_dev)
    squares = jnp.stack(
        [
            group_sums(layer_mats, layer_side, head_mat, row_ids),
            group_sums(mats_dir, side_dir, head_dir, row_ids),
        ]
    )
    norms = jnp.sqrt(jnp.sum(spread_over(squares, "fsdp"), axis=0))
    mats_rate, side_rate, head_rate = rate_maps(norms[0] / norms[1], row_ids)
    mats_new = layer_mats - mats_rate[:, :, None] * mats_dir
    side_new = layer_side - side_rate[:, :, None] * side_dir
    vecs_new = layer_vecs - RATE_VECTOR * vecs_dir
    head_new = head_mat - head_rate[None, :] * head_dir
    bias_new = fc_bias - RATE_VECTOR * bias_dir
    return (
        loss_value,
        mats_new, mats_moment, mats_square,
        side_new, side_moment, side_square,
        vecs_new, vecs_moment, vecs_square,
        head_new, head_moment, head_square,
        bias_new, bias_moment, bias_square,
        norms,
    )


def solution(mesh):
    rows, columns = P(None, "fsdp", None), P(None, None, "fsdp")
    vecs, heads = P(None, "fsdp"), P("fsdp", None)
    return jax.shard_map(
        body,
        mesh=mesh,
        in_specs=(
            P(BOTH, None, None), P(BOTH), P(BOTH, None), P(BOTH), P(),
            rows, columns, vecs, heads, P(),
            rows, rows, columns, columns, vecs, vecs, heads, heads, P(), P(),
        ),
        out_specs=(
            P(),
            rows, rows, rows,
            columns, columns, columns,
            vecs, vecs, vecs,
            heads, heads, heads,
            P(), P(), P(), P(),
        ),
        check_vma=False,
    )
```

```python
import functools
import types

import jax
import jax.numpy as jnp
from jax import lax
from jax.experimental import pallas as pl
from jax.experimental.pallas import tpu as pltpu
from jax.sharding import PartitionSpec as P

WIDTH = 256
EXPAND = 1536
SQUEEZE = 64
HEAD = 1280
CLASSES = 1000
LOGITS = 1024
EDGE = 4
LAYERS = 3
MAP = 16
SIDE = 142
SIDE_PAD = 144
VECS = 576
HEADCOLS = 1258
HEADPAD = 1280

EPS_BN = 0.001
BETA_ONE = 0.9
BETA_TWO = 0.999
EPS_ADAM = 1e-06
DECAY_RATE = 0.01
RATE_MATRIX = 0.5
RATE_VECTOR = 0.25

REPLICAS, OWNERS = BOTH = ("dp", "fsdp")
F32 = jnp.float32
BF16 = jnp.bfloat16
LANE = 128
TILE = 8
ROWS = MAP * TILE
CHUNK = 256
PARTS = CHUNK // LANE
VMEM_BYTES = 60 * 1024 * 1024

NT = (((1,), (1,)), ((), ()))
TN = (((0,), (0,)), ((), ()))


NEAR, FAR, RAW = range(3)


class Refs:
    def __init__(self, names, refs, loads, stores):
        for name, ref in zip(names, refs):
            setattr(self, name, ref)
        self.loads = loads
        self.stores = {id(getattr(self, name)): (k, self.far(name)) for k, name in enumerate(stores)}
        self.pending = {}

    def far(self, name):
        return getattr(self, name + "_far")

    def start(self):
        for index, (name, where) in enumerate(self.loads):
            source = self.far(name) if where is None else self.far(name).at[where]
            near = getattr(self, name)
            copy = pltpu.make_async_copy(source, near, self.load_sem.at[index])
            copy.start()
            self.pending[id(near)] = copy

    def wait(self, *refs):
        for ref in refs:
            self.pending.pop(id(ref)).wait()

    def send(self, *refs):
        for ref in refs:
            index, far = self.stores[id(ref)]
            copy = pltpu.make_async_copy(ref, far, self.store_sem.at[index])
            copy.start()
            self.pending[id(far)] = copy

    def part(self, ref, index, at):
        far = self.stores[id(ref)][1]
        return pltpu.make_async_copy(ref.at[:, at], far.at[:, at], self.part_sem.at[index])

    def finish(self, ref=None):
        for key in list(self.pending):
            self.pending.pop(key).wait()
        if ref is not None:
            for index in range(ref.shape[1] // CHUNK):
                self.part(ref, index, pl.ds(index * CHUNK, CHUNK)).wait()


def shape(dims, dtype=F32):
    return jax.ShapeDtypeStruct(dims, dtype)


def vmem(dims, dtype=F32):
    return pltpu.VMEM(dims, dtype)


def call(kernel, ins, outs, scratch, alias=()):
    near, far = pl.BlockSpec(memory_space=pltpu.VMEM), pl.BlockSpec(memory_space=pltpu.HBM)
    names, arrays, in_specs, loads, stores, extra = [], [], [], [], [], {}
    for name, (array, place) in ins.items():
        arrays.append(array)
        in_specs.append(near if place == NEAR else far)
        if place == NEAR or place == RAW:
            names.append(name)
            continue
        names.append(name + "_far")
        dims, where = array.shape, None
        if place != FAR:
            starts = [part.indices(size)[:2] for part, size in zip(place, dims)]
            dims = tuple(stop - start for start, stop in starts)
            where = tuple(pl.ds(start, stop - start) for start, stop in starts)
        loads.append((name, where))
        extra[name] = vmem(dims, array.dtype)
    for name, (struct, place) in outs.items():
        names.append(name + "_far" if place == FAR else name)
        if place == FAR:
            stores.append(name)
            extra[name] = vmem(struct.shape, struct.dtype)
    extra.update(scratch)
    extra.update(
        load_sem=pltpu.SemaphoreType.DMA((max(len(loads), 1),)),
        store_sem=pltpu.SemaphoreType.DMA((max(len(stores), 1),)),
        part_sem=pltpu.SemaphoreType.DMA((EXPAND // CHUNK,)),
    )

    def flat(*refs):
        kernel(Refs(names + list(extra), refs, loads, stores))

    results = pl.pallas_call(
        flat,
        out_shape=[struct for struct, _ in outs.values()],
        in_specs=in_specs,
        out_specs=[near if place == NEAR else far for _, place in outs.values()],
        scratch_shapes=list(extra.values()),
        input_output_aliases={list(ins).index(a): list(outs).index(b) for a, b in alias},
        compiler_params=pltpu.CompilerParams(vmem_limit_bytes=VMEM_BYTES),
    )(*arrays)
    return types.SimpleNamespace(**dict(zip(outs, results)))


def dot(left, right):
    return jnp.dot(left, right, preferred_element_type=F32)


def dot_nt(left, right):
    return lax.dot_general(left, right, NT, preferred_element_type=F32)


def dot_tn(left, right):
    return lax.dot_general(left, right, TN, preferred_element_type=F32)


def halves(value):
    high = value.astype(BF16)
    return high, (value - high.astype(F32)).astype(BF16)


def stacked(value):
    return jnp.concatenate(halves(value), axis=0)


def folded(value):
    count = value.shape[0] // 2
    return value[:count] + value[count:]


def sigmoid(value):
    return 0.5 * jnp.tanh(0.5 * value) + 0.5


def chunk_at(index, size=CHUNK):
    return pl.ds(pl.multiple_of(index * size, size), size)


def tile_rows(tile):
    return slice(tile * ROWS, (tile + 1) * ROWS)


def tile_images(tile):
    return slice(tile * TILE, (tile + 1) * TILE)


def as_tile(block):
    return block.reshape(MAP, TILE, LANE)


def spread(rows, first, count):
    return jnp.concatenate([rows[first + k : first + k + 1, :] for k in range(count)], axis=1)


def fold(vectors, rows):
    pieces = [
        vector[:, k * LANE : (k + 1) * LANE]
        for vector in vectors
        for k in range(vector.shape[1] // LANE)
    ]
    if rows > len(pieces):
        pieces.append(jnp.zeros((rows - len(pieces), LANE), F32))
    return jnp.concatenate(pieces, axis=0)


def column_sum(value):
    return jnp.sum(value, axis=0, keepdims=True)


def slice_rows(devices):
    return max(1, WIDTH // devices)


def write_alike(pay_ref, rows):
    pay_ref[...] = jnp.broadcast_to(rows.astype(BF16)[None], pay_ref.shape)


def write_with_slices(pay_ref, rows, matrix):
    devices = pay_ref.shape[0]
    part = slice_rows(devices)
    first = rows.shape[0]
    low = rows.astype(BF16)
    for device in range(devices):
        own = matrix[device * part : (device + 1) * part, :]
        block = jnp.concatenate([own[:, :LANE], own[:, LANE:]], axis=0)
        if 2 * part < 16:
            block = jnp.concatenate([block, jnp.zeros((16 - 2 * part, LANE), F32)], axis=0)
        pay_ref[device, 0:first, :] = low
        pay_ref[device, first : first + 16, :] = block.astype(BF16)


def read_matrix(recv_ref, first):
    devices, rows = recv_ref.shape[:2]
    part = slice_rows(devices)
    if part == TILE:
        values = recv_ref[...].astype(F32)
        left = values[:, first : first + part].reshape(WIDTH, LANE)
        right = values[:, first + part : first + 2 * part].reshape(WIDTH, LANE)
        return jnp.concatenate([left, right], axis=1)
    flat = recv_ref[...].reshape(devices * rows, LANE)
    row = lax.broadcasted_iota(jnp.int32, (WIDTH, devices * rows), 0)
    column = lax.broadcasted_iota(jnp.int32, (WIDTH, devices * rows), 1)
    source = row // part * rows + first + row % part
    left = dot(jnp.where(column == source, 1.0, 0.0).astype(BF16), flat)
    right = dot(jnp.where(column == source + part, 1.0, 0.0).astype(BF16), flat)
    return jnp.concatenate([left, right], axis=1)


def moment_rows(columns):
    return -(-3 * columns // LANE // 8) * 8


def centred(total, squares, count):
    return jnp.maximum(squares - total * total / count, 0.0)


def pack_moments(total, squares, count):
    mean = total / count
    high = mean.astype(BF16).astype(F32)
    return fold([high, mean - high, centred(total, squares, count)], moment_rows(total.shape[1]))


def read_moments(recv_ref, columns, count):
    groups = columns // LANE
    devices = recv_ref.shape[0]
    parts = recv_ref[...].astype(F32)
    means = parts[:, :groups] + parts[:, groups : 2 * groups]
    mean = jnp.sum(means, axis=0) / devices
    apart = means - mean[None]
    spread_sum = jnp.sum(parts[:, 2 * groups : 3 * groups], axis=0) / count
    variance = (spread_sum + jnp.sum(apart * apart, axis=0)) / devices
    return spread(mean, 0, groups), lax.rsqrt(spread(variance, 0, groups) + EPS_BN)


def pack_product_moments(x_ref, total, squares, count):
    sums = column_sum(x_ref[...].astype(F32))
    high = sums.astype(BF16).astype(F32)
    return fold([high, sums - high, centred(total, squares, count)], 16)


def read_product_moments(recv_ref, weights, transposed, columns, count):
    devices, rows = recv_ref.shape[:2]
    values = recv_ref[...]
    flat = values.reshape(devices * rows, LANE)
    row = lax.broadcasted_iota(jnp.int32, (devices, devices * rows), 0)
    column = lax.broadcasted_iota(jnp.int32, (devices, devices * rows), 1) - row * rows
    left = dot(jnp.where((column == 0) | (column == 2), 1.0, 0.0).astype(BF16), flat)
    right = dot(jnp.where((column == 1) | (column == 3), 1.0, 0.0).astype(BF16), flat)
    sums = stacked(jnp.concatenate([left, right], axis=1) / count)
    means = folded(dot_nt(sums, weights) if transposed else dot(sums, weights))
    mean = column_sum(means) / devices
    apart = means - mean
    squares = jnp.sum(values.astype(F32), axis=0)
    variance = (spread(squares, 4, columns // LANE) / count + column_sum(apart * apart)) / devices
    return mean, lax.rsqrt(variance + EPS_BN)


def read_sums(recv_ref):
    return jnp.sum(recv_ref[...].astype(F32), axis=0)


def keep_norm(norm_ref, mean, inverse, gain, bias):
    scale = inverse * gain
    norm_ref[0:1, :] = mean
    norm_ref[1:2, :] = inverse
    norm_ref[2:3, :] = scale
    norm_ref[3:4, :] = bias - mean * scale
    norm_ref[4:8, :] = jnp.zeros((4, norm_ref.shape[1]), F32)


def product_sums(x_ref, w_ref, transposed, h_ref, stat_ref):
    def step(index, carry):
        at = chunk_at(index)
        if transposed:
            h_ref[...] = dot_nt(x_ref[...], w_ref[at, :])
        else:
            h_ref[...] = dot(x_ref[...], w_ref[:, at])
        hidden = h_ref[...]
        stat_ref[0:1, at] = column_sum(hidden)
        stat_ref[1:2, at] = column_sum(hidden * hidden)
        return carry

    lax.fori_loop(0, stat_ref.shape[1] // CHUNK, step, 0)


def mix_kernel(r):
    count = r.images.shape[0]
    pixels = r.images[...]
    row = lax.broadcasted_iota(jnp.int32, (ROWS, count), 0)
    column = lax.broadcasted_iota(jnp.int32, (ROWS, count), 1)
    place = lax.shift_right_logical(row, 3)
    inside = jnp.bitwise_and(row, 7)
    pair = r.mix[...].astype(F32)
    mixing = pair[:, 0:1] / (pair[:, 0:1] + pair[:, 1:2])
    for tile in range(count // ROWS):
        near = tile_images(tile)
        other = jnp.concatenate([r.partner[near, :]] * MAP, axis=0)
        weight = jnp.concatenate([mixing[near, :]] * MAP, axis=0)
        own_hot = jnp.where(column == (tile * TILE + inside) * MAP + place, 1.0, 0.0).astype(BF16)
        other_hot = jnp.where(column == other * MAP + place, 1.0, 0.0).astype(BF16)
        mixed = weight * dot(own_hot, pixels) + (1.0 - weight) * dot(other_hot, pixels)
        r.x[tile_rows(tile), :] = mixed
    r.xb[...] = r.x[...].astype(BF16)
    r.send(r.x, r.xb)
    r.finish()


def mix(images, partner, mix_pair):
    dims = images.shape
    return call(
        mix_kernel,
        dict(images=(images, NEAR), partner=(partner, NEAR), mix=(mix_pair, NEAR)),
        dict(x=(shape(dims), FAR), xb=(shape(dims, BF16), FAR)),
        {},
    )


def first_kernel(r):
    count = r.xb.shape[0]
    r.start()
    r.wait(r.xb, r.w)
    product_sums(r.xb, r.w, False, r.h, r.stat)
    write_alike(r.pay, pack_product_moments(r.xb, r.stat[0:1, :], r.stat[1:2, :], count))


def first(xb, mats, devices):
    count = xb.shape[0]
    return call(
        first_kernel,
        dict(xb=(xb, FAR), w=(mats, (slice(0, WIDTH), slice(None)))),
        dict(pay=(shape((devices, 16, LANE), BF16), NEAR)),
        dict(h=vmem((count, CHUNK), F32), stat=vmem((8, EXPAND), F32)),
    )


def tap_terms():
    for row in range(EDGE):
        for col in range(EDGE):
            for row_shift in range(3):
                for col_shift in range(3):
                    from_row, from_col = row + row_shift - 1, col + col_shift - 1
                    if 0 <= from_row < EDGE and 0 <= from_col < EDGE:
                        yield EDGE * row + col, 3 * row_shift + col_shift, EDGE * from_row + from_col


TERMS = list(tap_terms())


def spatial_kernel(r):
    count = r.xb.shape[0]
    r.start()
    r.wait(r.side, r.w, r.xb)
    rows = r.side[...].astype(F32)
    r.taps[0:9, :] = rows[0:9, :]
    mean, inverse = read_product_moments(r.recv, r.w[...], False, EXPAND, count)
    keep_norm(r.norm, mean, inverse, rows[10:11, :], rows[11:12, :])
    r.send(r.norm)
    if r.recv.shape[1] > 16:
        r.cross[...] = jnp.sum(r.recv[...].astype(F32)[:, 16:32], axis=0)

    def step(index, carry):
        at_chunk = chunk_at(index)
        r.h[...] = dot(r.xb[...], r.w[:, at_chunk])
        for part in range(PARTS):
            lanes = chunk_at(index * PARTS + part, LANE)
            taps = [jnp.broadcast_to(r.taps[k : k + 1, lanes], (TILE, LANE)) for k in range(9)]
            scale_row = r.norm[2:3, lanes]
            shift_row = r.norm[3:4, lanes]

            def tile_step(tile, sums):
                at = chunk_at(tile, ROWS)
                pre = r.h[at, part * LANE : (part + 1) * LANE] * scale_row + shift_row
                active = as_tile(pre * sigmoid(pre))
                result = [None] * MAP
                for target, tap, source in TERMS:
                    term = active[source] * taps[tap]
                    result[target] = term if result[target] is None else result[target] + term
                total, squares = sums
                for value in result:
                    total = total + value
                    squares = squares + value * value
                r.d[at, lanes] = jnp.concatenate(result, axis=0).astype(BF16)
                return total, squares

            zero = jnp.zeros((TILE, LANE), F32)
            total, squares = lax.fori_loop(0, count // ROWS, tile_step, (zero, zero))
            r.stat[0:1, lanes] = column_sum(total)
            r.stat[1:2, lanes] = column_sum(squares)
        r.part(r.d, index, at_chunk).start()
        return carry

    lax.fori_loop(0, EXPAND // CHUNK, step, 0)
    write_alike(r.pay, pack_moments(r.stat[0:1, :], r.stat[1:2, :], count))
    r.finish(r.d)


def spatial(xb, mats, side, recv):
    count = xb.shape[0]
    devices = recv.shape[0]
    outs = dict(
        d=(shape((count, EXPAND), BF16), FAR),
        pay=(shape((devices, moment_rows(EXPAND), LANE), BF16), NEAR),
        norm=(shape((8, EXPAND)), FAR),
    )
    if recv.shape[1] > 16:
        outs["cross"] = (shape((16, LANE)), NEAR)
    return call(
        spatial_kernel,
        dict(
            recv=(recv, NEAR),
            side=(side, (slice(2 * SQUEEZE, SIDE_PAD), slice(None))),
            xb=(xb, FAR),
            w=(mats, (slice(0, WIDTH), slice(None))),
        ),
        outs,
        dict(
            h=vmem((count, CHUNK), F32),
            taps=vmem((16, EXPAND), F32),
            stat=vmem((8, EXPAND), F32),
        ),
    )


def project_kernel(with_cross, owners, r):
    count = r.d.shape[0]
    tiles = count // ROWS
    r.start()
    mean, inverse = read_moments(r.recv, EXPAND, count)
    r.wait(r.side)
    rows = r.side[2 * SQUEEZE : SIDE_PAD, :].astype(F32)
    keep_norm(r.norm, mean, inverse, rows[12:13, :], rows[13:14, :])
    r.send(r.norm)
    width, vec_width = EXPAND // owners, VECS // owners
    vec = jnp.concatenate(
        [rows[14:15, k * width : k * width + vec_width] for k in range(owners)], axis=1
    )
    r.vec[...] = jnp.concatenate(
        [vec[:, SQUEEZE : SQUEEZE + WIDTH], vec[:, SQUEEZE + WIDTH :], jnp.zeros((6, WIDTH), F32)], axis=0
    )
    r.wait(r.d)

    def activate(index, carry):
        lanes = chunk_at(index, LANE)
        scale_row = r.norm[2:3, lanes]
        shift_row = r.norm[3:4, lanes]
        for tile in range(tiles):
            at = tile_rows(tile)
            pre = r.d[at, lanes].astype(F32) * scale_row + shift_row
            active = pre * sigmoid(pre)
            r.a[at, lanes] = active
            r.pooled[tile_images(tile), lanes] = jnp.sum(as_tile(active), axis=0) / MAP
        return carry

    lax.fori_loop(0, EXPAND // LANE, activate, 0)
    r.send(r.pooled)
    before = folded(dot_nt(stacked(r.pooled[...]), r.side[0:SQUEEZE, :])) + vec[:, :SQUEEZE]
    r.squeeze[...] = before
    r.send(r.squeeze)
    opened = folded(dot(stacked(before * sigmoid(before)), r.side[SQUEEZE : 2 * SQUEEZE, :]))
    r.excite[...] = sigmoid(opened + rows[9:10, :])
    r.send(r.excite)

    def gate(index, carry):
        lanes = chunk_at(index, LANE)
        for tile in range(tiles):
            at = tile_rows(tile)
            scaled = as_tile(r.a[at, lanes]) * r.excite[tile_images(tile), lanes][None]
            r.y[at, lanes] = scaled.reshape(ROWS, LANE).astype(BF16)
        return carry

    lax.fori_loop(0, EXPAND // LANE, gate, 0)
    r.wait(r.w)
    projected = dot_nt(r.y[...], r.w[...])
    r.p[...] = projected
    r.send(r.p)
    moments = pack_moments(column_sum(projected), column_sum(projected * projected), count)
    if with_cross:
        moments = jnp.concatenate([moments, r.cross[...]], axis=0)
    write_alike(r.pay, moments)
    r.finish()


def project(d, mats, side, recv, cross, owners):
    count = d.shape[0]
    images = count // MAP
    devices = recv.shape[0]
    ins = dict(
        recv=(recv, NEAR),
        side=(side, FAR),
        d=(d, FAR),
        w=(mats, (slice(WIDTH, 2 * WIDTH), slice(None))),
    )
    rows = moment_rows(WIDTH)
    if cross is not None:
        ins["cross"] = (cross, NEAR)
        rows += 16
    return call(
        functools.partial(project_kernel, cross is not None, owners),
        ins,
        dict(
            p=(shape((count, WIDTH)), FAR),
            vec=(shape((8, WIDTH)), NEAR),
            pay=(shape((devices, rows, LANE), BF16), NEAR),
            norm=(shape((8, EXPAND)), FAR),
            pooled=(shape((images, EXPAND)), FAR),
            excite=(shape((images, EXPAND)), FAR),
            squeeze=(shape((images, SQUEEZE)), FAR),
        ),
        dict(a=vmem((count, EXPAND), F32), y=vmem((count, EXPAND), BF16)),
    )


def residual_kernel(transposed, with_cross, r):
    count = r.p.shape[0]
    r.start()
    mean, inverse = read_moments(r.recv, WIDTH, count)
    keep_norm(r.norm, mean, inverse, r.vec[0:1, :], r.vec[1:2, :])
    if with_cross:
        r.cross[...] = read_matrix(r.recv, moment_rows(WIDTH))
        r.send(r.cross)
    r.wait(r.p)
    normed = (r.p[...] - mean) * inverse
    r.normed[...] = normed
    r.wait(r.before)
    result = r.before[...] + (normed * r.vec[0:1, :] + r.vec[1:2, :])
    r.x[...] = result
    r.xb[...] = result.astype(BF16)
    r.send(r.norm, r.normed, r.x, r.xb)
    cross = dot_tn(normed.astype(BF16), r.xb[...])
    r.wait(r.w)
    product_sums(r.xb, r.w, transposed, r.h, r.stat)
    moments = pack_product_moments(r.xb, r.stat[0:1, :], r.stat[1:2, :], count)
    write_with_slices(r.pay, moments, cross)
    r.finish()


def residual(x, p, vec, recv, weights, transposed):
    count = x.shape[0]
    devices = recv.shape[0]
    with_cross = recv.shape[1] > moment_rows(WIDTH)
    columns = HEAD if transposed else EXPAND
    where = (slice(0, HEAD), slice(0, WIDTH)) if transposed else (slice(0, WIDTH), slice(None))
    outs = dict(
        x=(shape((count, WIDTH)), FAR),
        xb=(shape((count, WIDTH), BF16), FAR),
        normed=(shape((count, WIDTH)), FAR),
        pay=(shape((devices, 32, LANE), BF16), NEAR),
        norm=(shape((8, WIDTH)), FAR),
    )
    if with_cross:
        outs["cross"] = (shape((WIDTH, WIDTH)), FAR)
    return call(
        functools.partial(residual_kernel, transposed, with_cross),
        dict(
            recv=(recv, NEAR), vec=(vec, NEAR), p=(p, FAR), before=(x, FAR), w=(weights, where)
        ),
        outs,
        dict(h=vmem((count, CHUNK), F32), stat=vmem((8, columns), F32)),
    )


def head_rows(last_columns):
    pick_row = lax.broadcasted_iota(jnp.int32, (TILE, LANE), 0)
    pick_col = lax.broadcasted_iota(jnp.int32, (TILE, LANE), 1)
    first_col = WIDTH + CLASSES - (HEADPAD - LANE)
    pick = jnp.where((pick_col == pick_row + first_col) & (pick_row < 2), 1.0, 0.0).astype(BF16)
    return dot_nt(pick, last_columns)


def head_kernel(image_count, r):
    count = r.xb.shape[0]
    tiles = count // ROWS
    images = count // MAP
    r.start()
    r.wait(r.xb, r.w)
    mean, inverse = read_product_moments(r.recv, r.w[...], True, HEAD, count)
    cross = jnp.sum(r.recv[...].astype(F32)[:, 16:32], axis=0)
    r.wait(r.classifier)
    gain_bias = head_rows(r.classifier[:, LOGITS - LANE :])
    keep_norm(r.norm, mean, inverse, gain_bias[0:1, :], gain_bias[1:2, :])
    r.send(r.norm)

    def features(index, carry):
        at_chunk = chunk_at(index)
        r.h[:, at_chunk] = dot_nt(r.xb[...], r.w[at_chunk, :])
        for part in range(PARTS):
            lanes = chunk_at(index * PARTS + part, LANE)
            scale_row = r.norm[2:3, lanes]
            shift_row = r.norm[3:4, lanes]
            for tile in range(tiles):
                pre = r.h[tile_rows(tile), lanes] * scale_row + shift_row
                active = as_tile(pre * sigmoid(pre))
                r.f[tile_images(tile), lanes] = jnp.sum(active, axis=0) / MAP
        return carry

    lax.fori_loop(0, HEAD // CHUNK, features, 0)
    features_low = r.f[...].astype(BF16)
    classifier = r.classifier[...]
    ids = lax.broadcasted_iota(jnp.int32, (images, LOGITS), 1)
    logits = dot(features_low, classifier) + r.bias[...]
    logits = jnp.where(ids < CLASSES, logits, -1e30)
    row_max = jnp.max(logits, axis=1, keepdims=True)
    log_total = row_max + jnp.log(jnp.sum(jnp.exp(logits - row_max), axis=1, keepdims=True))
    pair = r.mix[...].astype(F32)
    mixing = pair[:, 0:1] / (pair[:, 0:1] + pair[:, 1:2])
    people = lax.broadcasted_iota(jnp.int32, (images, images), 1)
    label_row = jnp.broadcast_to(r.label_row[...].astype(F32), (images, images))
    partner_label = jnp.sum(
        jnp.where(people == r.partner[...], label_row, 0.0), axis=1, keepdims=True
    ).astype(jnp.int32)
    own_hot = jnp.where(ids == r.label_col[...], 1.0, 0.0)
    other_hot = jnp.where(ids == partner_label, 1.0, 0.0)
    own_logit = jnp.sum(own_hot * logits, axis=1, keepdims=True)
    other_logit = jnp.sum(other_hot * logits, axis=1, keepdims=True)
    loss = column_sum(mixing * (log_total - own_logit) + (1.0 - mixing) * (log_total - other_logit))
    grad_logits = (
        jnp.exp(logits - log_total) - mixing * own_hot - (1.0 - mixing) * other_hot
    ) / image_count
    grad_low = grad_logits.astype(BF16)
    r.grad_fc[...] = dot_tn(features_low, grad_low).astype(BF16)
    fc_copy = pltpu.make_async_copy(r.grad_fc, r.grad_head.at[:, pl.ds(WIDTH, LOGITS)], r.part_sem.at[0])
    fc_copy.start()
    r.f[...] = dot_nt(grad_low, classifier) / MAP
    bias_sum = column_sum(grad_logits)
    bias_ids = lax.broadcasted_iota(jnp.int32, (1, LOGITS), 1)
    loss_high = loss.astype(BF16).astype(F32)
    bias_sum = jnp.where(bias_ids == CLASSES, loss_high, bias_sum)
    bias_sum = jnp.where(bias_ids == CLASSES + 1, loss - loss_high, bias_sum)

    def back(index, carry):
        lanes = chunk_at(index, LANE)
        scale_row = r.norm[2:3, lanes]
        shift_row = r.norm[3:4, lanes]
        mean_row = r.norm[0:1, lanes]
        total = jnp.zeros((TILE, LANE), F32)
        weighted = jnp.zeros((TILE, LANE), F32)
        for tile in range(tiles):
            at = tile_rows(tile)
            hidden = r.h[at, lanes]
            pre = hidden * scale_row + shift_row
            gate = sigmoid(pre)
            slope = as_tile(gate * (1.0 + pre * (1.0 - gate)))
            grad = slope * r.f[tile_images(tile), lanes][None]
            total = total + jnp.sum(grad, axis=0)
            weighted = weighted + jnp.sum(grad * as_tile(hidden - mean_row), axis=0)
            flat = grad.reshape(ROWS, LANE)
            r.dz[at, lanes] = flat.astype(BF16)
            r.q[at, lanes] = (flat * scale_row).astype(BF16)
        r.stat[0:1, lanes] = column_sum(total)
        r.stat[1:2, lanes] = column_sum(weighted)
        return carry

    lax.fori_loop(0, HEAD // LANE, back, 0)
    r.send(r.dz)
    below = dot(r.q[...], r.w[...])
    r.wait(r.normed)
    rows = fold(
        [
            r.stat[0:1, :], r.stat[1:2, :] * inverse,
            column_sum(below), column_sum(below * r.normed[...]), bias_sum,
        ],
        32,
    )
    write_alike(r.pay, jnp.concatenate([rows, cross], axis=0))
    fc_copy.wait()
    r.finish()


def head(xb, head_full, bias, label_col, label_row, partner, mix_pair, normed, recv, image_count):
    count = xb.shape[0]
    images = count // MAP
    devices = recv.shape[0]
    return call(
        functools.partial(head_kernel, image_count),
        dict(
            recv=(recv, NEAR),
            xb=(xb, FAR),
            bias=(bias, NEAR),
            label_col=(label_col, NEAR),
            label_row=(label_row, NEAR),
            partner=(partner, NEAR),
            mix=(mix_pair, NEAR),
            w=(head_full, (slice(0, HEAD), slice(0, WIDTH))),
            classifier=(head_full, (slice(0, HEAD), slice(WIDTH, HEADPAD))),
            normed=(normed, FAR),
        ),
        dict(
            dz=(shape((count, HEAD), BF16), FAR),
            pay=(shape((devices, 48, LANE), BF16), NEAR),
            norm=(shape((8, HEAD)), FAR),
            grad_head=(shape((HEAD, HEADPAD), BF16), RAW),
        ),
        dict(
            h=vmem((count, HEAD), F32),
            grad_fc=vmem((HEAD, LOGITS), BF16),
            f=vmem((images, HEAD), F32),
            q=vmem((count, HEAD), BF16),
            stat=vmem((8, HEAD), F32),
        ),
    )


def product_back(is_head, row_count, sums, columns, r):
    groups = columns // LANE
    sum_bias = spread(sums, 0, groups)
    sum_gain = spread(sums, groups, groups)
    r.glob[0:1, :] = sum_gain
    r.glob[1:2, :] = sum_bias
    r.glob[2:8, :] = jnp.zeros((6, columns), F32)
    r.send(r.glob)
    r.wait(r.unorm, r.xb, r.w, r.dz)
    mean = r.unorm[0:1, :]
    scale = r.unorm[2:3, :]
    slant = scale * r.unorm[1:2, :] * (sum_gain / row_count)
    r.coef[0:1, :columns] = slant
    r.coef[1:2, :columns] = mean * slant - scale * (sum_bias / row_count)
    r.xt[...] = r.xb[...].T
    count = r.xb.shape[0]

    def step(index, carry):
        at = chunk_at(index)
        if is_head:
            r.h[...] = dot_nt(r.xb[...], r.w[at, :])
        else:
            r.h[...] = dot(r.xb[...], r.w[:, at])
        grad = r.dz[:, at].astype(F32) * r.unorm[2:3, at] - r.h[...] * r.coef[0:1, at] + r.coef[1:2, at]
        low = grad.astype(BF16)
        r.dh[0:count, at] = low
        if is_head:
            r.grad_w[at, :] = dot_tn(low, r.xb[...]).astype(r.grad_w.dtype)
        else:
            r.grad_w[:, at] = dot(r.xt[...], low).astype(r.grad_w.dtype)
        return carry

    lax.fori_loop(0, columns // CHUNK, step, 0)
    return scale * sum_bias, slant


def owner_blocks(r, owners, row_of_owner, taps):
    rows_dev = 2 * WIDTH // owners
    width = EXPAND // owners
    vec_width = VECS // owners
    chunks = EXPAND // CHUNK
    squeeze_sums = jnp.concatenate([r.squeeze_sum[...], jnp.zeros((1, VECS - LANE), F32)], axis=1)
    for owner in range(owners):
        at = slice(owner * width, (owner + 1) * width)
        squeeze_row = squeeze_sums[:, owner * vec_width : (owner + 1) * vec_width]
        squeeze_row = jnp.concatenate([squeeze_row, jnp.zeros((1, width - vec_width), F32)], axis=1)
        pieces = [r.excite_sum[:, at], squeeze_row]
        pieces.append(taps[0:9, at] if taps is not None else jnp.zeros((9, width), F32))
        pieces.append(jnp.zeros((5, width), F32))
        first_row = chunks * rows_dev
        r.grads[owner, first_row : first_row + 2 * SQUEEZE, 0:width] = r.rx[:, at].astype(BF16)
        last_row = first_row + 2 * SQUEEZE
        r.grads[owner, last_row : last_row + 16, 0:width] = jnp.concatenate(pieces, axis=0).astype(BF16)


def gate_kernel(is_head, row_count, owners, r):
    columns = HEAD if is_head else EXPAND
    groups = columns // LANE
    count = r.xb.shape[0]
    tiles = count // ROWS
    rows_dev = 2 * WIDTH // owners
    r.start()
    sums = read_sums(r.recv)
    bias_pull, slant = product_back(is_head, row_count, sums, columns, r)
    if is_head:
        head_copy = pltpu.make_async_copy(r.grad_w, r.grad_head.at[:, pl.ds(0, WIDTH)], r.part_sem.at[0])
        head_copy.start()
        weights = r.w[...].astype(F32)
        column = lax.broadcasted_iota(jnp.int32, (1, WIDTH), 1)
        high, low = halves(jnp.broadcast_to(bias_pull, (TILE, columns)))
        pull = column_sum(dot(high, r.w[...]) + dot(low, r.w[...])) / TILE
        turned = jnp.broadcast_to(slant, (LANE, columns)).T
        slanted = (weights * jnp.concatenate([turned, turned], axis=1)).astype(BF16)
        square = dot_tn(slanted, r.w[...])
        stream = dot(r.dh[0:count, :columns], r.w[...])
        cross = read_matrix(r.recv, 32)
    else:
        r.dh[count : count + WIDTH, :] = (r.w[...].astype(F32) * slant).astype(BF16)
        high, low = halves(bias_pull)
        r.dh[count + WIDTH :, :] = jnp.concatenate(
            [high.astype(F32), low.astype(F32), jnp.zeros((14, columns), F32)], axis=0
        ).astype(BF16)
        product = dot_nt(r.dh[...], r.w[...])
        square = product[count : count + WIDTH]
        pull = column_sum(product[count + WIDTH : count + WIDTH + 2])
        stream = r.stream_in[...] + product[0:count]
        r.wait(r.cross)
        cross = r.cross[...]
    r.stream[...] = stream
    sum_bias = spread(sums, 2 * groups, WIDTH // LANE) - pull
    corrected = column_sum(cross.T * square)
    sum_gain = spread(sums, 2 * groups + WIDTH // LANE, WIDTH // LANE) - corrected
    r.glob3[0:1, :] = sum_gain
    r.glob3[1:2, :] = sum_bias
    if is_head:
        first_row = 2 * groups + 2 * WIDTH // LANE
        r.glob3[2:6, :] = jnp.concatenate(
            [spread(sums, first_row + PARTS * k, PARTS) for k in range(LOGITS // WIDTH)], axis=0
        )
    else:
        r.glob3[2:6, :] = jnp.zeros((4, WIDTH), F32)
    r.glob3[6:8, :] = jnp.zeros((2, WIDTH), F32)
    r.send(r.glob3)
    r.wait(r.norm3, r.normed)
    grad_p = r.norm3[2:3, :] * (
        stream - sum_bias / row_count - r.normed[...] * (sum_gain / row_count)
    )
    r.gp[...] = grad_p.astype(BF16)
    r.gt[...] = r.gp[...].T
    r.wait(r.wp, r.d, r.norm2, r.excite)
    half = owners // 2

    def first(index, carry):
        at_chunk = chunk_at(index)
        r.h[...] = dot(r.gp[...], r.wp[:, at_chunk])
        for part in range(PARTS):
            lanes = chunk_at(index * PARTS + part, LANE)
            scale_row = r.norm2[2:3, lanes]
            shift_row = r.norm2[3:4, lanes]
            for tile in range(tiles):
                at = tile_rows(tile)
                near = tile_images(tile)
                pre = r.d[at, lanes].astype(F32) * scale_row + shift_row
                gate = sigmoid(pre)
                active = pre * gate
                slope = gate + active - active * gate
                grad = r.h[at, part * LANE : (part + 1) * LANE]
                factor = r.excite[near, lanes]
                r.ge[near, lanes] = jnp.sum(as_tile(grad * active), axis=0)
                r.y[at, lanes] = (as_tile(active) * factor[None]).reshape(ROWS, LANE).astype(BF16)
                r.slope[at, lanes] = slope
                r.u[at, lanes] = (as_tile(grad * slope) * factor[None]).reshape(ROWS, LANE)
        grad_p_chunk = dot(r.gt[...], r.y[:, at_chunk])
        place = pl.ds(pl.multiple_of(index * rows_dev, rows_dev), rows_dev)
        for owner in range(half):
            cut = slice(owner * rows_dev, (owner + 1) * rows_dev)
            r.grads[half + owner, place, :] = grad_p_chunk[cut, :].astype(BF16)
            if is_head:
                r.grads[owner, place, :] = jnp.zeros((rows_dev, CHUNK), BF16)
            else:
                r.grads[owner, place, :] = r.grad_w[cut, at_chunk]
        return carry

    lax.fori_loop(0, EXPAND // CHUNK, first, 0)
    r.wait(r.pooled, r.squeeze, r.side)
    excite = r.excite[...]
    grad_gate = r.ge[...] * excite * (1.0 - excite)
    before = r.squeeze[...]
    opened = sigmoid(before)
    squeezed = before * opened
    reduce_mat = r.side[0:SQUEEZE, :]
    excite_mat = r.side[SQUEEZE:, :]
    gate_high, gate_low = halves(grad_gate)
    grad_squeezed = folded(dot_nt(jnp.concatenate([gate_high, gate_low], axis=0), excite_mat))
    grad_pre = grad_squeezed * (opened * (1.0 + before * (1.0 - opened)))
    r.pool[...] = folded(dot(stacked(grad_pre), reduce_mat)) / MAP

    def second(index, carry):
        lanes = chunk_at(index, LANE)
        mean_row = r.norm2[0:1, lanes]
        total = jnp.zeros((TILE, LANE), F32)
        weighted = jnp.zeros((TILE, LANE), F32)
        for tile in range(tiles):
            at = tile_rows(tile)
            pool = r.pool[tile_images(tile), lanes]
            grad = as_tile(r.u[at, lanes]) + as_tile(r.slope[at, lanes]) * pool[None]
            total = total + jnp.sum(grad, axis=0)
            weighted = weighted + jnp.sum(
                grad * as_tile(r.d[at, lanes].astype(F32) - mean_row), axis=0
            )
            r.dz2[at, lanes] = grad.reshape(ROWS, LANE).astype(BF16)
        r.stat[0:1, lanes] = column_sum(total)
        r.stat[1:2, lanes] = column_sum(weighted)
        return carry

    lax.fori_loop(0, EXPAND // LANE, second, 0)
    r.send(r.dz2)
    write_alike(r.pay, fold([r.stat[0:1, :], r.stat[1:2, :] * r.norm2[1:2, :]], 24))
    squeezed_high, squeezed_low = halves(squeezed)
    pre_high, pre_low = halves(grad_pre)
    pooled_high, pooled_low = halves(r.pooled[...])
    r.rx[SQUEEZE:, :] = dot_tn(
        jnp.concatenate([squeezed_high, squeezed_low, squeezed_high], axis=0),
        jnp.concatenate([gate_high, gate_high, gate_low], axis=0),
    )
    r.rx[0:SQUEEZE, :] = dot_tn(
        jnp.concatenate([pre_high, pre_low, pre_high], axis=0),
        jnp.concatenate([pooled_high, pooled_high, pooled_low], axis=0),
    )
    r.excite_sum[...] = column_sum(grad_gate)
    r.squeeze_sum[...] = jnp.concatenate(
        [column_sum(grad_pre), jnp.zeros((1, LANE - SQUEEZE), F32)], axis=1
    )
    taps = None
    if not is_head:
        r.wait(r.taps)
        taps = r.taps[...]
    owner_blocks(r, owners, half, taps)
    room = r.grads.shape[1]
    place = pl.ds((r.blocks.shape[1] - room) * (not is_head), room)
    blocks_copy = pltpu.make_async_copy(r.grads, r.blocks.at[:, place, :], r.part_sem.at[1])
    blocks_copy.start()
    blocks_copy.wait()
    if is_head:
        head_copy.wait()
    r.finish()


def gate_back(is_head, row_count, owners, recv, upper, cross, stream, lower, blocks, extra_room):
    count = upper.xb.shape[0]
    images = count // MAP
    devices = recv.shape[0]
    columns = HEAD if is_head else EXPAND
    block = EXPAND // CHUNK * (2 * WIDTH // owners) + 2 * SQUEEZE + 16
    where = (slice(0, HEAD), slice(0, WIDTH)) if is_head else (slice(0, WIDTH), slice(None))
    ins = dict(
        recv=(recv, NEAR),
        unorm=(upper.norm, FAR),
        xb=(upper.xb, FAR),
        w=(upper.weights, where),
        dz=(upper.dz, FAR),
        norm3=(lower.norm3, FAR),
        normed=(lower.normed, FAR),
        norm2=(lower.norm2, FAR),
        wp=(lower.mats, (slice(WIDTH, 2 * WIDTH), slice(None))),
        d=(lower.d, FAR),
        excite=(lower.excite, FAR),
        pooled=(lower.pooled, FAR),
        squeeze=(lower.squeeze, FAR),
        side=(lower.side, (slice(0, 2 * SQUEEZE), slice(None))),
    )
    outs = dict(
        dz2=(shape((count, EXPAND), BF16), FAR),
        pay=(shape((devices, 24, LANE), BF16), NEAR),
        stream=(shape((count, WIDTH)), NEAR),
        blocks=(shape((owners, block * (1 + extra_room), CHUNK), BF16), RAW),
        glob=(shape((8, columns)), FAR),
        glob3=(shape((8, WIDTH)), FAR),
    )
    scratch = dict(
        grads=vmem((owners, block, CHUNK), BF16),
        xt=vmem((WIDTH, count), BF16),
        h=vmem((count, CHUNK), F32),
        coef=vmem((8, EXPAND), F32),
        dh=vmem((count + WIDTH + 16, columns), BF16),
        u=vmem((count, EXPAND), F32),
        slope=vmem((count, EXPAND), F32),
        y=vmem((count, EXPAND), BF16),
        gp=vmem((count, WIDTH), BF16),
        gt=vmem((WIDTH, count), BF16),
        ge=vmem((images, EXPAND), F32),
        pool=vmem((images, EXPAND), F32),
        rx=vmem((2 * SQUEEZE, EXPAND), F32),
        excite_sum=vmem((1, EXPAND), F32),
        squeeze_sum=vmem((1, LANE), F32),
        stat=vmem((8, EXPAND), F32),
    )
    alias = []
    if is_head:
        ins["grad_head_in"] = (upper.grad_head, RAW)
        outs["grad_head"] = (shape((HEAD, HEADPAD), BF16), RAW)
        scratch["grad_w"] = vmem((HEAD, WIDTH), BF16)
        alias.append(("grad_head_in", "grad_head"))
    else:
        ins["cross"] = (cross, FAR)
        ins["stream_in"] = (stream, NEAR)
        ins["taps"] = (upper.taps, FAR)
        scratch["grad_w"] = vmem((WIDTH, EXPAND), BF16)
        if blocks is not None:
            ins["blocks_in"] = (blocks, RAW)
            outs["blocks"] = (shape(blocks.shape, BF16), RAW)
            alias.append(("blocks_in", "blocks"))
    return call(functools.partial(gate_kernel, is_head, row_count, owners), ins, outs, scratch, alias)


def tap_kernel(is_first, row_count, r):
    count = r.dz2.shape[0]
    groups = EXPAND // LANE
    r.start()
    sums = read_sums(r.recv)
    sum_bias = spread(sums, 0, groups)
    sum_gain = spread(sums, groups, groups)
    r.glob[0:1, :] = sum_gain
    r.glob[1:2, :] = sum_bias
    r.glob[2:8, :] = jnp.zeros((6, EXPAND), F32)
    r.send(r.glob)
    r.wait(r.side, r.norm2)
    scale2 = r.norm2[2:3, :]
    slant2 = scale2 * r.norm2[1:2, :] * (sum_gain / row_count)
    r.coef[0:9, :] = r.side[...].astype(F32)[0:9, :]
    r.coef[9:10, :] = slant2
    r.coef[10:11, :] = r.norm2[0:1, :] * slant2 - scale2 * (sum_bias / row_count)
    r.wait(r.norm1, r.xb, r.w, r.d, r.dz2)

    def step(index, carry):
        at_chunk = chunk_at(index)
        r.h[...] = dot(r.xb[...], r.w[:, at_chunk])
        for part in range(PARTS):
            lanes = chunk_at(index * PARTS + part, LANE)
            near = slice(part * LANE, (part + 1) * LANE)
            taps = [jnp.broadcast_to(r.coef[k : k + 1, lanes], (TILE, LANE)) for k in range(9)]

            def tile_step(tile, sums_in):
                at = chunk_at(tile, ROWS)
                grad_d = as_tile(
                    r.dz2[at, lanes].astype(F32) * r.norm2[2:3, lanes]
                    - r.d[at, lanes].astype(F32) * r.coef[9:10, lanes]
                    + r.coef[10:11, lanes]
                )
                hidden = r.h[at, near]
                pre = hidden * r.norm1[2:3, lanes] + r.norm1[3:4, lanes]
                gate = sigmoid(pre)
                flat = pre * gate
                active = as_tile(flat)
                slope = as_tile(gate + flat - flat * gate)
                apart = as_tile(hidden - r.norm1[0:1, lanes])
                grad_a = [None] * MAP
                tap_sums = [None] * 9
                for target, tap, source in TERMS:
                    term = grad_d[target] * taps[tap]
                    grad_a[source] = term if grad_a[source] is None else grad_a[source] + term
                    term = grad_d[target] * active[source]
                    tap_sums[tap] = term if tap_sums[tap] is None else tap_sums[tap] + term
                total, weighted = sums_in[9], sums_in[10]
                grads = []
                for place in range(MAP):
                    grad = grad_a[place] * slope[place]
                    total = total + grad
                    weighted = weighted + grad * apart[place]
                    grads.append(grad)
                grad = jnp.concatenate(grads, axis=0)
                r.dz[at, lanes] = grad.astype(BF16)
                if not is_first:
                    r.q[at, lanes] = (grad * r.norm1[2:3, lanes]).astype(BF16)
                return (*[sums_in[k] + tap_sums[k] for k in range(9)], total, weighted)

            zero = jnp.zeros((TILE, LANE), F32)
            result = lax.fori_loop(0, count // ROWS, tile_step, (zero,) * 11)
            for k in range(9):
                r.taps[k : k + 1, lanes] = column_sum(result[k])
            r.stat[0:1, lanes] = column_sum(result[9])
            r.stat[1:2, lanes] = column_sum(result[10])
        r.part(r.dz, index, at_chunk).start()
        return carry

    lax.fori_loop(0, EXPAND // CHUNK, step, 0)
    r.taps[9:16, :] = jnp.zeros((7, EXPAND), F32)
    r.send(r.taps)
    vectors = [r.stat[0:1, :], r.stat[1:2, :] * r.norm1[1:2, :]]
    if not is_first:
        below = r.stream[...] + dot_nt(r.q[...], r.w[...])
        r.wait(r.normed)
        vectors.append(column_sum(below))
        vectors.append(column_sum(below * r.normed[...]))
    write_alike(r.pay, fold(vectors, r.pay.shape[1]))
    r.finish(r.dz)


def tap_back(is_first, row_count, recv, dz2, layer, stream, below):
    count = dz2.shape[0]
    devices = recv.shape[0]
    ins = dict(
        recv=(recv, NEAR),
        side=(layer.side, (slice(2 * SQUEEZE, SIDE_PAD), slice(None))),
        norm2=(layer.norm2, FAR),
        norm1=(layer.norm1, FAR),
        xb=(layer.xb, FAR),
        w=(layer.mats, (slice(0, WIDTH), slice(None))),
        dz2=(dz2, FAR),
        d=(layer.d, FAR),
    )
    scratch = dict(
        h=vmem((count, CHUNK), F32),
        coef=vmem((16, EXPAND), F32),
        stat=vmem((8, EXPAND), F32),
    )
    if not is_first:
        ins["stream"] = (stream, NEAR)
        ins["normed"] = (below.normed, FAR)
        scratch["q"] = vmem((count, EXPAND), BF16)
    return call(
        functools.partial(tap_kernel, is_first, row_count),
        ins,
        dict(
            dz=(shape((count, EXPAND), BF16), FAR),
            pay=(shape((devices, 24 if is_first else 32, LANE), BF16), NEAR),
            taps=(shape((16, EXPAND)), FAR),
            glob=(shape((8, EXPAND)), FAR),
        ),
        scratch,
    )


def last_kernel(row_count, replicas, owners, r):
    r.start()
    product_back(False, row_count, read_sums(r.recv), EXPAND, r)
    half = owners // 2
    part = slice_rows(replicas * owners)
    rows_dev = 2 * WIDTH // owners
    chunks = EXPAND // CHUNK
    pad = r.grads.shape[1] - chunks * part
    for replica in range(replicas):
        for owner in range(owners):
            first_row = rows_dev * (owner % half) + (2 * replica + owner // half) * part
            own = r.grad_w[first_row : first_row + part, :]
            block = jnp.concatenate(
                [own[:, k * CHUNK : (k + 1) * CHUNK] for k in range(chunks)]
                + ([jnp.zeros((pad, CHUNK), F32)] if pad else []),
                axis=0,
            )
            r.grads[replica * owners + owner, :, :] = block.astype(BF16)
    r.finish()


def last_back(row_count, replicas, owners, recv, layer, dz):
    count = dz.shape[0]
    devices = recv.shape[0]
    block = -(-EXPAND // CHUNK * slice_rows(devices) // 16) * 16
    return call(
        functools.partial(last_kernel, row_count, replicas, owners),
        dict(
            recv=(recv, NEAR),
            dz=(dz, FAR),
            unorm=(layer.norm1, FAR),
            xb=(layer.xb, FAR),
            w=(layer.mats, (slice(0, WIDTH), slice(None))),
        ),
        dict(
            grads=(shape((devices, block, CHUNK), BF16), NEAR),
            glob=(shape((8, EXPAND)), FAR),
        ),
        dict(
            xt=vmem((WIDTH, count), BF16),
            h=vmem((count, CHUNK), F32),
            coef=vmem((8, EXPAND), F32),
            dh=vmem((count, EXPAND), BF16),
            grad_w=vmem((WIDTH, EXPAND), F32),
        ),
    )


def lamb_moments(weight, moment_one, moment_two, gradient, decay_mask, step_float):
    first_new = BETA_ONE * moment_one + (1.0 - BETA_ONE) * gradient
    second_new = BETA_TWO * moment_two + (1.0 - BETA_TWO) * gradient * gradient
    corrected = (
        first_new
        / (1.0 - BETA_ONE**step_float)
        / (jnp.sqrt(second_new / (1.0 - BETA_TWO**step_float)) + EPS_ADAM)
    )
    return (first_new, second_new, corrected + DECAY_RATE * decay_mask * weight)


def group_sums(mats, side, head_shard, row_ids):
    rows = jnp.sum(mats * mats, axis=2)
    is_expand = (row_ids < WIDTH)[None, :]
    side_rows = jnp.sum(side * side, axis=2)
    head_cols = jnp.sum(head_shard * head_shard, axis=0)
    per_layer = jnp.stack(
        [
            jnp.sum(jnp.where(is_expand, rows, 0.0), axis=1),
            jnp.sum(jnp.where(is_expand, 0.0, rows), axis=1),
            jnp.sum(side_rows[:, :9], axis=1),
            jnp.sum(side_rows[:, 9 : 9 + SQUEEZE], axis=1),
            jnp.sum(side_rows[:, 9 + SQUEEZE : 9 + 2 * SQUEEZE], axis=1),
        ],
        axis=1,
    )
    tail = jnp.stack([jnp.sum(head_cols[:WIDTH]), jnp.sum(head_cols[WIDTH : WIDTH + CLASSES])])
    return jnp.concatenate([per_layer.reshape(-1), tail])


def rate_maps(trust_ratio, row_ids):
    groups = trust_ratio[: 5 * LAYERS].reshape(LAYERS, 5)
    mats_rate = RATE_MATRIX * jnp.where(row_ids[None, :] < WIDTH, groups[:, 0:1], groups[:, 1:2])
    side_ids = jnp.arange(SIDE)[None, :]
    side_rate = jnp.where(
        side_ids < 9,
        RATE_MATRIX * groups[:, 2:3],
        jnp.where(
            side_ids < 9 + SQUEEZE,
            RATE_MATRIX * groups[:, 3:4],
            jnp.where(side_ids < 9 + 2 * SQUEEZE, RATE_MATRIX * groups[:, 4:5], RATE_VECTOR),
        ),
    )
    col_ids = jnp.arange(HEADCOLS)
    head_rate = jnp.where(
        col_ids < WIDTH,
        RATE_MATRIX * trust_ratio[5 * LAYERS],
        jnp.where(
            col_ids < WIDTH + CLASSES, RATE_MATRIX * trust_ratio[5 * LAYERS + 1], RATE_VECTOR
        ),
    )
    return (mats_rate, side_rate, head_rate)


def exchange(payload):
    return lax.all_to_all(payload, BOTH, 0, 0)


def before(value, *others):
    return lax.optimization_barrier((value, *others))[0]


def spread_over(array, axis):
    copies = jnp.broadcast_to(array[None], (lax.axis_size(axis), *array.shape))
    return lax.all_to_all(copies, axis, 0, 0)


def replica_sum(array):
    count = lax.axis_size(REPLICAS)
    total = array.astype(F32)
    for turn in range(1, count):
        pairs = [(k, (k + turn) % count) for k in range(count)]
        total = total + lax.ppermute(array, REPLICAS, pairs).astype(F32)
    return total


def body(
    images, partner, mix_pair, labels, step,
    layer_mats, layer_side, layer_vecs, head_mat, fc_bias,
    mats_first, mats_second, side_first, side_second, vecs_first, vecs_second,
    head_first, head_second, bias_first, bias_second,
):
    local_images = images.shape[0]
    owners = lax.axis_size(OWNERS)
    replicas = lax.axis_size(REPLICAS)
    devices = owners * replicas
    image_count = float(local_images * devices)
    count = local_images * MAP
    row_count = float(count * devices)
    mine = lax.axis_index(OWNERS)
    side_width = layer_side.shape[2]
    vec_width = layer_vecs.shape[1]
    rows_dev = layer_mats.shape[1]
    half = owners // 2

    side_low = jnp.concatenate(
        [
            layer_side[:, 9 : 9 + 2 * SQUEEZE],
            layer_side[:, :9],
            layer_side[:, 9 + 2 * SQUEEZE :],
            jnp.pad(layer_vecs, ((0, 0), (0, side_width - vec_width)))[:, None, :],
            jnp.zeros((LAYERS, 1, side_width), F32),
        ],
        axis=1,
    ).astype(BF16)
    mats_all = [
        lax.all_gather(layer_mats[k].astype(BF16), OWNERS, axis=0, tiled=True) for k in range(LAYERS)
    ]
    side_zero = lax.all_gather(side_low[0], OWNERS, axis=1, tiled=True)
    side_room = -(-side_width // CHUNK) * CHUNK
    side_rest = lax.all_gather(
        jnp.pad(side_low[1:], ((0, 0), (0, 0), (0, side_room - side_width))), OWNERS, axis=0
    )
    side_rest = jnp.moveaxis(side_rest[..., :side_width], 0, 2).reshape(LAYERS - 1, SIDE_PAD, EXPAND)
    side_all = [side_zero, side_rest[0], side_rest[1]]
    head_full = lax.all_gather(
        jnp.pad(head_mat, ((0, 0), (0, HEADPAD - HEADCOLS))).astype(BF16), OWNERS, axis=0, tiled=True
    )

    partner_col = partner[:, None]
    layers = []
    crosses = []
    entry = mix(before(images, side_zero).reshape(count, WIDTH), partner_col, mix_pair)
    x, xb = entry.x, entry.xb
    pay = first(xb, mats_all[0], devices).pay
    for k in range(LAYERS):
        mats, side = mats_all[k], side_all[k]
        one = spatial(xb, mats, side, exchange(pay))
        two = project(one.d, mats, side, exchange(one.pay), getattr(one, "cross", None), owners)
        last = k == LAYERS - 1
        three = residual(
            x, two.p, two.vec, exchange(two.pay), head_full if last else mats_all[k + 1], last
        )
        if k:
            crosses.append(three.cross)
        layers.append(
            types.SimpleNamespace(
                xb=xb, d=one.d, norm1=one.norm, norm2=two.norm,
                pooled=two.pooled, excite=two.excite, squeeze=two.squeeze,
                norm3=three.norm, normed=three.normed, mats=mats, weights=mats, side=side,
            )
        )
        x, xb, pay = three.x, three.xb, three.pay
    top = head(
        xb, head_full, jnp.pad(fc_bias, (0, LOGITS - CLASSES))[None], labels[:, None], labels[None, :],
        partner_col, mix_pair, layers[-1].normed, exchange(pay), image_count,
    )

    def to_owner(blocks):
        return lax.psum_scatter(
            blocks.reshape(-1, blocks.shape[-1]), OWNERS, scatter_dimension=0, tiled=True
        )

    upper = types.SimpleNamespace(
        xb=xb, weights=head_full, dz=top.dz, norm=top.norm, grad_head=top.grad_head
    )
    pay = top.pay
    stream = None
    blocks = None
    waiting = []
    globs_one, globs_two, globs_three = [None] * LAYERS, [None] * LAYERS, [None] * LAYERS
    for k in reversed(range(LAYERS)):
        layer = layers[k]
        is_head = k == LAYERS - 1
        gate = gate_back(
            is_head, row_count, owners, exchange(pay), upper,
            None if is_head else crosses[k], stream, layer, blocks, is_head,
        )
        stream = gate.stream
        globs_three[k] = gate.glob3
        if is_head:
            head_glob, bias_loss = gate.glob, gate.glob3[2:6].reshape(LOGITS)
            shard_head = to_owner(gate.grad_head)
            blocks = gate.blocks
        else:
            globs_one[k + 1] = gate.glob
            if k:
                pair = to_owner(gate.blocks)
                blocks = None
            else:
                shard_zero = to_owner(gate.blocks)
        tap = tap_back(
            k == 0, row_count, exchange(gate.pay), gate.dz2, layer, stream, layers[max(k - 1, 0)]
        )
        globs_two[k] = tap.glob
        pay = tap.pay
        if k == 1:
            shard_head = replica_sum(shard_head)
            pay = before(pay, shard_head)
        upper = types.SimpleNamespace(
            xb=layer.xb, weights=layer.mats, dz=tap.dz, norm=layer.norm1, taps=tap.taps
        )
    pair = replica_sum(pair)
    pay = before(pay, pair)
    late_taps = jnp.moveaxis(tap.taps[:9].astype(BF16).reshape(9, owners, side_width), 1, 0)
    late_taps = jnp.broadcast_to(late_taps[None], (replicas, *late_taps.shape))
    late_taps = exchange(late_taps.reshape(devices, 9, side_width))
    final = last_back(row_count, replicas, owners, exchange(pay), layers[0], tap.dz)
    globs_one[0] = final.glob
    late_taps = jnp.sum(late_taps.astype(F32), axis=0)
    room = pair.shape[0] // 2
    shards = [replica_sum(shard_zero), pair[room:], pair[:room]]

    part = slice_rows(devices)
    chunks = EXPAND // CHUNK
    late = jnp.sum(exchange(final.grads).astype(F32), axis=0).astype(BF16)
    other = lax.ppermute(late, OWNERS, [(half + k, k) for k in range(half)])
    late = spread_over(jnp.stack([late, other]), REPLICAS)[:, :, : chunks * part]
    late = jnp.moveaxis(late.reshape(replicas, 2, chunks, part, CHUNK), 2, 3)
    late = late.reshape(rows_dev, EXPAND).astype(F32)

    def mats_of(shard):
        rows = shard[: chunks * rows_dev].reshape(chunks, rows_dev, CHUNK)
        return jnp.moveaxis(rows, 0, 1).reshape(rows_dev, EXPAND)

    from_mats = [late] + [mats_of(shard) for shard in shards]
    owns_expand = mine < half
    grad_mats = jnp.stack(
        [jnp.where(owns_expand, from_mats[k], from_mats[k + 1]) for k in range(LAYERS)]
    )

    def own_columns(vector, width):
        return lax.dynamic_slice_in_dim(vector, mine * width, width, axis=-1)

    first_row = chunks * rows_dev
    last_row = first_row + 2 * SQUEEZE
    vec_ids = mine * vec_width + jnp.arange(vec_width)
    side_list, vec_list = [], []
    for k in range(LAYERS):
        shard = shards[k][:, :side_width]
        taps = late_taps if k == 0 else shards[k - 1][last_row + 2 : last_row + 11, :side_width]
        norms_part = own_columns(
            jnp.concatenate([globs_one[k][0:2], globs_two[k][0:2]], axis=0), side_width
        )
        side_list.append(
            jnp.concatenate([taps, shard[first_row : last_row + 1], norms_part], axis=0)
        )
        outer = globs_three[k]
        outer = own_columns(
            jnp.concatenate([jnp.zeros((SQUEEZE,), F32), outer[0], outer[1]]), vec_width
        )
        vec_list.append(jnp.where(vec_ids < SQUEEZE, shard[last_row + 1, :vec_width], outer))
    grad_side = jnp.stack(side_list)
    grad_vecs = jnp.stack(vec_list)
    head_tail = own_columns(head_glob[0:2], head_mat.shape[0]).T
    grad_head = jnp.concatenate([shard_head[:, : WIDTH + CLASSES], head_tail], axis=1)
    grad_bias = bias_loss[:CLASSES]
    loss_value = (bias_loss[CLASSES] + bias_loss[CLASSES + 1]) / image_count

    step_float = step[0].astype(F32)
    side_decay = (jnp.arange(SIDE) < 9 + 2 * SQUEEZE).astype(F32)[None, :, None]
    head_decay = (jnp.arange(HEADCOLS) < WIDTH + CLASSES).astype(F32)[None, :]
    mats_moment, mats_square, mats_dir = lamb_moments(
        layer_mats, mats_first, mats_second, grad_mats, 1.0, step_float
    )
    side_moment, side_square, side_dir = lamb_moments(
        layer_side, side_first, side_second, grad_side, side_decay, step_float
    )
    vecs_moment, vecs_square, vecs_dir = lamb_moments(
        layer_vecs, vecs_first, vecs_second, grad_vecs, 0.0, step_float
    )
    head_moment, head_square, head_dir = lamb_moments(
        head_mat, head_first, head_second, grad_head, head_decay, step_float
    )
    bias_moment, bias_square, bias_dir = lamb_moments(
        fc_bias, bias_first, bias_second, grad_bias, 0.0, step_float
    )
    row_ids = mine * rows_dev + jnp.arange(rows_dev)
    squares = jnp.stack(
        [
            group_sums(layer_mats, layer_side, head_mat, row_ids),
            group_sums(mats_dir, side_dir, head_dir, row_ids),
        ]
    )
    norms = jnp.sqrt(jnp.sum(spread_over(squares, OWNERS), axis=0))
    mats_rate, side_rate, head_rate = rate_maps(norms[0] / norms[1], row_ids)
    mats_new = layer_mats - mats_rate[:, :, None] * mats_dir
    side_new = layer_side - side_rate[:, :, None] * side_dir
    vecs_new = layer_vecs - RATE_VECTOR * vecs_dir
    head_new = head_mat - head_rate[None, :] * head_dir
    bias_new = fc_bias - RATE_VECTOR * bias_dir
    return (
        loss_value,
        mats_new, mats_moment, mats_square,
        side_new, side_moment, side_square,
        vecs_new, vecs_moment, vecs_square,
        head_new, head_moment, head_square,
        bias_new, bias_moment, bias_square,
        norms,
    )


def solution(mesh):
    rows, columns = P(None, OWNERS, None), P(None, None, OWNERS)
    vecs, heads = P(None, OWNERS), P(OWNERS, None)
    return jax.shard_map(
        body,
        mesh=mesh,
        in_specs=(
            P(BOTH, None, None), P(BOTH), P(BOTH, None), P(BOTH), P(),
            rows, columns, vecs, heads, P(),
            rows, rows, columns, columns, vecs, vecs, heads, heads, P(), P(),
        ),
        out_specs=(
            P(),
            rows, rows, rows,
            columns, columns, columns,
            vecs, vecs, vecs,
            heads, heads, heads,
            P(), P(), P(), P(),
        ),
        check_vma=False,
    )
```

```python
import functools
import types

import jax
import jax.numpy as jnp
from jax import lax
from jax.experimental import pallas as pl
from jax.experimental.pallas import tpu as pltpu
from jax.sharding import PartitionSpec as P

WIDTH = 256
EXPAND = 1536
SQUEEZE = 64
HEAD = 1280
CLASSES = 1000
LOGITS = 1024
EDGE = 4
LAYERS = 3
MAP = 16
SIDE = 142
SIDE_PAD = 144
VECS = 576
HEADCOLS = 1258
HEADPAD = 1280

EPS_BN = 0.001
BETA_ONE = 0.9
BETA_TWO = 0.999
EPS_ADAM = 1e-06
DECAY_RATE = 0.01
RATE_MATRIX = 0.5
RATE_VECTOR = 0.25

REPLICAS, OWNERS = BOTH = ("dp", "fsdp")
F32 = jnp.float32
BF16 = jnp.bfloat16
LANE = 128
TILE = 8
ROWS = MAP * TILE
CHUNK = 256
PARTS = CHUNK // LANE
VMEM_BYTES = 60 * 1024 * 1024

NT = (((1,), (1,)), ((), ()))
TN = (((0,), (0,)), ((), ()))


NEAR, FAR, RAW, CHUNKS = range(4)


class Refs:
    def __init__(self, names, refs, loads, stores):
        for name, ref in zip(names, refs):
            setattr(self, name, ref)
        self.loads = loads
        self.stores = {id(getattr(self, name)): (k, self.far(name)) for k, name in enumerate(stores)}
        self.pending = {}
        self.chunks = {}

    def far(self, name):
        return getattr(self, name + "_far")

    def start(self):
        for index, (name, where) in enumerate(self.loads):
            source = self.far(name) if where is None or where == CHUNKS else self.far(name).at[where]
            near = getattr(self, name)
            if where == CHUNKS:
                self.chunks[id(near)] = (self.far(name), index)
                for turn in range(near.shape[1] // CHUNK):
                    self.chunk(near, turn, pl.ds(turn * CHUNK, CHUNK)).start()
                continue
            copy = pltpu.make_async_copy(source, near, self.load_sem.at[index])
            copy.start()
            self.pending[id(near)] = copy

    def chunk(self, near, turn, at):
        far, index = self.chunks[id(near)]
        semaphore = self.load_sem.at[len(self.loads) + index * (EXPAND // CHUNK) + turn]
        return pltpu.make_async_copy(far.at[:, at], near.at[:, at], semaphore)

    def wait(self, *refs):
        for ref in refs:
            self.pending.pop(id(ref)).wait()

    def send(self, *refs):
        for ref in refs:
            index, far = self.stores[id(ref)]
            copy = pltpu.make_async_copy(ref, far, self.store_sem.at[index])
            copy.start()
            self.pending[id(far)] = copy

    def part(self, ref, index, at):
        far = self.stores[id(ref)][1]
        return pltpu.make_async_copy(ref.at[:, at], far.at[:, at], self.part_sem.at[index])

    def finish(self, ref=None):
        for key in list(self.pending):
            self.pending.pop(key).wait()
        if ref is not None:
            for index in range(ref.shape[1] // CHUNK):
                self.part(ref, index, pl.ds(index * CHUNK, CHUNK)).wait()


def shape(dims, dtype=F32):
    return jax.ShapeDtypeStruct(dims, dtype)


def vmem(dims, dtype=F32):
    return pltpu.VMEM(dims, dtype)


def call(kernel, ins, outs, scratch, alias=()):
    near, far = pl.BlockSpec(memory_space=pltpu.VMEM), pl.BlockSpec(memory_space=pltpu.HBM)
    names, arrays, in_specs, loads, stores, extra = [], [], [], [], [], {}
    for name, (array, place) in ins.items():
        arrays.append(array)
        in_specs.append(near if place == NEAR else far)
        if place == NEAR or place == RAW:
            names.append(name)
            continue
        names.append(name + "_far")
        dims, where = array.shape, None
        if place == CHUNKS:
            where = CHUNKS
        elif place != FAR:
            starts = [part.indices(size)[:2] for part, size in zip(place, dims)]
            dims = tuple(stop - start for start, stop in starts)
            where = tuple(pl.ds(start, stop - start) for start, stop in starts)
        loads.append((name, where))
        extra[name] = vmem(dims, array.dtype)
    for name, (struct, place) in outs.items():
        names.append(name + "_far" if place == FAR else name)
        if place == FAR:
            stores.append(name)
            extra[name] = vmem(struct.shape, struct.dtype)
    extra.update(scratch)
    extra.update(
        load_sem=pltpu.SemaphoreType.DMA((max(len(loads), 1) * (1 + EXPAND // CHUNK),)),
        store_sem=pltpu.SemaphoreType.DMA((max(len(stores), 1),)),
        part_sem=pltpu.SemaphoreType.DMA((EXPAND // CHUNK,)),
    )

    def flat(*refs):
        kernel(Refs(names + list(extra), refs, loads, stores))

    results = pl.pallas_call(
        flat,
        out_shape=[struct for struct, _ in outs.values()],
        in_specs=in_specs,
        out_specs=[near if place == NEAR else far for _, place in outs.values()],
        scratch_shapes=list(extra.values()),
        input_output_aliases={list(ins).index(a): list(outs).index(b) for a, b in alias},
        compiler_params=pltpu.CompilerParams(vmem_limit_bytes=VMEM_BYTES),
    )(*arrays)
    return types.SimpleNamespace(**dict(zip(outs, results)))


def dot(left, right):
    return jnp.dot(left, right, preferred_element_type=F32)


def dot_nt(left, right):
    return lax.dot_general(left, right, NT, preferred_element_type=F32)


def dot_tn(left, right):
    return lax.dot_general(left, right, TN, preferred_element_type=F32)


def halves(value):
    high = value.astype(BF16)
    return high, (value - high.astype(F32)).astype(BF16)


def stacked(value):
    return jnp.concatenate(halves(value), axis=0)


def folded(value):
    count = value.shape[0] // 2
    return value[:count] + value[count:]


def sigmoid(value):
    return 0.5 * jnp.tanh(0.5 * value) + 0.5


def chunk_at(index, size=CHUNK):
    return pl.ds(pl.multiple_of(index * size, size), size)


def tile_rows(tile):
    return slice(tile * ROWS, (tile + 1) * ROWS)


def tile_images(tile):
    return slice(tile * TILE, (tile + 1) * TILE)


def as_tile(block):
    return block.reshape(MAP, TILE, LANE)


def spread(rows, first, count):
    return jnp.concatenate([rows[first + k : first + k + 1, :] for k in range(count)], axis=1)


def fold(vectors, rows):
    pieces = [
        vector[:, k * LANE : (k + 1) * LANE]
        for vector in vectors
        for k in range(vector.shape[1] // LANE)
    ]
    if rows > len(pieces):
        pieces.append(jnp.zeros((rows - len(pieces), LANE), F32))
    return jnp.concatenate(pieces, axis=0)


def column_sum(value):
    return jnp.sum(value, axis=0, keepdims=True)


def slice_rows(devices):
    return max(1, WIDTH // devices)


def write_alike(pay_ref, rows):
    pay_ref[...] = jnp.broadcast_to(rows.astype(BF16)[None], pay_ref.shape)


def write_with_slices(pay_ref, rows, matrix):
    devices = pay_ref.shape[0]
    part = slice_rows(devices)
    first = rows.shape[0]
    low = rows.astype(BF16)
    for device in range(devices):
        own = matrix[device * part : (device + 1) * part, :]
        block = jnp.concatenate([own[:, :LANE], own[:, LANE:]], axis=0)
        if 2 * part < 16:
            block = jnp.concatenate([block, jnp.zeros((16 - 2 * part, LANE), F32)], axis=0)
        pay_ref[device, 0:first, :] = low
        pay_ref[device, first : first + 16, :] = block.astype(BF16)


def read_matrix(recv_ref, first):
    devices, rows = recv_ref.shape[:2]
    part = slice_rows(devices)
    if part == TILE:
        values = recv_ref[...].astype(F32)
        left = values[:, first : first + part].reshape(WIDTH, LANE)
        right = values[:, first + part : first + 2 * part].reshape(WIDTH, LANE)
        return jnp.concatenate([left, right], axis=1)
    flat = recv_ref[...].reshape(devices * rows, LANE)
    row = lax.broadcasted_iota(jnp.int32, (WIDTH, devices * rows), 0)
    column = lax.broadcasted_iota(jnp.int32, (WIDTH, devices * rows), 1)
    source = row // part * rows + first + row % part
    left = dot(jnp.where(column == source, 1.0, 0.0).astype(BF16), flat)
    right = dot(jnp.where(column == source + part, 1.0, 0.0).astype(BF16), flat)
    return jnp.concatenate([left, right], axis=1)


def moment_rows(columns):
    return -(-3 * columns // LANE // 8) * 8


def centred(total, squares, count):
    return jnp.maximum(squares - total * total / count, 0.0)


def pack_moments(total, squares, count):
    mean = total / count
    high = mean.astype(BF16).astype(F32)
    return fold([high, mean - high, centred(total, squares, count)], moment_rows(total.shape[1]))


def read_moments(recv_ref, columns, count):
    groups = columns // LANE
    devices = recv_ref.shape[0]
    parts = recv_ref[...].astype(F32)
    means = parts[:, :groups] + parts[:, groups : 2 * groups]
    mean = jnp.sum(means, axis=0) / devices
    apart = means - mean[None]
    spread_sum = jnp.sum(parts[:, 2 * groups : 3 * groups], axis=0) / count
    variance = (spread_sum + jnp.sum(apart * apart, axis=0)) / devices
    return spread(mean, 0, groups), lax.rsqrt(spread(variance, 0, groups) + EPS_BN)


def read_product_moments(recv_ref, weights, transposed, columns, count):
    devices, rows = recv_ref.shape[:2]
    values = recv_ref[...]
    flat = values.reshape(devices * rows, LANE)
    row = lax.broadcasted_iota(jnp.int32, (devices, devices * rows), 0)
    column = lax.broadcasted_iota(jnp.int32, (devices, devices * rows), 1) - row * rows
    left = dot(jnp.where((column == 0) | (column == 2), 1.0, 0.0).astype(BF16), flat)
    right = dot(jnp.where((column == 1) | (column == 3), 1.0, 0.0).astype(BF16), flat)
    sums = stacked(jnp.concatenate([left, right], axis=1) / count)
    means = folded(dot_nt(sums, weights) if transposed else dot(sums, weights))
    mean = column_sum(means) / devices
    apart = means - mean
    squares = jnp.sum(values.astype(F32), axis=0)
    variance = (spread(squares, 4, columns // LANE) / count + column_sum(apart * apart)) / devices
    return mean, lax.rsqrt(variance + EPS_BN)


def read_sums(recv_ref):
    return jnp.sum(recv_ref[...].astype(F32), axis=0)


def keep_norm(norm_ref, mean, inverse, gain, bias):
    scale = inverse * gain
    norm_ref[0:1, :] = mean
    norm_ref[1:2, :] = inverse
    norm_ref[2:3, :] = scale
    norm_ref[3:4, :] = bias - mean * scale
    norm_ref[4:8, :] = jnp.zeros((4, norm_ref.shape[1]), F32)


def product_moments(x_ref, w_ref, transposed, columns, left_ref, stat_ref, beside=None):
    count = x_ref.shape[0]
    values = x_ref[...]
    if beside is None:
        square = dot_tn(values, values)
    else:
        product = dot_tn(jnp.concatenate([values, beside], axis=1), values)
        square, cross = product[:WIDTH], product[WIDTH:]
    sums = column_sum(values.astype(F32))
    left_ref[0 : 2 * WIDTH, :] = stacked(square)
    tail = jnp.concatenate([half.astype(F32) for half in halves(sums)] + [jnp.zeros((14, WIDTH), F32)], axis=0)
    left_ref[2 * WIDTH :, :] = tail.astype(BF16)

    def step(index, carry):
        at = chunk_at(index)
        weights = w_ref[at, :].T if transposed else w_ref[:, at]
        product = dot(left_ref[...], weights)
        total = column_sum(product[2 * WIDTH : 2 * WIDTH + 2])
        squares = column_sum(folded(product[: 2 * WIDTH]) * weights.astype(F32))
        stat_ref[0:1, at] = jnp.maximum(squares - total * total / count, 0.0)
        return carry

    lax.fori_loop(0, columns // CHUNK, step, 0, unroll=True)
    high = sums.astype(BF16).astype(F32)
    rows = fold([high, sums - high, stat_ref[0:1, :]], 16)
    return rows if beside is None else (rows, cross)


def mix_kernel(r):
    count = r.images.shape[0]
    pixels = r.images[...]
    row = lax.broadcasted_iota(jnp.int32, (ROWS, count), 0)
    column = lax.broadcasted_iota(jnp.int32, (ROWS, count), 1)
    place = lax.shift_right_logical(row, 3)
    inside = jnp.bitwise_and(row, 7)
    pair = r.mix[...].astype(F32)
    mixing = pair[:, 0:1] / (pair[:, 0:1] + pair[:, 1:2])
    for tile in range(count // ROWS):
        near = tile_images(tile)
        other = jnp.concatenate([r.partner[near, :]] * MAP, axis=0)
        weight = jnp.concatenate([mixing[near, :]] * MAP, axis=0)
        own_hot = jnp.where(column == (tile * TILE + inside) * MAP + place, 1.0, 0.0).astype(BF16)
        other_hot = jnp.where(column == other * MAP + place, 1.0, 0.0).astype(BF16)
        mixed = weight * dot(own_hot, pixels) + (1.0 - weight) * dot(other_hot, pixels)
        r.x[tile_rows(tile), :] = mixed
    r.xb[...] = r.x[...].astype(BF16)
    r.send(r.x, r.xb)
    r.finish()


def mix(images, partner, mix_pair):
    dims = images.shape
    return call(
        mix_kernel,
        dict(images=(images, NEAR), partner=(partner, NEAR), mix=(mix_pair, NEAR)),
        dict(x=(shape(dims), FAR), xb=(shape(dims, BF16), FAR)),
        {},
    )


def first_kernel(r):
    r.start()
    r.wait(r.xb, r.w)
    write_alike(r.pay, product_moments(r.xb, r.w, False, EXPAND, r.left, r.stat))
    r.send(r.pay)
    r.finish()


def first(xb, mats, devices):
    return call(
        first_kernel,
        dict(xb=(xb, FAR), w=(mats, (slice(0, WIDTH), slice(None)))),
        dict(pay=(shape((devices, 16, LANE), BF16), FAR)),
        dict(left=vmem((2 * WIDTH + 16, WIDTH), BF16), stat=vmem((8, EXPAND))),
    )


def tap_terms():
    for row in range(EDGE):
        for col in range(EDGE):
            for row_shift in range(3):
                for col_shift in range(3):
                    from_row, from_col = row + row_shift - 1, col + col_shift - 1
                    if 0 <= from_row < EDGE and 0 <= from_col < EDGE:
                        yield EDGE * row + col, 3 * row_shift + col_shift, EDGE * from_row + from_col


TERMS = list(tap_terms())


def spatial_kernel(r):
    count = r.xb.shape[0]
    r.start()
    r.wait(r.recv, r.side, r.w, r.xb)
    rows = r.side[...].astype(F32)
    r.taps[0:9, :] = rows[0:9, :]
    mean, inverse = read_product_moments(r.recv, r.w[...], False, EXPAND, count)
    keep_norm(r.norm, mean, inverse, rows[10:11, :], rows[11:12, :])
    r.send(r.norm)
    if r.recv.shape[1] > 16:
        r.cross[...] = jnp.sum(r.recv[...].astype(F32)[:, 16:32], axis=0)
        r.send(r.cross)

    def step(index, carry):
        at_chunk = chunk_at(index)
        r.h[...] = dot(r.xb[...], r.w[:, at_chunk])
        for part in range(PARTS):
            lanes = chunk_at(index * PARTS + part, LANE)
            taps = [jnp.broadcast_to(r.taps[k : k + 1, lanes], (TILE, LANE)) for k in range(9)]
            scale_row = r.norm[2:3, lanes]
            shift_row = r.norm[3:4, lanes]

            def tile_step(tile, sums):
                at = chunk_at(tile, ROWS)
                pre = r.h[at, part * LANE : (part + 1) * LANE] * scale_row + shift_row
                active = as_tile(pre * sigmoid(pre))
                result = [None] * MAP
                for target, tap, source in TERMS:
                    term = active[source] * taps[tap]
                    result[target] = term if result[target] is None else result[target] + term
                total, squares = sums
                for value in result:
                    total = total + value
                    squares = squares + value * value
                r.d[at, lanes] = jnp.concatenate(result, axis=0).astype(BF16)
                return total, squares

            zero = jnp.zeros((TILE, LANE), F32)
            total, squares = lax.fori_loop(0, count // ROWS, tile_step, (zero, zero), unroll=True)
            r.stat[0:1, lanes] = column_sum(total)
            r.stat[1:2, lanes] = column_sum(squares)
        r.part(r.d, index, at_chunk).start()
        return carry

    lax.fori_loop(0, EXPAND // CHUNK, step, 0)
    write_alike(r.pay, pack_moments(r.stat[0:1, :], r.stat[1:2, :], count))
    r.send(r.pay)
    r.finish(r.d)


def spatial(xb, mats, side, recv):
    count = xb.shape[0]
    devices = recv.shape[0]
    outs = dict(
        d=(shape((count, EXPAND), BF16), FAR),
        pay=(shape((devices, moment_rows(EXPAND), LANE), BF16), FAR),
        norm=(shape((8, EXPAND)), FAR),
    )
    if recv.shape[1] > 16:
        outs["cross"] = (shape((16, LANE)), FAR)
    return call(
        spatial_kernel,
        dict(
            recv=(recv, FAR),
            side=(side, (slice(2 * SQUEEZE, SIDE_PAD), slice(None))),
            xb=(xb, FAR),
            w=(mats, (slice(0, WIDTH), slice(None))),
        ),
        outs,
        dict(
            h=vmem((count, CHUNK), F32),
            taps=vmem((16, EXPAND), F32),
            stat=vmem((8, EXPAND), F32),
        ),
    )


def project_kernel(with_cross, owners, r):
    count = r.d.shape[0]
    tiles = count // ROWS
    r.start()
    r.wait(r.recv)
    mean, inverse = read_moments(r.recv, EXPAND, count)
    r.wait(r.side)
    rows = r.side[2 * SQUEEZE : SIDE_PAD, :].astype(F32)
    keep_norm(r.norm, mean, inverse, rows[12:13, :], rows[13:14, :])
    r.send(r.norm)
    width, vec_width = EXPAND // owners, VECS // owners
    vec = jnp.concatenate(
        [rows[14:15, k * width : k * width + vec_width] for k in range(owners)], axis=1
    )
    r.vec[...] = jnp.concatenate(
        [vec[:, SQUEEZE : SQUEEZE + WIDTH], vec[:, SQUEEZE + WIDTH :], jnp.zeros((6, WIDTH), F32)], axis=0
    )
    r.send(r.vec)

    def activate(index, carry):
        r.chunk(r.d, index, chunk_at(index)).wait()
        for part in range(PARTS):
            lanes = chunk_at(index * PARTS + part, LANE)
            scale_row = r.norm[2:3, lanes]
            shift_row = r.norm[3:4, lanes]
            for tile in range(tiles):
                at = tile_rows(tile)
                pre = r.d[at, lanes].astype(F32) * scale_row + shift_row
                active = pre * sigmoid(pre)
                r.a[at, lanes] = active
                r.pooled[tile_images(tile), lanes] = jnp.sum(as_tile(active), axis=0) / MAP
        return carry

    lax.fori_loop(0, EXPAND // CHUNK, activate, 0)
    r.send(r.pooled)
    before = folded(dot_nt(stacked(r.pooled[...]), r.side[0:SQUEEZE, :])) + vec[:, :SQUEEZE]
    r.squeeze[...] = before
    r.send(r.squeeze)
    opened = folded(dot(stacked(before * sigmoid(before)), r.side[SQUEEZE : 2 * SQUEEZE, :]))
    r.excite[...] = sigmoid(opened + rows[9:10, :])
    r.send(r.excite)

    def gate(index, carry):
        lanes = chunk_at(index, LANE)
        for tile in range(tiles):
            at = tile_rows(tile)
            scaled = as_tile(r.a[at, lanes]) * r.excite[tile_images(tile), lanes][None]
            r.y[at, lanes] = scaled.reshape(ROWS, LANE).astype(BF16)
        return carry

    lax.fori_loop(0, EXPAND // LANE, gate, 0)
    r.wait(r.w)
    projected = dot_nt(r.y[...], r.w[...])
    r.p[...] = projected
    r.send(r.p)
    moments = pack_moments(column_sum(projected), column_sum(projected * projected), count)
    if with_cross:
        r.wait(r.cross)
        moments = jnp.concatenate([moments, r.cross[...]], axis=0)
    write_alike(r.pay, moments)
    r.send(r.pay)
    r.finish()


def project(d, mats, side, recv, cross, owners):
    count = d.shape[0]
    images = count // MAP
    devices = recv.shape[0]
    ins = dict(
        recv=(recv, FAR),
        side=(side, FAR),
        d=(d, CHUNKS),
        w=(mats, (slice(WIDTH, 2 * WIDTH), slice(None))),
    )
    rows = moment_rows(WIDTH)
    if cross is not None:
        ins["cross"] = (cross, FAR)
        rows += 16
    return call(
        functools.partial(project_kernel, cross is not None, owners),
        ins,
        dict(
            p=(shape((count, WIDTH)), FAR),
            vec=(shape((8, WIDTH)), FAR),
            pay=(shape((devices, rows, LANE), BF16), FAR),
            norm=(shape((8, EXPAND)), FAR),
            pooled=(shape((images, EXPAND)), FAR),
            excite=(shape((images, EXPAND)), FAR),
            squeeze=(shape((images, SQUEEZE)), FAR),
        ),
        dict(a=vmem((count, EXPAND), F32), y=vmem((count, EXPAND), BF16)),
    )


def residual_kernel(transposed, with_cross, r):
    count = r.p.shape[0]
    r.start()
    r.wait(r.recv, r.vec)
    mean, inverse = read_moments(r.recv, WIDTH, count)
    keep_norm(r.norm, mean, inverse, r.vec[0:1, :], r.vec[1:2, :])
    if with_cross:
        r.cross[...] = read_matrix(r.recv, moment_rows(WIDTH))
        r.send(r.cross)
    r.wait(r.p)
    normed = (r.p[...] - mean) * inverse
    r.normed[...] = normed
    r.wait(r.before)
    result = r.before[...] + (normed * r.vec[0:1, :] + r.vec[1:2, :])
    r.x[...] = result
    r.xb[...] = result.astype(BF16)
    r.send(r.norm, r.normed, r.x, r.xb)
    r.wait(r.w)
    moments, cross = product_moments(
        r.xb, r.w, transposed, r.stat.shape[1], r.left, r.stat, normed.astype(BF16)
    )
    write_with_slices(r.pay, moments, cross)
    r.send(r.pay)
    r.finish()


def residual(x, p, vec, recv, weights, transposed):
    count = x.shape[0]
    devices = recv.shape[0]
    with_cross = recv.shape[1] > moment_rows(WIDTH)
    columns = HEAD if transposed else EXPAND
    where = (slice(0, HEAD), slice(0, WIDTH)) if transposed else (slice(0, WIDTH), slice(None))
    outs = dict(
        x=(shape((count, WIDTH)), FAR),
        xb=(shape((count, WIDTH), BF16), FAR),
        normed=(shape((count, WIDTH)), FAR),
        pay=(shape((devices, 32, LANE), BF16), FAR),
        norm=(shape((8, WIDTH)), FAR),
    )
    if with_cross:
        outs["cross"] = (shape((WIDTH, WIDTH)), FAR)
    return call(
        functools.partial(residual_kernel, transposed, with_cross),
        dict(
            recv=(recv, FAR), vec=(vec, FAR), p=(p, FAR), before=(x, FAR), w=(weights, where)
        ),
        outs,
        dict(left=vmem((2 * WIDTH + 16, WIDTH), BF16), stat=vmem((8, columns))),
    )


def head_rows(last_columns):
    pick_row = lax.broadcasted_iota(jnp.int32, (TILE, LANE), 0)
    pick_col = lax.broadcasted_iota(jnp.int32, (TILE, LANE), 1)
    first_col = WIDTH + CLASSES - (HEADPAD - LANE)
    pick = jnp.where((pick_col == pick_row + first_col) & (pick_row < 2), 1.0, 0.0).astype(BF16)
    return dot_nt(pick, last_columns)


def head_kernel(image_count, r):
    count = r.xb.shape[0]
    tiles = count // ROWS
    images = count // MAP
    r.start()
    r.wait(r.recv, r.xb, r.w)
    mean, inverse = read_product_moments(r.recv, r.w[...], True, HEAD, count)
    cross = jnp.sum(r.recv[...].astype(F32)[:, 16:32], axis=0)
    r.wait(r.classifier)
    gain_bias = head_rows(r.classifier[:, LOGITS - LANE :])
    keep_norm(r.norm, mean, inverse, gain_bias[0:1, :], gain_bias[1:2, :])
    r.send(r.norm)

    def features(index, carry):
        at_chunk = chunk_at(index)
        r.h[:, at_chunk] = dot_nt(r.xb[...], r.w[at_chunk, :])
        for part in range(PARTS):
            lanes = chunk_at(index * PARTS + part, LANE)
            scale_row = r.norm[2:3, lanes]
            shift_row = r.norm[3:4, lanes]
            for tile in range(tiles):
                pre = r.h[tile_rows(tile), lanes] * scale_row + shift_row
                active = as_tile(pre * sigmoid(pre))
                r.f[tile_images(tile), lanes] = jnp.sum(active, axis=0) / MAP
        return carry

    lax.fori_loop(0, HEAD // CHUNK, features, 0)
    features_low = r.f[...].astype(BF16)
    classifier = r.classifier[...]
    ids = lax.broadcasted_iota(jnp.int32, (images, LOGITS), 1)
    logits = dot(features_low, classifier) + r.bias[...]
    logits = jnp.where(ids < CLASSES, logits, -1e30)
    row_max = jnp.max(logits, axis=1, keepdims=True)
    log_total = row_max + jnp.log(jnp.sum(jnp.exp(logits - row_max), axis=1, keepdims=True))
    pair = r.mix[...].astype(F32)
    mixing = pair[:, 0:1] / (pair[:, 0:1] + pair[:, 1:2])
    people = lax.broadcasted_iota(jnp.int32, (images, images), 1)
    label_row = jnp.broadcast_to(r.label_row[...].astype(F32), (images, images))
    partner_label = jnp.sum(
        jnp.where(people == r.partner[...], label_row, 0.0), axis=1, keepdims=True
    ).astype(jnp.int32)
    own_hot = jnp.where(ids == r.label_col[...], 1.0, 0.0)
    other_hot = jnp.where(ids == partner_label, 1.0, 0.0)
    own_logit = jnp.sum(own_hot * logits, axis=1, keepdims=True)
    other_logit = jnp.sum(other_hot * logits, axis=1, keepdims=True)
    loss = column_sum(mixing * (log_total - own_logit) + (1.0 - mixing) * (log_total - other_logit))
    grad_logits = (
        jnp.exp(logits - log_total) - mixing * own_hot - (1.0 - mixing) * other_hot
    ) / image_count
    grad_low = grad_logits.astype(BF16)
    r.grad_fc[...] = dot_tn(features_low, grad_low).astype(BF16)
    fc_copy = pltpu.make_async_copy(r.grad_fc, r.grad_head.at[:, pl.ds(WIDTH, LOGITS)], r.part_sem.at[0])
    fc_copy.start()
    r.f[...] = dot_nt(grad_low, classifier) / MAP
    bias_sum = column_sum(grad_logits)
    bias_ids = lax.broadcasted_iota(jnp.int32, (1, LOGITS), 1)
    loss_high = loss.astype(BF16).astype(F32)
    bias_sum = jnp.where(bias_ids == CLASSES, loss_high, bias_sum)
    bias_sum = jnp.where(bias_ids == CLASSES + 1, loss - loss_high, bias_sum)

    def back(index, carry):
        lanes = chunk_at(index, LANE)
        scale_row = r.norm[2:3, lanes]
        shift_row = r.norm[3:4, lanes]
        mean_row = r.norm[0:1, lanes]
        total = jnp.zeros((TILE, LANE), F32)
        weighted = jnp.zeros((TILE, LANE), F32)
        for tile in range(tiles):
            at = tile_rows(tile)
            hidden = r.h[at, lanes]
            pre = hidden * scale_row + shift_row
            gate = sigmoid(pre)
            slope = as_tile(gate * (1.0 + pre * (1.0 - gate)))
            grad = slope * r.f[tile_images(tile), lanes][None]
            total = total + jnp.sum(grad, axis=0)
            weighted = weighted + jnp.sum(grad * as_tile(hidden - mean_row), axis=0)
            flat = grad.reshape(ROWS, LANE)
            r.dz[at, lanes] = flat.astype(BF16)
            r.q[at, lanes] = (flat * scale_row).astype(BF16)
        r.stat[0:1, lanes] = column_sum(total)
        r.stat[1:2, lanes] = column_sum(weighted)
        return carry

    lax.fori_loop(0, HEAD // LANE, back, 0)
    r.send(r.dz)
    below = dot(r.q[...], r.w[...])
    r.wait(r.normed)
    rows = fold(
        [
            r.stat[0:1, :], r.stat[1:2, :] * inverse,
            column_sum(below), column_sum(below * r.normed[...]), bias_sum,
        ],
        32,
    )
    write_alike(r.pay, jnp.concatenate([rows, cross], axis=0))
    r.send(r.pay)
    fc_copy.wait()
    r.finish()


def head(xb, head_full, bias, label_col, label_row, partner, mix_pair, normed, recv, image_count):
    count = xb.shape[0]
    images = count // MAP
    devices = recv.shape[0]
    return call(
        functools.partial(head_kernel, image_count),
        dict(
            recv=(recv, FAR),
            xb=(xb, FAR),
            bias=(bias, NEAR),
            label_col=(label_col, NEAR),
            label_row=(label_row, NEAR),
            partner=(partner, NEAR),
            mix=(mix_pair, NEAR),
            w=(head_full, (slice(0, HEAD), slice(0, WIDTH))),
            classifier=(head_full, (slice(0, HEAD), slice(WIDTH, HEADPAD))),
            normed=(normed, FAR),
        ),
        dict(
            dz=(shape((count, HEAD), BF16), FAR),
            pay=(shape((devices, 48, LANE), BF16), FAR),
            norm=(shape((8, HEAD)), FAR),
            grad_head=(shape((HEAD, HEADPAD), BF16), RAW),
        ),
        dict(
            h=vmem((count, HEAD), F32),
            grad_fc=vmem((HEAD, LOGITS), BF16),
            f=vmem((images, HEAD), F32),
            q=vmem((count, HEAD), BF16),
            stat=vmem((8, HEAD), F32),
        ),
    )


def product_back(is_head, row_count, sums, columns, r):
    groups = columns // LANE
    sum_bias = spread(sums, 0, groups)
    sum_gain = spread(sums, groups, groups)
    r.glob[0:1, :] = sum_gain
    r.glob[1:2, :] = sum_bias
    r.glob[2:8, :] = jnp.zeros((6, columns), F32)
    r.send(r.glob)
    r.wait(r.unorm, r.xb, r.w)
    mean = r.unorm[0:1, :]
    scale = r.unorm[2:3, :]
    slant = scale * r.unorm[1:2, :] * (sum_gain / row_count)
    r.coef[0:1, :columns] = slant
    r.coef[1:2, :columns] = mean * slant - scale * (sum_bias / row_count)
    r.xt[...] = r.xb[...].T
    count = r.xb.shape[0]

    def step(index, carry):
        at = chunk_at(index)
        r.chunk(r.dz, index, at).wait()
        if is_head:
            r.h[...] = dot_nt(r.xb[...], r.w[at, :])
        else:
            r.h[...] = dot(r.xb[...], r.w[:, at])
        grad = r.dz[:, at].astype(F32) * r.unorm[2:3, at] - r.h[...] * r.coef[0:1, at] + r.coef[1:2, at]
        low = grad.astype(BF16)
        r.dh[0:count, at] = low
        if is_head:
            r.grad_w[at, :] = dot_tn(low, r.xb[...]).astype(r.grad_w.dtype)
        else:
            r.grad_w[:, at] = dot(r.xt[...], low).astype(r.grad_w.dtype)
        return carry

    lax.fori_loop(0, columns // CHUNK, step, 0, unroll=True)
    return scale * sum_bias, slant


def owner_blocks(r, owners, row_of_owner, taps):
    rows_dev = 2 * WIDTH // owners
    width = EXPAND // owners
    vec_width = VECS // owners
    chunks = EXPAND // CHUNK
    squeeze_sums = jnp.concatenate([r.squeeze_sum[...], jnp.zeros((1, VECS - LANE), F32)], axis=1)
    for owner in range(owners):
        at = slice(owner * width, (owner + 1) * width)
        squeeze_row = squeeze_sums[:, owner * vec_width : (owner + 1) * vec_width]
        squeeze_row = jnp.concatenate([squeeze_row, jnp.zeros((1, width - vec_width), F32)], axis=1)
        pieces = [r.excite_sum[:, at], squeeze_row]
        pieces.append(taps[0:9, at] if taps is not None else jnp.zeros((9, width), F32))
        pieces.append(jnp.zeros((5, width), F32))
        first_row = chunks * rows_dev
        r.grads[owner, first_row : first_row + 2 * SQUEEZE, 0:width] = r.rx[:, at].astype(BF16)
        last_row = first_row + 2 * SQUEEZE
        r.grads[owner, last_row : last_row + 16, 0:width] = jnp.concatenate(pieces, axis=0).astype(BF16)


def gate_kernel(is_head, row_count, owners, r):
    columns = HEAD if is_head else EXPAND
    groups = columns // LANE
    count = r.xb.shape[0]
    tiles = count // ROWS
    rows_dev = 2 * WIDTH // owners
    r.start()
    r.wait(r.recv)
    sums = read_sums(r.recv)
    bias_pull, slant = product_back(is_head, row_count, sums, columns, r)
    if is_head:
        head_copy = pltpu.make_async_copy(r.grad_w, r.grad_head.at[:, pl.ds(0, WIDTH)], r.own_sem.at[0])
        head_copy.start()
        weights = r.w[...].astype(F32)
        column = lax.broadcasted_iota(jnp.int32, (1, WIDTH), 1)
        high, low = halves(jnp.broadcast_to(bias_pull, (TILE, columns)))
        pull = column_sum(dot(high, r.w[...]) + dot(low, r.w[...])) / TILE
        turned = jnp.broadcast_to(slant, (LANE, columns)).T
        slanted = (weights * jnp.concatenate([turned, turned], axis=1)).astype(BF16)
        square = dot_tn(slanted, r.w[...])
        stream = dot(r.dh[0:count, :columns], r.w[...])
        cross = read_matrix(r.recv, 32)
    else:
        r.dh[count : count + WIDTH, :] = (r.w[...].astype(F32) * slant).astype(BF16)
        high, low = halves(bias_pull)
        r.dh[count + WIDTH :, :] = jnp.concatenate(
            [high.astype(F32), low.astype(F32), jnp.zeros((14, columns), F32)], axis=0
        ).astype(BF16)
        product = dot_nt(r.dh[...], r.w[...])
        square = product[count : count + WIDTH]
        pull = column_sum(product[count + WIDTH : count + WIDTH + 2])
        r.wait(r.cross, r.stream_in)
        stream = r.stream_in[...] + product[0:count]
        cross = r.cross[...]
    r.stream[...] = stream
    r.send(r.stream)
    sum_bias = spread(sums, 2 * groups, WIDTH // LANE) - pull
    corrected = column_sum(cross.T * square)
    sum_gain = spread(sums, 2 * groups + WIDTH // LANE, WIDTH // LANE) - corrected
    r.glob3[0:1, :] = sum_gain
    r.glob3[1:2, :] = sum_bias
    if is_head:
        first_row = 2 * groups + 2 * WIDTH // LANE
        r.glob3[2:6, :] = jnp.concatenate(
            [spread(sums, first_row + PARTS * k, PARTS) for k in range(LOGITS // WIDTH)], axis=0
        )
    else:
        r.glob3[2:6, :] = jnp.zeros((4, WIDTH), F32)
    r.glob3[6:8, :] = jnp.zeros((2, WIDTH), F32)
    r.send(r.glob3)
    r.wait(r.norm3, r.normed)
    grad_p = r.norm3[2:3, :] * (
        stream - sum_bias / row_count - r.normed[...] * (sum_gain / row_count)
    )
    r.gp[...] = grad_p.astype(BF16)
    r.gt[...] = r.gp[...].T
    r.wait(r.wp, r.norm2, r.excite)
    half = owners // 2

    def first(index, carry):
        at_chunk = chunk_at(index)
        r.chunk(r.d, index, at_chunk).wait()
        r.h[...] = dot(r.gp[...], r.wp[:, at_chunk])
        for part in range(PARTS):
            lanes = chunk_at(index * PARTS + part, LANE)
            scale_row = r.norm2[2:3, lanes]
            shift_row = r.norm2[3:4, lanes]
            for tile in range(tiles):
                at = tile_rows(tile)
                near = tile_images(tile)
                pre = r.d[at, lanes].astype(F32) * scale_row + shift_row
                gate = sigmoid(pre)
                active = pre * gate
                slope = gate + active - active * gate
                grad = r.h[at, part * LANE : (part + 1) * LANE]
                factor = r.excite[near, lanes]
                r.ge[near, lanes] = jnp.sum(as_tile(grad * active), axis=0)
                r.y[at, lanes] = (as_tile(active) * factor[None]).reshape(ROWS, LANE).astype(BF16)
                r.slope[at, lanes] = slope.astype(r.slope.dtype)
                r.u[at, lanes] = (
                    (as_tile(grad * slope) * factor[None]).reshape(ROWS, LANE).astype(r.u.dtype)
                )
        grad_p_chunk = dot(r.gt[...], r.y[:, at_chunk])
        place = pl.ds(pl.multiple_of(index * rows_dev, rows_dev), rows_dev)
        for owner in range(half):
            cut = slice(owner * rows_dev, (owner + 1) * rows_dev)
            r.grads[half + owner, place, :] = grad_p_chunk[cut, :].astype(BF16)
            if is_head:
                r.grads[owner, place, :] = jnp.zeros((rows_dev, CHUNK), BF16)
            else:
                r.grads[owner, place, :] = r.grad_w[cut, at_chunk]
        return carry

    lax.fori_loop(0, EXPAND // CHUNK, first, 0)
    r.wait(r.pooled, r.squeeze, r.side)
    excite = r.excite[...]
    grad_gate = r.ge[...] * excite * (1.0 - excite)
    before = r.squeeze[...]
    opened = sigmoid(before)
    squeezed = before * opened
    reduce_mat = r.side[0:SQUEEZE, :]
    excite_mat = r.side[SQUEEZE:, :]
    gate_high, gate_low = halves(grad_gate)
    grad_squeezed = folded(dot_nt(jnp.concatenate([gate_high, gate_low], axis=0), excite_mat))
    grad_pre = grad_squeezed * (opened * (1.0 + before * (1.0 - opened)))
    r.pool[...] = folded(dot(stacked(grad_pre), reduce_mat)) / MAP

    squeezed_high, squeezed_low = halves(squeezed)
    pre_high, pre_low = halves(grad_pre)
    pooled_high, pooled_low = halves(r.pooled[...])
    r.rx[SQUEEZE:, :] = dot_tn(
        jnp.concatenate([squeezed_high, squeezed_low, squeezed_high], axis=0),
        jnp.concatenate([gate_high, gate_high, gate_low], axis=0),
    )
    r.rx[0:SQUEEZE, :] = dot_tn(
        jnp.concatenate([pre_high, pre_low, pre_high], axis=0),
        jnp.concatenate([pooled_high, pooled_high, pooled_low], axis=0),
    )
    r.excite_sum[...] = column_sum(grad_gate)
    r.squeeze_sum[...] = jnp.concatenate(
        [column_sum(grad_pre), jnp.zeros((1, LANE - SQUEEZE), F32)], axis=1
    )
    taps = None
    if not is_head:
        r.wait(r.taps)
        taps = r.taps[...]
    owner_blocks(r, owners, half, taps)
    room = r.grads.shape[1]
    place = pl.ds((r.blocks.shape[1] - room) * (not is_head), room)
    blocks_copy = pltpu.make_async_copy(r.grads, r.blocks.at[:, place, :], r.own_sem.at[1])
    blocks_copy.start()

    def second(index, carry):
        for part in range(PARTS):
            lanes = chunk_at(index * PARTS + part, LANE)
            mean_row = r.norm2[0:1, lanes]
            total = jnp.zeros((TILE, LANE), F32)
            weighted = jnp.zeros((TILE, LANE), F32)
            for tile in range(tiles):
                at = tile_rows(tile)
                pool = r.pool[tile_images(tile), lanes]
                grad = as_tile(r.u[at, lanes].astype(F32)) + as_tile(r.slope[at, lanes].astype(F32)) * pool[None]
                total = total + jnp.sum(grad, axis=0)
                weighted = weighted + jnp.sum(
                    grad * as_tile(r.d[at, lanes].astype(F32) - mean_row), axis=0
                )
                r.dz2[at, lanes] = grad.reshape(ROWS, LANE).astype(BF16)
            r.stat[0:1, lanes] = column_sum(total)
            r.stat[1:2, lanes] = column_sum(weighted)
        r.part(r.dz2, index, chunk_at(index)).start()
        return carry

    lax.fori_loop(0, EXPAND // CHUNK, second, 0)
    write_alike(r.pay, fold([r.stat[0:1, :], r.stat[1:2, :] * r.norm2[1:2, :]], 24))
    r.send(r.pay)
    blocks_copy.wait()
    if is_head:
        head_copy.wait()
    r.finish(r.dz2)


def gate_back(is_head, row_count, owners, recv, upper, cross, stream, lower, blocks, extra_room):
    count = upper.xb.shape[0]
    images = count // MAP
    devices = recv.shape[0]
    columns = HEAD if is_head else EXPAND
    block = EXPAND // CHUNK * (2 * WIDTH // owners) + 2 * SQUEEZE + 16
    where = (slice(0, HEAD), slice(0, WIDTH)) if is_head else (slice(0, WIDTH), slice(None))
    ins = dict(
        recv=(recv, FAR),
        unorm=(upper.norm, FAR),
        xb=(upper.xb, FAR),
        w=(upper.weights, where),
        dz=(upper.dz, CHUNKS),
        norm3=(lower.norm3, FAR),
        normed=(lower.normed, FAR),
        norm2=(lower.norm2, FAR),
        wp=(lower.mats, (slice(WIDTH, 2 * WIDTH), slice(None))),
        d=(lower.d, CHUNKS),
        excite=(lower.excite, FAR),
        pooled=(lower.pooled, FAR),
        squeeze=(lower.squeeze, FAR),
        side=(lower.side, (slice(0, 2 * SQUEEZE), slice(None))),
    )
    outs = dict(
        dz2=(shape((count, EXPAND), BF16), FAR),
        pay=(shape((devices, 24, LANE), BF16), FAR),
        stream=(shape((count, WIDTH)), FAR),
        blocks=(shape((owners, block * (1 + extra_room), CHUNK), BF16), RAW),
        glob=(shape((8, columns)), FAR),
        glob3=(shape((8, WIDTH)), FAR),
    )
    scratch = dict(
        grads=vmem((owners, block, CHUNK), BF16),
        xt=vmem((WIDTH, count), BF16),
        h=vmem((count, CHUNK), F32),
        coef=vmem((8, EXPAND), F32),
        dh=vmem((count + WIDTH + 16, columns), BF16),
        u=vmem((count, EXPAND), BF16),
        slope=vmem((count, EXPAND), BF16),
        y=vmem((count, EXPAND), BF16),
        gp=vmem((count, WIDTH), BF16),
        gt=vmem((WIDTH, count), BF16),
        ge=vmem((images, EXPAND), F32),
        pool=vmem((images, EXPAND), F32),
        rx=vmem((2 * SQUEEZE, EXPAND), F32),
        excite_sum=vmem((1, EXPAND), F32),
        squeeze_sum=vmem((1, LANE), F32),
        stat=vmem((8, EXPAND), F32),
        own_sem=pltpu.SemaphoreType.DMA((2,)),
    )
    alias = []
    if is_head:
        ins["grad_head_in"] = (upper.grad_head, RAW)
        outs["grad_head"] = (shape((HEAD, HEADPAD), BF16), RAW)
        scratch["grad_w"] = vmem((HEAD, WIDTH), BF16)
        alias.append(("grad_head_in", "grad_head"))
    else:
        ins["cross"] = (cross, FAR)
        ins["stream_in"] = (stream, FAR)
        ins["taps"] = (upper.taps, FAR)
        scratch["grad_w"] = vmem((WIDTH, EXPAND), BF16)
        if blocks is not None:
            ins["blocks_in"] = (blocks, RAW)
            outs["blocks"] = (shape(blocks.shape, BF16), RAW)
            alias.append(("blocks_in", "blocks"))
    return call(functools.partial(gate_kernel, is_head, row_count, owners), ins, outs, scratch, alias)


def tap_kernel(is_first, row_count, r):
    count = r.dz2.shape[0]
    groups = EXPAND // LANE
    r.start()
    r.wait(r.recv)
    sums = read_sums(r.recv)
    sum_bias = spread(sums, 0, groups)
    sum_gain = spread(sums, groups, groups)
    r.glob[0:1, :] = sum_gain
    r.glob[1:2, :] = sum_bias
    r.glob[2:8, :] = jnp.zeros((6, EXPAND), F32)
    r.send(r.glob)
    r.wait(r.side, r.norm2)
    scale2 = r.norm2[2:3, :]
    slant2 = scale2 * r.norm2[1:2, :] * (sum_gain / row_count)
    r.coef[0:9, :] = r.side[...].astype(F32)[0:9, :]
    r.coef[9:10, :] = slant2
    r.coef[10:11, :] = r.norm2[0:1, :] * slant2 - scale2 * (sum_bias / row_count)
    r.wait(r.norm1, r.xb, r.w)

    def step(index, carry):
        at_chunk = chunk_at(index)
        r.chunk(r.dz2, index, at_chunk).wait()
        r.chunk(r.d, index, at_chunk).wait()
        r.h[...] = dot(r.xb[...], r.w[:, at_chunk])
        for part in range(PARTS):
            lanes = chunk_at(index * PARTS + part, LANE)
            near = slice(part * LANE, (part + 1) * LANE)
            taps = [jnp.broadcast_to(r.coef[k : k + 1, lanes], (TILE, LANE)) for k in range(9)]

            def tile_step(tile, sums_in):
                at = chunk_at(tile, ROWS)
                grad_d = as_tile(
                    r.dz2[at, lanes].astype(F32) * r.norm2[2:3, lanes]
                    - r.d[at, lanes].astype(F32) * r.coef[9:10, lanes]
                    + r.coef[10:11, lanes]
                )
                hidden = r.h[at, near]
                pre = hidden * r.norm1[2:3, lanes] + r.norm1[3:4, lanes]
                gate = sigmoid(pre)
                flat = pre * gate
                active = as_tile(flat)
                slope = as_tile(gate + flat - flat * gate)
                apart = as_tile(hidden - r.norm1[0:1, lanes])
                grad_a = [None] * MAP
                tap_sums = [None] * 9
                for target, tap, source in TERMS:
                    term = grad_d[target] * taps[tap]
                    grad_a[source] = term if grad_a[source] is None else grad_a[source] + term
                    term = grad_d[target] * active[source]
                    tap_sums[tap] = term if tap_sums[tap] is None else tap_sums[tap] + term
                total, weighted = sums_in[9], sums_in[10]
                grads = []
                for place in range(MAP):
                    grad = grad_a[place] * slope[place]
                    total = total + grad
                    weighted = weighted + grad * apart[place]
                    grads.append(grad)
                grad = jnp.concatenate(grads, axis=0)
                r.dz[at, lanes] = grad.astype(BF16)
                if not is_first:
                    r.q[at, lanes] = (grad * r.norm1[2:3, lanes]).astype(BF16)
                return (*[sums_in[k] + tap_sums[k] for k in range(9)], total, weighted)

            zero = jnp.zeros((TILE, LANE), F32)
            result = lax.fori_loop(0, count // ROWS, tile_step, (zero,) * 11, unroll=True)
            for k in range(9):
                r.taps[k : k + 1, lanes] = column_sum(result[k])
            r.stat[0:1, lanes] = column_sum(result[9])
            r.stat[1:2, lanes] = column_sum(result[10])
        r.part(r.dz, index, at_chunk).start()
        return carry

    lax.fori_loop(0, EXPAND // CHUNK, step, 0)
    r.taps[9:16, :] = jnp.zeros((7, EXPAND), F32)
    r.send(r.taps)
    vectors = [r.stat[0:1, :], r.stat[1:2, :] * r.norm1[1:2, :]]
    if not is_first:
        r.wait(r.normed, r.stream)
        below = r.stream[...] + dot_nt(r.q[...], r.w[...])
        vectors.append(column_sum(below))
        vectors.append(column_sum(below * r.normed[...]))
    write_alike(r.pay, fold(vectors, r.pay.shape[1]))
    r.send(r.pay)
    r.finish(r.dz)


def tap_back(is_first, row_count, recv, dz2, layer, stream, below):
    count = dz2.shape[0]
    devices = recv.shape[0]
    ins = dict(
        recv=(recv, FAR),
        side=(layer.side, (slice(2 * SQUEEZE, SIDE_PAD), slice(None))),
        norm2=(layer.norm2, FAR),
        norm1=(layer.norm1, FAR),
        xb=(layer.xb, FAR),
        w=(layer.mats, (slice(0, WIDTH), slice(None))),
        dz2=(dz2, CHUNKS),
        d=(layer.d, CHUNKS),
    )
    scratch = dict(
        h=vmem((count, CHUNK), F32),
        coef=vmem((16, EXPAND), F32),
        stat=vmem((8, EXPAND), F32),
    )
    if not is_first:
        ins["stream"] = (stream, FAR)
        ins["normed"] = (below.normed, FAR)
        scratch["q"] = vmem((count, EXPAND), BF16)
    return call(
        functools.partial(tap_kernel, is_first, row_count),
        ins,
        dict(
            dz=(shape((count, EXPAND), BF16), FAR),
            pay=(shape((devices, 24 if is_first else 32, LANE), BF16), FAR),
            taps=(shape((16, EXPAND)), FAR),
            glob=(shape((8, EXPAND)), FAR),
        ),
        scratch,
    )


def last_kernel(row_count, replicas, owners, r):
    r.start()
    r.wait(r.recv)
    product_back(False, row_count, read_sums(r.recv), EXPAND, r)
    half = owners // 2
    part = slice_rows(replicas * owners)
    rows_dev = 2 * WIDTH // owners
    chunks = EXPAND // CHUNK
    for device in range(replicas * owners):
        replica, owner = device // owners, device % owners
        first_row = rows_dev * (owner % half) + (2 * replica + owner // half) * part
        for k in range(chunks):
            r.shares[device, k * part : (k + 1) * part, :] = r.grad_w[
                first_row : first_row + part, k * CHUNK : (k + 1) * CHUNK
            ]
    if r.shares.shape[1] > chunks * part:
        r.shares[:, chunks * part :, :] = jnp.zeros(
            (replicas * owners, r.shares.shape[1] - chunks * part, CHUNK), F32
        )
    r.grads[...] = r.shares[...].astype(BF16)
    r.send(r.grads)
    r.finish()


def last_back(row_count, replicas, owners, recv, layer, dz):
    count = dz.shape[0]
    devices = recv.shape[0]
    block = -(-EXPAND // CHUNK * slice_rows(devices) // 16) * 16
    return call(
        functools.partial(last_kernel, row_count, replicas, owners),
        dict(
            recv=(recv, FAR),
            dz=(dz, CHUNKS),
            unorm=(layer.norm1, FAR),
            xb=(layer.xb, FAR),
            w=(layer.mats, (slice(0, WIDTH), slice(None))),
        ),
        dict(
            grads=(shape((devices, block, CHUNK), BF16), FAR),
            glob=(shape((8, EXPAND)), FAR),
        ),
        dict(
            xt=vmem((WIDTH, count), BF16),
            h=vmem((count, CHUNK), F32),
            coef=vmem((8, EXPAND), F32),
            dh=vmem((count, EXPAND), BF16),
            grad_w=vmem((WIDTH, EXPAND), F32),
            shares=vmem((devices, block, CHUNK), F32),
        ),
    )


def lamb_moments(weight, moment_one, moment_two, gradient, decay_mask, step_float):
    first_new = BETA_ONE * moment_one + (1.0 - BETA_ONE) * gradient
    second_new = BETA_TWO * moment_two + (1.0 - BETA_TWO) * gradient * gradient
    corrected = (
        first_new
        / (1.0 - BETA_ONE**step_float)
        / (jnp.sqrt(second_new / (1.0 - BETA_TWO**step_float)) + EPS_ADAM)
    )
    return (first_new, second_new, corrected + DECAY_RATE * decay_mask * weight)


def group_sums(mats, side, head_shard, row_ids):
    rows = jnp.sum(mats * mats, axis=2)
    is_expand = (row_ids < WIDTH)[None, :]
    side_rows = jnp.sum(side * side, axis=2)
    head_cols = jnp.sum(head_shard * head_shard, axis=0)
    per_layer = jnp.stack(
        [
            jnp.sum(jnp.where(is_expand, rows, 0.0), axis=1),
            jnp.sum(jnp.where(is_expand, 0.0, rows), axis=1),
            jnp.sum(side_rows[:, :9], axis=1),
            jnp.sum(side_rows[:, 9 : 9 + SQUEEZE], axis=1),
            jnp.sum(side_rows[:, 9 + SQUEEZE : 9 + 2 * SQUEEZE], axis=1),
        ],
        axis=1,
    )
    tail = jnp.stack([jnp.sum(head_cols[:WIDTH]), jnp.sum(head_cols[WIDTH : WIDTH + CLASSES])])
    return jnp.concatenate([per_layer.reshape(-1), tail])


def rate_maps(trust_ratio, row_ids):
    groups = trust_ratio[: 5 * LAYERS].reshape(LAYERS, 5)
    mats_rate = RATE_MATRIX * jnp.where(row_ids[None, :] < WIDTH, groups[:, 0:1], groups[:, 1:2])
    side_ids = jnp.arange(SIDE)[None, :]
    side_rate = jnp.where(
        side_ids < 9,
        RATE_MATRIX * groups[:, 2:3],
        jnp.where(
            side_ids < 9 + SQUEEZE,
            RATE_MATRIX * groups[:, 3:4],
            jnp.where(side_ids < 9 + 2 * SQUEEZE, RATE_MATRIX * groups[:, 4:5], RATE_VECTOR),
        ),
    )
    col_ids = jnp.arange(HEADCOLS)
    head_rate = jnp.where(
        col_ids < WIDTH,
        RATE_MATRIX * trust_ratio[5 * LAYERS],
        jnp.where(
            col_ids < WIDTH + CLASSES, RATE_MATRIX * trust_ratio[5 * LAYERS + 1], RATE_VECTOR
        ),
    )
    return (mats_rate, side_rate, head_rate)


def exchange(payload):
    return lax.all_to_all(payload, BOTH, 0, 0)


def before(value, *others):
    return lax.optimization_barrier((value, *others))[0]


def spread_over(array, axis):
    copies = jnp.broadcast_to(array[None], (lax.axis_size(axis), *array.shape))
    return lax.all_to_all(copies, axis, 0, 0)


def replica_sum(array):
    count = lax.axis_size(REPLICAS)
    total = array.astype(F32)
    for turn in range(1, count):
        pairs = [(k, (k + turn) % count) for k in range(count)]
        total = total + lax.ppermute(array, REPLICAS, pairs).astype(F32)
    return total


def body(
    images, partner, mix_pair, labels, step,
    layer_mats, layer_side, layer_vecs, head_mat, fc_bias,
    mats_first, mats_second, side_first, side_second, vecs_first, vecs_second,
    head_first, head_second, bias_first, bias_second,
):
    local_images = images.shape[0]
    owners = lax.axis_size(OWNERS)
    replicas = lax.axis_size(REPLICAS)
    devices = owners * replicas
    image_count = float(local_images * devices)
    count = local_images * MAP
    row_count = float(count * devices)
    mine = lax.axis_index(OWNERS)
    side_width = layer_side.shape[2]
    vec_width = layer_vecs.shape[1]
    rows_dev = layer_mats.shape[1]
    half = owners // 2

    side_low = jnp.concatenate(
        [
            layer_side[:, 9 : 9 + 2 * SQUEEZE],
            layer_side[:, :9],
            layer_side[:, 9 + 2 * SQUEEZE :],
            jnp.pad(layer_vecs, ((0, 0), (0, side_width - vec_width)))[:, None, :],
            jnp.zeros((LAYERS, 1, side_width), F32),
        ],
        axis=1,
    ).astype(BF16)
    mats_all = [
        lax.all_gather(layer_mats[k].astype(BF16), OWNERS, axis=0, tiled=True) for k in range(LAYERS)
    ]
    side_zero = lax.all_gather(side_low[0], OWNERS, axis=1, tiled=True)
    side_room = -(-side_width // CHUNK) * CHUNK
    side_rest = lax.all_gather(
        jnp.pad(side_low[1:], ((0, 0), (0, 0), (0, side_room - side_width))), OWNERS, axis=0
    )
    side_rest = jnp.moveaxis(side_rest[..., :side_width], 0, 2).reshape(LAYERS - 1, SIDE_PAD, EXPAND)
    side_all = [side_zero, side_rest[0], side_rest[1]]
    head_full = lax.all_gather(
        jnp.pad(head_mat, ((0, 0), (0, HEADPAD - HEADCOLS))).astype(BF16), OWNERS, axis=0, tiled=True
    )

    partner_col = partner[:, None]
    layers = []
    crosses = []
    entry = mix(before(images, side_zero).reshape(count, WIDTH), partner_col, mix_pair)
    x, xb = entry.x, entry.xb
    pay = first(xb, mats_all[0], devices).pay
    for k in range(LAYERS):
        mats, side = mats_all[k], side_all[k]
        one = spatial(xb, mats, side, exchange(pay))
        two = project(one.d, mats, side, exchange(one.pay), getattr(one, "cross", None), owners)
        last = k == LAYERS - 1
        three = residual(
            x, two.p, two.vec, exchange(two.pay), head_full if last else mats_all[k + 1], last
        )
        if k:
            crosses.append(three.cross)
        layers.append(
            types.SimpleNamespace(
                xb=xb, d=one.d, norm1=one.norm, norm2=two.norm,
                pooled=two.pooled, excite=two.excite, squeeze=two.squeeze,
                norm3=three.norm, normed=three.normed, mats=mats, weights=mats, side=side,
            )
        )
        x, xb, pay = three.x, three.xb, three.pay
    top = head(
        xb, head_full, jnp.pad(fc_bias, (0, LOGITS - CLASSES))[None], labels[:, None], labels[None, :],
        partner_col, mix_pair, layers[-1].normed, exchange(pay), image_count,
    )

    def to_owner(blocks):
        return lax.psum_scatter(
            blocks.reshape(-1, blocks.shape[-1]), OWNERS, scatter_dimension=0, tiled=True
        )

    upper = types.SimpleNamespace(
        xb=xb, weights=head_full, dz=top.dz, norm=top.norm, grad_head=top.grad_head
    )
    pay = top.pay
    stream = None
    blocks = None
    waiting = []
    globs_one, globs_two, globs_three = [None] * LAYERS, [None] * LAYERS, [None] * LAYERS
    for k in reversed(range(LAYERS)):
        layer = layers[k]
        is_head = k == LAYERS - 1
        gate = gate_back(
            is_head, row_count, owners, exchange(pay), upper,
            None if is_head else crosses[k], stream, layer, blocks, is_head,
        )
        stream = gate.stream
        globs_three[k] = gate.glob3
        if is_head:
            head_glob, bias_loss = gate.glob, gate.glob3[2:6].reshape(LOGITS)
            shard_head = to_owner(gate.grad_head)
            blocks = gate.blocks
        else:
            globs_one[k + 1] = gate.glob
            if k:
                pair = to_owner(gate.blocks)
                blocks = None
            else:
                shard_zero = to_owner(gate.blocks)
        tap = tap_back(
            k == 0, row_count, exchange(gate.pay), gate.dz2, layer, stream, layers[max(k - 1, 0)]
        )
        globs_two[k] = tap.glob
        pay = tap.pay
        if k == 1:
            shard_head = replica_sum(shard_head)
            pay = before(pay, shard_head)
        upper = types.SimpleNamespace(
            xb=layer.xb, weights=layer.mats, dz=tap.dz, norm=layer.norm1, taps=tap.taps
        )
    pair = replica_sum(pair)
    pay = before(pay, pair)
    late_taps = jnp.moveaxis(tap.taps[:9].astype(BF16).reshape(9, owners, side_width), 1, 0)
    late_taps = jnp.broadcast_to(late_taps[None], (replicas, *late_taps.shape))
    late_taps = exchange(late_taps.reshape(devices, 9, side_width))
    final = last_back(row_count, replicas, owners, exchange(pay), layers[0], tap.dz)
    globs_one[0] = final.glob
    late_taps = jnp.sum(late_taps.astype(F32), axis=0)
    room = pair.shape[0] // 2
    shards = [replica_sum(shard_zero), pair[room:], pair[:room]]

    part = slice_rows(devices)
    chunks = EXPAND // CHUNK
    late = jnp.sum(exchange(final.grads).astype(F32), axis=0).astype(BF16)
    other = lax.ppermute(late, OWNERS, [(half + k, k) for k in range(half)])
    late = spread_over(jnp.stack([late, other]), REPLICAS)[:, :, : chunks * part]
    late = jnp.moveaxis(late.reshape(replicas, 2, chunks, part, CHUNK), 2, 3)
    late = late.reshape(rows_dev, EXPAND).astype(F32)

    def mats_of(shard):
        rows = shard[: chunks * rows_dev].reshape(chunks, rows_dev, CHUNK)
        return jnp.moveaxis(rows, 0, 1).reshape(rows_dev, EXPAND)

    from_mats = [late] + [mats_of(shard) for shard in shards]
    owns_expand = mine < half
    grad_mats = jnp.stack(
        [jnp.where(owns_expand, from_mats[k], from_mats[k + 1]) for k in range(LAYERS)]
    )

    def own_columns(vector, width):
        return lax.dynamic_slice_in_dim(vector, mine * width, width, axis=-1)

    first_row = chunks * rows_dev
    last_row = first_row + 2 * SQUEEZE
    vec_ids = mine * vec_width + jnp.arange(vec_width)
    side_list, vec_list = [], []
    for k in range(LAYERS):
        shard = shards[k][:, :side_width]
        taps = late_taps if k == 0 else shards[k - 1][last_row + 2 : last_row + 11, :side_width]
        norms_part = own_columns(
            jnp.concatenate([globs_one[k][0:2], globs_two[k][0:2]], axis=0), side_width
        )
        side_list.append(
            jnp.concatenate([taps, shard[first_row : last_row + 1], norms_part], axis=0)
        )
        outer = globs_three[k]
        outer = own_columns(
            jnp.concatenate([jnp.zeros((SQUEEZE,), F32), outer[0], outer[1]]), vec_width
        )
        vec_list.append(jnp.where(vec_ids < SQUEEZE, shard[last_row + 1, :vec_width], outer))
    grad_side = jnp.stack(side_list)
    grad_vecs = jnp.stack(vec_list)
    head_tail = own_columns(head_glob[0:2], head_mat.shape[0]).T
    grad_head = jnp.concatenate([shard_head[:, : WIDTH + CLASSES], head_tail], axis=1)
    grad_bias = bias_loss[:CLASSES]
    loss_value = (bias_loss[CLASSES] + bias_loss[CLASSES + 1]) / image_count

    step_float = step[0].astype(F32)
    side_decay = (jnp.arange(SIDE) < 9 + 2 * SQUEEZE).astype(F32)[None, :, None]
    head_decay = (jnp.arange(HEADCOLS) < WIDTH + CLASSES).astype(F32)[None, :]
    mats_moment, mats_square, mats_dir = lamb_moments(
        layer_mats, mats_first, mats_second, grad_mats, 1.0, step_float
    )
    side_moment, side_square, side_dir = lamb_moments(
        layer_side, side_first, side_second, grad_side, side_decay, step_float
    )
    vecs_moment, vecs_square, vecs_dir = lamb_moments(
        layer_vecs, vecs_first, vecs_second, grad_vecs, 0.0, step_float
    )
    head_moment, head_square, head_dir = lamb_moments(
        head_mat, head_first, head_second, grad_head, head_decay, step_float
    )
    bias_moment, bias_square, bias_dir = lamb_moments(
        fc_bias, bias_first, bias_second, grad_bias, 0.0, step_float
    )
    row_ids = mine * rows_dev + jnp.arange(rows_dev)
    squares = jnp.stack(
        [
            group_sums(layer_mats, layer_side, head_mat, row_ids),
            group_sums(mats_dir, side_dir, head_dir, row_ids),
        ]
    )
    norms = jnp.sqrt(jnp.sum(spread_over(squares, OWNERS), axis=0))
    mats_rate, side_rate, head_rate = rate_maps(norms[0] / norms[1], row_ids)
    mats_new = layer_mats - mats_rate[:, :, None] * mats_dir
    side_new = layer_side - side_rate[:, :, None] * side_dir
    vecs_new = layer_vecs - RATE_VECTOR * vecs_dir
    head_new = head_mat - head_rate[None, :] * head_dir
    bias_new = fc_bias - RATE_VECTOR * bias_dir
    return (
        loss_value,
        mats_new, mats_moment, mats_square,
        side_new, side_moment, side_square,
        vecs_new, vecs_moment, vecs_square,
        head_new, head_moment, head_square,
        bias_new, bias_moment, bias_square,
        norms,
    )


def solution(mesh):
    rows, columns = P(None, OWNERS, None), P(None, None, OWNERS)
    vecs, heads = P(None, OWNERS), P(OWNERS, None)
    return jax.shard_map(
        body,
        mesh=mesh,
        in_specs=(
            P(BOTH, None, None), P(BOTH), P(BOTH, None), P(BOTH), P(),
            rows, columns, vecs, heads, P(),
            rows, rows, columns, columns, vecs, vecs, heads, heads, P(), P(),
        ),
        out_specs=(
            P(),
            rows, rows, rows,
            columns, columns, columns,
            vecs, vecs, vecs,
            heads, heads, heads,
            P(), P(), P(), P(),
        ),
        check_vma=False,
    )
```

```python
import functools
import types

import jax
import jax.numpy as jnp
from jax import lax
from jax.experimental import pallas as pl
from jax.experimental.pallas import tpu as pltpu
from jax.sharding import PartitionSpec as P

WIDTH = 256
EXPAND = 1536
SQUEEZE = 64
HEAD = 1280
CLASSES = 1000
LOGITS = 1024
EDGE = 4
LAYERS = 3
MAP = 16
SIDE = 142
SIDE_PAD = 144
VECS = 576
HEADCOLS = 1258
HEADPAD = 1280

EPS_BN = 0.001
BETA_ONE = 0.9
BETA_TWO = 0.999
EPS_ADAM = 1e-06
DECAY_RATE = 0.01
RATE_MATRIX = 0.5
RATE_VECTOR = 0.25

REPLICAS, OWNERS = BOTH = ("dp", "fsdp")
F32 = jnp.float32
BF16 = jnp.bfloat16
LANE = 128
TILE = 8
ROWS = MAP * TILE
CHUNK = 256
PARTS = CHUNK // LANE
VMEM_BYTES = 60 * 1024 * 1024

NT = (((1,), (1,)), ((), ()))
TN = (((0,), (0,)), ((), ()))


NEAR, FAR, RAW, CHUNKS, LOOSE = range(5)


class Refs:
    def __init__(self, names, refs, loads, stores):
        for name, ref in zip(names, refs):
            setattr(self, name, ref)
        self.loads = loads
        self.stores = {id(getattr(self, name)): (k, self.far(name)) for k, name in enumerate(stores)}
        self.pending = {}
        self.chunks = {}

    def far(self, name):
        return getattr(self, name + "_far")

    def start(self):
        for index, (name, where) in enumerate(self.loads):
            source = self.far(name) if where is None or where == CHUNKS else self.far(name).at[where]
            near = getattr(self, name)
            if where == CHUNKS:
                self.chunks[id(near)] = (self.far(name), index)
                for turn in range(near.shape[1] // CHUNK):
                    self.chunk(near, turn, pl.ds(turn * CHUNK, CHUNK)).start()
                continue
            copy = pltpu.make_async_copy(source, near, self.load_sem.at[index])
            copy.start()
            self.pending[id(near)] = copy

    def chunk(self, near, turn, at):
        far, index = self.chunks[id(near)]
        semaphore = self.load_sem.at[len(self.loads) + index * (EXPAND // CHUNK) + turn]
        return pltpu.make_async_copy(far.at[:, at], near.at[:, at], semaphore)

    def wait(self, *refs):
        for ref in refs:
            self.pending.pop(id(ref)).wait()

    def send(self, *refs):
        for ref in refs:
            index, far = self.stores[id(ref)]
            copy = pltpu.make_async_copy(ref, far, self.store_sem.at[index])
            copy.start()
            self.pending[id(far)] = copy

    def part(self, ref, index, at):
        far = self.stores[id(ref)][1]
        return pltpu.make_async_copy(ref.at[:, at], far.at[:, at], self.part_sem.at[index])

    def finish(self, ref=None):
        for key in list(self.pending):
            self.pending.pop(key).wait()
        if ref is not None:
            for index in range(ref.shape[1] // CHUNK):
                self.part(ref, index, pl.ds(index * CHUNK, CHUNK)).wait()


def shape(dims, dtype=F32):
    return jax.ShapeDtypeStruct(dims, dtype)


def vmem(dims, dtype=F32):
    return pltpu.VMEM(dims, dtype)


def call(kernel, ins, outs, scratch, alias=()):
    near, far, loose = (
        pl.BlockSpec(memory_space=space) for space in (pltpu.VMEM, pltpu.HBM, pl.ANY)
    )
    names, arrays, in_specs, loads, stores, extra = [], [], [], [], [], {}
    for name, (array, place) in ins.items():
        arrays.append(array)
        in_specs.append(near if place == NEAR else loose if place == LOOSE else far)
        if place == NEAR or place == RAW:
            names.append(name)
            continue
        names.append(name + "_far")
        dims, where = array.shape, None
        if place == CHUNKS:
            where = CHUNKS
        elif place != FAR and place != LOOSE:
            starts = [part.indices(size)[:2] for part, size in zip(place, dims)]
            dims = tuple(stop - start for start, stop in starts)
            where = tuple(pl.ds(start, stop - start) for start, stop in starts)
        loads.append((name, where))
        extra[name] = vmem(dims, array.dtype)
    for name, (struct, place) in outs.items():
        names.append(name + "_far" if place == FAR else name)
        if place == FAR:
            stores.append(name)
            extra[name] = vmem(struct.shape, struct.dtype)
    extra.update(scratch)
    extra.update(
        load_sem=pltpu.SemaphoreType.DMA((max(len(loads), 1) * (1 + EXPAND // CHUNK),)),
        store_sem=pltpu.SemaphoreType.DMA((max(len(stores), 1),)),
        part_sem=pltpu.SemaphoreType.DMA((EXPAND // CHUNK,)),
    )

    def flat(*refs):
        kernel(Refs(names + list(extra), refs, loads, stores))

    results = pl.pallas_call(
        flat,
        out_shape=[struct for struct, _ in outs.values()],
        in_specs=in_specs,
        out_specs=[near if place == NEAR else far for _, place in outs.values()],
        scratch_shapes=list(extra.values()),
        input_output_aliases={list(ins).index(a): list(outs).index(b) for a, b in alias},
        compiler_params=pltpu.CompilerParams(vmem_limit_bytes=VMEM_BYTES),
    )(*arrays)
    return types.SimpleNamespace(**dict(zip(outs, results)))


def dot(left, right):
    return jnp.dot(left, right, preferred_element_type=F32)


def dot_nt(left, right):
    return lax.dot_general(left, right, NT, preferred_element_type=F32)


def dot_tn(left, right):
    return lax.dot_general(left, right, TN, preferred_element_type=F32)


def halves(value):
    high = value.astype(BF16)
    return high, (value - high.astype(F32)).astype(BF16)


def stacked(value):
    return jnp.concatenate(halves(value), axis=0)


def folded(value):
    count = value.shape[0] // 2
    return value[:count] + value[count:]


def sigmoid(value):
    return 0.5 * jnp.tanh(0.5 * value) + 0.5


def chunk_at(index, size=CHUNK):
    return pl.ds(pl.multiple_of(index * size, size), size)


def tile_rows(tile):
    return slice(tile * ROWS, (tile + 1) * ROWS)


def tile_images(tile):
    return slice(tile * TILE, (tile + 1) * TILE)


def as_tile(block):
    return block.reshape(MAP, TILE, LANE)


def spread(rows, first, count):
    return jnp.concatenate([rows[first + k : first + k + 1, :] for k in range(count)], axis=1)


def fold(vectors, rows):
    pieces = [
        vector[:, k * LANE : (k + 1) * LANE]
        for vector in vectors
        for k in range(vector.shape[1] // LANE)
    ]
    if rows > len(pieces):
        pieces.append(jnp.zeros((rows - len(pieces), LANE), F32))
    return jnp.concatenate(pieces, axis=0)


def column_sum(value):
    return jnp.sum(value, axis=0, keepdims=True)


def slice_rows(devices):
    return max(1, WIDTH // devices)


def write_alike(pay_ref, rows):
    pay_ref[...] = jnp.broadcast_to(rows.astype(BF16)[None], pay_ref.shape)


def write_with_slices(pay_ref, rows, matrix):
    devices = pay_ref.shape[0]
    part = slice_rows(devices)
    first = rows.shape[0]
    low = rows.astype(BF16)
    for device in range(devices):
        own = matrix[device * part : (device + 1) * part, :]
        block = jnp.concatenate([own[:, :LANE], own[:, LANE:]], axis=0)
        if 2 * part < 16:
            block = jnp.concatenate([block, jnp.zeros((16 - 2 * part, LANE), F32)], axis=0)
        pay_ref[device, 0:first, :] = low
        pay_ref[device, first : first + 16, :] = block.astype(BF16)


def read_matrix(recv_ref, first):
    devices, rows = recv_ref.shape[:2]
    part = slice_rows(devices)
    if part == TILE:
        values = recv_ref[...].astype(F32)
        left = values[:, first : first + part].reshape(WIDTH, LANE)
        right = values[:, first + part : first + 2 * part].reshape(WIDTH, LANE)
        return jnp.concatenate([left, right], axis=1)
    flat = recv_ref[...].reshape(devices * rows, LANE)
    row = lax.broadcasted_iota(jnp.int32, (WIDTH, devices * rows), 0)
    column = lax.broadcasted_iota(jnp.int32, (WIDTH, devices * rows), 1)
    source = row // part * rows + first + row % part
    left = dot(jnp.where(column == source, 1.0, 0.0).astype(BF16), flat)
    right = dot(jnp.where(column == source + part, 1.0, 0.0).astype(BF16), flat)
    return jnp.concatenate([left, right], axis=1)


def mean_parts(columns):
    return 1 if columns == EXPAND else 2


def moment_rows(columns):
    return -(-(mean_parts(columns) + 1) * columns // LANE // 8) * 8


def centred(total, squares, count):
    return jnp.maximum(squares - total * total / count, 0.0)


def pack_moments(total, squares, count):
    mean = total / count
    high = mean.astype(BF16).astype(F32)
    parts = [high, mean - high][: mean_parts(total.shape[1])]
    return fold(parts + [centred(total, squares, count)], moment_rows(total.shape[1]))


def read_moments(recv_ref, columns, count):
    groups = columns // LANE
    devices = recv_ref.shape[0]
    parts = recv_ref[...].astype(F32)
    given = mean_parts(columns)
    means = parts[:, :groups]
    if given > 1:
        means = means + parts[:, groups : 2 * groups]
    mean = jnp.sum(means, axis=0) / devices
    apart = means - mean[None]
    spread_sum = jnp.sum(parts[:, given * groups : (given + 1) * groups], axis=0) / count
    variance = (spread_sum + jnp.sum(apart * apart, axis=0)) / devices
    return spread(mean, 0, groups), lax.rsqrt(spread(variance, 0, groups) + EPS_BN)


def read_product_moments(recv_ref, weights, transposed, columns, count):
    devices, rows = recv_ref.shape[:2]
    values = recv_ref[...]
    flat = values.reshape(devices * rows, LANE)
    row = lax.broadcasted_iota(jnp.int32, (devices, devices * rows), 0)
    column = lax.broadcasted_iota(jnp.int32, (devices, devices * rows), 1) - row * rows
    left = dot(jnp.where((column == 0) | (column == 2), 1.0, 0.0).astype(BF16), flat)
    right = dot(jnp.where((column == 1) | (column == 3), 1.0, 0.0).astype(BF16), flat)
    sums = stacked(jnp.concatenate([left, right], axis=1) / count)
    means = folded(dot_nt(sums, weights) if transposed else dot(sums, weights))
    mean = column_sum(means) / devices
    apart = means - mean
    squares = jnp.sum(values.astype(F32), axis=0)
    variance = (spread(squares, 4, columns // LANE) / count + column_sum(apart * apart)) / devices
    return mean, lax.rsqrt(variance + EPS_BN)


def read_sums(recv_ref):
    return jnp.sum(recv_ref[...].astype(F32), axis=0)


def keep_norm(norm_ref, mean, inverse, gain, bias):
    scale = inverse * gain
    norm_ref[0:1, :] = mean
    norm_ref[1:2, :] = inverse
    norm_ref[2:3, :] = scale
    norm_ref[3:4, :] = bias - mean * scale
    norm_ref[4:8, :] = jnp.zeros((4, norm_ref.shape[1]), F32)


def product_moments(x_ref, w_ref, transposed, columns, left_ref, stat_ref, beside=None):
    count = x_ref.shape[0]
    values = x_ref[...]
    if beside is None:
        square = dot_tn(values, values)
    else:
        product = dot_tn(jnp.concatenate([values, beside], axis=1), values)
        square, cross = product[:WIDTH], product[WIDTH:]
    sums = column_sum(values.astype(F32))
    left_ref[0 : 2 * WIDTH, :] = stacked(square)
    tail = jnp.concatenate([half.astype(F32) for half in halves(sums)] + [jnp.zeros((14, WIDTH), F32)], axis=0)
    left_ref[2 * WIDTH :, :] = tail.astype(BF16)

    def step(index, carry):
        at = chunk_at(index)
        weights = w_ref[at, :].T if transposed else w_ref[:, at]
        product = dot(left_ref[...], weights)
        total = column_sum(product[2 * WIDTH : 2 * WIDTH + 2])
        squares = column_sum(folded(product[: 2 * WIDTH]) * weights.astype(F32))
        stat_ref[0:1, at] = jnp.maximum(squares - total * total / count, 0.0)
        return carry

    lax.fori_loop(0, columns // CHUNK, step, 0, unroll=True)
    high = sums.astype(BF16).astype(F32)
    rows = fold([high, sums - high, stat_ref[0:1, :]], 16)
    return rows if beside is None else (rows, cross)


def mix_kernel(r):
    count = r.images.shape[0]
    pixels = r.images[...]
    row = lax.broadcasted_iota(jnp.int32, (ROWS, count), 0)
    column = lax.broadcasted_iota(jnp.int32, (ROWS, count), 1)
    place = lax.shift_right_logical(row, 3)
    inside = jnp.bitwise_and(row, 7)
    pair = r.mix[...].astype(F32)
    mixing = pair[:, 0:1] / (pair[:, 0:1] + pair[:, 1:2])
    for tile in range(count // ROWS):
        near = tile_images(tile)
        other = jnp.concatenate([r.partner[near, :]] * MAP, axis=0)
        weight = jnp.concatenate([mixing[near, :]] * MAP, axis=0)
        own_hot = jnp.where(column == (tile * TILE + inside) * MAP + place, 1.0, 0.0).astype(BF16)
        other_hot = jnp.where(column == other * MAP + place, 1.0, 0.0).astype(BF16)
        mixed = weight * dot(own_hot, pixels) + (1.0 - weight) * dot(other_hot, pixels)
        r.x[tile_rows(tile), :] = mixed
    r.xb[...] = r.x[...].astype(BF16)
    r.send(r.x, r.xb)
    r.finish()


def mix(images, partner, mix_pair):
    dims = images.shape
    return call(
        mix_kernel,
        dict(images=(images, NEAR), partner=(partner, NEAR), mix=(mix_pair, NEAR)),
        dict(x=(shape(dims), FAR), xb=(shape(dims, BF16), FAR)),
        {},
    )


def first_kernel(r):
    r.start()
    r.wait(r.xb, r.w)
    write_alike(r.pay, product_moments(r.xb, r.w, False, EXPAND, r.left, r.stat))
    r.send(r.pay)
    r.finish()


def first(xb, mats, devices):
    return call(
        first_kernel,
        dict(xb=(xb, FAR), w=(mats, (slice(0, WIDTH), slice(None)))),
        dict(pay=(shape((devices, 16, LANE), BF16), FAR)),
        dict(left=vmem((2 * WIDTH + 16, WIDTH), BF16), stat=vmem((8, EXPAND))),
    )


def tap_terms():
    for row in range(EDGE):
        for col in range(EDGE):
            for row_shift in range(3):
                for col_shift in range(3):
                    from_row, from_col = row + row_shift - 1, col + col_shift - 1
                    if 0 <= from_row < EDGE and 0 <= from_col < EDGE:
                        yield EDGE * row + col, 3 * row_shift + col_shift, EDGE * from_row + from_col


TERMS = list(tap_terms())


def spatial_kernel(r):
    count = r.xb.shape[0]
    r.start()
    r.wait(r.recv, r.side, r.w, r.xb)
    rows = r.side[...].astype(F32)
    r.taps[0:9, :] = rows[0:9, :]
    mean, inverse = read_product_moments(r.recv, r.w[...], False, EXPAND, count)
    keep_norm(r.norm, mean, inverse, rows[10:11, :], rows[11:12, :])
    r.send(r.norm)
    if r.recv.shape[1] > 16:
        r.cross[...] = jnp.sum(r.recv[...].astype(F32)[:, 16:32], axis=0)
        r.send(r.cross)

    def step(index, carry):
        at_chunk = chunk_at(index)
        r.h[...] = dot(r.xb[...], r.w[:, at_chunk])
        for part in range(PARTS):
            lanes = chunk_at(index * PARTS + part, LANE)
            taps = [jnp.broadcast_to(r.taps[k : k + 1, lanes], (TILE, LANE)) for k in range(9)]
            scale_row = r.norm[2:3, lanes]
            shift_row = r.norm[3:4, lanes]

            def tile_step(tile, sums):
                at = chunk_at(tile, ROWS)
                pre = r.h[at, part * LANE : (part + 1) * LANE] * scale_row + shift_row
                active = as_tile(pre * sigmoid(pre))
                result = [None] * MAP
                for target, tap, source in TERMS:
                    term = active[source] * taps[tap]
                    result[target] = term if result[target] is None else result[target] + term
                total, squares = sums
                for value in result:
                    total = total + value
                    squares = squares + value * value
                r.d[at, lanes] = jnp.concatenate(result, axis=0).astype(BF16)
                return total, squares

            zero = jnp.zeros((TILE, LANE), F32)
            total, squares = lax.fori_loop(0, count // ROWS, tile_step, (zero, zero), unroll=True)
            r.stat[0:1, lanes] = column_sum(total)
            r.stat[1:2, lanes] = column_sum(squares)
        r.part(r.d, index, at_chunk).start()
        return carry

    lax.fori_loop(0, EXPAND // CHUNK, step, 0)
    write_alike(r.pay, pack_moments(r.stat[0:1, :], r.stat[1:2, :], count))
    r.send(r.pay)
    r.finish(r.d)


def spatial(xb, mats, side, recv):
    count = xb.shape[0]
    devices = recv.shape[0]
    outs = dict(
        d=(shape((count, EXPAND), BF16), FAR),
        pay=(shape((devices, moment_rows(EXPAND), LANE), BF16), FAR),
        norm=(shape((8, EXPAND)), FAR),
    )
    if recv.shape[1] > 16:
        outs["cross"] = (shape((16, LANE)), FAR)
    return call(
        spatial_kernel,
        dict(
            recv=(recv, LOOSE),
            side=(side, (slice(2 * SQUEEZE, SIDE_PAD), slice(None))),
            xb=(xb, FAR),
            w=(mats, (slice(0, WIDTH), slice(None))),
        ),
        outs,
        dict(
            h=vmem((count, CHUNK), F32),
            taps=vmem((16, EXPAND), F32),
            stat=vmem((8, EXPAND), F32),
        ),
    )


def project_kernel(with_cross, owners, r):
    count = r.d.shape[0]
    tiles = count // ROWS
    r.start()
    r.wait(r.recv)
    mean, inverse = read_moments(r.recv, EXPAND, count)
    r.wait(r.side)
    rows = r.side[2 * SQUEEZE : SIDE_PAD, :].astype(F32)
    keep_norm(r.norm, mean, inverse, rows[12:13, :], rows[13:14, :])
    r.send(r.norm)
    width, vec_width = EXPAND // owners, VECS // owners
    vec = jnp.concatenate(
        [rows[14:15, k * width : k * width + vec_width] for k in range(owners)], axis=1
    )
    r.vec[...] = jnp.concatenate(
        [vec[:, SQUEEZE : SQUEEZE + WIDTH], vec[:, SQUEEZE + WIDTH :], jnp.zeros((6, WIDTH), F32)], axis=0
    )
    r.send(r.vec)

    def activate(index, carry):
        r.chunk(r.d, index, chunk_at(index)).wait()
        for part in range(PARTS):
            lanes = chunk_at(index * PARTS + part, LANE)
            scale_row = r.norm[2:3, lanes]
            shift_row = r.norm[3:4, lanes]
            for tile in range(tiles):
                at = tile_rows(tile)
                pre = r.d[at, lanes].astype(F32) * scale_row + shift_row
                active = pre * sigmoid(pre)
                r.a[at, lanes] = active
                r.pooled[tile_images(tile), lanes] = jnp.sum(as_tile(active), axis=0) / MAP
        return carry

    lax.fori_loop(0, EXPAND // CHUNK, activate, 0)
    r.send(r.pooled)
    before = folded(dot_nt(stacked(r.pooled[...]), r.side[0:SQUEEZE, :])) + vec[:, :SQUEEZE]
    r.squeeze[...] = before
    r.send(r.squeeze)
    opened = folded(dot(stacked(before * sigmoid(before)), r.side[SQUEEZE : 2 * SQUEEZE, :]))
    r.excite[...] = sigmoid(opened + rows[9:10, :])
    r.send(r.excite)

    def gate(index, carry):
        lanes = chunk_at(index, LANE)
        for tile in range(tiles):
            at = tile_rows(tile)
            scaled = as_tile(r.a[at, lanes]) * r.excite[tile_images(tile), lanes][None]
            r.y[at, lanes] = scaled.reshape(ROWS, LANE).astype(BF16)
        return carry

    lax.fori_loop(0, EXPAND // LANE, gate, 0)
    r.wait(r.w)
    projected = dot_nt(r.y[...], r.w[...])
    r.p[...] = projected
    r.send(r.p)
    moments = pack_moments(column_sum(projected), column_sum(projected * projected), count)
    if with_cross:
        r.wait(r.cross)
        moments = jnp.concatenate([moments, r.cross[...]], axis=0)
    write_alike(r.pay, moments)
    r.send(r.pay)
    r.finish()


def project(d, mats, side, recv, cross, owners):
    count = d.shape[0]
    images = count // MAP
    devices = recv.shape[0]
    ins = dict(
        recv=(recv, LOOSE),
        side=(side, FAR),
        d=(d, CHUNKS),
        w=(mats, (slice(WIDTH, 2 * WIDTH), slice(None))),
    )
    rows = moment_rows(WIDTH)
    if cross is not None:
        ins["cross"] = (cross, FAR)
        rows += 16
    return call(
        functools.partial(project_kernel, cross is not None, owners),
        ins,
        dict(
            p=(shape((count, WIDTH)), FAR),
            vec=(shape((8, WIDTH)), FAR),
            pay=(shape((devices, rows, LANE), BF16), FAR),
            norm=(shape((8, EXPAND)), FAR),
            pooled=(shape((images, EXPAND)), FAR),
            excite=(shape((images, EXPAND)), FAR),
            squeeze=(shape((images, SQUEEZE)), FAR),
        ),
        dict(a=vmem((count, EXPAND), F32), y=vmem((count, EXPAND), BF16)),
    )


def residual_kernel(transposed, with_cross, r):
    count = r.p.shape[0]
    r.start()
    r.wait(r.recv, r.vec)
    mean, inverse = read_moments(r.recv, WIDTH, count)
    keep_norm(r.norm, mean, inverse, r.vec[0:1, :], r.vec[1:2, :])
    if with_cross:
        r.cross[...] = read_matrix(r.recv, moment_rows(WIDTH))
        r.send(r.cross)
    r.wait(r.p)
    normed = (r.p[...] - mean) * inverse
    r.normed[...] = normed
    r.wait(r.before)
    result = r.before[...] + (normed * r.vec[0:1, :] + r.vec[1:2, :])
    r.x[...] = result
    r.xb[...] = result.astype(BF16)
    r.send(r.norm, r.normed, r.x, r.xb)
    r.wait(r.w)
    moments, cross = product_moments(
        r.xb, r.w, transposed, r.stat.shape[1], r.left, r.stat, normed.astype(BF16)
    )
    write_with_slices(r.pay, moments, cross)
    r.send(r.pay)
    r.finish()


def residual(x, p, vec, recv, weights, transposed):
    count = x.shape[0]
    devices = recv.shape[0]
    with_cross = recv.shape[1] > moment_rows(WIDTH)
    columns = HEAD if transposed else EXPAND
    where = (slice(0, HEAD), slice(0, WIDTH)) if transposed else (slice(0, WIDTH), slice(None))
    outs = dict(
        x=(shape((count, WIDTH)), FAR),
        xb=(shape((count, WIDTH), BF16), FAR),
        normed=(shape((count, WIDTH)), FAR),
        pay=(shape((devices, 32, LANE), BF16), FAR),
        norm=(shape((8, WIDTH)), FAR),
    )
    if with_cross:
        outs["cross"] = (shape((WIDTH, WIDTH)), FAR)
    return call(
        functools.partial(residual_kernel, transposed, with_cross),
        dict(
            recv=(recv, LOOSE), vec=(vec, FAR), p=(p, FAR), before=(x, FAR), w=(weights, where)
        ),
        outs,
        dict(left=vmem((2 * WIDTH + 16, WIDTH), BF16), stat=vmem((8, columns))),
    )


def head_rows(last_columns):
    pick_row = lax.broadcasted_iota(jnp.int32, (TILE, LANE), 0)
    pick_col = lax.broadcasted_iota(jnp.int32, (TILE, LANE), 1)
    first_col = WIDTH + CLASSES - (HEADPAD - LANE)
    pick = jnp.where((pick_col == pick_row + first_col) & (pick_row < 2), 1.0, 0.0).astype(BF16)
    return dot_nt(pick, last_columns)


def head_kernel(image_count, r):
    count = r.xb.shape[0]
    tiles = count // ROWS
    images = count // MAP
    r.start()
    r.wait(r.recv, r.xb, r.w)
    mean, inverse = read_product_moments(r.recv, r.w[...], True, HEAD, count)
    cross = jnp.sum(r.recv[...].astype(F32)[:, 16:32], axis=0)
    r.wait(r.classifier)
    gain_bias = head_rows(r.classifier[:, LOGITS - LANE :])
    keep_norm(r.norm, mean, inverse, gain_bias[0:1, :], gain_bias[1:2, :])
    r.send(r.norm)

    def features(index, carry):
        at_chunk = chunk_at(index)
        r.h[:, at_chunk] = dot_nt(r.xb[...], r.w[at_chunk, :])
        for part in range(PARTS):
            lanes = chunk_at(index * PARTS + part, LANE)
            scale_row = r.norm[2:3, lanes]
            shift_row = r.norm[3:4, lanes]
            for tile in range(tiles):
                pre = r.h[tile_rows(tile), lanes] * scale_row + shift_row
                active = as_tile(pre * sigmoid(pre))
                r.f[tile_images(tile), lanes] = jnp.sum(active, axis=0) / MAP
        return carry

    lax.fori_loop(0, HEAD // CHUNK, features, 0)
    features_low = r.f[...].astype(BF16)
    classifier = r.classifier[...]
    ids = lax.broadcasted_iota(jnp.int32, (images, LOGITS), 1)
    logits = dot(features_low, classifier) + r.bias[...]
    logits = jnp.where(ids < CLASSES, logits, -1e30)
    row_max = jnp.max(logits, axis=1, keepdims=True)
    log_total = row_max + jnp.log(jnp.sum(jnp.exp(logits - row_max), axis=1, keepdims=True))
    pair = r.mix[...].astype(F32)
    mixing = pair[:, 0:1] / (pair[:, 0:1] + pair[:, 1:2])
    people = lax.broadcasted_iota(jnp.int32, (images, images), 1)
    label_row = jnp.broadcast_to(r.label_row[...].astype(F32), (images, images))
    partner_label = jnp.sum(
        jnp.where(people == r.partner[...], label_row, 0.0), axis=1, keepdims=True
    ).astype(jnp.int32)
    own_hot = jnp.where(ids == r.label_col[...], 1.0, 0.0)
    other_hot = jnp.where(ids == partner_label, 1.0, 0.0)
    own_logit = jnp.sum(own_hot * logits, axis=1, keepdims=True)
    other_logit = jnp.sum(other_hot * logits, axis=1, keepdims=True)
    loss = column_sum(mixing * (log_total - own_logit) + (1.0 - mixing) * (log_total - other_logit))
    grad_logits = (
        jnp.exp(logits - log_total) - mixing * own_hot - (1.0 - mixing) * other_hot
    ) / image_count
    grad_low = grad_logits.astype(BF16)
    r.grad_fc[...] = dot_tn(features_low, grad_low).astype(BF16)
    fc_copy = pltpu.make_async_copy(r.grad_fc, r.grad_head.at[:, pl.ds(WIDTH, LOGITS)], r.part_sem.at[0])
    fc_copy.start()
    r.f[...] = dot_nt(grad_low, classifier) / MAP
    bias_sum = column_sum(grad_logits)
    bias_ids = lax.broadcasted_iota(jnp.int32, (1, LOGITS), 1)
    loss_high = loss.astype(BF16).astype(F32)
    bias_sum = jnp.where(bias_ids == CLASSES, loss_high, bias_sum)
    bias_sum = jnp.where(bias_ids == CLASSES + 1, loss - loss_high, bias_sum)

    def back(index, carry):
        lanes = chunk_at(index, LANE)
        scale_row = r.norm[2:3, lanes]
        shift_row = r.norm[3:4, lanes]
        mean_row = r.norm[0:1, lanes]
        total = jnp.zeros((TILE, LANE), F32)
        weighted = jnp.zeros((TILE, LANE), F32)
        for tile in range(tiles):
            at = tile_rows(tile)
            hidden = r.h[at, lanes]
            pre = hidden * scale_row + shift_row
            gate = sigmoid(pre)
            slope = as_tile(gate * (1.0 + pre * (1.0 - gate)))
            grad = slope * r.f[tile_images(tile), lanes][None]
            total = total + jnp.sum(grad, axis=0)
            weighted = weighted + jnp.sum(grad * as_tile(hidden), axis=0)
            flat = grad.reshape(ROWS, LANE)
            r.dz[at, lanes] = flat.astype(BF16)
            r.q[at, lanes] = (flat * scale_row).astype(BF16)
        r.stat[0:1, lanes] = column_sum(total)
        r.stat[1:2, lanes] = column_sum(weighted) - mean_row * column_sum(total)
        return carry

    lax.fori_loop(0, HEAD // LANE, back, 0)
    r.send(r.dz)
    below = dot(r.q[...], r.w[...])
    r.wait(r.normed)
    rows = fold(
        [
            r.stat[0:1, :], r.stat[1:2, :] * inverse,
            column_sum(below), column_sum(below * r.normed[...]), bias_sum,
        ],
        32,
    )
    write_alike(r.pay, jnp.concatenate([rows, cross], axis=0))
    r.send(r.pay)
    fc_copy.wait()
    r.finish()


def head(xb, head_full, bias, label_col, label_row, partner, mix_pair, normed, recv, image_count):
    count = xb.shape[0]
    images = count // MAP
    devices = recv.shape[0]
    return call(
        functools.partial(head_kernel, image_count),
        dict(
            recv=(recv, LOOSE),
            xb=(xb, FAR),
            bias=(bias, NEAR),
            label_col=(label_col, NEAR),
            label_row=(label_row, NEAR),
            partner=(partner, NEAR),
            mix=(mix_pair, NEAR),
            w=(head_full, (slice(0, HEAD), slice(0, WIDTH))),
            classifier=(head_full, (slice(0, HEAD), slice(WIDTH, HEADPAD))),
            normed=(normed, FAR),
        ),
        dict(
            dz=(shape((count, HEAD), BF16), FAR),
            pay=(shape((devices, 48, LANE), BF16), FAR),
            norm=(shape((8, HEAD)), FAR),
            grad_head=(shape((HEAD, HEADPAD), BF16), RAW),
        ),
        dict(
            h=vmem((count, HEAD), F32),
            grad_fc=vmem((HEAD, LOGITS), BF16),
            f=vmem((images, HEAD), F32),
            q=vmem((count, HEAD), BF16),
            stat=vmem((8, HEAD), F32),
        ),
    )


def product_back(is_head, row_count, sums, columns, r):
    groups = columns // LANE
    sum_bias = spread(sums, 0, groups)
    sum_gain = spread(sums, groups, groups)
    r.glob[0:1, :] = sum_gain
    r.glob[1:2, :] = sum_bias
    r.glob[2:8, :] = jnp.zeros((6, columns), F32)
    r.send(r.glob)
    r.wait(r.unorm, r.xb, r.w)
    mean = r.unorm[0:1, :]
    scale = r.unorm[2:3, :]
    slant = scale * r.unorm[1:2, :] * (sum_gain / row_count)
    r.coef[0:1, :columns] = slant
    r.coef[1:2, :columns] = mean * slant - scale * (sum_bias / row_count)
    r.xt[...] = r.xb[...].T
    count = r.xb.shape[0]

    def step(index, carry):
        at = chunk_at(index)
        r.chunk(r.dz, index, at).wait()
        if is_head:
            r.h[...] = dot_nt(r.xb[...], r.w[at, :])
        else:
            r.h[...] = dot(r.xb[...], r.w[:, at])
        grad = r.dz[:, at].astype(F32) * r.unorm[2:3, at] - r.h[...] * r.coef[0:1, at] + r.coef[1:2, at]
        low = grad.astype(BF16)
        r.dh[0:count, at] = low
        if is_head:
            r.grad_w[at, :] = dot_tn(low, r.xb[...]).astype(r.grad_w.dtype)
        else:
            r.grad_w[:, at] = dot(r.xt[...], low).astype(r.grad_w.dtype)
        return carry

    lax.fori_loop(0, columns // CHUNK, step, 0, unroll=True)
    return scale * sum_bias, slant


def owner_blocks(r, owners, row_of_owner, taps):
    rows_dev = 2 * WIDTH // owners
    width = EXPAND // owners
    vec_width = VECS // owners
    chunks = EXPAND // CHUNK
    squeeze_sums = jnp.concatenate([r.squeeze_sum[...], jnp.zeros((1, VECS - LANE), F32)], axis=1)
    for owner in range(owners):
        at = slice(owner * width, (owner + 1) * width)
        squeeze_row = squeeze_sums[:, owner * vec_width : (owner + 1) * vec_width]
        squeeze_row = jnp.concatenate([squeeze_row, jnp.zeros((1, width - vec_width), F32)], axis=1)
        pieces = [r.excite_sum[:, at], squeeze_row]
        pieces.append(taps[0:9, at] if taps is not None else jnp.zeros((9, width), F32))
        pieces.append(jnp.zeros((5, width), F32))
        first_row = chunks * rows_dev
        r.grads[owner, first_row : first_row + 2 * SQUEEZE, 0:width] = r.rx[:, at].astype(BF16)
        last_row = first_row + 2 * SQUEEZE
        r.grads[owner, last_row : last_row + 16, 0:width] = jnp.concatenate(pieces, axis=0).astype(BF16)


def gate_kernel(is_head, row_count, owners, r):
    columns = HEAD if is_head else EXPAND
    groups = columns // LANE
    count = r.xb.shape[0]
    tiles = count // ROWS
    rows_dev = 2 * WIDTH // owners
    r.start()
    r.wait(r.recv)
    sums = read_sums(r.recv)
    bias_pull, slant = product_back(is_head, row_count, sums, columns, r)
    if is_head:
        head_copy = pltpu.make_async_copy(r.grad_w, r.grad_head.at[:, pl.ds(0, WIDTH)], r.own_sem.at[0])
        head_copy.start()
        weights = r.w[...].astype(F32)
        column = lax.broadcasted_iota(jnp.int32, (1, WIDTH), 1)
        high, low = halves(jnp.broadcast_to(bias_pull, (TILE, columns)))
        pull = column_sum(dot(high, r.w[...]) + dot(low, r.w[...])) / TILE
        turned = jnp.broadcast_to(slant, (LANE, columns)).T
        slanted = (weights * jnp.concatenate([turned, turned], axis=1)).astype(BF16)
        square = dot_tn(slanted, r.w[...])
        stream = dot(r.dh[0:count, :columns], r.w[...])
        cross = read_matrix(r.recv, 32)
    else:
        r.dh[count : count + WIDTH, :] = (r.w[...].astype(F32) * slant).astype(BF16)
        high, low = halves(bias_pull)
        r.dh[count + WIDTH :, :] = jnp.concatenate(
            [high.astype(F32), low.astype(F32), jnp.zeros((14, columns), F32)], axis=0
        ).astype(BF16)
        product = dot_nt(r.dh[...], r.w[...])
        square = product[count : count + WIDTH]
        pull = column_sum(product[count + WIDTH : count + WIDTH + 2])
        r.wait(r.cross, r.stream_in)
        stream = r.stream_in[...] + product[0:count]
        cross = r.cross[...]
    r.stream[...] = stream
    r.send(r.stream)
    sum_bias = spread(sums, 2 * groups, WIDTH // LANE) - pull
    corrected = column_sum(cross.T * square)
    sum_gain = spread(sums, 2 * groups + WIDTH // LANE, WIDTH // LANE) - corrected
    r.glob3[0:1, :] = sum_gain
    r.glob3[1:2, :] = sum_bias
    if is_head:
        first_row = 2 * groups + 2 * WIDTH // LANE
        r.glob3[2:6, :] = jnp.concatenate(
            [spread(sums, first_row + PARTS * k, PARTS) for k in range(LOGITS // WIDTH)], axis=0
        )
    else:
        r.glob3[2:6, :] = jnp.zeros((4, WIDTH), F32)
    r.glob3[6:8, :] = jnp.zeros((2, WIDTH), F32)
    r.send(r.glob3)
    r.wait(r.norm3, r.normed)
    grad_p = r.norm3[2:3, :] * (
        stream - sum_bias / row_count - r.normed[...] * (sum_gain / row_count)
    )
    r.gp[...] = grad_p.astype(BF16)
    r.gt[...] = r.gp[...].T
    r.wait(r.wp, r.norm2, r.excite)
    half = owners // 2

    def first(index, carry):
        at_chunk = chunk_at(index)
        r.chunk(r.d, index, at_chunk).wait()
        r.h[...] = dot(r.gp[...], r.wp[:, at_chunk])
        for part in range(PARTS):
            lanes = chunk_at(index * PARTS + part, LANE)
            scale_row = r.norm2[2:3, lanes]
            shift_row = r.norm2[3:4, lanes]
            for tile in range(tiles):
                at = tile_rows(tile)
                near = tile_images(tile)
                pre = r.d[at, lanes].astype(F32) * scale_row + shift_row
                gate = sigmoid(pre)
                active = pre * gate
                slope = gate + active - active * gate
                grad = r.h[at, part * LANE : (part + 1) * LANE]
                factor = r.excite[near, lanes]
                r.ge[near, lanes] = jnp.sum(as_tile(grad * active), axis=0)
                r.y[at, lanes] = (as_tile(active) * factor[None]).reshape(ROWS, LANE).astype(BF16)
                r.slope[at, lanes] = slope.astype(r.slope.dtype)
                r.u[at, lanes] = (
                    (as_tile(grad * slope) * factor[None]).reshape(ROWS, LANE).astype(r.u.dtype)
                )
        grad_p_chunk = dot(r.gt[...], r.y[:, at_chunk])
        place = pl.ds(pl.multiple_of(index * rows_dev, rows_dev), rows_dev)
        for owner in range(half):
            cut = slice(owner * rows_dev, (owner + 1) * rows_dev)
            r.grads[half + owner, place, :] = grad_p_chunk[cut, :].astype(BF16)
            if is_head:
                r.grads[owner, place, :] = jnp.zeros((rows_dev, CHUNK), BF16)
            else:
                r.grads[owner, place, :] = r.grad_w[cut, at_chunk]
        return carry

    lax.fori_loop(0, EXPAND // CHUNK, first, 0)
    r.wait(r.pooled, r.squeeze, r.side)
    excite = r.excite[...]
    grad_gate = r.ge[...] * excite * (1.0 - excite)
    before = r.squeeze[...]
    opened = sigmoid(before)
    squeezed = before * opened
    reduce_mat = r.side[0:SQUEEZE, :]
    excite_mat = r.side[SQUEEZE:, :]
    gate_high, gate_low = halves(grad_gate)
    grad_squeezed = folded(dot_nt(jnp.concatenate([gate_high, gate_low], axis=0), excite_mat))
    grad_pre = grad_squeezed * (opened * (1.0 + before * (1.0 - opened)))
    r.pool[...] = folded(dot(stacked(grad_pre), reduce_mat)) / MAP

    squeezed_high, squeezed_low = halves(squeezed)
    pre_high, pre_low = halves(grad_pre)
    pooled_high, pooled_low = halves(r.pooled[...])
    r.rx[SQUEEZE:, :] = dot_tn(
        jnp.concatenate([squeezed_high, squeezed_low, squeezed_high], axis=0),
        jnp.concatenate([gate_high, gate_high, gate_low], axis=0),
    )
    r.rx[0:SQUEEZE, :] = dot_tn(
        jnp.concatenate([pre_high, pre_low, pre_high], axis=0),
        jnp.concatenate([pooled_high, pooled_high, pooled_low], axis=0),
    )
    r.excite_sum[...] = column_sum(grad_gate)
    r.squeeze_sum[...] = jnp.concatenate(
        [column_sum(grad_pre), jnp.zeros((1, LANE - SQUEEZE), F32)], axis=1
    )
    taps = None
    if not is_head:
        r.wait(r.taps)
        taps = r.taps[...]
    owner_blocks(r, owners, half, taps)
    room = r.grads.shape[1]
    place = pl.ds((r.blocks.shape[1] - room) * (not is_head), room)
    blocks_copy = pltpu.make_async_copy(r.grads, r.blocks.at[:, place, :], r.own_sem.at[1])
    blocks_copy.start()

    def second(index, carry):
        for part in range(PARTS):
            lanes = chunk_at(index * PARTS + part, LANE)
            mean_row = r.norm2[0:1, lanes]
            total = jnp.zeros((TILE, LANE), F32)
            weighted = jnp.zeros((TILE, LANE), F32)
            for tile in range(tiles):
                at = tile_rows(tile)
                pool = r.pool[tile_images(tile), lanes]
                grad = as_tile(r.u[at, lanes].astype(F32)) + as_tile(r.slope[at, lanes].astype(F32)) * pool[None]
                total = total + jnp.sum(grad, axis=0)
                weighted = weighted + jnp.sum(grad * as_tile(r.d[at, lanes].astype(F32)), axis=0)
                r.dz2[at, lanes] = grad.reshape(ROWS, LANE).astype(BF16)
            r.stat[0:1, lanes] = column_sum(total)
            r.stat[1:2, lanes] = column_sum(weighted) - mean_row * column_sum(total)
        r.part(r.dz2, index, chunk_at(index)).start()
        return carry

    lax.fori_loop(0, EXPAND // CHUNK, second, 0)
    write_alike(r.pay, fold([r.stat[0:1, :], r.stat[1:2, :] * r.norm2[1:2, :]], 24))
    r.send(r.pay)
    blocks_copy.wait()
    if is_head:
        head_copy.wait()
    r.finish(r.dz2)


def gate_back(is_head, row_count, owners, recv, upper, cross, stream, lower, blocks, extra_room):
    count = upper.xb.shape[0]
    images = count // MAP
    devices = recv.shape[0]
    columns = HEAD if is_head else EXPAND
    block = EXPAND // CHUNK * (2 * WIDTH // owners) + 2 * SQUEEZE + 16
    where = (slice(0, HEAD), slice(0, WIDTH)) if is_head else (slice(0, WIDTH), slice(None))
    ins = dict(
        recv=(recv, LOOSE),
        unorm=(upper.norm, FAR),
        xb=(upper.xb, FAR),
        w=(upper.weights, where),
        dz=(upper.dz, CHUNKS),
        norm3=(lower.norm3, FAR),
        normed=(lower.normed, FAR),
        norm2=(lower.norm2, FAR),
        wp=(lower.mats, (slice(WIDTH, 2 * WIDTH), slice(None))),
        d=(lower.d, CHUNKS),
        excite=(lower.excite, FAR),
        pooled=(lower.pooled, FAR),
        squeeze=(lower.squeeze, FAR),
        side=(lower.side, (slice(0, 2 * SQUEEZE), slice(None))),
    )
    outs = dict(
        dz2=(shape((count, EXPAND), BF16), FAR),
        pay=(shape((devices, 24, LANE), BF16), FAR),
        stream=(shape((count, WIDTH)), FAR),
        blocks=(shape((owners, block * (1 + extra_room), CHUNK), BF16), RAW),
        glob=(shape((8, columns)), FAR),
        glob3=(shape((8, WIDTH)), FAR),
    )
    scratch = dict(
        grads=vmem((owners, block, CHUNK), BF16),
        xt=vmem((WIDTH, count), BF16),
        h=vmem((count, CHUNK), F32),
        coef=vmem((8, EXPAND), F32),
        dh=vmem((count + WIDTH + 16, columns), BF16),
        u=vmem((count, EXPAND), BF16),
        slope=vmem((count, EXPAND), BF16),
        y=vmem((count, EXPAND), BF16),
        gp=vmem((count, WIDTH), BF16),
        gt=vmem((WIDTH, count), BF16),
        ge=vmem((images, EXPAND), F32),
        pool=vmem((images, EXPAND), F32),
        rx=vmem((2 * SQUEEZE, EXPAND), F32),
        excite_sum=vmem((1, EXPAND), F32),
        squeeze_sum=vmem((1, LANE), F32),
        stat=vmem((8, EXPAND), F32),
        own_sem=pltpu.SemaphoreType.DMA((2,)),
    )
    alias = []
    if is_head:
        ins["grad_head_in"] = (upper.grad_head, RAW)
        outs["grad_head"] = (shape((HEAD, HEADPAD), BF16), RAW)
        scratch["grad_w"] = vmem((HEAD, WIDTH), BF16)
        alias.append(("grad_head_in", "grad_head"))
    else:
        ins["cross"] = (cross, FAR)
        ins["stream_in"] = (stream, FAR)
        ins["taps"] = (upper.taps, FAR)
        scratch["grad_w"] = vmem((WIDTH, EXPAND), BF16)
        if blocks is not None:
            ins["blocks_in"] = (blocks, RAW)
            outs["blocks"] = (shape(blocks.shape, BF16), RAW)
            alias.append(("blocks_in", "blocks"))
    return call(functools.partial(gate_kernel, is_head, row_count, owners), ins, outs, scratch, alias)


def tap_kernel(is_first, row_count, r):
    count = r.dz2.shape[0]
    groups = EXPAND // LANE
    r.start()
    r.wait(r.recv)
    sums = read_sums(r.recv)
    sum_bias = spread(sums, 0, groups)
    sum_gain = spread(sums, groups, groups)
    r.glob[0:1, :] = sum_gain
    r.glob[1:2, :] = sum_bias
    r.glob[2:8, :] = jnp.zeros((6, EXPAND), F32)
    r.send(r.glob)
    r.wait(r.side, r.norm2)
    scale2 = r.norm2[2:3, :]
    slant2 = scale2 * r.norm2[1:2, :] * (sum_gain / row_count)
    r.coef[0:9, :] = r.side[...].astype(F32)[0:9, :]
    r.coef[9:10, :] = slant2
    r.coef[10:11, :] = r.norm2[0:1, :] * slant2 - scale2 * (sum_bias / row_count)
    r.wait(r.norm1, r.xb, r.w)

    def step(index, carry):
        at_chunk = chunk_at(index)
        r.chunk(r.dz2, index, at_chunk).wait()
        r.chunk(r.d, index, at_chunk).wait()
        r.h[...] = dot(r.xb[...], r.w[:, at_chunk])
        for part in range(PARTS):
            lanes = chunk_at(index * PARTS + part, LANE)
            near = slice(part * LANE, (part + 1) * LANE)
            taps = [jnp.broadcast_to(r.coef[k : k + 1, lanes], (TILE, LANE)) for k in range(9)]

            def tile_step(tile, sums_in):
                at = chunk_at(tile, ROWS)
                grad_d = as_tile(
                    r.dz2[at, lanes].astype(F32) * r.norm2[2:3, lanes]
                    - r.d[at, lanes].astype(F32) * r.coef[9:10, lanes]
                    + r.coef[10:11, lanes]
                )
                hidden = r.h[at, near]
                pre = hidden * r.norm1[2:3, lanes] + r.norm1[3:4, lanes]
                gate = sigmoid(pre)
                flat = pre * gate
                active = as_tile(flat)
                slope = as_tile(gate + flat - flat * gate)
                hidden = as_tile(hidden)
                grad_a = [None] * MAP
                tap_sums = [None] * 9
                for target, tap, source in TERMS:
                    term = grad_d[target] * taps[tap]
                    grad_a[source] = term if grad_a[source] is None else grad_a[source] + term
                    term = grad_d[target] * active[source]
                    tap_sums[tap] = term if tap_sums[tap] is None else tap_sums[tap] + term
                total, weighted = sums_in[9], sums_in[10]
                grads = []
                for place in range(MAP):
                    grad = grad_a[place] * slope[place]
                    total = total + grad
                    weighted = weighted + grad * hidden[place]
                    grads.append(grad)
                grad = jnp.concatenate(grads, axis=0)
                r.dz[at, lanes] = grad.astype(BF16)
                if not is_first:
                    r.q[at, lanes] = (grad * r.norm1[2:3, lanes]).astype(BF16)
                return (*[sums_in[k] + tap_sums[k] for k in range(9)], total, weighted)

            zero = jnp.zeros((TILE, LANE), F32)
            result = lax.fori_loop(0, count // ROWS, tile_step, (zero,) * 11, unroll=True)
            for k in range(9):
                r.taps[k : k + 1, lanes] = column_sum(result[k])
            total = column_sum(result[9])
            r.stat[0:1, lanes] = total
            r.stat[1:2, lanes] = column_sum(result[10]) - r.norm1[0:1, lanes] * total
        r.part(r.dz, index, at_chunk).start()
        return carry

    lax.fori_loop(0, EXPAND // CHUNK, step, 0)
    r.taps[9:16, :] = jnp.zeros((7, EXPAND), F32)
    r.send(r.taps)
    vectors = [r.stat[0:1, :], r.stat[1:2, :] * r.norm1[1:2, :]]
    if not is_first:
        r.wait(r.normed, r.stream)
        below = r.stream[...] + dot_nt(r.q[...], r.w[...])
        vectors.append(column_sum(below))
        vectors.append(column_sum(below * r.normed[...]))
    write_alike(r.pay, fold(vectors, r.pay.shape[1]))
    r.send(r.pay)
    r.finish(r.dz)


def tap_back(is_first, row_count, recv, dz2, layer, stream, below):
    count = dz2.shape[0]
    devices = recv.shape[0]
    ins = dict(
        recv=(recv, LOOSE),
        side=(layer.side, (slice(2 * SQUEEZE, SIDE_PAD), slice(None))),
        norm2=(layer.norm2, FAR),
        norm1=(layer.norm1, FAR),
        xb=(layer.xb, FAR),
        w=(layer.mats, (slice(0, WIDTH), slice(None))),
        dz2=(dz2, CHUNKS),
        d=(layer.d, CHUNKS),
    )
    scratch = dict(
        h=vmem((count, CHUNK), F32),
        coef=vmem((16, EXPAND), F32),
        stat=vmem((8, EXPAND), F32),
    )
    if not is_first:
        ins["stream"] = (stream, FAR)
        ins["normed"] = (below.normed, FAR)
        scratch["q"] = vmem((count, EXPAND), BF16)
    return call(
        functools.partial(tap_kernel, is_first, row_count),
        ins,
        dict(
            dz=(shape((count, EXPAND), BF16), FAR),
            pay=(shape((devices, 24 if is_first else 32, LANE), BF16), FAR),
            taps=(shape((16, EXPAND)), FAR),
            glob=(shape((8, EXPAND)), FAR),
        ),
        scratch,
    )


def last_kernel(row_count, replicas, owners, r):
    r.start()
    r.wait(r.recv)
    product_back(False, row_count, read_sums(r.recv), EXPAND, r)
    half = owners // 2
    part = slice_rows(replicas * owners)
    rows_dev = 2 * WIDTH // owners
    chunks = EXPAND // CHUNK
    for device in range(replicas * owners):
        replica, owner = device // owners, device % owners
        first_row = rows_dev * (owner % half) + (2 * replica + owner // half) * part
        for k in range(chunks):
            r.shares[device, k * part : (k + 1) * part, :] = r.grad_w[
                first_row : first_row + part, k * CHUNK : (k + 1) * CHUNK
            ]
    if r.shares.shape[1] > chunks * part:
        r.shares[:, chunks * part :, :] = jnp.zeros(
            (replicas * owners, r.shares.shape[1] - chunks * part, CHUNK), F32
        )
    r.grads[...] = r.shares[...].astype(BF16)
    r.send(r.grads)
    r.finish()


def last_back(row_count, replicas, owners, recv, layer, dz):
    count = dz.shape[0]
    devices = recv.shape[0]
    block = -(-EXPAND // CHUNK * slice_rows(devices) // 16) * 16
    return call(
        functools.partial(last_kernel, row_count, replicas, owners),
        dict(
            recv=(recv, LOOSE),
            dz=(dz, CHUNKS),
            unorm=(layer.norm1, FAR),
            xb=(layer.xb, FAR),
            w=(layer.mats, (slice(0, WIDTH), slice(None))),
        ),
        dict(
            grads=(shape((devices, block, CHUNK), BF16), FAR),
            glob=(shape((8, EXPAND)), FAR),
        ),
        dict(
            xt=vmem((WIDTH, count), BF16),
            h=vmem((count, CHUNK), F32),
            coef=vmem((8, EXPAND), F32),
            dh=vmem((count, EXPAND), BF16),
            grad_w=vmem((WIDTH, EXPAND), F32),
            shares=vmem((devices, block, CHUNK), F32),
        ),
    )


def lamb_moments(weight, moment_one, moment_two, gradient, decay_mask, step_float):
    first_new = BETA_ONE * moment_one + (1.0 - BETA_ONE) * gradient
    second_new = BETA_TWO * moment_two + (1.0 - BETA_TWO) * gradient * gradient
    corrected = (
        first_new
        / (1.0 - BETA_ONE**step_float)
        / (jnp.sqrt(second_new / (1.0 - BETA_TWO**step_float)) + EPS_ADAM)
    )
    return (first_new, second_new, corrected + DECAY_RATE * decay_mask * weight)


def group_sums(mats, side, head_shard, row_ids):
    rows = jnp.sum(mats * mats, axis=2)
    is_expand = (row_ids < WIDTH)[None, :]
    side_rows = jnp.sum(side * side, axis=2)
    head_cols = jnp.sum(head_shard * head_shard, axis=0)
    per_layer = jnp.stack(
        [
            jnp.sum(jnp.where(is_expand, rows, 0.0), axis=1),
            jnp.sum(jnp.where(is_expand, 0.0, rows), axis=1),
            jnp.sum(side_rows[:, :9], axis=1),
            jnp.sum(side_rows[:, 9 : 9 + SQUEEZE], axis=1),
            jnp.sum(side_rows[:, 9 + SQUEEZE : 9 + 2 * SQUEEZE], axis=1),
        ],
        axis=1,
    )
    tail = jnp.stack([jnp.sum(head_cols[:WIDTH]), jnp.sum(head_cols[WIDTH : WIDTH + CLASSES])])
    return jnp.concatenate([per_layer.reshape(-1), tail])


def rate_maps(trust_ratio, row_ids):
    groups = trust_ratio[: 5 * LAYERS].reshape(LAYERS, 5)
    mats_rate = RATE_MATRIX * jnp.where(row_ids[None, :] < WIDTH, groups[:, 0:1], groups[:, 1:2])
    side_ids = jnp.arange(SIDE)[None, :]
    side_rate = jnp.where(
        side_ids < 9,
        RATE_MATRIX * groups[:, 2:3],
        jnp.where(
            side_ids < 9 + SQUEEZE,
            RATE_MATRIX * groups[:, 3:4],
            jnp.where(side_ids < 9 + 2 * SQUEEZE, RATE_MATRIX * groups[:, 4:5], RATE_VECTOR),
        ),
    )
    col_ids = jnp.arange(HEADCOLS)
    head_rate = jnp.where(
        col_ids < WIDTH,
        RATE_MATRIX * trust_ratio[5 * LAYERS],
        jnp.where(
            col_ids < WIDTH + CLASSES, RATE_MATRIX * trust_ratio[5 * LAYERS + 1], RATE_VECTOR
        ),
    )
    return (mats_rate, side_rate, head_rate)


def exchange(payload):
    return lax.all_to_all(payload, BOTH, 0, 0)


def before(value, *others):
    return lax.optimization_barrier((value, *others))[0]


def spread_over(array, axis):
    copies = jnp.broadcast_to(array[None], (lax.axis_size(axis), *array.shape))
    return lax.all_to_all(copies, axis, 0, 0)


def replica_sum(array, turned=False):
    count = lax.axis_size(REPLICAS)
    steps = [1 << k for k in range(count.bit_length() - 1)]
    total = array
    for step in reversed(steps) if turned else steps:
        other = lax.ppermute(total, REPLICAS, [(k, k ^ step) for k in range(count)])
        total = (total.astype(F32) + other.astype(F32)).astype(BF16)
    return total.astype(F32)


def body(
    images, partner, mix_pair, labels, step,
    layer_mats, layer_side, layer_vecs, head_mat, fc_bias,
    mats_first, mats_second, side_first, side_second, vecs_first, vecs_second,
    head_first, head_second, bias_first, bias_second,
):
    local_images = images.shape[0]
    owners = lax.axis_size(OWNERS)
    replicas = lax.axis_size(REPLICAS)
    devices = owners * replicas
    image_count = float(local_images * devices)
    count = local_images * MAP
    row_count = float(count * devices)
    mine = lax.axis_index(OWNERS)
    side_width = layer_side.shape[2]
    vec_width = layer_vecs.shape[1]
    rows_dev = layer_mats.shape[1]
    half = owners // 2

    side_low = jnp.concatenate(
        [
            layer_side[:, 9 : 9 + 2 * SQUEEZE],
            layer_side[:, :9],
            layer_side[:, 9 + 2 * SQUEEZE :],
            jnp.pad(layer_vecs, ((0, 0), (0, side_width - vec_width)))[:, None, :],
            jnp.zeros((LAYERS, 1, side_width), F32),
        ],
        axis=1,
    ).astype(BF16)
    side_rows = -(-SIDE_PAD * side_width // EXPAND)
    side_flat = jnp.pad(side_low[0].reshape(-1), (0, side_rows * EXPAND - SIDE_PAD * side_width))
    packed = lax.all_gather(
        jnp.concatenate([layer_mats[0].astype(BF16), side_flat.reshape(side_rows, EXPAND)], axis=0),
        OWNERS, axis=0,
    )
    mats_all = [packed[:, :rows_dev].reshape(2 * WIDTH, EXPAND)] + [
        lax.all_gather(layer_mats[k].astype(BF16), OWNERS, axis=0, tiled=True) for k in range(1, LAYERS)
    ]
    side_room = -(-side_width // CHUNK) * CHUNK
    side_rest = lax.all_gather(
        jnp.pad(side_low[1:], ((0, 0), (0, 0), (0, side_room - side_width))), OWNERS, axis=0
    )
    side_rest = jnp.moveaxis(side_rest[..., :side_width], 0, 2).reshape(LAYERS - 1, SIDE_PAD, EXPAND)
    head_full = lax.all_gather(
        jnp.pad(head_mat, ((0, 0), (0, HEADPAD - HEADCOLS))).astype(BF16), OWNERS, axis=0, tiled=True
    )

    partner_col = partner[:, None]
    layers = []
    crosses = []
    entry = mix(images.reshape(count, WIDTH), partner_col, mix_pair)
    x, xb = entry.x, entry.xb
    pay = first(xb, mats_all[0], devices).pay
    side_flat = before(packed, pay)[:, rows_dev:].reshape(owners, -1)[:, : SIDE_PAD * side_width]
    side_zero = jnp.moveaxis(side_flat.reshape(owners, SIDE_PAD, side_width), 0, 1).reshape(SIDE_PAD, EXPAND)
    side_all = [side_zero, side_rest[0], side_rest[1]]
    for k in range(LAYERS):
        mats, side = mats_all[k], side_all[k]
        one = spatial(xb, mats, side, exchange(pay))
        two = project(one.d, mats, side, exchange(one.pay), getattr(one, "cross", None), owners)
        last = k == LAYERS - 1
        three = residual(
            x, two.p, two.vec, exchange(two.pay), head_full if last else mats_all[k + 1], last
        )
        if k:
            crosses.append(three.cross)
        layers.append(
            types.SimpleNamespace(
                xb=xb, d=one.d, norm1=one.norm, norm2=two.norm,
                pooled=two.pooled, excite=two.excite, squeeze=two.squeeze,
                norm3=three.norm, normed=three.normed, mats=mats, weights=mats, side=side,
            )
        )
        x, xb, pay = three.x, three.xb, three.pay
    top = head(
        xb, head_full, jnp.pad(fc_bias, (0, LOGITS - CLASSES))[None], labels[:, None], labels[None, :],
        partner_col, mix_pair, layers[-1].normed, exchange(pay), image_count,
    )

    def to_owner(blocks):
        return lax.psum_scatter(
            blocks.reshape(-1, blocks.shape[-1]), OWNERS, scatter_dimension=0, tiled=True
        )

    upper = types.SimpleNamespace(
        xb=xb, weights=head_full, dz=top.dz, norm=top.norm, grad_head=top.grad_head
    )
    pay = top.pay
    stream = None
    blocks = None
    waiting = []
    globs_one, globs_two, globs_three = [None] * LAYERS, [None] * LAYERS, [None] * LAYERS
    for k in reversed(range(LAYERS)):
        layer = layers[k]
        is_head = k == LAYERS - 1
        gate = gate_back(
            is_head, row_count, owners, exchange(pay), upper,
            None if is_head else crosses[k], stream, layer, blocks, is_head,
        )
        stream = gate.stream
        globs_three[k] = gate.glob3
        if is_head:
            head_glob, bias_loss = gate.glob, gate.glob3[2:6].reshape(LOGITS)
            shard_head = to_owner(gate.grad_head)
            blocks = gate.blocks
        else:
            globs_one[k + 1] = gate.glob
            if k:
                pair = to_owner(gate.blocks)
                blocks = None
            else:
                shard_zero = to_owner(gate.blocks)
        tap = tap_back(
            k == 0, row_count, exchange(gate.pay), gate.dz2, layer, stream, layers[max(k - 1, 0)]
        )
        globs_two[k] = tap.glob
        pay = tap.pay
        if k == 1:
            pay = before(pay, shard_head)
        upper = types.SimpleNamespace(
            xb=layer.xb, weights=layer.mats, dz=tap.dz, norm=layer.norm1, taps=tap.taps
        )
    pay = before(pay, pair)
    late_taps = jnp.moveaxis(tap.taps[:9].astype(BF16).reshape(9, owners, side_width), 1, 0)
    late_taps = jnp.broadcast_to(late_taps[None], (replicas, *late_taps.shape))
    received = exchange(pay)
    final = last_back(row_count, replicas, owners, received, layers[0], tap.dz)
    globs_one[0] = final.glob
    shard_head = replica_sum(before(shard_head, received))
    pair = replica_sum(before(pair, received), True)
    room = pair.shape[0] // 2
    shards = [replica_sum(shard_zero), pair[room:], pair[:room]]

    part = slice_rows(devices)
    chunks = EXPAND // CHUNK
    late = jnp.sum(exchange(final.grads).astype(F32), axis=0).astype(BF16)
    other = lax.ppermute(late, OWNERS, [(half + k, k) for k in range(half)])
    late_taps = exchange(before(late_taps.reshape(devices, 9, side_width), received))
    late_taps = jnp.sum(late_taps.astype(F32), axis=0)
    late = spread_over(jnp.stack([late, other]), REPLICAS)[:, :, : chunks * part]
    late = jnp.moveaxis(late.reshape(replicas, 2, chunks, part, CHUNK), 2, 3)
    late = late.reshape(rows_dev, EXPAND).astype(F32)

    def mats_of(shard):
        rows = shard[: chunks * rows_dev].reshape(chunks, rows_dev, CHUNK)
        return jnp.moveaxis(rows, 0, 1).reshape(rows_dev, EXPAND)

    from_mats = [late] + [mats_of(shard) for shard in shards]
    owns_expand = mine < half
    grad_mats = jnp.stack(
        [jnp.where(owns_expand, from_mats[k], from_mats[k + 1]) for k in range(LAYERS)]
    )

    def own_columns(vector, width):
        return lax.dynamic_slice_in_dim(vector, mine * width, width, axis=-1)

    first_row = chunks * rows_dev
    last_row = first_row + 2 * SQUEEZE
    vec_ids = mine * vec_width + jnp.arange(vec_width)
    side_list, vec_list = [], []
    for k in range(LAYERS):
        shard = shards[k][:, :side_width]
        taps = late_taps if k == 0 else shards[k - 1][last_row + 2 : last_row + 11, :side_width]
        norms_part = own_columns(
            jnp.concatenate([globs_one[k][0:2], globs_two[k][0:2]], axis=0), side_width
        )
        side_list.append(
            jnp.concatenate([taps, shard[first_row : last_row + 1], norms_part], axis=0)
        )
        outer = globs_three[k]
        outer = own_columns(
            jnp.concatenate([jnp.zeros((SQUEEZE,), F32), outer[0], outer[1]]), vec_width
        )
        vec_list.append(jnp.where(vec_ids < SQUEEZE, shard[last_row + 1, :vec_width], outer))
    grad_side = jnp.stack(side_list)
    grad_vecs = jnp.stack(vec_list)
    head_tail = own_columns(head_glob[0:2], head_mat.shape[0]).T
    grad_head = jnp.concatenate([shard_head[:, : WIDTH + CLASSES], head_tail], axis=1)
    grad_bias = bias_loss[:CLASSES]
    loss_value = (bias_loss[CLASSES] + bias_loss[CLASSES + 1]) / image_count

    step_float = step[0].astype(F32)
    side_decay = (jnp.arange(SIDE) < 9 + 2 * SQUEEZE).astype(F32)[None, :, None]
    head_decay = (jnp.arange(HEADCOLS) < WIDTH + CLASSES).astype(F32)[None, :]
    mats_moment, mats_square, mats_dir = lamb_moments(
        layer_mats, mats_first, mats_second, grad_mats, 1.0, step_float
    )
    side_moment, side_square, side_dir = lamb_moments(
        layer_side, side_first, side_second, grad_side, side_decay, step_float
    )
    vecs_moment, vecs_square, vecs_dir = lamb_moments(
        layer_vecs, vecs_first, vecs_second, grad_vecs, 0.0, step_float
    )
    head_moment, head_square, head_dir = lamb_moments(
        head_mat, head_first, head_second, grad_head, head_decay, step_float
    )
    bias_moment, bias_square, bias_dir = lamb_moments(
        fc_bias, bias_first, bias_second, grad_bias, 0.0, step_float
    )
    row_ids = mine * rows_dev + jnp.arange(rows_dev)
    squares = jnp.stack(
        [
            group_sums(layer_mats, layer_side, head_mat, row_ids),
            group_sums(mats_dir, side_dir, head_dir, row_ids),
        ]
    )
    norms = jnp.sqrt(jnp.sum(spread_over(squares, OWNERS), axis=0))
    mats_rate, side_rate, head_rate = rate_maps(norms[0] / norms[1], row_ids)
    mats_new = layer_mats - mats_rate[:, :, None] * mats_dir
    side_new = layer_side - side_rate[:, :, None] * side_dir
    vecs_new = layer_vecs - RATE_VECTOR * vecs_dir
    head_new = head_mat - head_rate[None, :] * head_dir
    bias_new = fc_bias - RATE_VECTOR * bias_dir
    return (
        loss_value,
        mats_new, mats_moment, mats_square,
        side_new, side_moment, side_square,
        vecs_new, vecs_moment, vecs_square,
        head_new, head_moment, head_square,
        bias_new, bias_moment, bias_square,
        norms,
    )


def solution(mesh):
    rows, columns = P(None, OWNERS, None), P(None, None, OWNERS)
    vecs, heads = P(None, OWNERS), P(OWNERS, None)
    return jax.shard_map(
        body,
        mesh=mesh,
        in_specs=(
            P(BOTH, None, None), P(BOTH), P(BOTH, None), P(BOTH), P(),
            rows, columns, vecs, heads, P(),
            rows, rows, columns, columns, vecs, vecs, heads, heads, P(), P(),
        ),
        out_specs=(
            P(),
            rows, rows, rows,
            columns, columns, columns,
            vecs, vecs, vecs,
            heads, heads, heads,
            P(), P(), P(), P(),
        ),
        check_vma=False,
    )
```

```python
import functools
import types

import jax
import jax.numpy as jnp
from jax import lax
from jax.experimental import pallas as pl
from jax.experimental.pallas import tpu as pltpu
from jax.sharding import PartitionSpec as P

WIDTH = 256
EXPAND = 1536
SQUEEZE = 64
HEAD = 1280
CLASSES = 1000
LOGITS = 1024
EDGE = 4
LAYERS = 3
MAP = 16
SIDE = 142
SIDE_PAD = 144
VECS = 576
HEADCOLS = 1258
HEADPAD = 1280

EPS_BN = 0.001
BETA_ONE = 0.9
BETA_TWO = 0.999
EPS_ADAM = 1e-06
DECAY_RATE = 0.01
RATE_MATRIX = 0.5
RATE_VECTOR = 0.25

REPLICAS, OWNERS = BOTH = ("dp", "fsdp")
F32 = jnp.float32
BF16 = jnp.bfloat16
LANE = 128
TILE = 8
ROWS = MAP * TILE
CHUNK = 256
PARTS = CHUNK // LANE
VMEM_BYTES = 60 * 1024 * 1024

NT = (((1,), (1,)), ((), ()))
TN = (((0,), (0,)), ((), ()))


NEAR, FAR, RAW, CHUNKS, LOOSE = range(5)


class Refs:
    def __init__(self, names, refs, loads, stores):
        for name, ref in zip(names, refs):
            setattr(self, name, ref)
        self.loads = loads
        self.stores = {id(getattr(self, name)): (k, self.far(name)) for k, name in enumerate(stores)}
        self.pending = {}
        self.chunks = {}

    def far(self, name):
        return getattr(self, name + "_far")

    def start(self):
        for index, (name, where) in enumerate(self.loads):
            source = self.far(name) if where is None or where == CHUNKS else self.far(name).at[where]
            near = getattr(self, name)
            if where == CHUNKS:
                self.chunks[id(near)] = (self.far(name), index)
                for turn in range(near.shape[1] // CHUNK):
                    self.chunk(near, turn, pl.ds(turn * CHUNK, CHUNK)).start()
                continue
            copy = pltpu.make_async_copy(source, near, self.load_sem.at[index])
            copy.start()
            self.pending[id(near)] = copy

    def chunk(self, near, turn, at):
        far, index = self.chunks[id(near)]
        semaphore = self.load_sem.at[len(self.loads) + index * (EXPAND // CHUNK) + turn]
        return pltpu.make_async_copy(far.at[:, at], near.at[:, at], semaphore)

    def wait(self, *refs):
        for ref in refs:
            self.pending.pop(id(ref)).wait()

    def send(self, *refs):
        for ref in refs:
            index, far = self.stores[id(ref)]
            copy = pltpu.make_async_copy(ref, far, self.store_sem.at[index])
            copy.start()
            self.pending[id(far)] = copy

    def part(self, ref, index, at):
        far = self.stores[id(ref)][1]
        return pltpu.make_async_copy(ref.at[:, at], far.at[:, at], self.part_sem.at[index])

    def finish(self, ref=None):
        for key in list(self.pending):
            self.pending.pop(key).wait()
        if ref is not None:
            for index in range(ref.shape[1] // CHUNK):
                self.part(ref, index, pl.ds(index * CHUNK, CHUNK)).wait()


def shape(dims, dtype=F32):
    return jax.ShapeDtypeStruct(dims, dtype)


def vmem(dims, dtype=F32):
    return pltpu.VMEM(dims, dtype)


def call(kernel, ins, outs, scratch, alias=()):
    near, far, loose = (
        pl.BlockSpec(memory_space=space) for space in (pltpu.VMEM, pltpu.HBM, pl.ANY)
    )
    names, arrays, in_specs, loads, stores, extra = [], [], [], [], [], {}
    for name, (array, place) in ins.items():
        arrays.append(array)
        in_specs.append(near if place == NEAR else loose if place == LOOSE else far)
        if place == NEAR or place == RAW:
            names.append(name)
            continue
        names.append(name + "_far")
        dims, where = array.shape, None
        if place == CHUNKS:
            where = CHUNKS
        elif place != FAR and place != LOOSE:
            starts = [part.indices(size)[:2] for part, size in zip(place, dims)]
            dims = tuple(stop - start for start, stop in starts)
            where = tuple(pl.ds(start, stop - start) for start, stop in starts)
        loads.append((name, where))
        extra[name] = vmem(dims, array.dtype)
    for name, (struct, place) in outs.items():
        names.append(name + "_far" if place == FAR else name)
        if place == FAR:
            stores.append(name)
            extra[name] = vmem(struct.shape, struct.dtype)
    extra.update(scratch)
    extra.update(
        load_sem=pltpu.SemaphoreType.DMA((max(len(loads), 1) * (1 + EXPAND // CHUNK),)),
        store_sem=pltpu.SemaphoreType.DMA((max(len(stores), 1),)),
        part_sem=pltpu.SemaphoreType.DMA((EXPAND // CHUNK,)),
    )

    def flat(*refs):
        kernel(Refs(names + list(extra), refs, loads, stores))

    results = pl.pallas_call(
        flat,
        out_shape=[struct for struct, _ in outs.values()],
        in_specs=in_specs,
        out_specs=[near if place == NEAR else far for _, place in outs.values()],
        scratch_shapes=list(extra.values()),
        input_output_aliases={list(ins).index(a): list(outs).index(b) for a, b in alias},
        compiler_params=pltpu.CompilerParams(vmem_limit_bytes=VMEM_BYTES),
    )(*arrays)
    return types.SimpleNamespace(**dict(zip(outs, results)))


def dot(left, right):
    return jnp.dot(left, right, preferred_element_type=F32)


def dot_nt(left, right):
    return lax.dot_general(left, right, NT, preferred_element_type=F32)


def dot_tn(left, right):
    return lax.dot_general(left, right, TN, preferred_element_type=F32)


def halves(value):
    high = value.astype(BF16)
    return high, (value - high.astype(F32)).astype(BF16)


def stacked(value):
    return jnp.concatenate(halves(value), axis=0)


def folded(value):
    count = value.shape[0] // 2
    return value[:count] + value[count:]


def sigmoid(value):
    return 0.5 * jnp.tanh(0.5 * value) + 0.5


def chunk_at(index, size=CHUNK):
    return pl.ds(pl.multiple_of(index * size, size), size)


def tile_rows(tile):
    return slice(tile * ROWS, (tile + 1) * ROWS)


def tile_images(tile):
    return slice(tile * TILE, (tile + 1) * TILE)


def as_tile(block):
    return block.reshape(MAP, TILE, LANE)


def spread(rows, first, count):
    return jnp.concatenate([rows[first + k : first + k + 1, :] for k in range(count)], axis=1)


def fold(vectors, rows):
    pieces = [
        vector[:, k * LANE : (k + 1) * LANE]
        for vector in vectors
        for k in range(vector.shape[1] // LANE)
    ]
    if rows > len(pieces):
        pieces.append(jnp.zeros((rows - len(pieces), LANE), F32))
    return jnp.concatenate(pieces, axis=0)


def column_sum(value):
    return jnp.sum(value, axis=0, keepdims=True)


def slice_rows(devices):
    return max(1, WIDTH // devices)


def write_alike(pay_ref, rows):
    pay_ref[...] = jnp.broadcast_to(rows.astype(BF16)[None], pay_ref.shape)


def write_with_slices(pay_ref, rows, matrix):
    devices = pay_ref.shape[0]
    part = slice_rows(devices)
    first = rows.shape[0]
    low = rows.astype(BF16)
    for device in range(devices):
        own = matrix[device * part : (device + 1) * part, :]
        block = jnp.concatenate([own[:, :LANE], own[:, LANE:]], axis=0)
        if 2 * part < 16:
            block = jnp.concatenate([block, jnp.zeros((16 - 2 * part, LANE), F32)], axis=0)
        pay_ref[device, 0:first, :] = low
        pay_ref[device, first : first + 16, :] = block.astype(BF16)


def read_matrix(recv_ref, first):
    devices, rows = recv_ref.shape[:2]
    part = slice_rows(devices)
    if part == TILE:
        values = recv_ref[...].astype(F32)
        left = values[:, first : first + part].reshape(WIDTH, LANE)
        right = values[:, first + part : first + 2 * part].reshape(WIDTH, LANE)
        return jnp.concatenate([left, right], axis=1)
    flat = recv_ref[...].reshape(devices * rows, LANE)
    row = lax.broadcasted_iota(jnp.int32, (WIDTH, devices * rows), 0)
    column = lax.broadcasted_iota(jnp.int32, (WIDTH, devices * rows), 1)
    source = row // part * rows + first + row % part
    left = dot(jnp.where(column == source, 1.0, 0.0).astype(BF16), flat)
    right = dot(jnp.where(column == source + part, 1.0, 0.0).astype(BF16), flat)
    return jnp.concatenate([left, right], axis=1)


def mean_parts(columns):
    return 1 if columns == EXPAND else 2


def moment_rows(columns):
    return -(-(mean_parts(columns) + 1) * columns // LANE // 8) * 8


def centred(total, squares, count):
    return jnp.maximum(squares - total * total / count, 0.0)


def pack_moments(total, squares, count):
    mean = total / count
    high = mean.astype(BF16).astype(F32)
    parts = [high, mean - high][: mean_parts(total.shape[1])]
    return fold(parts + [centred(total, squares, count)], moment_rows(total.shape[1]))


def read_moments(recv_ref, columns, count):
    groups = columns // LANE
    devices = recv_ref.shape[0]
    parts = recv_ref[...].astype(F32)
    given = mean_parts(columns)
    means = parts[:, :groups]
    if given > 1:
        means = means + parts[:, groups : 2 * groups]
    mean = jnp.sum(means, axis=0) / devices
    apart = means - mean[None]
    spread_sum = jnp.sum(parts[:, given * groups : (given + 1) * groups], axis=0) / count
    variance = (spread_sum + jnp.sum(apart * apart, axis=0)) / devices
    return spread(mean, 0, groups), lax.rsqrt(spread(variance, 0, groups) + EPS_BN)


def product_means(recv_ref, weights, transposed, count):
    devices, rows = recv_ref.shape[:2]
    values = recv_ref[...]
    flat = values.reshape(devices * rows, LANE)
    row = lax.broadcasted_iota(jnp.int32, (devices, devices * rows), 0)
    column = lax.broadcasted_iota(jnp.int32, (devices, devices * rows), 1) - row * rows
    left = dot(jnp.where((column == 0) | (column == 2), 1.0, 0.0).astype(BF16), flat)
    right = dot(jnp.where((column == 1) | (column == 3), 1.0, 0.0).astype(BF16), flat)
    sums = stacked(jnp.concatenate([left, right], axis=1) / count)
    return folded(dot_nt(sums, weights) if transposed else dot(sums, weights))


def read_square_moments(recv_ref, square_ref, w_ref, left_ref, stat_ref, count):
    devices = recv_ref.shape[0]
    means = product_means(recv_ref, w_ref[...], False, count)
    mean = column_sum(means) / devices
    apart = means - mean
    left_ref[...] = jnp.concatenate(
        [read_matrix(square_ref, 0), read_matrix(square_ref, 16)], axis=0
    ).astype(BF16)

    def step(index, carry):
        at = chunk_at(index)
        weights = w_ref[:, at]
        squares = column_sum(folded(dot(left_ref[...], weights)) * weights.astype(F32))
        stat_ref[0:1, at] = jnp.maximum(squares, 0.0)
        return carry

    lax.fori_loop(0, w_ref.shape[1] // CHUNK, step, 0, unroll=True)
    variance = (stat_ref[0:1, :] / count + column_sum(apart * apart)) / devices
    return mean, lax.rsqrt(variance + EPS_BN)


def read_product_moments(recv_ref, weights, transposed, columns, count):
    devices = recv_ref.shape[0]
    values = recv_ref[...]
    means = product_means(recv_ref, weights, transposed, count)
    mean = column_sum(means) / devices
    apart = means - mean
    squares = jnp.sum(values.astype(F32), axis=0)
    variance = (spread(squares, 4, columns // LANE) / count + column_sum(apart * apart)) / devices
    return mean, lax.rsqrt(variance + EPS_BN)


def read_sums(recv_ref):
    return jnp.sum(recv_ref[...].astype(F32), axis=0)


def keep_norm(norm_ref, mean, inverse, gain, bias):
    scale = inverse * gain
    norm_ref[0:1, :] = mean
    norm_ref[1:2, :] = inverse
    norm_ref[2:3, :] = scale
    norm_ref[3:4, :] = bias - mean * scale
    norm_ref[4:8, :] = jnp.zeros((4, norm_ref.shape[1]), F32)


def product_moments(x_ref, w_ref, transposed, columns, left_ref, stat_ref, beside):
    count = x_ref.shape[0]
    values = x_ref[...]
    product = dot_tn(jnp.concatenate([values, beside], axis=1), values)
    square, cross = product[:WIDTH], product[WIDTH:]
    sums = column_sum(values.astype(F32))
    left_ref[0 : 2 * WIDTH, :] = stacked(square)
    tail = jnp.concatenate([half.astype(F32) for half in halves(sums)] + [jnp.zeros((14, WIDTH), F32)], axis=0)
    left_ref[2 * WIDTH :, :] = tail.astype(BF16)

    def step(index, carry):
        at = chunk_at(index)
        weights = w_ref[at, :].T if transposed else w_ref[:, at]
        product = dot(left_ref[...], weights)
        total = column_sum(product[2 * WIDTH : 2 * WIDTH + 2])
        squares = column_sum(folded(product[: 2 * WIDTH]) * weights.astype(F32))
        stat_ref[0:1, at] = jnp.maximum(squares - total * total / count, 0.0)
        return carry

    lax.fori_loop(0, columns // CHUNK, step, 0, unroll=True)
    high = sums.astype(BF16).astype(F32)
    return fold([high, sums - high, stat_ref[0:1, :]], 16), cross


def mix_kernel(r):
    count = r.images.shape[0]
    pixels = r.images[...]
    row = lax.broadcasted_iota(jnp.int32, (ROWS, count), 0)
    column = lax.broadcasted_iota(jnp.int32, (ROWS, count), 1)
    place = lax.shift_right_logical(row, 3)
    inside = jnp.bitwise_and(row, 7)
    pair = r.mix[...].astype(F32)
    mixing = pair[:, 0:1] / (pair[:, 0:1] + pair[:, 1:2])
    for tile in range(count // ROWS):
        near = tile_images(tile)
        other = jnp.concatenate([r.partner[near, :]] * MAP, axis=0)
        weight = jnp.concatenate([mixing[near, :]] * MAP, axis=0)
        own_hot = jnp.where(column == (tile * TILE + inside) * MAP + place, 1.0, 0.0).astype(BF16)
        other_hot = jnp.where(column == other * MAP + place, 1.0, 0.0).astype(BF16)
        mixed = weight * dot(own_hot, pixels) + (1.0 - weight) * dot(other_hot, pixels)
        r.x[tile_rows(tile), :] = mixed
    r.xb[...] = r.x[...].astype(BF16)
    r.send(r.x, r.xb)
    low = r.xb[...]
    sums = column_sum(low.astype(F32))
    padded = jnp.concatenate([sums, jnp.zeros((TILE - 1, WIDTH), F32)], axis=0)
    outer = lax.dot_general(
        padded, padded, TN, preferred_element_type=F32, precision=lax.Precision.HIGHEST
    )
    square = dot_tn(low, low) - outer / count
    high = sums.astype(BF16).astype(F32)
    rows = fold([high, sums - high], 8)
    devices = r.pay.shape[0]
    part = slice_rows(devices)
    for device in range(devices):
        own = square[device * part : (device + 1) * part, :]
        block = [rows, own[:, :LANE], own[:, LANE:]]
        if 2 * part < 16:
            block.append(jnp.zeros((16 - 2 * part, LANE), F32))
        r.pay[device, :, :] = jnp.concatenate(block, axis=0).astype(BF16)
    r.send(r.pay)
    r.finish()


def mix(images, partner, mix_pair, devices):
    dims = images.shape
    return call(
        mix_kernel,
        dict(images=(images, NEAR), partner=(partner, NEAR), mix=(mix_pair, NEAR)),
        dict(
            x=(shape(dims), FAR),
            xb=(shape(dims, BF16), FAR),
            pay=(shape((devices, 24, LANE), BF16), FAR),
        ),
        {},
    )


def share_kernel(r):
    r.start()
    r.wait(r.recv)
    high, low = halves(jnp.sum(r.recv[...].astype(F32), axis=0)[8:24])
    write_alike(r.pay, jnp.concatenate([high.astype(F32), low.astype(F32)], axis=0))
    r.send(r.pay)
    r.finish()


def share(recv):
    return call(
        share_kernel,
        dict(recv=(recv, LOOSE)),
        dict(pay=(shape((recv.shape[0], 32, LANE), BF16), FAR)),
        {},
    )


def tap_terms():
    for row in range(EDGE):
        for col in range(EDGE):
            for row_shift in range(3):
                for col_shift in range(3):
                    from_row, from_col = row + row_shift - 1, col + col_shift - 1
                    if 0 <= from_row < EDGE and 0 <= from_col < EDGE:
                        yield EDGE * row + col, 3 * row_shift + col_shift, EDGE * from_row + from_col


TERMS = list(tap_terms())


def spatial_kernel(from_square, r):
    count = r.xb.shape[0]
    r.start()
    r.wait(r.recv, r.side, r.w, r.xb)
    rows = r.side[...].astype(F32)
    r.taps[0:9, :] = rows[0:9, :]
    if from_square:
        r.wait(r.square)
        mean, inverse = read_square_moments(r.recv, r.square, r.w, r.left, r.stat, count)
    else:
        mean, inverse = read_product_moments(r.recv, r.w[...], False, EXPAND, count)
    keep_norm(r.norm, mean, inverse, rows[10:11, :], rows[11:12, :])
    r.send(r.norm)
    if not from_square:
        r.cross[...] = jnp.sum(r.recv[...].astype(F32)[:, 16:32], axis=0)
        r.send(r.cross)

    def step(index, carry):
        at_chunk = chunk_at(index)
        r.h[...] = dot(r.xb[...], r.w[:, at_chunk])
        for part in range(PARTS):
            lanes = chunk_at(index * PARTS + part, LANE)
            taps = [jnp.broadcast_to(r.taps[k : k + 1, lanes], (TILE, LANE)) for k in range(9)]
            scale_row = r.norm[2:3, lanes]
            shift_row = r.norm[3:4, lanes]

            def tile_step(tile, sums):
                at = chunk_at(tile, ROWS)
                pre = r.h[at, part * LANE : (part + 1) * LANE] * scale_row + shift_row
                active = as_tile(pre * sigmoid(pre))
                result = [None] * MAP
                for target, tap, source in TERMS:
                    term = active[source] * taps[tap]
                    result[target] = term if result[target] is None else result[target] + term
                total, squares = sums
                for value in result:
                    total = total + value
                    squares = squares + value * value
                r.d[at, lanes] = jnp.concatenate(result, axis=0).astype(BF16)
                return total, squares

            zero = jnp.zeros((TILE, LANE), F32)
            total, squares = lax.fori_loop(0, count // ROWS, tile_step, (zero, zero), unroll=True)
            r.stat[0:1, lanes] = column_sum(total)
            r.stat[1:2, lanes] = column_sum(squares)
        r.part(r.d, index, at_chunk).start()
        return carry

    lax.fori_loop(0, EXPAND // CHUNK, step, 0)
    write_alike(r.pay, pack_moments(r.stat[0:1, :], r.stat[1:2, :], count))
    r.send(r.pay)
    r.finish(r.d)


def spatial(xb, mats, side, recv, square):
    count = xb.shape[0]
    devices = recv.shape[0]
    outs = dict(
        d=(shape((count, EXPAND), BF16), FAR),
        pay=(shape((devices, moment_rows(EXPAND), LANE), BF16), FAR),
        norm=(shape((8, EXPAND)), FAR),
    )
    ins = dict(
        recv=(recv, LOOSE),
        side=(side, (slice(2 * SQUEEZE, SIDE_PAD), slice(None))),
        xb=(xb, FAR),
        w=(mats, (slice(0, WIDTH), slice(None))),
    )
    if square is None:
        outs["cross"] = (shape((16, LANE)), FAR)
    else:
        ins["square"] = (square, LOOSE)
    return call(
        functools.partial(spatial_kernel, square is not None),
        ins,
        outs,
        dict(
            left=vmem((2 * WIDTH, WIDTH), BF16),
            h=vmem((count, CHUNK), F32),
            taps=vmem((16, EXPAND), F32),
            stat=vmem((8, EXPAND), F32),
        ),
    )


def project_kernel(with_cross, owners, r):
    count = r.d.shape[0]
    tiles = count // ROWS
    r.start()
    r.wait(r.recv)
    mean, inverse = read_moments(r.recv, EXPAND, count)
    r.wait(r.side)
    rows = r.side[2 * SQUEEZE : SIDE_PAD, :].astype(F32)
    keep_norm(r.norm, mean, inverse, rows[12:13, :], rows[13:14, :])
    r.send(r.norm)
    width, vec_width = EXPAND // owners, VECS // owners
    vec = jnp.concatenate(
        [rows[14:15, k * width : k * width + vec_width] for k in range(owners)], axis=1
    )
    r.vec[...] = jnp.concatenate(
        [vec[:, SQUEEZE : SQUEEZE + WIDTH], vec[:, SQUEEZE + WIDTH :], jnp.zeros((6, WIDTH), F32)], axis=0
    )
    r.send(r.vec)

    def activate(index, carry):
        r.chunk(r.d, index, chunk_at(index)).wait()
        for part in range(PARTS):
            lanes = chunk_at(index * PARTS + part, LANE)
            scale_row = r.norm[2:3, lanes]
            shift_row = r.norm[3:4, lanes]
            for tile in range(tiles):
                at = tile_rows(tile)
                pre = r.d[at, lanes].astype(F32) * scale_row + shift_row
                active = pre * sigmoid(pre)
                r.a[at, lanes] = active
                r.pooled[tile_images(tile), lanes] = jnp.sum(as_tile(active), axis=0) / MAP
        return carry

    lax.fori_loop(0, EXPAND // CHUNK, activate, 0)
    r.send(r.pooled)
    before = folded(dot_nt(stacked(r.pooled[...]), r.side[0:SQUEEZE, :])) + vec[:, :SQUEEZE]
    r.squeeze[...] = before
    r.send(r.squeeze)
    opened = folded(dot(stacked(before * sigmoid(before)), r.side[SQUEEZE : 2 * SQUEEZE, :]))
    r.excite[...] = sigmoid(opened + rows[9:10, :])
    r.send(r.excite)

    def gate(index, carry):
        lanes = chunk_at(index, LANE)
        for tile in range(tiles):
            at = tile_rows(tile)
            scaled = as_tile(r.a[at, lanes]) * r.excite[tile_images(tile), lanes][None]
            r.y[at, lanes] = scaled.reshape(ROWS, LANE).astype(BF16)
        return carry

    lax.fori_loop(0, EXPAND // LANE, gate, 0)
    r.wait(r.w)
    projected = dot_nt(r.y[...], r.w[...])
    r.p[...] = projected
    r.send(r.p)
    moments = pack_moments(column_sum(projected), column_sum(projected * projected), count)
    if with_cross:
        r.wait(r.cross)
        moments = jnp.concatenate([moments, r.cross[...]], axis=0)
    write_alike(r.pay, moments)
    r.send(r.pay)
    r.finish()


def project(d, mats, side, recv, cross, owners):
    count = d.shape[0]
    images = count // MAP
    devices = recv.shape[0]
    ins = dict(
        recv=(recv, LOOSE),
        side=(side, FAR),
        d=(d, CHUNKS),
        w=(mats, (slice(WIDTH, 2 * WIDTH), slice(None))),
    )
    rows = moment_rows(WIDTH)
    if cross is not None:
        ins["cross"] = (cross, FAR)
        rows += 16
    return call(
        functools.partial(project_kernel, cross is not None, owners),
        ins,
        dict(
            p=(shape((count, WIDTH)), FAR),
            vec=(shape((8, WIDTH)), FAR),
            pay=(shape((devices, rows, LANE), BF16), FAR),
            norm=(shape((8, EXPAND)), FAR),
            pooled=(shape((images, EXPAND)), FAR),
            excite=(shape((images, EXPAND)), FAR),
            squeeze=(shape((images, SQUEEZE)), FAR),
        ),
        dict(a=vmem((count, EXPAND), F32), y=vmem((count, EXPAND), BF16)),
    )


def residual_kernel(transposed, with_cross, r):
    count = r.p.shape[0]
    r.start()
    r.wait(r.recv, r.vec)
    mean, inverse = read_moments(r.recv, WIDTH, count)
    keep_norm(r.norm, mean, inverse, r.vec[0:1, :], r.vec[1:2, :])
    if with_cross:
        r.cross[...] = read_matrix(r.recv, moment_rows(WIDTH))
        r.send(r.cross)
    r.wait(r.p)
    normed = (r.p[...] - mean) * inverse
    r.normed[...] = normed
    r.wait(r.before)
    result = r.before[...] + (normed * r.vec[0:1, :] + r.vec[1:2, :])
    r.x[...] = result
    r.xb[...] = result.astype(BF16)
    r.send(r.norm, r.normed, r.x, r.xb)
    r.wait(r.w)
    moments, cross = product_moments(
        r.xb, r.w, transposed, r.stat.shape[1], r.left, r.stat, normed.astype(BF16)
    )
    write_with_slices(r.pay, moments, cross)
    r.send(r.pay)
    r.finish()


def residual(x, p, vec, recv, weights, transposed):
    count = x.shape[0]
    devices = recv.shape[0]
    with_cross = recv.shape[1] > moment_rows(WIDTH)
    columns = HEAD if transposed else EXPAND
    where = (slice(0, HEAD), slice(0, WIDTH)) if transposed else (slice(0, WIDTH), slice(None))
    outs = dict(
        x=(shape((count, WIDTH)), FAR),
        xb=(shape((count, WIDTH), BF16), FAR),
        normed=(shape((count, WIDTH)), FAR),
        pay=(shape((devices, 32, LANE), BF16), FAR),
        norm=(shape((8, WIDTH)), FAR),
    )
    if with_cross:
        outs["cross"] = (shape((WIDTH, WIDTH)), FAR)
    return call(
        functools.partial(residual_kernel, transposed, with_cross),
        dict(
            recv=(recv, LOOSE), vec=(vec, FAR), p=(p, FAR), before=(x, FAR), w=(weights, where)
        ),
        outs,
        dict(left=vmem((2 * WIDTH + 16, WIDTH), BF16), stat=vmem((8, columns))),
    )


def head_rows(last_columns):
    pick_row = lax.broadcasted_iota(jnp.int32, (TILE, LANE), 0)
    pick_col = lax.broadcasted_iota(jnp.int32, (TILE, LANE), 1)
    first_col = WIDTH + CLASSES - (HEADPAD - LANE)
    pick = jnp.where((pick_col == pick_row + first_col) & (pick_row < 2), 1.0, 0.0).astype(BF16)
    return dot_nt(pick, last_columns)


def head_kernel(image_count, r):
    count = r.xb.shape[0]
    tiles = count // ROWS
    images = count // MAP
    r.start()
    r.wait(r.recv, r.xb, r.w)
    mean, inverse = read_product_moments(r.recv, r.w[...], True, HEAD, count)
    cross = jnp.sum(r.recv[...].astype(F32)[:, 16:32], axis=0)
    r.wait(r.classifier)
    gain_bias = head_rows(r.classifier[:, LOGITS - LANE :])
    keep_norm(r.norm, mean, inverse, gain_bias[0:1, :], gain_bias[1:2, :])
    r.send(r.norm)

    def features(index, carry):
        at_chunk = chunk_at(index)
        r.h[:, at_chunk] = dot_nt(r.xb[...], r.w[at_chunk, :])
        for part in range(PARTS):
            lanes = chunk_at(index * PARTS + part, LANE)
            scale_row = r.norm[2:3, lanes]
            shift_row = r.norm[3:4, lanes]
            for tile in range(tiles):
                pre = r.h[tile_rows(tile), lanes] * scale_row + shift_row
                active = as_tile(pre * sigmoid(pre))
                r.f[tile_images(tile), lanes] = jnp.sum(active, axis=0) / MAP
        return carry

    lax.fori_loop(0, HEAD // CHUNK, features, 0, unroll=True)
    features_low = r.f[...].astype(BF16)
    classifier = r.classifier[...]
    ids = lax.broadcasted_iota(jnp.int32, (images, LOGITS), 1)
    logits = dot(features_low, classifier) + r.bias[...]
    logits = jnp.where(ids < CLASSES, logits, -1e30)
    row_max = jnp.max(logits, axis=1, keepdims=True)
    log_total = row_max + jnp.log(jnp.sum(jnp.exp(logits - row_max), axis=1, keepdims=True))
    pair = r.mix[...].astype(F32)
    mixing = pair[:, 0:1] / (pair[:, 0:1] + pair[:, 1:2])
    people = lax.broadcasted_iota(jnp.int32, (images, images), 1)
    label_row = jnp.broadcast_to(r.label_row[...].astype(F32), (images, images))
    partner_label = jnp.sum(
        jnp.where(people == r.partner[...], label_row, 0.0), axis=1, keepdims=True
    ).astype(jnp.int32)
    own_hot = jnp.where(ids == r.label_col[...], 1.0, 0.0)
    other_hot = jnp.where(ids == partner_label, 1.0, 0.0)
    own_logit = jnp.sum(own_hot * logits, axis=1, keepdims=True)
    other_logit = jnp.sum(other_hot * logits, axis=1, keepdims=True)
    loss = column_sum(mixing * (log_total - own_logit) + (1.0 - mixing) * (log_total - other_logit))
    grad_logits = (
        jnp.exp(logits - log_total) - mixing * own_hot - (1.0 - mixing) * other_hot
    ) / image_count
    grad_low = grad_logits.astype(BF16)
    r.grad_fc[...] = dot_tn(features_low, grad_low).astype(BF16)
    fc_copy = pltpu.make_async_copy(r.grad_fc, r.grad_head.at[:, pl.ds(WIDTH, LOGITS)], r.part_sem.at[0])
    fc_copy.start()
    r.f[...] = dot_nt(grad_low, classifier) / MAP
    bias_sum = column_sum(grad_logits)
    bias_ids = lax.broadcasted_iota(jnp.int32, (1, LOGITS), 1)
    loss_high = loss.astype(BF16).astype(F32)
    bias_sum = jnp.where(bias_ids == CLASSES, loss_high, bias_sum)
    bias_sum = jnp.where(bias_ids == CLASSES + 1, loss - loss_high, bias_sum)

    def back(index, carry):
        lanes = chunk_at(index, LANE)
        scale_row = r.norm[2:3, lanes]
        shift_row = r.norm[3:4, lanes]
        mean_row = r.norm[0:1, lanes]
        total = jnp.zeros((TILE, LANE), F32)
        weighted = jnp.zeros((TILE, LANE), F32)
        for tile in range(tiles):
            at = tile_rows(tile)
            hidden = r.h[at, lanes]
            pre = hidden * scale_row + shift_row
            gate = sigmoid(pre)
            slope = as_tile(gate * (1.0 + pre * (1.0 - gate)))
            grad = slope * r.f[tile_images(tile), lanes][None]
            total = total + jnp.sum(grad, axis=0)
            weighted = weighted + jnp.sum(grad * as_tile(hidden), axis=0)
            flat = grad.reshape(ROWS, LANE)
            r.dz[at, lanes] = flat.astype(BF16)
            r.q[at, lanes] = (flat * scale_row).astype(BF16)
        r.stat[0:1, lanes] = column_sum(total)
        r.stat[1:2, lanes] = column_sum(weighted) - mean_row * column_sum(total)
        return carry

    lax.fori_loop(0, HEAD // LANE, back, 0)
    r.send(r.dz)
    below = dot(r.q[...], r.w[...])
    r.wait(r.normed)
    rows = fold(
        [
            r.stat[0:1, :], r.stat[1:2, :] * inverse,
            column_sum(below), column_sum(below * r.normed[...]), bias_sum,
        ],
        32,
    )
    write_alike(r.pay, jnp.concatenate([rows, cross], axis=0))
    r.send(r.pay)
    fc_copy.wait()
    r.finish()


def head(xb, head_full, bias, label_col, label_row, partner, mix_pair, normed, recv, image_count):
    count = xb.shape[0]
    images = count // MAP
    devices = recv.shape[0]
    return call(
        functools.partial(head_kernel, image_count),
        dict(
            recv=(recv, LOOSE),
            xb=(xb, FAR),
            bias=(bias, NEAR),
            label_col=(label_col, NEAR),
            label_row=(label_row, NEAR),
            partner=(partner, NEAR),
            mix=(mix_pair, NEAR),
            w=(head_full, (slice(0, HEAD), slice(0, WIDTH))),
            classifier=(head_full, (slice(0, HEAD), slice(WIDTH, HEADPAD))),
            normed=(normed, FAR),
        ),
        dict(
            dz=(shape((count, HEAD), BF16), FAR),
            pay=(shape((devices, 48, LANE), BF16), FAR),
            norm=(shape((8, HEAD)), FAR),
            grad_head=(shape((HEAD, HEADPAD), BF16), RAW),
        ),
        dict(
            h=vmem((count, HEAD), F32),
            grad_fc=vmem((HEAD, LOGITS), BF16),
            f=vmem((images, HEAD), F32),
            q=vmem((count, HEAD), BF16),
            stat=vmem((8, HEAD), F32),
        ),
    )


def product_back(is_head, row_count, sums, columns, r):
    groups = columns // LANE
    sum_bias = spread(sums, 0, groups)
    sum_gain = spread(sums, groups, groups)
    r.glob[0:1, :] = sum_gain
    r.glob[1:2, :] = sum_bias
    r.glob[2:8, :] = jnp.zeros((6, columns), F32)
    r.send(r.glob)
    r.wait(r.unorm, r.xb, r.w)
    mean = r.unorm[0:1, :]
    scale = r.unorm[2:3, :]
    slant = scale * r.unorm[1:2, :] * (sum_gain / row_count)
    r.coef[0:1, :columns] = slant
    r.coef[1:2, :columns] = mean * slant - scale * (sum_bias / row_count)
    r.xt[...] = r.xb[...].T
    count = r.xb.shape[0]

    def step(index, carry):
        at = chunk_at(index)
        r.chunk(r.dz, index, at).wait()
        if is_head:
            r.h[...] = dot_nt(r.xb[...], r.w[at, :])
        else:
            r.h[...] = dot(r.xb[...], r.w[:, at])
        grad = r.dz[:, at].astype(F32) * r.unorm[2:3, at] - r.h[...] * r.coef[0:1, at] + r.coef[1:2, at]
        low = grad.astype(BF16)
        r.dh[0:count, at] = low
        if is_head:
            r.grad_w[at, :] = dot_tn(low, r.xb[...]).astype(r.grad_w.dtype)
        else:
            r.grad_w[:, at] = dot(r.xt[...], low).astype(r.grad_w.dtype)
        return carry

    lax.fori_loop(0, columns // CHUNK, step, 0, unroll=True)
    return scale * sum_bias, slant


def owner_blocks(r, owners, row_of_owner, taps):
    rows_dev = 2 * WIDTH // owners
    width = EXPAND // owners
    vec_width = VECS // owners
    chunks = EXPAND // CHUNK
    squeeze_sums = jnp.concatenate([r.squeeze_sum[...], jnp.zeros((1, VECS - LANE), F32)], axis=1)
    for owner in range(owners):
        at = slice(owner * width, (owner + 1) * width)
        squeeze_row = squeeze_sums[:, owner * vec_width : (owner + 1) * vec_width]
        squeeze_row = jnp.concatenate([squeeze_row, jnp.zeros((1, width - vec_width), F32)], axis=1)
        pieces = [r.excite_sum[:, at], squeeze_row]
        pieces.append(taps[0:9, at] if taps is not None else jnp.zeros((9, width), F32))
        pieces.append(jnp.zeros((5, width), F32))
        first_row = chunks * rows_dev
        r.grads[owner, first_row : first_row + 2 * SQUEEZE, 0:width] = r.rx[:, at].astype(BF16)
        last_row = first_row + 2 * SQUEEZE
        r.grads[owner, last_row : last_row + 16, 0:width] = jnp.concatenate(pieces, axis=0).astype(BF16)


def gate_kernel(is_head, row_count, owners, r):
    columns = HEAD if is_head else EXPAND
    groups = columns // LANE
    count = r.xb.shape[0]
    tiles = count // ROWS
    rows_dev = 2 * WIDTH // owners
    r.start()
    r.wait(r.recv)
    sums = read_sums(r.recv)
    bias_pull, slant = product_back(is_head, row_count, sums, columns, r)
    if is_head:
        head_copy = pltpu.make_async_copy(r.grad_w, r.grad_head.at[:, pl.ds(0, WIDTH)], r.own_sem.at[0])
        head_copy.start()
        weights = r.w[...].astype(F32)
        column = lax.broadcasted_iota(jnp.int32, (1, WIDTH), 1)
        high, low = halves(jnp.broadcast_to(bias_pull, (TILE, columns)))
        pull = column_sum(dot(high, r.w[...]) + dot(low, r.w[...])) / TILE
        turned = jnp.broadcast_to(slant, (LANE, columns)).T
        slanted = (weights * jnp.concatenate([turned, turned], axis=1)).astype(BF16)
        square = dot_tn(slanted, r.w[...])
        stream = dot(r.dh[0:count, :columns], r.w[...])
        cross = read_matrix(r.recv, 32)
    else:
        r.dh[count : count + WIDTH, :] = (r.w[...].astype(F32) * slant).astype(BF16)
        high, low = halves(bias_pull)
        r.dh[count + WIDTH :, :] = jnp.concatenate(
            [high.astype(F32), low.astype(F32), jnp.zeros((14, columns), F32)], axis=0
        ).astype(BF16)
        product = dot_nt(r.dh[...], r.w[...])
        square = product[count : count + WIDTH]
        pull = column_sum(product[count + WIDTH : count + WIDTH + 2])
        r.wait(r.cross, r.stream_in)
        stream = r.stream_in[...] + product[0:count]
        cross = r.cross[...]
    r.stream[...] = stream
    r.send(r.stream)
    sum_bias = spread(sums, 2 * groups, WIDTH // LANE) - pull
    corrected = column_sum(cross.T * square)
    sum_gain = spread(sums, 2 * groups + WIDTH // LANE, WIDTH // LANE) - corrected
    r.glob3[0:1, :] = sum_gain
    r.glob3[1:2, :] = sum_bias
    if is_head:
        first_row = 2 * groups + 2 * WIDTH // LANE
        r.glob3[2:6, :] = jnp.concatenate(
            [spread(sums, first_row + PARTS * k, PARTS) for k in range(LOGITS // WIDTH)], axis=0
        )
    else:
        r.glob3[2:6, :] = jnp.zeros((4, WIDTH), F32)
    r.glob3[6:8, :] = jnp.zeros((2, WIDTH), F32)
    r.send(r.glob3)
    r.wait(r.norm3, r.normed)
    grad_p = r.norm3[2:3, :] * (
        stream - sum_bias / row_count - r.normed[...] * (sum_gain / row_count)
    )
    r.gp[...] = grad_p.astype(BF16)
    r.gt[...] = r.gp[...].T
    r.wait(r.wp, r.norm2, r.excite)
    half = owners // 2

    def first(index, carry):
        at_chunk = chunk_at(index)
        r.chunk(r.d, index, at_chunk).wait()
        r.h[...] = dot(r.gp[...], r.wp[:, at_chunk])
        for part in range(PARTS):
            lanes = chunk_at(index * PARTS + part, LANE)
            scale_row = r.norm2[2:3, lanes]
            shift_row = r.norm2[3:4, lanes]
            for tile in range(tiles):
                at = tile_rows(tile)
                near = tile_images(tile)
                pre = r.d[at, lanes].astype(F32) * scale_row + shift_row
                gate = sigmoid(pre)
                active = pre * gate
                slope = gate + active - active * gate
                grad = r.h[at, part * LANE : (part + 1) * LANE]
                factor = r.excite[near, lanes]
                r.ge[near, lanes] = jnp.sum(as_tile(grad * active), axis=0)
                r.y[at, lanes] = (as_tile(active) * factor[None]).reshape(ROWS, LANE).astype(BF16)
                r.slope[at, lanes] = slope.astype(r.slope.dtype)
                r.u[at, lanes] = (
                    (as_tile(grad * slope) * factor[None]).reshape(ROWS, LANE).astype(r.u.dtype)
                )
        grad_p_chunk = dot(r.gt[...], r.y[:, at_chunk])
        place = pl.ds(pl.multiple_of(index * rows_dev, rows_dev), rows_dev)
        for owner in range(half):
            cut = slice(owner * rows_dev, (owner + 1) * rows_dev)
            r.grads[half + owner, place, :] = grad_p_chunk[cut, :].astype(BF16)
            if is_head:
                r.grads[owner, place, :] = jnp.zeros((rows_dev, CHUNK), BF16)
            else:
                r.grads[owner, place, :] = r.grad_w[cut, at_chunk]
        return carry

    lax.fori_loop(0, EXPAND // CHUNK, first, 0)
    r.wait(r.pooled, r.squeeze, r.side)
    excite = r.excite[...]
    grad_gate = r.ge[...] * excite * (1.0 - excite)
    before = r.squeeze[...]
    opened = sigmoid(before)
    squeezed = before * opened
    reduce_mat = r.side[0:SQUEEZE, :]
    excite_mat = r.side[SQUEEZE:, :]
    gate_high, gate_low = halves(grad_gate)
    grad_squeezed = folded(dot_nt(jnp.concatenate([gate_high, gate_low], axis=0), excite_mat))
    grad_pre = grad_squeezed * (opened * (1.0 + before * (1.0 - opened)))
    r.pool[...] = folded(dot(stacked(grad_pre), reduce_mat)) / MAP

    squeezed_high, squeezed_low = halves(squeezed)
    pre_high, pre_low = halves(grad_pre)
    pooled_high, pooled_low = halves(r.pooled[...])
    r.rx[SQUEEZE:, :] = dot_tn(
        jnp.concatenate([squeezed_high, squeezed_low, squeezed_high], axis=0),
        jnp.concatenate([gate_high, gate_high, gate_low], axis=0),
    )
    r.rx[0:SQUEEZE, :] = dot_tn(
        jnp.concatenate([pre_high, pre_low, pre_high], axis=0),
        jnp.concatenate([pooled_high, pooled_high, pooled_low], axis=0),
    )
    r.excite_sum[...] = column_sum(grad_gate)
    r.squeeze_sum[...] = jnp.concatenate(
        [column_sum(grad_pre), jnp.zeros((1, LANE - SQUEEZE), F32)], axis=1
    )
    taps = None
    if not is_head:
        r.wait(r.taps)
        taps = r.taps[...]
    owner_blocks(r, owners, half, taps)
    room = r.grads.shape[1]
    place = pl.ds((r.blocks.shape[1] - room) * (not is_head), room)
    blocks_copy = pltpu.make_async_copy(r.grads, r.blocks.at[:, place, :], r.own_sem.at[1])
    blocks_copy.start()

    def second(index, carry):
        for part in range(PARTS):
            lanes = chunk_at(index * PARTS + part, LANE)
            mean_row = r.norm2[0:1, lanes]
            total = jnp.zeros((TILE, LANE), F32)
            weighted = jnp.zeros((TILE, LANE), F32)
            for tile in range(tiles):
                at = tile_rows(tile)
                pool = r.pool[tile_images(tile), lanes]
                grad = as_tile(r.u[at, lanes].astype(F32)) + as_tile(r.slope[at, lanes].astype(F32)) * pool[None]
                total = total + jnp.sum(grad, axis=0)
                weighted = weighted + jnp.sum(grad * as_tile(r.d[at, lanes].astype(F32)), axis=0)
                r.dz2[at, lanes] = grad.reshape(ROWS, LANE).astype(BF16)
            r.stat[0:1, lanes] = column_sum(total)
            r.stat[1:2, lanes] = column_sum(weighted) - mean_row * column_sum(total)
        r.part(r.dz2, index, chunk_at(index)).start()
        return carry

    lax.fori_loop(0, EXPAND // CHUNK, second, 0)
    write_alike(r.pay, fold([r.stat[0:1, :], r.stat[1:2, :] * r.norm2[1:2, :]], 24))
    r.send(r.pay)
    blocks_copy.wait()
    if is_head:
        head_copy.wait()
    r.finish(r.dz2)


def gate_back(is_head, row_count, owners, recv, upper, cross, stream, lower, blocks, extra_room):
    count = upper.xb.shape[0]
    images = count // MAP
    devices = recv.shape[0]
    columns = HEAD if is_head else EXPAND
    block = EXPAND // CHUNK * (2 * WIDTH // owners) + 2 * SQUEEZE + 16
    where = (slice(0, HEAD), slice(0, WIDTH)) if is_head else (slice(0, WIDTH), slice(None))
    ins = dict(
        recv=(recv, LOOSE),
        unorm=(upper.norm, FAR),
        xb=(upper.xb, FAR),
        w=(upper.weights, where),
        dz=(upper.dz, CHUNKS),
        norm3=(lower.norm3, FAR),
        normed=(lower.normed, FAR),
        norm2=(lower.norm2, FAR),
        wp=(lower.mats, (slice(WIDTH, 2 * WIDTH), slice(None))),
        d=(lower.d, CHUNKS),
        excite=(lower.excite, FAR),
        pooled=(lower.pooled, FAR),
        squeeze=(lower.squeeze, FAR),
        side=(lower.side, (slice(0, 2 * SQUEEZE), slice(None))),
    )
    outs = dict(
        dz2=(shape((count, EXPAND), BF16), FAR),
        pay=(shape((devices, 24, LANE), BF16), FAR),
        stream=(shape((count, WIDTH)), FAR),
        blocks=(shape((owners, block * (1 + extra_room), CHUNK), BF16), RAW),
        glob=(shape((8, columns)), FAR),
        glob3=(shape((8, WIDTH)), FAR),
    )
    scratch = dict(
        grads=vmem((owners, block, CHUNK), BF16),
        xt=vmem((WIDTH, count), BF16),
        h=vmem((count, CHUNK), F32),
        coef=vmem((8, EXPAND), F32),
        dh=vmem((count + WIDTH + 16, columns), BF16),
        u=vmem((count, EXPAND), BF16),
        slope=vmem((count, EXPAND), BF16),
        y=vmem((count, EXPAND), BF16),
        gp=vmem((count, WIDTH), BF16),
        gt=vmem((WIDTH, count), BF16),
        ge=vmem((images, EXPAND), F32),
        pool=vmem((images, EXPAND), F32),
        rx=vmem((2 * SQUEEZE, EXPAND), F32),
        excite_sum=vmem((1, EXPAND), F32),
        squeeze_sum=vmem((1, LANE), F32),
        stat=vmem((8, EXPAND), F32),
        own_sem=pltpu.SemaphoreType.DMA((2,)),
    )
    alias = []
    if is_head:
        ins["grad_head_in"] = (upper.grad_head, RAW)
        outs["grad_head"] = (shape((HEAD, HEADPAD), BF16), RAW)
        scratch["grad_w"] = vmem((HEAD, WIDTH), BF16)
        alias.append(("grad_head_in", "grad_head"))
    else:
        ins["cross"] = (cross, FAR)
        ins["stream_in"] = (stream, FAR)
        ins["taps"] = (upper.taps, FAR)
        scratch["grad_w"] = vmem((WIDTH, EXPAND), BF16)
        if blocks is not None:
            ins["blocks_in"] = (blocks, RAW)
            outs["blocks"] = (shape(blocks.shape, BF16), RAW)
            alias.append(("blocks_in", "blocks"))
    return call(functools.partial(gate_kernel, is_head, row_count, owners), ins, outs, scratch, alias)


def tap_kernel(is_first, row_count, r):
    count = r.dz2.shape[0]
    groups = EXPAND // LANE
    r.start()
    r.wait(r.recv)
    sums = read_sums(r.recv)
    sum_bias = spread(sums, 0, groups)
    sum_gain = spread(sums, groups, groups)
    r.glob[0:1, :] = sum_gain
    r.glob[1:2, :] = sum_bias
    r.glob[2:8, :] = jnp.zeros((6, EXPAND), F32)
    r.send(r.glob)
    r.wait(r.side, r.norm2)
    scale2 = r.norm2[2:3, :]
    slant2 = scale2 * r.norm2[1:2, :] * (sum_gain / row_count)
    r.coef[0:9, :] = r.side[...].astype(F32)[0:9, :]
    r.coef[9:10, :] = slant2
    r.coef[10:11, :] = r.norm2[0:1, :] * slant2 - scale2 * (sum_bias / row_count)
    r.wait(r.norm1, r.xb, r.w)

    def step(index, carry):
        at_chunk = chunk_at(index)
        r.chunk(r.dz2, index, at_chunk).wait()
        r.chunk(r.d, index, at_chunk).wait()
        r.h[...] = dot(r.xb[...], r.w[:, at_chunk])
        for part in range(PARTS):
            lanes = chunk_at(index * PARTS + part, LANE)
            near = slice(part * LANE, (part + 1) * LANE)
            taps = [jnp.broadcast_to(r.coef[k : k + 1, lanes], (TILE, LANE)) for k in range(9)]

            def tile_step(tile, sums_in):
                at = chunk_at(tile, ROWS)
                grad_d = as_tile(
                    r.dz2[at, lanes].astype(F32) * r.norm2[2:3, lanes]
                    - r.d[at, lanes].astype(F32) * r.coef[9:10, lanes]
                    + r.coef[10:11, lanes]
                )
                hidden = r.h[at, near]
                pre = hidden * r.norm1[2:3, lanes] + r.norm1[3:4, lanes]
                gate = sigmoid(pre)
                flat = pre * gate
                active = as_tile(flat)
                slope = as_tile(gate + flat - flat * gate)
                hidden = as_tile(hidden)
                grad_a = [None] * MAP
                tap_sums = [None] * 9
                for target, tap, source in TERMS:
                    term = grad_d[target] * taps[tap]
                    grad_a[source] = term if grad_a[source] is None else grad_a[source] + term
                    term = grad_d[target] * active[source]
                    tap_sums[tap] = term if tap_sums[tap] is None else tap_sums[tap] + term
                total, weighted = sums_in[9], sums_in[10]
                grads = []
                for place in range(MAP):
                    grad = grad_a[place] * slope[place]
                    total = total + grad
                    weighted = weighted + grad * hidden[place]
                    grads.append(grad)
                grad = jnp.concatenate(grads, axis=0)
                r.dz[at, lanes] = grad.astype(BF16)
                if not is_first:
                    r.q[at, lanes] = (grad * r.norm1[2:3, lanes]).astype(BF16)
                return (*[sums_in[k] + tap_sums[k] for k in range(9)], total, weighted)

            zero = jnp.zeros((TILE, LANE), F32)
            result = lax.fori_loop(0, count // ROWS, tile_step, (zero,) * 11, unroll=True)
            for k in range(9):
                r.taps[k : k + 1, lanes] = column_sum(result[k])
            total = column_sum(result[9])
            r.stat[0:1, lanes] = total
            r.stat[1:2, lanes] = column_sum(result[10]) - r.norm1[0:1, lanes] * total
        r.part(r.dz, index, at_chunk).start()
        return carry

    lax.fori_loop(0, EXPAND // CHUNK, step, 0)
    r.taps[9:16, :] = jnp.zeros((7, EXPAND), F32)
    r.send(r.taps)
    vectors = [r.stat[0:1, :], r.stat[1:2, :] * r.norm1[1:2, :]]
    if not is_first:
        r.wait(r.normed, r.stream)
        below = r.stream[...] + dot_nt(r.q[...], r.w[...])
        vectors.append(column_sum(below))
        vectors.append(column_sum(below * r.normed[...]))
    write_alike(r.pay, fold(vectors, r.pay.shape[1]))
    r.send(r.pay)
    r.finish(r.dz)


def tap_back(is_first, row_count, recv, dz2, layer, stream, below):
    count = dz2.shape[0]
    devices = recv.shape[0]
    ins = dict(
        recv=(recv, LOOSE),
        side=(layer.side, (slice(2 * SQUEEZE, SIDE_PAD), slice(None))),
        norm2=(layer.norm2, FAR),
        norm1=(layer.norm1, FAR),
        xb=(layer.xb, FAR),
        w=(layer.mats, (slice(0, WIDTH), slice(None))),
        dz2=(dz2, CHUNKS),
        d=(layer.d, CHUNKS),
    )
    scratch = dict(
        h=vmem((count, CHUNK), F32),
        coef=vmem((16, EXPAND), F32),
        stat=vmem((8, EXPAND), F32),
    )
    if not is_first:
        ins["stream"] = (stream, FAR)
        ins["normed"] = (below.normed, FAR)
        scratch["q"] = vmem((count, EXPAND), BF16)
    return call(
        functools.partial(tap_kernel, is_first, row_count),
        ins,
        dict(
            dz=(shape((count, EXPAND), BF16), FAR),
            pay=(shape((devices, 24 if is_first else 32, LANE), BF16), FAR),
            taps=(shape((16, EXPAND)), FAR),
            glob=(shape((8, EXPAND)), FAR),
        ),
        scratch,
    )


def last_kernel(row_count, replicas, owners, r):
    r.start()
    r.wait(r.recv)
    product_back(False, row_count, read_sums(r.recv), EXPAND, r)
    half = owners // 2
    part = slice_rows(replicas * owners)
    rows_dev = 2 * WIDTH // owners
    chunks = EXPAND // CHUNK
    for device in range(replicas * owners):
        replica, owner = device // owners, device % owners
        first_row = rows_dev * (owner % half) + (2 * replica + owner // half) * part
        for k in range(chunks):
            r.shares[device, k * part : (k + 1) * part, :] = r.grad_w[
                first_row : first_row + part, k * CHUNK : (k + 1) * CHUNK
            ]
    if r.shares.shape[1] > chunks * part:
        r.shares[:, chunks * part :, :] = jnp.zeros(
            (replicas * owners, r.shares.shape[1] - chunks * part, CHUNK), F32
        )
    r.grads[...] = r.shares[...].astype(BF16)
    r.send(r.grads)
    r.finish()


def last_back(row_count, replicas, owners, recv, layer, dz):
    count = dz.shape[0]
    devices = recv.shape[0]
    block = -(-EXPAND // CHUNK * slice_rows(devices) // 16) * 16
    return call(
        functools.partial(last_kernel, row_count, replicas, owners),
        dict(
            recv=(recv, LOOSE),
            dz=(dz, CHUNKS),
            unorm=(layer.norm1, FAR),
            xb=(layer.xb, FAR),
            w=(layer.mats, (slice(0, WIDTH), slice(None))),
        ),
        dict(
            grads=(shape((devices, block, CHUNK), BF16), FAR),
            glob=(shape((8, EXPAND)), FAR),
        ),
        dict(
            xt=vmem((WIDTH, count), BF16),
            h=vmem((count, CHUNK), F32),
            coef=vmem((8, EXPAND), F32),
            dh=vmem((count, EXPAND), BF16),
            grad_w=vmem((WIDTH, EXPAND), F32),
            shares=vmem((devices, block, CHUNK), F32),
        ),
    )


def lamb_moments(weight, moment_one, moment_two, gradient, decay_mask, step_float):
    first_new = BETA_ONE * moment_one + (1.0 - BETA_ONE) * gradient
    second_new = BETA_TWO * moment_two + (1.0 - BETA_TWO) * gradient * gradient
    corrected = (
        first_new
        / (1.0 - BETA_ONE**step_float)
        / (jnp.sqrt(second_new / (1.0 - BETA_TWO**step_float)) + EPS_ADAM)
    )
    return (first_new, second_new, corrected + DECAY_RATE * decay_mask * weight)


def group_sums(mats, side, head_shard, row_ids):
    rows = jnp.sum(mats * mats, axis=2)
    is_expand = (row_ids < WIDTH)[None, :]
    side_rows = jnp.sum(side * side, axis=2)
    head_cols = jnp.sum(head_shard * head_shard, axis=0)
    per_layer = jnp.stack(
        [
            jnp.sum(jnp.where(is_expand, rows, 0.0), axis=1),
            jnp.sum(jnp.where(is_expand, 0.0, rows), axis=1),
            jnp.sum(side_rows[:, :9], axis=1),
            jnp.sum(side_rows[:, 9 : 9 + SQUEEZE], axis=1),
            jnp.sum(side_rows[:, 9 + SQUEEZE : 9 + 2 * SQUEEZE], axis=1),
        ],
        axis=1,
    )
    tail = jnp.stack([jnp.sum(head_cols[:WIDTH]), jnp.sum(head_cols[WIDTH : WIDTH + CLASSES])])
    return jnp.concatenate([per_layer.reshape(-1), tail])


def rate_maps(trust_ratio, row_ids):
    groups = trust_ratio[: 5 * LAYERS].reshape(LAYERS, 5)
    mats_rate = RATE_MATRIX * jnp.where(row_ids[None, :] < WIDTH, groups[:, 0:1], groups[:, 1:2])
    side_ids = jnp.arange(SIDE)[None, :]
    side_rate = jnp.where(
        side_ids < 9,
        RATE_MATRIX * groups[:, 2:3],
        jnp.where(
            side_ids < 9 + SQUEEZE,
            RATE_MATRIX * groups[:, 3:4],
            jnp.where(side_ids < 9 + 2 * SQUEEZE, RATE_MATRIX * groups[:, 4:5], RATE_VECTOR),
        ),
    )
    col_ids = jnp.arange(HEADCOLS)
    head_rate = jnp.where(
        col_ids < WIDTH,
        RATE_MATRIX * trust_ratio[5 * LAYERS],
        jnp.where(
            col_ids < WIDTH + CLASSES, RATE_MATRIX * trust_ratio[5 * LAYERS + 1], RATE_VECTOR
        ),
    )
    return (mats_rate, side_rate, head_rate)


def exchange(payload):
    return lax.all_to_all(payload, BOTH, 0, 0)


def before(value, *others):
    return lax.optimization_barrier((value, *others))[0]


def spread_over(array, axis):
    copies = jnp.broadcast_to(array[None], (lax.axis_size(axis), *array.shape))
    return lax.all_to_all(copies, axis, 0, 0)


def replica_sum(array, turned=False):
    count = lax.axis_size(REPLICAS)
    steps = [1 << k for k in range(count.bit_length() - 1)]
    total = array
    for step in reversed(steps) if turned else steps:
        other = lax.ppermute(total, REPLICAS, [(k, k ^ step) for k in range(count)])
        total = (total.astype(F32) + other.astype(F32)).astype(BF16)
    return total.astype(F32)


def body(
    images, partner, mix_pair, labels, step,
    layer_mats, layer_side, layer_vecs, head_mat, fc_bias,
    mats_first, mats_second, side_first, side_second, vecs_first, vecs_second,
    head_first, head_second, bias_first, bias_second,
):
    local_images = images.shape[0]
    owners = lax.axis_size(OWNERS)
    replicas = lax.axis_size(REPLICAS)
    devices = owners * replicas
    image_count = float(local_images * devices)
    count = local_images * MAP
    row_count = float(count * devices)
    mine = lax.axis_index(OWNERS)
    side_width = layer_side.shape[2]
    vec_width = layer_vecs.shape[1]
    rows_dev = layer_mats.shape[1]
    half = owners // 2

    def side_as_sent(side, vecs):
        blank = jnp.zeros((side.shape[0], 1, side_width), F32)
        vecs = jnp.pad(vecs, ((0, 0), (0, side_width - vec_width)))[:, None, :]
        pieces = [side[:, 9 : 9 + 2 * SQUEEZE], side[:, :9], side[:, 9 + 2 * SQUEEZE :], vecs, blank]
        return jnp.concatenate(pieces, axis=1).astype(BF16)

    side_rows = -(-SIDE_PAD * side_width // EXPAND)
    side_flat = jnp.pad(side_as_sent(layer_side[:1], layer_vecs[:1]).reshape(-1), (0, side_rows * EXPAND - SIDE_PAD * side_width))
    packed = lax.all_gather(
        jnp.concatenate([layer_mats[0].astype(BF16), side_flat.reshape(side_rows, EXPAND)], axis=0),
        OWNERS, axis=0,
    )
    partner_col = partner[:, None]
    layers = []
    crosses = []
    entry = mix(images.reshape(count, WIDTH), partner_col, mix_pair, devices)
    x, xb = entry.x, entry.xb
    received = exchange(entry.pay)
    shared = share(received).pay
    later_mats, later_side, later_vecs, later_head, _ = lax.optimization_barrier(
        (layer_mats, layer_side, layer_vecs, head_mat, shared)
    )
    mats_all = [None] + [
        lax.all_gather(later_mats[k].astype(BF16), OWNERS, axis=0, tiled=True) for k in range(1, LAYERS)
    ]
    side_room = -(-side_width // CHUNK) * CHUNK
    side_rest = lax.all_gather(
        jnp.pad(side_as_sent(later_side[1:], later_vecs[1:]), ((0, 0), (0, 0), (0, side_room - side_width))), OWNERS, axis=0
    )
    side_rest = jnp.moveaxis(side_rest[..., :side_width], 0, 2).reshape(LAYERS - 1, SIDE_PAD, EXPAND)
    head_full = lax.all_gather(
        jnp.pad(later_head, ((0, 0), (0, HEADPAD - HEADCOLS))).astype(BF16), OWNERS, axis=0, tiled=True
    )

    square = exchange(shared)
    packed = before(packed, shared)
    mats_all[0] = packed[:, :rows_dev].reshape(2 * WIDTH, EXPAND)
    side_flat = packed[:, rows_dev:].reshape(owners, -1)[:, : SIDE_PAD * side_width]
    side_zero = jnp.moveaxis(side_flat.reshape(owners, SIDE_PAD, side_width), 0, 1).reshape(SIDE_PAD, EXPAND)
    side_all = [side_zero, side_rest[0], side_rest[1]]
    for k in range(LAYERS):
        mats, side = mats_all[k], side_all[k]
        if k:
            received, square = exchange(pay), None
        one = spatial(xb, mats, side, received, square)
        two = project(one.d, mats, side, exchange(one.pay), getattr(one, "cross", None), owners)
        last = k == LAYERS - 1
        three = residual(
            x, two.p, two.vec, exchange(two.pay), head_full if last else mats_all[k + 1], last
        )
        if k:
            crosses.append(three.cross)
        layers.append(
            types.SimpleNamespace(
                xb=xb, d=one.d, norm1=one.norm, norm2=two.norm,
                pooled=two.pooled, excite=two.excite, squeeze=two.squeeze,
                norm3=three.norm, normed=three.normed, mats=mats, weights=mats, side=side,
            )
        )
        x, xb, pay = three.x, three.xb, three.pay
    top = head(
        xb, head_full, jnp.pad(fc_bias, (0, LOGITS - CLASSES))[None], labels[:, None], labels[None, :],
        partner_col, mix_pair, layers[-1].normed, exchange(pay), image_count,
    )

    def to_owner(blocks):
        return lax.psum_scatter(
            blocks.reshape(-1, blocks.shape[-1]), OWNERS, scatter_dimension=0, tiled=True
        )

    upper = types.SimpleNamespace(
        xb=xb, weights=head_full, dz=top.dz, norm=top.norm, grad_head=top.grad_head
    )
    pay = top.pay
    stream = None
    blocks = None
    waiting = []
    globs_one, globs_two, globs_three = [None] * LAYERS, [None] * LAYERS, [None] * LAYERS
    for k in reversed(range(LAYERS)):
        layer = layers[k]
        is_head = k == LAYERS - 1
        gate = gate_back(
            is_head, row_count, owners, exchange(pay), upper,
            None if is_head else crosses[k], stream, layer, blocks, is_head,
        )
        stream = gate.stream
        globs_three[k] = gate.glob3
        if is_head:
            head_glob, bias_loss = gate.glob, gate.glob3[2:6].reshape(LOGITS)
            shard_head = to_owner(gate.grad_head)
            blocks = gate.blocks
        else:
            globs_one[k + 1] = gate.glob
            if k:
                pair = to_owner(gate.blocks)
                blocks = None
            else:
                shard_zero = to_owner(gate.blocks)
        tap = tap_back(
            k == 0, row_count, exchange(gate.pay), gate.dz2, layer, stream, layers[max(k - 1, 0)]
        )
        globs_two[k] = tap.glob
        pay = tap.pay
        if k == 1:
            pay = before(pay, shard_head)
        upper = types.SimpleNamespace(
            xb=layer.xb, weights=layer.mats, dz=tap.dz, norm=layer.norm1, taps=tap.taps
        )
    pay = before(pay, pair)
    late_taps = jnp.moveaxis(tap.taps[:9].astype(BF16).reshape(9, owners, side_width), 1, 0)
    late_taps = jnp.broadcast_to(late_taps[None], (replicas, *late_taps.shape))
    received = exchange(pay)
    final = last_back(row_count, replicas, owners, received, layers[0], tap.dz)
    globs_one[0] = final.glob
    shard_head = replica_sum(before(shard_head, received))
    pair = replica_sum(before(pair, received), True)
    room = pair.shape[0] // 2
    shards = [replica_sum(shard_zero), pair[room:], pair[:room]]

    part = slice_rows(devices)
    chunks = EXPAND // CHUNK
    late = jnp.sum(exchange(final.grads).astype(F32), axis=0).astype(BF16)
    other = lax.ppermute(late, OWNERS, [(half + k, k) for k in range(half)])
    late_taps = exchange(before(late_taps.reshape(devices, 9, side_width), received))
    late_taps = jnp.sum(late_taps.astype(F32), axis=0)
    late = spread_over(jnp.stack([late, other]), REPLICAS)[:, :, : chunks * part]
    late = jnp.moveaxis(late.reshape(replicas, 2, chunks, part, CHUNK), 2, 3)
    late = late.reshape(rows_dev, EXPAND).astype(F32)

    def mats_of(shard):
        rows = shard[: chunks * rows_dev].reshape(chunks, rows_dev, CHUNK)
        return jnp.moveaxis(rows, 0, 1).reshape(rows_dev, EXPAND)

    from_mats = [late] + [mats_of(shard) for shard in shards]
    owns_expand = mine < half
    grad_mats = jnp.stack(
        [jnp.where(owns_expand, from_mats[k], from_mats[k + 1]) for k in range(LAYERS)]
    )

    def own_columns(vector, width):
        return lax.dynamic_slice_in_dim(vector, mine * width, width, axis=-1)

    first_row = chunks * rows_dev
    last_row = first_row + 2 * SQUEEZE
    vec_ids = mine * vec_width + jnp.arange(vec_width)
    side_list, vec_list = [], []
    for k in range(LAYERS):
        shard = shards[k][:, :side_width]
        taps = late_taps if k == 0 else shards[k - 1][last_row + 2 : last_row + 11, :side_width]
        norms_part = own_columns(
            jnp.concatenate([globs_one[k][0:2], globs_two[k][0:2]], axis=0), side_width
        )
        side_list.append(
            jnp.concatenate([taps, shard[first_row : last_row + 1], norms_part], axis=0)
        )
        outer = globs_three[k]
        outer = own_columns(
            jnp.concatenate([jnp.zeros((SQUEEZE,), F32), outer[0], outer[1]]), vec_width
        )
        vec_list.append(jnp.where(vec_ids < SQUEEZE, shard[last_row + 1, :vec_width], outer))
    grad_side = jnp.stack(side_list)
    grad_vecs = jnp.stack(vec_list)
    head_tail = own_columns(head_glob[0:2], head_mat.shape[0]).T
    grad_head = jnp.concatenate([shard_head[:, : WIDTH + CLASSES], head_tail], axis=1)
    grad_bias = bias_loss[:CLASSES]
    loss_value = (bias_loss[CLASSES] + bias_loss[CLASSES + 1]) / image_count

    step_float = step[0].astype(F32)
    side_decay = (jnp.arange(SIDE) < 9 + 2 * SQUEEZE).astype(F32)[None, :, None]
    head_decay = (jnp.arange(HEADCOLS) < WIDTH + CLASSES).astype(F32)[None, :]
    mats_moment, mats_square, mats_dir = lamb_moments(
        layer_mats, mats_first, mats_second, grad_mats, 1.0, step_float
    )
    side_moment, side_square, side_dir = lamb_moments(
        layer_side, side_first, side_second, grad_side, side_decay, step_float
    )
    vecs_moment, vecs_square, vecs_dir = lamb_moments(
        layer_vecs, vecs_first, vecs_second, grad_vecs, 0.0, step_float
    )
    head_moment, head_square, head_dir = lamb_moments(
        head_mat, head_first, head_second, grad_head, head_decay, step_float
    )
    bias_moment, bias_square, bias_dir = lamb_moments(
        fc_bias, bias_first, bias_second, grad_bias, 0.0, step_float
    )
    row_ids = mine * rows_dev + jnp.arange(rows_dev)
    squares = jnp.stack(
        [
            group_sums(layer_mats, layer_side, head_mat, row_ids),
            group_sums(mats_dir, side_dir, head_dir, row_ids),
        ]
    )
    norms = jnp.sqrt(jnp.sum(spread_over(squares, OWNERS), axis=0))
    mats_rate, side_rate, head_rate = rate_maps(norms[0] / norms[1], row_ids)
    mats_new = layer_mats - mats_rate[:, :, None] * mats_dir
    side_new = layer_side - side_rate[:, :, None] * side_dir
    vecs_new = layer_vecs - RATE_VECTOR * vecs_dir
    head_new = head_mat - head_rate[None, :] * head_dir
    bias_new = fc_bias - RATE_VECTOR * bias_dir
    return (
        loss_value,
        mats_new, mats_moment, mats_square,
        side_new, side_moment, side_square,
        vecs_new, vecs_moment, vecs_square,
        head_new, head_moment, head_square,
        bias_new, bias_moment, bias_square,
        norms,
    )


def solution(mesh):
    rows, columns = P(None, OWNERS, None), P(None, None, OWNERS)
    vecs, heads = P(None, OWNERS), P(OWNERS, None)
    return jax.shard_map(
        body,
        mesh=mesh,
        in_specs=(
            P(BOTH, None, None), P(BOTH), P(BOTH, None), P(BOTH), P(),
            rows, columns, vecs, heads, P(),
            rows, rows, columns, columns, vecs, vecs, heads, heads, P(), P(),
        ),
        out_specs=(
            P(),
            rows, rows, rows,
            columns, columns, columns,
            vecs, vecs, vecs,
            heads, heads, heads,
            P(), P(), P(), P(),
        ),
        check_vma=False,
    )
```

```python
import functools
import types

import jax
import jax.numpy as jnp
from jax import lax
from jax.experimental import pallas as pl
from jax.experimental.pallas import tpu as pltpu
from jax.sharding import PartitionSpec as P

WIDTH = 256
EXPAND = 1536
SQUEEZE = 64
HEAD = 1280
CLASSES = 1000
LOGITS = 1024
EDGE = 4
LAYERS = 3
MAP = 16
SIDE = 142
SIDE_PAD = 144
VECS = 576
HEADCOLS = 1258
HEADPAD = 1280

EPS_BN = 0.001
BETA_ONE = 0.9
BETA_TWO = 0.999
EPS_ADAM = 1e-06
DECAY_RATE = 0.01
RATE_MATRIX = 0.5
RATE_VECTOR = 0.25

REPLICAS, OWNERS = BOTH = ("dp", "fsdp")
F32 = jnp.float32
BF16 = jnp.bfloat16
LANE = 128
TILE = 8
ROWS = MAP * TILE
CHUNK = 256
PARTS = CHUNK // LANE
VMEM_BYTES = 60 * 1024 * 1024

NT = (((1,), (1,)), ((), ()))
TN = (((0,), (0,)), ((), ()))


NEAR, FAR, RAW, CHUNKS, LOOSE = range(5)


class Blocks:
    def __init__(self, first, count, rows):
        self.first, self.count, self.rows = first, count, rows


def expand_rows(mats):
    return (mats, half_of(mats, 0))


def project_rows(mats):
    return (mats, half_of(mats, 1))


def half_of(mats, part):
    if mats.ndim == 2:
        return (slice(part * WIDTH, (part + 1) * WIDTH), slice(None))
    count = mats.shape[0] // 2
    return Blocks(part * count, count, WIDTH // count)


class Refs:
    def __init__(self, names, refs, loads, stores):
        for name, ref in zip(names, refs):
            setattr(self, name, ref)
        self.loads = loads
        self.stores = {id(getattr(self, name)): (k, self.far(name)) for k, name in enumerate(stores)}
        self.pending = {}
        self.chunks = {}

    def far(self, name):
        return getattr(self, name + "_far")

    def start(self):
        later = len(self.loads) * (1 + EXPAND // CHUNK)
        for index, (name, where) in enumerate(self.loads):
            near = getattr(self, name)
            if isinstance(where, Blocks):
                copies = []
                for k in range(where.count):
                    source = self.far(name).at[where.first + k, pl.ds(0, where.rows), :]
                    target = near.at[pl.ds(k * where.rows, where.rows), :]
                    copies.append(pltpu.make_async_copy(source, target, self.load_sem.at[later + k]))
                    copies[-1].start()
                later += where.count
                self.pending[id(near)] = copies
                continue
            source = self.far(name) if where is None or where == CHUNKS else self.far(name).at[where]
            if where == CHUNKS:
                self.chunks[id(near)] = (self.far(name), index)
                for turn in range(near.shape[1] // CHUNK):
                    self.chunk(near, turn, pl.ds(turn * CHUNK, CHUNK)).start()
                continue
            copy = pltpu.make_async_copy(source, near, self.load_sem.at[index])
            copy.start()
            self.pending[id(near)] = [copy]

    def chunk(self, near, turn, at):
        far, index = self.chunks[id(near)]
        semaphore = self.load_sem.at[len(self.loads) + index * (EXPAND // CHUNK) + turn]
        return pltpu.make_async_copy(far.at[:, at], near.at[:, at], semaphore)

    def wait(self, *refs):
        for ref in refs:
            for copy in self.pending.pop(id(ref)):
                copy.wait()

    def send(self, *refs):
        for ref in refs:
            index, far = self.stores[id(ref)]
            copy = pltpu.make_async_copy(ref, far, self.store_sem.at[index])
            copy.start()
            self.pending[id(far)] = [copy]

    def part(self, ref, index, at):
        far = self.stores[id(ref)][1]
        return pltpu.make_async_copy(ref.at[:, at], far.at[:, at], self.part_sem.at[index])

    def finish(self, ref=None):
        for key in list(self.pending):
            for copy in self.pending.pop(key):
                copy.wait()
        if ref is not None:
            for index in range(ref.shape[1] // CHUNK):
                self.part(ref, index, pl.ds(index * CHUNK, CHUNK)).wait()


def shape(dims, dtype=F32):
    return jax.ShapeDtypeStruct(dims, dtype)


def vmem(dims, dtype=F32):
    return pltpu.VMEM(dims, dtype)


def call(kernel, ins, outs, scratch, alias=()):
    near, far, loose = (
        pl.BlockSpec(memory_space=space) for space in (pltpu.VMEM, pltpu.HBM, pl.ANY)
    )
    names, arrays, in_specs, loads, stores, extra = [], [], [], [], [], {}
    for name, (array, place) in ins.items():
        arrays.append(array)
        in_specs.append(near if place == NEAR else loose if place == LOOSE else far)
        if place == NEAR or place == RAW:
            names.append(name)
            continue
        names.append(name + "_far")
        dims, where = array.shape, None
        if isinstance(place, Blocks):
            dims, where = (place.count * place.rows, dims[2]), place
        elif place == CHUNKS:
            where = CHUNKS
        elif place != FAR and place != LOOSE:
            starts = [part.indices(size)[:2] for part, size in zip(place, dims)]
            dims = tuple(stop - start for start, stop in starts)
            where = tuple(pl.ds(start, stop - start) for start, stop in starts)
        loads.append((name, where))
        extra[name] = vmem(dims, array.dtype)
    for name, (struct, place) in outs.items():
        names.append(name + "_far" if place == FAR else name)
        if place == FAR:
            stores.append(name)
            extra[name] = vmem(struct.shape, struct.dtype)
    extra.update(scratch)
    extra.update(
        load_sem=pltpu.SemaphoreType.DMA((
            max(len(loads), 1) * (1 + EXPAND // CHUNK)
            + sum(where.count for _, where in loads if isinstance(where, Blocks)),
        )),
        store_sem=pltpu.SemaphoreType.DMA((max(len(stores), 1),)),
        part_sem=pltpu.SemaphoreType.DMA((EXPAND // CHUNK,)),
    )

    def flat(*refs):
        kernel(Refs(names + list(extra), refs, loads, stores))

    results = pl.pallas_call(
        flat,
        out_shape=[struct for struct, _ in outs.values()],
        in_specs=in_specs,
        out_specs=[near if place == NEAR else far for _, place in outs.values()],
        scratch_shapes=list(extra.values()),
        input_output_aliases={list(ins).index(a): list(outs).index(b) for a, b in alias},
        compiler_params=pltpu.CompilerParams(vmem_limit_bytes=VMEM_BYTES),
    )(*arrays)
    return types.SimpleNamespace(**dict(zip(outs, results)))


def dot(left, right):
    return jnp.dot(left, right, preferred_element_type=F32)


def dot_nt(left, right):
    return lax.dot_general(left, right, NT, preferred_element_type=F32)


def dot_tn(left, right):
    return lax.dot_general(left, right, TN, preferred_element_type=F32)


def halves(value):
    high = value.astype(BF16)
    return high, (value - high.astype(F32)).astype(BF16)


def stacked(value):
    return jnp.concatenate(halves(value), axis=0)


def folded(value):
    count = value.shape[0] // 2
    return value[:count] + value[count:]


def sigmoid(value):
    return 0.5 * jnp.tanh(0.5 * value) + 0.5


def chunk_at(index, size=CHUNK):
    return pl.ds(pl.multiple_of(index * size, size), size)


def tile_rows(tile):
    return slice(tile * ROWS, (tile + 1) * ROWS)


def tile_images(tile):
    return slice(tile * TILE, (tile + 1) * TILE)


def as_tile(block):
    return block.reshape(MAP, TILE, LANE)


def spread(rows, first, count):
    return jnp.concatenate([rows[first + k : first + k + 1, :] for k in range(count)], axis=1)


def fold(vectors, rows):
    pieces = [
        vector[:, k * LANE : (k + 1) * LANE]
        for vector in vectors
        for k in range(vector.shape[1] // LANE)
    ]
    if rows > len(pieces):
        pieces.append(jnp.zeros((rows - len(pieces), LANE), F32))
    return jnp.concatenate(pieces, axis=0)


def column_sum(value):
    return jnp.sum(value, axis=0, keepdims=True)


def slice_rows(devices):
    return max(1, WIDTH // devices)


def write_alike(pay_ref, rows):
    pay_ref[...] = jnp.broadcast_to(rows.astype(BF16)[None], pay_ref.shape)


def write_with_slices(pay_ref, rows, matrix):
    devices = pay_ref.shape[0]
    part = slice_rows(devices)
    first = rows.shape[0]
    low = rows.astype(BF16)
    for device in range(devices):
        own = matrix[device * part : (device + 1) * part, :]
        block = jnp.concatenate([own[:, :LANE], own[:, LANE:]], axis=0)
        if 2 * part < 16:
            block = jnp.concatenate([block, jnp.zeros((16 - 2 * part, LANE), F32)], axis=0)
        pay_ref[device, 0:first, :] = low
        pay_ref[device, first : first + 16, :] = block.astype(BF16)


def read_matrix(recv_ref, first):
    devices, rows = recv_ref.shape[:2]
    part = slice_rows(devices)
    if part == TILE:
        values = recv_ref[...].astype(F32)
        left = values[:, first : first + part].reshape(WIDTH, LANE)
        right = values[:, first + part : first + 2 * part].reshape(WIDTH, LANE)
        return jnp.concatenate([left, right], axis=1)
    flat = recv_ref[...].reshape(devices * rows, LANE)
    row = lax.broadcasted_iota(jnp.int32, (WIDTH, devices * rows), 0)
    column = lax.broadcasted_iota(jnp.int32, (WIDTH, devices * rows), 1)
    source = row // part * rows + first + row % part
    left = dot(jnp.where(column == source, 1.0, 0.0).astype(BF16), flat)
    right = dot(jnp.where(column == source + part, 1.0, 0.0).astype(BF16), flat)
    return jnp.concatenate([left, right], axis=1)


def mean_parts(columns):
    return 1 if columns == EXPAND else 2


def moment_rows(columns):
    return -(-(mean_parts(columns) + 1) * columns // LANE // 8) * 8


def centred(total, squares, count):
    return jnp.maximum(squares - total * total / count, 0.0)


def pack_moments(total, squares, count):
    mean = total / count
    high = mean.astype(BF16).astype(F32)
    parts = [high, mean - high][: mean_parts(total.shape[1])]
    return fold(parts + [centred(total, squares, count)], moment_rows(total.shape[1]))


def read_moments(recv_ref, columns, count):
    groups = columns // LANE
    devices = recv_ref.shape[0]
    parts = recv_ref[...].astype(F32)
    given = mean_parts(columns)
    means = parts[:, :groups]
    if given > 1:
        means = means + parts[:, groups : 2 * groups]
    mean = jnp.sum(means, axis=0) / devices
    apart = means - mean[None]
    spread_sum = jnp.sum(parts[:, given * groups : (given + 1) * groups], axis=0) / count
    variance = (spread_sum + jnp.sum(apart * apart, axis=0)) / devices
    return spread(mean, 0, groups), lax.rsqrt(spread(variance, 0, groups) + EPS_BN)


def product_means(recv_ref, weights, transposed, count):
    devices, rows = recv_ref.shape[:2]
    values = recv_ref[...]
    flat = values.reshape(devices * rows, LANE)
    row = lax.broadcasted_iota(jnp.int32, (devices, devices * rows), 0)
    column = lax.broadcasted_iota(jnp.int32, (devices, devices * rows), 1) - row * rows
    left = dot(jnp.where((column == 0) | (column == 2), 1.0, 0.0).astype(BF16), flat)
    right = dot(jnp.where((column == 1) | (column == 3), 1.0, 0.0).astype(BF16), flat)
    sums = stacked(jnp.concatenate([left, right], axis=1) / count)
    return folded(dot_nt(sums, weights) if transposed else dot(sums, weights))


def read_square_moments(recv_ref, square_ref, w_ref, left_ref, stat_ref, count):
    devices = recv_ref.shape[0]
    means = product_means(recv_ref, w_ref[...], False, count)
    mean = column_sum(means) / devices
    apart = means - mean
    left_ref[...] = jnp.concatenate(
        [read_matrix(square_ref, 0), read_matrix(square_ref, 16)], axis=0
    ).astype(BF16)

    def step(index, carry):
        at = chunk_at(index)
        weights = w_ref[:, at]
        squares = column_sum(folded(dot(left_ref[...], weights)) * weights.astype(F32))
        stat_ref[0:1, at] = jnp.maximum(squares, 0.0)
        return carry

    lax.fori_loop(0, w_ref.shape[1] // CHUNK, step, 0, unroll=True)
    variance = (stat_ref[0:1, :] / count + column_sum(apart * apart)) / devices
    return mean, lax.rsqrt(variance + EPS_BN)


def read_product_moments(recv_ref, weights, transposed, columns, count):
    devices = recv_ref.shape[0]
    values = recv_ref[...]
    means = product_means(recv_ref, weights, transposed, count)
    mean = column_sum(means) / devices
    apart = means - mean
    squares = jnp.sum(values.astype(F32), axis=0)
    variance = (spread(squares, 4, columns // LANE) / count + column_sum(apart * apart)) / devices
    return mean, lax.rsqrt(variance + EPS_BN)


def read_sums(recv_ref):
    return jnp.sum(recv_ref[...].astype(F32), axis=0)


def keep_norm(norm_ref, mean, inverse, gain, bias):
    scale = inverse * gain
    norm_ref[0:1, :] = mean
    norm_ref[1:2, :] = inverse
    norm_ref[2:3, :] = scale
    norm_ref[3:4, :] = bias - mean * scale
    norm_ref[4:8, :] = jnp.zeros((4, norm_ref.shape[1]), F32)


def product_moments(x_ref, w_ref, transposed, columns, left_ref, stat_ref, beside):
    count = x_ref.shape[0]
    values = x_ref[...]
    product = dot_tn(jnp.concatenate([values, beside], axis=1), values)
    square, cross = product[:WIDTH], product[WIDTH:]
    sums = column_sum(values.astype(F32))
    left_ref[0 : 2 * WIDTH, :] = stacked(square)
    tail = jnp.concatenate([half.astype(F32) for half in halves(sums)] + [jnp.zeros((14, WIDTH), F32)], axis=0)
    left_ref[2 * WIDTH :, :] = tail.astype(BF16)

    def step(index, carry):
        at = chunk_at(index)
        weights = w_ref[at, :].T if transposed else w_ref[:, at]
        product = dot(left_ref[...], weights)
        total = column_sum(product[2 * WIDTH : 2 * WIDTH + 2])
        squares = column_sum(folded(product[: 2 * WIDTH]) * weights.astype(F32))
        stat_ref[0:1, at] = jnp.maximum(squares - total * total / count, 0.0)
        return carry

    lax.fori_loop(0, columns // CHUNK, step, 0, unroll=True)
    high = sums.astype(BF16).astype(F32)
    return fold([high, sums - high, stat_ref[0:1, :]], 16), cross


def mix_kernel(r):
    count = r.images.shape[0]
    pixels = r.images[...]
    row = lax.broadcasted_iota(jnp.int32, (ROWS, count), 0)
    column = lax.broadcasted_iota(jnp.int32, (ROWS, count), 1)
    place = lax.shift_right_logical(row, 3)
    inside = jnp.bitwise_and(row, 7)
    pair = r.mix[...].astype(F32)
    mixing = pair[:, 0:1] / (pair[:, 0:1] + pair[:, 1:2])
    for tile in range(count // ROWS):
        near = tile_images(tile)
        other = jnp.concatenate([r.partner[near, :]] * MAP, axis=0)
        weight = jnp.concatenate([mixing[near, :]] * MAP, axis=0)
        own_hot = jnp.where(column == (tile * TILE + inside) * MAP + place, 1.0, 0.0).astype(BF16)
        other_hot = jnp.where(column == other * MAP + place, 1.0, 0.0).astype(BF16)
        mixed = weight * dot(own_hot, pixels) + (1.0 - weight) * dot(other_hot, pixels)
        r.x[tile_rows(tile), :] = mixed
    r.xb[...] = r.x[...].astype(BF16)
    r.send(r.x, r.xb)
    low = r.xb[...]
    sums = column_sum(low.astype(F32))
    padded = jnp.concatenate([sums, jnp.zeros((TILE - 1, WIDTH), F32)], axis=0)
    outer = lax.dot_general(
        padded, padded, TN, preferred_element_type=F32, precision=lax.Precision.HIGHEST
    )
    square = dot_tn(low, low) - outer / count
    high = sums.astype(BF16).astype(F32)
    rows = fold([high, sums - high], 8)
    devices = r.pay.shape[0]
    part = slice_rows(devices)
    for device in range(devices):
        own = square[device * part : (device + 1) * part, :]
        block = [rows, own[:, :LANE], own[:, LANE:]]
        if 2 * part < 16:
            block.append(jnp.zeros((16 - 2 * part, LANE), F32))
        r.pay[device, :, :] = jnp.concatenate(block, axis=0).astype(BF16)
    r.send(r.pay)
    r.finish()


def mix(images, partner, mix_pair, devices):
    dims = images.shape
    return call(
        mix_kernel,
        dict(images=(images, NEAR), partner=(partner, NEAR), mix=(mix_pair, NEAR)),
        dict(
            x=(shape(dims), FAR),
            xb=(shape(dims, BF16), FAR),
            pay=(shape((devices, 24, LANE), BF16), FAR),
        ),
        {},
    )


def share_kernel(r):
    r.start()
    r.wait(r.recv)
    high, low = halves(jnp.sum(r.recv[...].astype(F32), axis=0)[8:24])
    write_alike(r.pay, jnp.concatenate([high.astype(F32), low.astype(F32)], axis=0))
    r.send(r.pay)
    r.finish()


def share(recv):
    return call(
        share_kernel,
        dict(recv=(recv, LOOSE)),
        dict(pay=(shape((recv.shape[0], 32, LANE), BF16), FAR)),
        {},
    )


def tap_terms():
    for row in range(EDGE):
        for col in range(EDGE):
            for row_shift in range(3):
                for col_shift in range(3):
                    from_row, from_col = row + row_shift - 1, col + col_shift - 1
                    if 0 <= from_row < EDGE and 0 <= from_col < EDGE:
                        yield EDGE * row + col, 3 * row_shift + col_shift, EDGE * from_row + from_col


TERMS = list(tap_terms())


def spatial_kernel(from_square, r):
    count = r.xb.shape[0]
    r.start()
    r.wait(r.recv, r.side, r.w, r.xb)
    rows = r.side[...].astype(F32)
    r.taps[0:9, :] = rows[0:9, :]
    if from_square:
        r.wait(r.square)
        mean, inverse = read_square_moments(r.recv, r.square, r.w, r.left, r.stat, count)
    else:
        mean, inverse = read_product_moments(r.recv, r.w[...], False, EXPAND, count)
    keep_norm(r.norm, mean, inverse, rows[10:11, :], rows[11:12, :])
    r.send(r.norm)
    if not from_square:
        r.cross[...] = jnp.sum(r.recv[...].astype(F32)[:, 16:32], axis=0)
        r.send(r.cross)

    def step(index, carry):
        at_chunk = chunk_at(index)
        r.h[...] = dot(r.xb[...], r.w[:, at_chunk])
        for part in range(PARTS):
            lanes = chunk_at(index * PARTS + part, LANE)
            taps = [jnp.broadcast_to(r.taps[k : k + 1, lanes], (TILE, LANE)) for k in range(9)]
            scale_row = r.norm[2:3, lanes]
            shift_row = r.norm[3:4, lanes]

            def tile_step(tile, sums):
                at = chunk_at(tile, ROWS)
                pre = r.h[at, part * LANE : (part + 1) * LANE] * scale_row + shift_row
                active = as_tile(pre * sigmoid(pre))
                result = [None] * MAP
                for target, tap, source in TERMS:
                    term = active[source] * taps[tap]
                    result[target] = term if result[target] is None else result[target] + term
                total, squares = sums
                for value in result:
                    total = total + value
                    squares = squares + value * value
                r.d[at, lanes] = jnp.concatenate(result, axis=0).astype(BF16)
                return total, squares

            zero = jnp.zeros((TILE, LANE), F32)
            total, squares = lax.fori_loop(0, count // ROWS, tile_step, (zero, zero), unroll=True)
            r.stat[0:1, lanes] = column_sum(total)
            r.stat[1:2, lanes] = column_sum(squares)
        r.part(r.d, index, at_chunk).start()
        return carry

    lax.fori_loop(0, EXPAND // CHUNK, step, 0)
    write_alike(r.pay, pack_moments(r.stat[0:1, :], r.stat[1:2, :], count))
    r.send(r.pay)
    r.finish(r.d)


def spatial(xb, mats, side, recv, square):
    count = xb.shape[0]
    devices = recv.shape[0]
    outs = dict(
        d=(shape((count, EXPAND), BF16), FAR),
        pay=(shape((devices, moment_rows(EXPAND), LANE), BF16), FAR),
        norm=(shape((8, EXPAND)), FAR),
    )
    ins = dict(
        recv=(recv, LOOSE),
        side=(side, (slice(2 * SQUEEZE, SIDE_PAD), slice(None))),
        xb=(xb, FAR),
        w=expand_rows(mats),
    )
    if square is None:
        outs["cross"] = (shape((16, LANE)), FAR)
    else:
        ins["square"] = (square, LOOSE)
    return call(
        functools.partial(spatial_kernel, square is not None),
        ins,
        outs,
        dict(
            left=vmem((2 * WIDTH, WIDTH), BF16),
            h=vmem((count, CHUNK), F32),
            taps=vmem((16, EXPAND), F32),
            stat=vmem((8, EXPAND), F32),
        ),
    )


def project_kernel(with_cross, owners, r):
    count = r.d.shape[0]
    tiles = count // ROWS
    r.start()
    r.wait(r.recv)
    mean, inverse = read_moments(r.recv, EXPAND, count)
    r.wait(r.side)
    rows = r.side[2 * SQUEEZE : SIDE_PAD, :].astype(F32)
    keep_norm(r.norm, mean, inverse, rows[12:13, :], rows[13:14, :])
    r.send(r.norm)
    width, vec_width = EXPAND // owners, VECS // owners
    vec = jnp.concatenate(
        [rows[14:15, k * width : k * width + vec_width] for k in range(owners)], axis=1
    )
    r.vec[...] = jnp.concatenate(
        [vec[:, SQUEEZE : SQUEEZE + WIDTH], vec[:, SQUEEZE + WIDTH :], jnp.zeros((6, WIDTH), F32)], axis=0
    )
    r.send(r.vec)

    def activate(index, carry):
        r.chunk(r.d, index, chunk_at(index)).wait()
        for part in range(PARTS):
            lanes = chunk_at(index * PARTS + part, LANE)
            scale_row = r.norm[2:3, lanes]
            shift_row = r.norm[3:4, lanes]
            for tile in range(tiles):
                at = tile_rows(tile)
                pre = r.d[at, lanes].astype(F32) * scale_row + shift_row
                active = pre * sigmoid(pre)
                r.a[at, lanes] = active
                r.pooled[tile_images(tile), lanes] = jnp.sum(as_tile(active), axis=0) / MAP
        return carry

    lax.fori_loop(0, EXPAND // CHUNK, activate, 0)
    r.send(r.pooled)
    before = folded(dot_nt(stacked(r.pooled[...]), r.side[0:SQUEEZE, :])) + vec[:, :SQUEEZE]
    r.squeeze[...] = before
    r.send(r.squeeze)
    opened = folded(dot(stacked(before * sigmoid(before)), r.side[SQUEEZE : 2 * SQUEEZE, :]))
    r.excite[...] = sigmoid(opened + rows[9:10, :])
    r.send(r.excite)

    def gate(index, carry):
        lanes = chunk_at(index, LANE)
        for tile in range(tiles):
            at = tile_rows(tile)
            scaled = as_tile(r.a[at, lanes]) * r.excite[tile_images(tile), lanes][None]
            r.y[at, lanes] = scaled.reshape(ROWS, LANE).astype(BF16)
        return carry

    lax.fori_loop(0, EXPAND // LANE, gate, 0)
    r.wait(r.w)
    projected = dot_nt(r.y[...], r.w[...])
    r.p[...] = projected
    r.send(r.p)
    moments = pack_moments(column_sum(projected), column_sum(projected * projected), count)
    if with_cross:
        r.wait(r.cross)
        moments = jnp.concatenate([moments, r.cross[...]], axis=0)
    write_alike(r.pay, moments)
    r.send(r.pay)
    r.finish()


def project(d, mats, side, recv, cross, owners):
    count = d.shape[0]
    images = count // MAP
    devices = recv.shape[0]
    ins = dict(
        recv=(recv, LOOSE),
        side=(side, FAR),
        d=(d, CHUNKS),
        w=project_rows(mats),
    )
    rows = moment_rows(WIDTH)
    if cross is not None:
        ins["cross"] = (cross, FAR)
        rows += 16
    return call(
        functools.partial(project_kernel, cross is not None, owners),
        ins,
        dict(
            p=(shape((count, WIDTH)), FAR),
            vec=(shape((8, WIDTH)), FAR),
            pay=(shape((devices, rows, LANE), BF16), FAR),
            norm=(shape((8, EXPAND)), FAR),
            pooled=(shape((images, EXPAND)), FAR),
            excite=(shape((images, EXPAND)), FAR),
            squeeze=(shape((images, SQUEEZE)), FAR),
        ),
        dict(a=vmem((count, EXPAND), F32), y=vmem((count, EXPAND), BF16)),
    )


def residual_kernel(transposed, with_cross, r):
    count = r.p.shape[0]
    r.start()
    r.wait(r.recv, r.vec)
    mean, inverse = read_moments(r.recv, WIDTH, count)
    keep_norm(r.norm, mean, inverse, r.vec[0:1, :], r.vec[1:2, :])
    if with_cross:
        r.cross[...] = read_matrix(r.recv, moment_rows(WIDTH))
        r.send(r.cross)
    r.wait(r.p)
    normed = (r.p[...] - mean) * inverse
    r.normed[...] = normed
    r.wait(r.before)
    result = r.before[...] + (normed * r.vec[0:1, :] + r.vec[1:2, :])
    r.x[...] = result
    r.xb[...] = result.astype(BF16)
    r.send(r.norm, r.normed, r.x, r.xb)
    r.wait(r.w)
    moments, cross = product_moments(
        r.xb, r.w, transposed, r.stat.shape[1], r.left, r.stat, normed.astype(BF16)
    )
    write_with_slices(r.pay, moments, cross)
    r.send(r.pay)
    r.finish()


def residual(x, p, vec, recv, weights, transposed):
    count = x.shape[0]
    devices = recv.shape[0]
    with_cross = recv.shape[1] > moment_rows(WIDTH)
    columns = HEAD if transposed else EXPAND
    where = (slice(0, HEAD), slice(0, WIDTH)) if transposed else (slice(0, WIDTH), slice(None))
    outs = dict(
        x=(shape((count, WIDTH)), FAR),
        xb=(shape((count, WIDTH), BF16), FAR),
        normed=(shape((count, WIDTH)), FAR),
        pay=(shape((devices, 32, LANE), BF16), FAR),
        norm=(shape((8, WIDTH)), FAR),
    )
    if with_cross:
        outs["cross"] = (shape((WIDTH, WIDTH)), FAR)
    return call(
        functools.partial(residual_kernel, transposed, with_cross),
        dict(
            recv=(recv, LOOSE), vec=(vec, FAR), p=(p, FAR), before=(x, FAR), w=(weights, where)
        ),
        outs,
        dict(left=vmem((2 * WIDTH + 16, WIDTH), BF16), stat=vmem((8, columns))),
    )


def head_rows(last_columns):
    pick_row = lax.broadcasted_iota(jnp.int32, (TILE, LANE), 0)
    pick_col = lax.broadcasted_iota(jnp.int32, (TILE, LANE), 1)
    first_col = WIDTH + CLASSES - (HEADPAD - LANE)
    pick = jnp.where((pick_col == pick_row + first_col) & (pick_row < 2), 1.0, 0.0).astype(BF16)
    return dot_nt(pick, last_columns)


def head_kernel(image_count, r):
    count = r.xb.shape[0]
    tiles = count // ROWS
    images = count // MAP
    r.start()
    r.wait(r.recv, r.xb, r.w)
    mean, inverse = read_product_moments(r.recv, r.w[...], True, HEAD, count)
    cross = jnp.sum(r.recv[...].astype(F32)[:, 16:32], axis=0)
    r.wait(r.classifier)
    gain_bias = head_rows(r.classifier[:, LOGITS - LANE :])
    keep_norm(r.norm, mean, inverse, gain_bias[0:1, :], gain_bias[1:2, :])
    r.send(r.norm)

    def features(index, carry):
        at_chunk = chunk_at(index)
        r.h[:, at_chunk] = dot_nt(r.xb[...], r.w[at_chunk, :])
        for part in range(PARTS):
            lanes = chunk_at(index * PARTS + part, LANE)
            scale_row = r.norm[2:3, lanes]
            shift_row = r.norm[3:4, lanes]
            for tile in range(tiles):
                pre = r.h[tile_rows(tile), lanes] * scale_row + shift_row
                active = as_tile(pre * sigmoid(pre))
                r.f[tile_images(tile), lanes] = jnp.sum(active, axis=0) / MAP
        return carry

    lax.fori_loop(0, HEAD // CHUNK, features, 0, unroll=True)
    features_low = r.f[...].astype(BF16)
    classifier = r.classifier[...]
    ids = lax.broadcasted_iota(jnp.int32, (images, LOGITS), 1)
    logits = dot(features_low, classifier) + r.bias[...]
    logits = jnp.where(ids < CLASSES, logits, -1e30)
    row_max = jnp.max(logits, axis=1, keepdims=True)
    log_total = row_max + jnp.log(jnp.sum(jnp.exp(logits - row_max), axis=1, keepdims=True))
    pair = r.mix[...].astype(F32)
    mixing = pair[:, 0:1] / (pair[:, 0:1] + pair[:, 1:2])
    people = lax.broadcasted_iota(jnp.int32, (images, images), 1)
    label_row = jnp.broadcast_to(r.label_row[...].astype(F32), (images, images))
    partner_label = jnp.sum(
        jnp.where(people == r.partner[...], label_row, 0.0), axis=1, keepdims=True
    ).astype(jnp.int32)
    own_hot = jnp.where(ids == r.label_col[...], 1.0, 0.0)
    other_hot = jnp.where(ids == partner_label, 1.0, 0.0)
    own_logit = jnp.sum(own_hot * logits, axis=1, keepdims=True)
    other_logit = jnp.sum(other_hot * logits, axis=1, keepdims=True)
    loss = column_sum(mixing * (log_total - own_logit) + (1.0 - mixing) * (log_total - other_logit))
    grad_logits = (
        jnp.exp(logits - log_total) - mixing * own_hot - (1.0 - mixing) * other_hot
    ) / image_count
    grad_low = grad_logits.astype(BF16)
    r.grad_fc[...] = dot_tn(features_low, grad_low).astype(BF16)
    fc_copy = pltpu.make_async_copy(r.grad_fc, r.grad_head.at[:, pl.ds(WIDTH, LOGITS)], r.part_sem.at[0])
    fc_copy.start()
    r.f[...] = dot_nt(grad_low, classifier) / MAP
    bias_sum = column_sum(grad_logits)
    bias_ids = lax.broadcasted_iota(jnp.int32, (1, LOGITS), 1)
    loss_high = loss.astype(BF16).astype(F32)
    bias_sum = jnp.where(bias_ids == CLASSES, loss_high, bias_sum)
    bias_sum = jnp.where(bias_ids == CLASSES + 1, loss - loss_high, bias_sum)

    def back(index, carry):
        lanes = chunk_at(index, LANE)
        scale_row = r.norm[2:3, lanes]
        shift_row = r.norm[3:4, lanes]
        mean_row = r.norm[0:1, lanes]
        total = jnp.zeros((TILE, LANE), F32)
        weighted = jnp.zeros((TILE, LANE), F32)
        for tile in range(tiles):
            at = tile_rows(tile)
            hidden = r.h[at, lanes]
            pre = hidden * scale_row + shift_row
            gate = sigmoid(pre)
            slope = as_tile(gate * (1.0 + pre * (1.0 - gate)))
            grad = slope * r.f[tile_images(tile), lanes][None]
            total = total + jnp.sum(grad, axis=0)
            weighted = weighted + jnp.sum(grad * as_tile(hidden), axis=0)
            flat = grad.reshape(ROWS, LANE)
            r.dz[at, lanes] = flat.astype(BF16)
            r.q[at, lanes] = (flat * scale_row).astype(BF16)
        r.stat[0:1, lanes] = column_sum(total)
        r.stat[1:2, lanes] = column_sum(weighted) - mean_row * column_sum(total)
        return carry

    lax.fori_loop(0, HEAD // LANE, back, 0)
    r.send(r.dz)
    below = dot(r.q[...], r.w[...])
    r.wait(r.normed)
    rows = fold(
        [
            r.stat[0:1, :], r.stat[1:2, :] * inverse,
            column_sum(below), column_sum(below * r.normed[...]), bias_sum,
        ],
        32,
    )
    write_alike(r.pay, jnp.concatenate([rows, cross], axis=0))
    r.send(r.pay)
    fc_copy.wait()
    r.finish()


def head(xb, head_full, bias, label_col, label_row, partner, mix_pair, normed, recv, image_count):
    count = xb.shape[0]
    images = count // MAP
    devices = recv.shape[0]
    return call(
        functools.partial(head_kernel, image_count),
        dict(
            recv=(recv, LOOSE),
            xb=(xb, FAR),
            bias=(bias, NEAR),
            label_col=(label_col, NEAR),
            label_row=(label_row, NEAR),
            partner=(partner, NEAR),
            mix=(mix_pair, NEAR),
            w=(head_full, (slice(0, HEAD), slice(0, WIDTH))),
            classifier=(head_full, (slice(0, HEAD), slice(WIDTH, HEADPAD))),
            normed=(normed, FAR),
        ),
        dict(
            dz=(shape((count, HEAD), BF16), FAR),
            pay=(shape((devices, 48, LANE), BF16), FAR),
            norm=(shape((8, HEAD)), FAR),
            grad_head=(shape((HEAD, HEADPAD), BF16), RAW),
        ),
        dict(
            h=vmem((count, HEAD), F32),
            grad_fc=vmem((HEAD, LOGITS), BF16),
            f=vmem((images, HEAD), F32),
            q=vmem((count, HEAD), BF16),
            stat=vmem((8, HEAD), F32),
        ),
    )


def product_back(is_head, row_count, sums, columns, r):
    groups = columns // LANE
    sum_bias = spread(sums, 0, groups)
    sum_gain = spread(sums, groups, groups)
    r.glob[0:1, :] = sum_gain
    r.glob[1:2, :] = sum_bias
    r.glob[2:8, :] = jnp.zeros((6, columns), F32)
    r.send(r.glob)
    r.wait(r.unorm, r.xb, r.w)
    mean = r.unorm[0:1, :]
    scale = r.unorm[2:3, :]
    slant = scale * r.unorm[1:2, :] * (sum_gain / row_count)
    r.coef[0:1, :columns] = slant
    r.coef[1:2, :columns] = mean * slant - scale * (sum_bias / row_count)
    r.xt[...] = r.xb[...].T
    count = r.xb.shape[0]

    def step(index, carry):
        at = chunk_at(index)
        r.chunk(r.dz, index, at).wait()
        if is_head:
            r.h[...] = dot_nt(r.xb[...], r.w[at, :])
        else:
            r.h[...] = dot(r.xb[...], r.w[:, at])
        grad = r.dz[:, at].astype(F32) * r.unorm[2:3, at] - r.h[...] * r.coef[0:1, at] + r.coef[1:2, at]
        low = grad.astype(BF16)
        r.dh[0:count, at] = low
        if is_head:
            r.grad_w[at, :] = dot_tn(low, r.xb[...]).astype(r.grad_w.dtype)
        else:
            r.grad_w[:, at] = dot(r.xt[...], low).astype(r.grad_w.dtype)
        return carry

    lax.fori_loop(0, columns // CHUNK, step, 0, unroll=True)
    return scale * sum_bias, slant


def owner_blocks(r, owners, row_of_owner, taps):
    rows_dev = 2 * WIDTH // owners
    width = EXPAND // owners
    vec_width = VECS // owners
    chunks = EXPAND // CHUNK
    squeeze_sums = jnp.concatenate([r.squeeze_sum[...], jnp.zeros((1, VECS - LANE), F32)], axis=1)
    for owner in range(owners):
        at = slice(owner * width, (owner + 1) * width)
        squeeze_row = squeeze_sums[:, owner * vec_width : (owner + 1) * vec_width]
        squeeze_row = jnp.concatenate([squeeze_row, jnp.zeros((1, width - vec_width), F32)], axis=1)
        pieces = [r.excite_sum[:, at], squeeze_row]
        pieces.append(taps[0:9, at] if taps is not None else jnp.zeros((9, width), F32))
        pieces.append(jnp.zeros((5, width), F32))
        first_row = chunks * rows_dev
        r.grads[owner, first_row : first_row + 2 * SQUEEZE, 0:width] = r.rx[:, at].astype(BF16)
        last_row = first_row + 2 * SQUEEZE
        r.grads[owner, last_row : last_row + 16, 0:width] = jnp.concatenate(pieces, axis=0).astype(BF16)


def gate_kernel(is_head, row_count, owners, r):
    columns = HEAD if is_head else EXPAND
    groups = columns // LANE
    count = r.xb.shape[0]
    tiles = count // ROWS
    rows_dev = 2 * WIDTH // owners
    r.start()
    r.wait(r.recv)
    sums = read_sums(r.recv)
    bias_pull, slant = product_back(is_head, row_count, sums, columns, r)
    if is_head:
        head_copy = pltpu.make_async_copy(r.grad_w, r.grad_head.at[:, pl.ds(0, WIDTH)], r.own_sem.at[0])
        head_copy.start()
        weights = r.w[...].astype(F32)
        column = lax.broadcasted_iota(jnp.int32, (1, WIDTH), 1)
        high, low = halves(jnp.broadcast_to(bias_pull, (TILE, columns)))
        pull = column_sum(dot(high, r.w[...]) + dot(low, r.w[...])) / TILE
        turned = jnp.broadcast_to(slant, (LANE, columns)).T
        slanted = (weights * jnp.concatenate([turned, turned], axis=1)).astype(BF16)
        square = dot_tn(slanted, r.w[...])
        stream = dot(r.dh[0:count, :columns], r.w[...])
        cross = read_matrix(r.recv, 32)
    else:
        r.dh[count : count + WIDTH, :] = (r.w[...].astype(F32) * slant).astype(BF16)
        high, low = halves(bias_pull)
        r.dh[count + WIDTH :, :] = jnp.concatenate(
            [high.astype(F32), low.astype(F32), jnp.zeros((14, columns), F32)], axis=0
        ).astype(BF16)
        product = dot_nt(r.dh[...], r.w[...])
        square = product[count : count + WIDTH]
        pull = column_sum(product[count + WIDTH : count + WIDTH + 2])
        r.wait(r.cross, r.stream_in)
        stream = r.stream_in[...] + product[0:count]
        cross = r.cross[...]
    r.stream[...] = stream
    r.send(r.stream)
    sum_bias = spread(sums, 2 * groups, WIDTH // LANE) - pull
    corrected = column_sum(cross.T * square)
    sum_gain = spread(sums, 2 * groups + WIDTH // LANE, WIDTH // LANE) - corrected
    r.glob3[0:1, :] = sum_gain
    r.glob3[1:2, :] = sum_bias
    if is_head:
        first_row = 2 * groups + 2 * WIDTH // LANE
        r.glob3[2:6, :] = jnp.concatenate(
            [spread(sums, first_row + PARTS * k, PARTS) for k in range(LOGITS // WIDTH)], axis=0
        )
    else:
        r.glob3[2:6, :] = jnp.zeros((4, WIDTH), F32)
    r.glob3[6:8, :] = jnp.zeros((2, WIDTH), F32)
    r.send(r.glob3)
    r.wait(r.norm3, r.normed)
    grad_p = r.norm3[2:3, :] * (
        stream - sum_bias / row_count - r.normed[...] * (sum_gain / row_count)
    )
    r.gp[...] = grad_p.astype(BF16)
    r.gt[...] = r.gp[...].T
    r.wait(r.wp, r.norm2, r.excite)
    half = owners // 2

    def first(index, carry):
        at_chunk = chunk_at(index)
        r.chunk(r.d, index, at_chunk).wait()
        r.h[...] = dot(r.gp[...], r.wp[:, at_chunk])
        for part in range(PARTS):
            lanes = chunk_at(index * PARTS + part, LANE)
            scale_row = r.norm2[2:3, lanes]
            shift_row = r.norm2[3:4, lanes]
            for tile in range(tiles):
                at = tile_rows(tile)
                near = tile_images(tile)
                pre = r.d[at, lanes].astype(F32) * scale_row + shift_row
                gate = sigmoid(pre)
                active = pre * gate
                slope = gate + active - active * gate
                grad = r.h[at, part * LANE : (part + 1) * LANE]
                factor = r.excite[near, lanes]
                r.ge[near, lanes] = jnp.sum(as_tile(grad * active), axis=0)
                r.y[at, lanes] = (as_tile(active) * factor[None]).reshape(ROWS, LANE).astype(BF16)
                r.slope[at, lanes] = slope.astype(r.slope.dtype)
                r.u[at, lanes] = (
                    (as_tile(grad * slope) * factor[None]).reshape(ROWS, LANE).astype(r.u.dtype)
                )
        grad_p_chunk = dot(r.gt[...], r.y[:, at_chunk])
        place = pl.ds(pl.multiple_of(index * rows_dev, rows_dev), rows_dev)
        for owner in range(half):
            cut = slice(owner * rows_dev, (owner + 1) * rows_dev)
            r.grads[half + owner, place, :] = grad_p_chunk[cut, :].astype(BF16)
            if is_head:
                r.grads[owner, place, :] = jnp.zeros((rows_dev, CHUNK), BF16)
            else:
                r.grads[owner, place, :] = r.grad_w[cut, at_chunk]
        return carry

    lax.fori_loop(0, EXPAND // CHUNK, first, 0)
    r.wait(r.pooled, r.squeeze, r.side)
    excite = r.excite[...]
    grad_gate = r.ge[...] * excite * (1.0 - excite)
    before = r.squeeze[...]
    opened = sigmoid(before)
    squeezed = before * opened
    reduce_mat = r.side[0:SQUEEZE, :]
    excite_mat = r.side[SQUEEZE:, :]
    gate_high, gate_low = halves(grad_gate)
    grad_squeezed = folded(dot_nt(jnp.concatenate([gate_high, gate_low], axis=0), excite_mat))
    grad_pre = grad_squeezed * (opened * (1.0 + before * (1.0 - opened)))
    r.pool[...] = folded(dot(stacked(grad_pre), reduce_mat)) / MAP

    squeezed_high, squeezed_low = halves(squeezed)
    pre_high, pre_low = halves(grad_pre)
    pooled_high, pooled_low = halves(r.pooled[...])
    r.rx[SQUEEZE:, :] = dot_tn(
        jnp.concatenate([squeezed_high, squeezed_low, squeezed_high], axis=0),
        jnp.concatenate([gate_high, gate_high, gate_low], axis=0),
    )
    r.rx[0:SQUEEZE, :] = dot_tn(
        jnp.concatenate([pre_high, pre_low, pre_high], axis=0),
        jnp.concatenate([pooled_high, pooled_high, pooled_low], axis=0),
    )
    r.excite_sum[...] = column_sum(grad_gate)
    r.squeeze_sum[...] = jnp.concatenate(
        [column_sum(grad_pre), jnp.zeros((1, LANE - SQUEEZE), F32)], axis=1
    )
    taps = None
    if not is_head:
        r.wait(r.taps)
        taps = r.taps[...]
    owner_blocks(r, owners, half, taps)
    room = r.grads.shape[1]
    place = pl.ds((r.blocks.shape[1] - room) * (not is_head), room)
    blocks_copy = pltpu.make_async_copy(r.grads, r.blocks.at[:, place, :], r.own_sem.at[1])
    blocks_copy.start()

    def second(index, carry):
        for part in range(PARTS):
            lanes = chunk_at(index * PARTS + part, LANE)
            mean_row = r.norm2[0:1, lanes]
            total = jnp.zeros((TILE, LANE), F32)
            weighted = jnp.zeros((TILE, LANE), F32)
            for tile in range(tiles):
                at = tile_rows(tile)
                pool = r.pool[tile_images(tile), lanes]
                grad = as_tile(r.u[at, lanes].astype(F32)) + as_tile(r.slope[at, lanes].astype(F32)) * pool[None]
                total = total + jnp.sum(grad, axis=0)
                weighted = weighted + jnp.sum(grad * as_tile(r.d[at, lanes].astype(F32)), axis=0)
                r.dz2[at, lanes] = grad.reshape(ROWS, LANE).astype(BF16)
            r.stat[0:1, lanes] = column_sum(total)
            r.stat[1:2, lanes] = column_sum(weighted) - mean_row * column_sum(total)
        r.part(r.dz2, index, chunk_at(index)).start()
        return carry

    lax.fori_loop(0, EXPAND // CHUNK, second, 0)
    write_alike(r.pay, fold([r.stat[0:1, :], r.stat[1:2, :] * r.norm2[1:2, :]], 24))
    r.send(r.pay)
    blocks_copy.wait()
    if is_head:
        head_copy.wait()
    r.finish(r.dz2)


def gate_back(is_head, row_count, owners, recv, upper, cross, stream, lower, blocks, extra_room):
    count = upper.xb.shape[0]
    images = count // MAP
    devices = recv.shape[0]
    columns = HEAD if is_head else EXPAND
    block = EXPAND // CHUNK * (2 * WIDTH // owners) + 2 * SQUEEZE + 16
    head_part = (slice(0, HEAD), slice(0, WIDTH))
    ins = dict(
        recv=(recv, LOOSE),
        unorm=(upper.norm, FAR),
        xb=(upper.xb, FAR),
        w=(upper.weights, head_part) if is_head else expand_rows(upper.weights),
        dz=(upper.dz, CHUNKS),
        norm3=(lower.norm3, FAR),
        normed=(lower.normed, FAR),
        norm2=(lower.norm2, FAR),
        wp=project_rows(lower.mats),
        d=(lower.d, CHUNKS),
        excite=(lower.excite, FAR),
        pooled=(lower.pooled, FAR),
        squeeze=(lower.squeeze, FAR),
        side=(lower.side, (slice(0, 2 * SQUEEZE), slice(None))),
    )
    outs = dict(
        dz2=(shape((count, EXPAND), BF16), FAR),
        pay=(shape((devices, 24, LANE), BF16), FAR),
        stream=(shape((count, WIDTH)), FAR),
        blocks=(shape((owners, block * (1 + extra_room), CHUNK), BF16), RAW),
        glob=(shape((8, columns)), FAR),
        glob3=(shape((8, WIDTH)), FAR),
    )
    scratch = dict(
        grads=vmem((owners, block, CHUNK), BF16),
        xt=vmem((WIDTH, count), BF16),
        h=vmem((count, CHUNK), F32),
        coef=vmem((8, EXPAND), F32),
        dh=vmem((count + WIDTH + 16, columns), BF16),
        u=vmem((count, EXPAND), BF16),
        slope=vmem((count, EXPAND), BF16),
        y=vmem((count, EXPAND), BF16),
        gp=vmem((count, WIDTH), BF16),
        gt=vmem((WIDTH, count), BF16),
        ge=vmem((images, EXPAND), F32),
        pool=vmem((images, EXPAND), F32),
        rx=vmem((2 * SQUEEZE, EXPAND), F32),
        excite_sum=vmem((1, EXPAND), F32),
        squeeze_sum=vmem((1, LANE), F32),
        stat=vmem((8, EXPAND), F32),
        own_sem=pltpu.SemaphoreType.DMA((2,)),
    )
    alias = []
    if is_head:
        ins["grad_head_in"] = (upper.grad_head, RAW)
        outs["grad_head"] = (shape((HEAD, HEADPAD), BF16), RAW)
        scratch["grad_w"] = vmem((HEAD, WIDTH), BF16)
        alias.append(("grad_head_in", "grad_head"))
    else:
        ins["cross"] = (cross, FAR)
        ins["stream_in"] = (stream, FAR)
        ins["taps"] = (upper.taps, FAR)
        scratch["grad_w"] = vmem((WIDTH, EXPAND), BF16)
        if blocks is not None:
            ins["blocks_in"] = (blocks, RAW)
            outs["blocks"] = (shape(blocks.shape, BF16), RAW)
            alias.append(("blocks_in", "blocks"))
    return call(functools.partial(gate_kernel, is_head, row_count, owners), ins, outs, scratch, alias)


def tap_kernel(is_first, row_count, r):
    count = r.dz2.shape[0]
    groups = EXPAND // LANE
    r.start()
    r.wait(r.recv)
    sums = read_sums(r.recv)
    sum_bias = spread(sums, 0, groups)
    sum_gain = spread(sums, groups, groups)
    r.glob[0:1, :] = sum_gain
    r.glob[1:2, :] = sum_bias
    r.glob[2:8, :] = jnp.zeros((6, EXPAND), F32)
    r.send(r.glob)
    r.wait(r.side, r.norm2)
    scale2 = r.norm2[2:3, :]
    slant2 = scale2 * r.norm2[1:2, :] * (sum_gain / row_count)
    r.coef[0:9, :] = r.side[...].astype(F32)[0:9, :]
    r.coef[9:10, :] = slant2
    r.coef[10:11, :] = r.norm2[0:1, :] * slant2 - scale2 * (sum_bias / row_count)
    r.wait(r.norm1, r.xb, r.w)

    def step(index, carry):
        at_chunk = chunk_at(index)
        r.chunk(r.dz2, index, at_chunk).wait()
        r.chunk(r.d, index, at_chunk).wait()
        r.h[...] = dot(r.xb[...], r.w[:, at_chunk])
        for part in range(PARTS):
            lanes = chunk_at(index * PARTS + part, LANE)
            near = slice(part * LANE, (part + 1) * LANE)
            taps = [jnp.broadcast_to(r.coef[k : k + 1, lanes], (TILE, LANE)) for k in range(9)]

            def tile_step(tile, sums_in):
                at = chunk_at(tile, ROWS)
                grad_d = as_tile(
                    r.dz2[at, lanes].astype(F32) * r.norm2[2:3, lanes]
                    - r.d[at, lanes].astype(F32) * r.coef[9:10, lanes]
                    + r.coef[10:11, lanes]
                )
                hidden = r.h[at, near]
                pre = hidden * r.norm1[2:3, lanes] + r.norm1[3:4, lanes]
                gate = sigmoid(pre)
                flat = pre * gate
                active = as_tile(flat)
                slope = as_tile(gate + flat - flat * gate)
                hidden = as_tile(hidden)
                grad_a = [None] * MAP
                tap_sums = [None] * 9
                for target, tap, source in TERMS:
                    term = grad_d[target] * taps[tap]
                    grad_a[source] = term if grad_a[source] is None else grad_a[source] + term
                    term = grad_d[target] * active[source]
                    tap_sums[tap] = term if tap_sums[tap] is None else tap_sums[tap] + term
                total, weighted = sums_in[9], sums_in[10]
                grads = []
                for place in range(MAP):
                    grad = grad_a[place] * slope[place]
                    total = total + grad
                    weighted = weighted + grad * hidden[place]
                    grads.append(grad)
                grad = jnp.concatenate(grads, axis=0)
                r.dz[at, lanes] = grad.astype(BF16)
                if not is_first:
                    r.q[at, lanes] = (grad * r.norm1[2:3, lanes]).astype(BF16)
                return (*[sums_in[k] + tap_sums[k] for k in range(9)], total, weighted)

            zero = jnp.zeros((TILE, LANE), F32)
            result = lax.fori_loop(0, count // ROWS, tile_step, (zero,) * 11, unroll=True)
            for k in range(9):
                r.taps[k : k + 1, lanes] = column_sum(result[k])
            total = column_sum(result[9])
            r.stat[0:1, lanes] = total
            r.stat[1:2, lanes] = column_sum(result[10]) - r.norm1[0:1, lanes] * total
        r.part(r.dz, index, at_chunk).start()
        return carry

    lax.fori_loop(0, EXPAND // CHUNK, step, 0)
    r.taps[9:16, :] = jnp.zeros((7, EXPAND), F32)
    r.send(r.taps)
    vectors = [r.stat[0:1, :], r.stat[1:2, :] * r.norm1[1:2, :]]
    if not is_first:
        r.wait(r.normed, r.stream)
        below = r.stream[...] + dot_nt(r.q[...], r.w[...])
        vectors.append(column_sum(below))
        vectors.append(column_sum(below * r.normed[...]))
    write_alike(r.pay, fold(vectors, r.pay.shape[1]))
    r.send(r.pay)
    r.finish(r.dz)


def tap_back(is_first, row_count, recv, dz2, layer, stream, below):
    count = dz2.shape[0]
    devices = recv.shape[0]
    ins = dict(
        recv=(recv, LOOSE),
        side=(layer.side, (slice(2 * SQUEEZE, SIDE_PAD), slice(None))),
        norm2=(layer.norm2, FAR),
        norm1=(layer.norm1, FAR),
        xb=(layer.xb, FAR),
        w=expand_rows(layer.mats),
        dz2=(dz2, CHUNKS),
        d=(layer.d, CHUNKS),
    )
    scratch = dict(
        h=vmem((count, CHUNK), F32),
        coef=vmem((16, EXPAND), F32),
        stat=vmem((8, EXPAND), F32),
    )
    if not is_first:
        ins["stream"] = (stream, FAR)
        ins["normed"] = (below.normed, FAR)
        scratch["q"] = vmem((count, EXPAND), BF16)
    return call(
        functools.partial(tap_kernel, is_first, row_count),
        ins,
        dict(
            dz=(shape((count, EXPAND), BF16), FAR),
            pay=(shape((devices, 24 if is_first else 32, LANE), BF16), FAR),
            taps=(shape((16, EXPAND)), FAR),
            glob=(shape((8, EXPAND)), FAR),
        ),
        scratch,
    )


def last_kernel(row_count, replicas, owners, r):
    r.start()
    r.wait(r.recv)
    product_back(False, row_count, read_sums(r.recv), EXPAND, r)
    half = owners // 2
    part = slice_rows(replicas * owners)
    rows_dev = 2 * WIDTH // owners
    chunks = EXPAND // CHUNK
    if chunks * part % 8:
        r.shares[...] = jnp.zeros(r.shares.shape, F32)
    for device in range(replicas * owners):
        replica, owner = device // owners, device % owners
        first_row = rows_dev * (owner % half) + (2 * replica + owner // half) * part
        for k in range(chunks):
            r.shares[device, k * part : (k + 1) * part, :] = r.grad_w[
                first_row : first_row + part, k * CHUNK : (k + 1) * CHUNK
            ]
    r.wait(r.taps)
    width = EXPAND // owners
    tap_rows = -(-9 * width // CHUNK)
    first_tap = -(-chunks * part // 8) * 8
    for owner in range(owners):
        pieces = [r.taps[k : k + 1, owner * width : (owner + 1) * width] for k in range(9)]
        pieces.append(jnp.zeros((1, tap_rows * CHUNK - 9 * width), F32))
        flat = jnp.concatenate(pieces, axis=1)
        lines = [flat[:, k * CHUNK : (k + 1) * CHUNK] for k in range(tap_rows)]
        lines.append(jnp.zeros((r.shares.shape[1] - first_tap - tap_rows, CHUNK), F32))
        lines = jnp.concatenate(lines, axis=0)
        for replica in range(replicas):
            r.shares[replica * owners + owner, first_tap:, :] = lines
    r.grads[...] = r.shares[...].astype(BF16)
    r.send(r.grads)
    r.finish()


def last_back(row_count, replicas, owners, recv, layer, dz, taps):
    count = dz.shape[0]
    devices = recv.shape[0]
    tap_rows = -(-9 * EXPAND // owners // CHUNK)
    block = -(-EXPAND // CHUNK * slice_rows(devices) // 8) * 8 + 8
    assert tap_rows <= 8
    return call(
        functools.partial(last_kernel, row_count, replicas, owners),
        dict(
            recv=(recv, LOOSE),
            dz=(dz, CHUNKS),
            unorm=(layer.norm1, FAR),
            xb=(layer.xb, FAR),
            w=expand_rows(layer.mats),
            taps=(taps, FAR),
        ),
        dict(
            grads=(shape((devices, block, CHUNK), BF16), FAR),
            glob=(shape((8, EXPAND)), FAR),
        ),
        dict(
            xt=vmem((WIDTH, count), BF16),
            h=vmem((count, CHUNK), F32),
            coef=vmem((8, EXPAND), F32),
            dh=vmem((count, EXPAND), BF16),
            grad_w=vmem((WIDTH, EXPAND), F32),
            shares=vmem((devices, block, CHUNK), F32),
        ),
    )


def lamb_moments(weight, moment_one, moment_two, gradient, decay_mask, step_float):
    first_new = BETA_ONE * moment_one + (1.0 - BETA_ONE) * gradient
    second_new = BETA_TWO * moment_two + (1.0 - BETA_TWO) * gradient * gradient
    corrected = (
        first_new
        / (1.0 - BETA_ONE**step_float)
        / (jnp.sqrt(second_new / (1.0 - BETA_TWO**step_float)) + EPS_ADAM)
    )
    return (first_new, second_new, corrected + DECAY_RATE * decay_mask * weight)


def group_sums(mats, side, head_shard, row_ids):
    rows = jnp.sum(mats * mats, axis=2)
    is_expand = (row_ids < WIDTH)[None, :]
    side_rows = jnp.sum(side * side, axis=2)
    head_cols = jnp.sum(head_shard * head_shard, axis=0)
    per_layer = jnp.stack(
        [
            jnp.sum(jnp.where(is_expand, rows, 0.0), axis=1),
            jnp.sum(jnp.where(is_expand, 0.0, rows), axis=1),
            jnp.sum(side_rows[:, :9], axis=1),
            jnp.sum(side_rows[:, 9 : 9 + SQUEEZE], axis=1),
            jnp.sum(side_rows[:, 9 + SQUEEZE : 9 + 2 * SQUEEZE], axis=1),
        ],
        axis=1,
    )
    tail = jnp.stack([jnp.sum(head_cols[:WIDTH]), jnp.sum(head_cols[WIDTH : WIDTH + CLASSES])])
    return jnp.concatenate([per_layer.reshape(-1), tail])


def rate_maps(trust_ratio, row_ids):
    groups = trust_ratio[: 5 * LAYERS].reshape(LAYERS, 5)
    mats_rate = RATE_MATRIX * jnp.where(row_ids[None, :] < WIDTH, groups[:, 0:1], groups[:, 1:2])
    side_ids = jnp.arange(SIDE)[None, :]
    side_rate = jnp.where(
        side_ids < 9,
        RATE_MATRIX * groups[:, 2:3],
        jnp.where(
            side_ids < 9 + SQUEEZE,
            RATE_MATRIX * groups[:, 3:4],
            jnp.where(side_ids < 9 + 2 * SQUEEZE, RATE_MATRIX * groups[:, 4:5], RATE_VECTOR),
        ),
    )
    col_ids = jnp.arange(HEADCOLS)
    head_rate = jnp.where(
        col_ids < WIDTH,
        RATE_MATRIX * trust_ratio[5 * LAYERS],
        jnp.where(
            col_ids < WIDTH + CLASSES, RATE_MATRIX * trust_ratio[5 * LAYERS + 1], RATE_VECTOR
        ),
    )
    return (mats_rate, side_rate, head_rate)


def exchange(payload):
    return lax.all_to_all(payload, BOTH, 0, 0)


def before(value, *others):
    return lax.optimization_barrier((value, *others))[0]


def spread_over(array, axis):
    copies = jnp.broadcast_to(array[None], (lax.axis_size(axis), *array.shape))
    return lax.all_to_all(copies, axis, 0, 0)


def replica_sum(array, turned=False):
    count = lax.axis_size(REPLICAS)
    steps = [1 << k for k in range(count.bit_length() - 1)]
    total = array
    for step in reversed(steps) if turned else steps:
        other = lax.ppermute(total, REPLICAS, [(k, k ^ step) for k in range(count)])
        total = (total.astype(F32) + other.astype(F32)).astype(BF16)
    return total.astype(F32)


def body(
    images, partner, mix_pair, labels, step,
    layer_mats, layer_side, layer_vecs, head_mat, fc_bias,
    mats_first, mats_second, side_first, side_second, vecs_first, vecs_second,
    head_first, head_second, bias_first, bias_second,
):
    local_images = images.shape[0]
    owners = lax.axis_size(OWNERS)
    replicas = lax.axis_size(REPLICAS)
    devices = owners * replicas
    image_count = float(local_images * devices)
    count = local_images * MAP
    row_count = float(count * devices)
    mine = lax.axis_index(OWNERS)
    side_width = layer_side.shape[2]
    vec_width = layer_vecs.shape[1]
    rows_dev = layer_mats.shape[1]
    half = owners // 2

    def side_as_sent(side, vecs):
        blank = jnp.zeros((side.shape[0], 1, side_width), F32)
        vecs = jnp.pad(vecs, ((0, 0), (0, side_width - vec_width)))[:, None, :]
        pieces = [side[:, 9 : 9 + 2 * SQUEEZE], side[:, :9], side[:, 9 + 2 * SQUEEZE :], vecs, blank]
        return jnp.concatenate(pieces, axis=1).astype(BF16)

    side_rows = -(-SIDE_PAD * side_width // EXPAND)
    side_flat = jnp.pad(side_as_sent(layer_side[:1], layer_vecs[:1]).reshape(-1), (0, side_rows * EXPAND - SIDE_PAD * side_width))
    packed = lax.all_gather(
        jnp.concatenate([layer_mats[0].astype(BF16), side_flat.reshape(side_rows, EXPAND)], axis=0),
        OWNERS, axis=0,
    )
    partner_col = partner[:, None]
    layers = []
    crosses = []
    entry = mix(images.reshape(count, WIDTH), partner_col, mix_pair, devices)
    x, xb = entry.x, entry.xb
    received = exchange(entry.pay)
    shared = share(received).pay
    later_mats, later_side, later_vecs, later_head, _ = lax.optimization_barrier(
        (layer_mats, layer_side, layer_vecs, head_mat, shared)
    )
    mats_all = [None] + [
        lax.all_gather(later_mats[k].astype(BF16), OWNERS, axis=0, tiled=True) for k in range(1, LAYERS)
    ]
    side_room = -(-side_width // CHUNK) * CHUNK
    side_rest = lax.all_gather(
        jnp.pad(side_as_sent(later_side[1:], later_vecs[1:]), ((0, 0), (0, 0), (0, side_room - side_width))), OWNERS, axis=0
    )
    side_rest = jnp.moveaxis(side_rest[..., :side_width], 0, 2).reshape(LAYERS - 1, SIDE_PAD, EXPAND)
    head_full = lax.all_gather(
        jnp.pad(later_head, ((0, 0), (0, HEADPAD - HEADCOLS))).astype(BF16), OWNERS, axis=0, tiled=True
    )

    square = exchange(shared)
    packed = before(packed, shared)
    mats_all[0] = packed
    side_flat = packed[:, rows_dev:].reshape(owners, -1)[:, : SIDE_PAD * side_width]
    side_zero = jnp.moveaxis(side_flat.reshape(owners, SIDE_PAD, side_width), 0, 1).reshape(SIDE_PAD, EXPAND)
    side_all = [side_zero, side_rest[0], side_rest[1]]
    for k in range(LAYERS):
        mats, side = mats_all[k], side_all[k]
        if k:
            received, square = exchange(pay), None
        one = spatial(xb, mats, side, received, square)
        two = project(one.d, mats, side, exchange(one.pay), getattr(one, "cross", None), owners)
        last = k == LAYERS - 1
        three = residual(
            x, two.p, two.vec, exchange(two.pay), head_full if last else mats_all[k + 1], last
        )
        if k:
            crosses.append(three.cross)
        layers.append(
            types.SimpleNamespace(
                xb=xb, d=one.d, norm1=one.norm, norm2=two.norm,
                pooled=two.pooled, excite=two.excite, squeeze=two.squeeze,
                norm3=three.norm, normed=three.normed, mats=mats, weights=mats, side=side,
            )
        )
        x, xb, pay = three.x, three.xb, three.pay
    top = head(
        xb, head_full, jnp.pad(fc_bias, (0, LOGITS - CLASSES))[None], labels[:, None], labels[None, :],
        partner_col, mix_pair, layers[-1].normed, exchange(pay), image_count,
    )

    def to_owner(blocks):
        return lax.psum_scatter(
            blocks.reshape(-1, blocks.shape[-1]), OWNERS, scatter_dimension=0, tiled=True
        )

    upper = types.SimpleNamespace(
        xb=xb, weights=head_full, dz=top.dz, norm=top.norm, grad_head=top.grad_head
    )
    pay = top.pay
    stream = None
    blocks = None
    waiting = []
    globs_one, globs_two, globs_three = [None] * LAYERS, [None] * LAYERS, [None] * LAYERS
    for k in reversed(range(LAYERS)):
        layer = layers[k]
        is_head = k == LAYERS - 1
        gate = gate_back(
            is_head, row_count, owners, exchange(pay), upper,
            None if is_head else crosses[k], stream, layer, blocks, is_head,
        )
        stream = gate.stream
        globs_three[k] = gate.glob3
        if is_head:
            head_glob, bias_loss = gate.glob, gate.glob3[2:6].reshape(LOGITS)
            shard_head = to_owner(gate.grad_head)
            blocks = gate.blocks
        else:
            globs_one[k + 1] = gate.glob
            if k:
                pair = to_owner(gate.blocks)
                blocks = None
            else:
                shard_zero = to_owner(gate.blocks)
        tap = tap_back(
            k == 0, row_count, exchange(gate.pay), gate.dz2, layer, stream, layers[max(k - 1, 0)]
        )
        globs_two[k] = tap.glob
        pay = tap.pay
        if k == 1:
            pay = before(pay, shard_head)
        upper = types.SimpleNamespace(
            xb=layer.xb, weights=layer.mats, dz=tap.dz, norm=layer.norm1, taps=tap.taps
        )
    pay = before(pay, pair)
    received = exchange(pay)
    final = last_back(row_count, replicas, owners, received, layers[0], tap.dz, tap.taps)
    globs_one[0] = final.glob
    shard_head = replica_sum(before(shard_head, received))
    pair = replica_sum(before(pair, received), True)
    room = pair.shape[0] // 2
    shards = [replica_sum(shard_zero), pair[room:], pair[:room]]

    part = slice_rows(devices)
    chunks = EXPAND // CHUNK
    summed = jnp.sum(exchange(final.grads).astype(F32), axis=0)
    first_tap = -(-chunks * part // 8) * 8
    late_taps = summed[first_tap:].reshape(-1)[: 9 * side_width].reshape(9, side_width)
    late = summed[: chunks * part].astype(BF16)
    other = lax.ppermute(late, OWNERS, [(half + k, k) for k in range(half)])
    late = spread_over(jnp.stack([late, other]), REPLICAS)
    late = jnp.moveaxis(late.reshape(replicas, 2, chunks, part, CHUNK), 2, 3)
    late = late.reshape(rows_dev, EXPAND).astype(F32)

    def mats_of(shard):
        rows = shard[: chunks * rows_dev].reshape(chunks, rows_dev, CHUNK)
        return jnp.moveaxis(rows, 0, 1).reshape(rows_dev, EXPAND)

    from_mats = [late] + [mats_of(shard) for shard in shards]
    owns_expand = mine < half
    grad_mats = jnp.stack(
        [jnp.where(owns_expand, from_mats[k], from_mats[k + 1]) for k in range(LAYERS)]
    )

    def own_columns(vector, width):
        return lax.dynamic_slice_in_dim(vector, mine * width, width, axis=-1)

    first_row = chunks * rows_dev
    last_row = first_row + 2 * SQUEEZE
    vec_ids = mine * vec_width + jnp.arange(vec_width)
    side_list, vec_list = [], []
    for k in range(LAYERS):
        shard = shards[k][:, :side_width]
        taps = late_taps if k == 0 else shards[k - 1][last_row + 2 : last_row + 11, :side_width]
        norms_part = own_columns(
            jnp.concatenate([globs_one[k][0:2], globs_two[k][0:2]], axis=0), side_width
        )
        side_list.append(
            jnp.concatenate([taps, shard[first_row : last_row + 1], norms_part], axis=0)
        )
        outer = globs_three[k]
        outer = own_columns(
            jnp.concatenate([jnp.zeros((SQUEEZE,), F32), outer[0], outer[1]]), vec_width
        )
        vec_list.append(jnp.where(vec_ids < SQUEEZE, shard[last_row + 1, :vec_width], outer))
    grad_side = jnp.stack(side_list)
    grad_vecs = jnp.stack(vec_list)
    head_tail = own_columns(head_glob[0:2], head_mat.shape[0]).T
    grad_head = jnp.concatenate([shard_head[:, : WIDTH + CLASSES], head_tail], axis=1)
    grad_bias = bias_loss[:CLASSES]
    loss_value = (bias_loss[CLASSES] + bias_loss[CLASSES + 1]) / image_count

    step_float = step[0].astype(F32)
    side_decay = (jnp.arange(SIDE) < 9 + 2 * SQUEEZE).astype(F32)[None, :, None]
    head_decay = (jnp.arange(HEADCOLS) < WIDTH + CLASSES).astype(F32)[None, :]
    mats_moment, mats_square, mats_dir = lamb_moments(
        layer_mats, mats_first, mats_second, grad_mats, 1.0, step_float
    )
    side_moment, side_square, side_dir = lamb_moments(
        layer_side, side_first, side_second, grad_side, side_decay, step_float
    )
    vecs_moment, vecs_square, vecs_dir = lamb_moments(
        layer_vecs, vecs_first, vecs_second, grad_vecs, 0.0, step_float
    )
    head_moment, head_square, head_dir = lamb_moments(
        head_mat, head_first, head_second, grad_head, head_decay, step_float
    )
    bias_moment, bias_square, bias_dir = lamb_moments(
        fc_bias, bias_first, bias_second, grad_bias, 0.0, step_float
    )
    row_ids = mine * rows_dev + jnp.arange(rows_dev)
    squares = jnp.stack(
        [
            group_sums(layer_mats, layer_side, head_mat, row_ids),
            group_sums(mats_dir, side_dir, head_dir, row_ids),
        ]
    )
    norms = jnp.sqrt(jnp.sum(spread_over(squares, OWNERS), axis=0))
    mats_rate, side_rate, head_rate = rate_maps(norms[0] / norms[1], row_ids)
    mats_new = layer_mats - mats_rate[:, :, None] * mats_dir
    side_new = layer_side - side_rate[:, :, None] * side_dir
    vecs_new = layer_vecs - RATE_VECTOR * vecs_dir
    head_new = head_mat - head_rate[None, :] * head_dir
    bias_new = fc_bias - RATE_VECTOR * bias_dir
    return (
        loss_value,
        mats_new, mats_moment, mats_square,
        side_new, side_moment, side_square,
        vecs_new, vecs_moment, vecs_square,
        head_new, head_moment, head_square,
        bias_new, bias_moment, bias_square,
        norms,
    )


def solution(mesh):
    rows, columns = P(None, OWNERS, None), P(None, None, OWNERS)
    vecs, heads = P(None, OWNERS), P(OWNERS, None)
    return jax.shard_map(
        body,
        mesh=mesh,
        in_specs=(
            P(BOTH, None, None), P(BOTH), P(BOTH, None), P(BOTH), P(),
            rows, columns, vecs, heads, P(),
            rows, rows, columns, columns, vecs, vecs, heads, heads, P(), P(),
        ),
        out_specs=(
            P(),
            rows, rows, rows,
            columns, columns, columns,
            vecs, vecs, vecs,
            heads, heads, heads,
            P(), P(), P(), P(),
        ),
        check_vma=False,
    )
```

```python
import functools
import types

import jax
import jax.numpy as jnp
from jax import lax
from jax.experimental import pallas as pl
from jax.experimental.pallas import tpu as pltpu
from jax.sharding import PartitionSpec as P

WIDTH = 256
EXPAND = 1536
SQUEEZE = 64
HEAD = 1280
CLASSES = 1000
LOGITS = 1024
EDGE = 4
LAYERS = 3
MAP = 16
SIDE = 142
SIDE_PAD = 144
VECS = 576
HEADCOLS = 1258
HEADPAD = 1280

EPS_BN = 0.001
BETA_ONE = 0.9
BETA_TWO = 0.999
EPS_ADAM = 1e-06
DECAY_RATE = 0.01
RATE_MATRIX = 0.5
RATE_VECTOR = 0.25

REPLICAS, OWNERS = BOTH = ("dp", "fsdp")
F32 = jnp.float32
BF16 = jnp.bfloat16
LANE = 128
TILE = 8
ROWS = MAP * TILE
CHUNK = 256
PARTS = CHUNK // LANE
VMEM_BYTES = 60 * 1024 * 1024

NT = (((1,), (1,)), ((), ()))
TN = (((0,), (0,)), ((), ()))


NEAR, FAR, RAW, CHUNKS, LOOSE = range(5)


class Blocks:
    def __init__(self, first, count, rows):
        self.first, self.count, self.rows = first, count, rows


def expand_rows(mats):
    return (mats, half_of(mats, 0))


def project_rows(mats):
    return (mats, half_of(mats, 1))


def half_of(mats, part):
    if mats.ndim == 2:
        return (slice(part * WIDTH, (part + 1) * WIDTH), slice(None))
    count = mats.shape[0] // 2
    return Blocks(part * count, count, WIDTH // count)


class Refs:
    def __init__(self, names, refs, loads, stores):
        for name, ref in zip(names, refs):
            setattr(self, name, ref)
        self.loads = loads
        self.stores = {id(getattr(self, name)): (k, self.far(name)) for k, name in enumerate(stores)}
        self.pending = {}
        self.chunks = {}

    def far(self, name):
        return getattr(self, name + "_far")

    def start(self):
        later = len(self.loads) * (1 + EXPAND // CHUNK)
        for index, (name, where) in enumerate(self.loads):
            near = getattr(self, name)
            if isinstance(where, Blocks):
                copies = []
                for k in range(where.count):
                    source = self.far(name).at[where.first + k, pl.ds(0, where.rows), :]
                    target = near.at[pl.ds(k * where.rows, where.rows), :]
                    copies.append(pltpu.make_async_copy(source, target, self.load_sem.at[later + k]))
                    copies[-1].start()
                later += where.count
                self.pending[id(near)] = copies
                continue
            source = self.far(name) if where is None or where == CHUNKS else self.far(name).at[where]
            if where == CHUNKS:
                self.chunks[id(near)] = (self.far(name), index)
                for turn in range(near.shape[1] // CHUNK):
                    self.chunk(near, turn, pl.ds(turn * CHUNK, CHUNK)).start()
                continue
            copy = pltpu.make_async_copy(source, near, self.load_sem.at[index])
            copy.start()
            self.pending[id(near)] = [copy]

    def chunk(self, near, turn, at):
        far, index = self.chunks[id(near)]
        semaphore = self.load_sem.at[len(self.loads) + index * (EXPAND // CHUNK) + turn]
        return pltpu.make_async_copy(far.at[:, at], near.at[:, at], semaphore)

    def wait(self, *refs):
        for ref in refs:
            for copy in self.pending.pop(id(ref)):
                copy.wait()

    def send(self, *refs):
        for ref in refs:
            index, far = self.stores[id(ref)]
            copy = pltpu.make_async_copy(ref, far, self.store_sem.at[index])
            copy.start()
            self.pending[id(far)] = [copy]

    def part(self, ref, index, at):
        far = self.stores[id(ref)][1]
        return pltpu.make_async_copy(ref.at[:, at], far.at[:, at], self.part_sem.at[index])

    def finish(self, ref=None):
        for key in list(self.pending):
            for copy in self.pending.pop(key):
                copy.wait()
        if ref is not None:
            for index in range(ref.shape[1] // CHUNK):
                self.part(ref, index, pl.ds(index * CHUNK, CHUNK)).wait()


def shape(dims, dtype=F32):
    return jax.ShapeDtypeStruct(dims, dtype)


def vmem(dims, dtype=F32):
    return pltpu.VMEM(dims, dtype)


def call(kernel, ins, outs, scratch, alias=()):
    near, far, loose = (
        pl.BlockSpec(memory_space=space) for space in (pltpu.VMEM, pltpu.HBM, pl.ANY)
    )
    names, arrays, in_specs, loads, stores, extra = [], [], [], [], [], {}
    for name, (array, place) in ins.items():
        arrays.append(array)
        in_specs.append(near if place == NEAR else loose if place == LOOSE else far)
        if place == NEAR or place == RAW:
            names.append(name)
            continue
        names.append(name + "_far")
        dims, where = array.shape, None
        if isinstance(place, Blocks):
            dims, where = (place.count * place.rows, dims[2]), place
        elif place == CHUNKS:
            where = CHUNKS
        elif place != FAR and place != LOOSE:
            starts = [part.indices(size)[:2] for part, size in zip(place, dims)]
            dims = tuple(stop - start for start, stop in starts)
            where = tuple(pl.ds(start, stop - start) for start, stop in starts)
        loads.append((name, where))
        extra[name] = vmem(dims, array.dtype)
    for name, (struct, place) in outs.items():
        names.append(name + "_far" if place == FAR else name)
        if place == FAR:
            stores.append(name)
            extra[name] = vmem(struct.shape, struct.dtype)
    extra.update(scratch)
    extra.update(
        load_sem=pltpu.SemaphoreType.DMA((
            max(len(loads), 1) * (1 + EXPAND // CHUNK)
            + sum(where.count for _, where in loads if isinstance(where, Blocks)),
        )),
        store_sem=pltpu.SemaphoreType.DMA((max(len(stores), 1),)),
        part_sem=pltpu.SemaphoreType.DMA((EXPAND // CHUNK,)),
    )

    def flat(*refs):
        kernel(Refs(names + list(extra), refs, loads, stores))

    results = pl.pallas_call(
        flat,
        out_shape=[struct for struct, _ in outs.values()],
        in_specs=in_specs,
        out_specs=[near if place == NEAR else far for _, place in outs.values()],
        scratch_shapes=list(extra.values()),
        input_output_aliases={list(ins).index(a): list(outs).index(b) for a, b in alias},
        compiler_params=pltpu.CompilerParams(vmem_limit_bytes=VMEM_BYTES),
    )(*arrays)
    return types.SimpleNamespace(**dict(zip(outs, results)))


def dot(left, right):
    return jnp.dot(left, right, preferred_element_type=F32)


def dot_nt(left, right):
    return lax.dot_general(left, right, NT, preferred_element_type=F32)


def dot_tn(left, right):
    return lax.dot_general(left, right, TN, preferred_element_type=F32)


def halves(value):
    high = value.astype(BF16)
    return high, (value - high.astype(F32)).astype(BF16)


def stacked(value):
    return jnp.concatenate(halves(value), axis=0)


def folded(value):
    count = value.shape[0] // 2
    return value[:count] + value[count:]


def sigmoid(value):
    return 0.5 * jnp.tanh(0.5 * value) + 0.5


def chunk_at(index, size=CHUNK):
    return pl.ds(pl.multiple_of(index * size, size), size)


def tile_rows(tile):
    return slice(tile * ROWS, (tile + 1) * ROWS)


def tile_images(tile):
    return slice(tile * TILE, (tile + 1) * TILE)


def as_tile(block):
    return block.reshape(MAP, TILE, LANE)


def spread(rows, first, count):
    return jnp.concatenate([rows[first + k : first + k + 1, :] for k in range(count)], axis=1)


def fold(vectors, rows):
    pieces = [
        vector[:, k * LANE : (k + 1) * LANE]
        for vector in vectors
        for k in range(vector.shape[1] // LANE)
    ]
    if rows > len(pieces):
        pieces.append(jnp.zeros((rows - len(pieces), LANE), F32))
    return jnp.concatenate(pieces, axis=0)


def column_sum(value):
    return jnp.sum(value, axis=0, keepdims=True)


def slice_rows(devices):
    return max(1, WIDTH // devices)


def write_alike(pay_ref, rows):
    pay_ref[...] = jnp.broadcast_to(rows.astype(BF16)[None], pay_ref.shape)


def write_with_slices(pay_ref, rows, matrix):
    devices = pay_ref.shape[0]
    part = slice_rows(devices)
    first = rows.shape[0]
    low = rows.astype(BF16)
    for device in range(devices):
        own = matrix[device * part : (device + 1) * part, :]
        block = jnp.concatenate([own[:, :LANE], own[:, LANE:]], axis=0)
        if 2 * part < 16:
            block = jnp.concatenate([block, jnp.zeros((16 - 2 * part, LANE), F32)], axis=0)
        pay_ref[device, 0:first, :] = low
        pay_ref[device, first : first + 16, :] = block.astype(BF16)


def read_matrix(recv_ref, first):
    devices, rows = recv_ref.shape[:2]
    part = slice_rows(devices)
    if part == TILE:
        values = recv_ref[...].astype(F32)
        left = values[:, first : first + part].reshape(WIDTH, LANE)
        right = values[:, first + part : first + 2 * part].reshape(WIDTH, LANE)
        return jnp.concatenate([left, right], axis=1)
    flat = recv_ref[...].reshape(devices * rows, LANE)
    row = lax.broadcasted_iota(jnp.int32, (WIDTH, devices * rows), 0)
    column = lax.broadcasted_iota(jnp.int32, (WIDTH, devices * rows), 1)
    source = row // part * rows + first + row % part
    left = dot(jnp.where(column == source, 1.0, 0.0).astype(BF16), flat)
    right = dot(jnp.where(column == source + part, 1.0, 0.0).astype(BF16), flat)
    return jnp.concatenate([left, right], axis=1)


def mean_parts(columns):
    return 1 if columns == EXPAND else 2


def moment_rows(columns):
    return -(-(mean_parts(columns) + 1) * columns // LANE // 8) * 8


def centred(total, squares, count):
    return jnp.maximum(squares - total * total / count, 0.0)


def pack_moments(total, squares, count):
    mean = total / count
    high = mean.astype(BF16).astype(F32)
    parts = [high, mean - high][: mean_parts(total.shape[1])]
    return fold(parts + [centred(total, squares, count)], moment_rows(total.shape[1]))


def read_moments(recv_ref, columns, count):
    groups = columns // LANE
    devices = recv_ref.shape[0]
    parts = recv_ref[...].astype(F32)
    given = mean_parts(columns)
    means = parts[:, :groups]
    if given > 1:
        means = means + parts[:, groups : 2 * groups]
    mean = jnp.sum(means, axis=0) / devices
    apart = means - mean[None]
    spread_sum = jnp.sum(parts[:, given * groups : (given + 1) * groups], axis=0) / count
    variance = (spread_sum + jnp.sum(apart * apart, axis=0)) / devices
    return spread(mean, 0, groups), lax.rsqrt(spread(variance, 0, groups) + EPS_BN)


def product_means(recv_ref, weights, transposed, count):
    devices, rows = recv_ref.shape[:2]
    values = recv_ref[...]
    flat = values.reshape(devices * rows, LANE)
    row = lax.broadcasted_iota(jnp.int32, (devices, devices * rows), 0)
    column = lax.broadcasted_iota(jnp.int32, (devices, devices * rows), 1) - row * rows
    left = dot(jnp.where((column == 0) | (column == 2), 1.0, 0.0).astype(BF16), flat)
    right = dot(jnp.where((column == 1) | (column == 3), 1.0, 0.0).astype(BF16), flat)
    sums = stacked(jnp.concatenate([left, right], axis=1) / count)
    return folded(dot_nt(sums, weights) if transposed else dot(sums, weights))


def read_square_moments(recv_ref, square_ref, w_ref, left_ref, stat_ref, count):
    devices = recv_ref.shape[0]
    means = product_means(recv_ref, w_ref[...], False, count)
    mean = column_sum(means) / devices
    apart = means - mean
    left_ref[...] = jnp.concatenate(
        [read_matrix(square_ref, 0), read_matrix(square_ref, 16)], axis=0
    ).astype(BF16)

    def step(index, carry):
        at = chunk_at(index)
        weights = w_ref[:, at]
        squares = column_sum(folded(dot(left_ref[...], weights)) * weights.astype(F32))
        stat_ref[0:1, at] = jnp.maximum(squares, 0.0)
        return carry

    lax.fori_loop(0, w_ref.shape[1] // CHUNK, step, 0, unroll=True)
    variance = (stat_ref[0:1, :] / count + column_sum(apart * apart)) / devices
    return mean, lax.rsqrt(variance + EPS_BN)


def read_product_moments(recv_ref, weights, transposed, columns, count):
    devices = recv_ref.shape[0]
    values = recv_ref[...]
    means = product_means(recv_ref, weights, transposed, count)
    mean = column_sum(means) / devices
    apart = means - mean
    squares = jnp.sum(values.astype(F32), axis=0)
    variance = (spread(squares, 4, columns // LANE) / count + column_sum(apart * apart)) / devices
    return mean, lax.rsqrt(variance + EPS_BN)


def read_sums(recv_ref):
    return jnp.sum(recv_ref[...].astype(F32), axis=0)


def keep_norm(norm_ref, mean, inverse, gain, bias):
    scale = inverse * gain
    norm_ref[0:1, :] = mean
    norm_ref[1:2, :] = inverse
    norm_ref[2:3, :] = scale
    norm_ref[3:4, :] = bias - mean * scale
    norm_ref[4:8, :] = jnp.zeros((4, norm_ref.shape[1]), F32)


def product_moments(x_ref, w_ref, transposed, columns, left_ref, stat_ref, beside):
    count = x_ref.shape[0]
    values = x_ref[...]
    product = dot_tn(jnp.concatenate([values, beside], axis=1), values)
    square, cross = product[:WIDTH], product[WIDTH:]
    sums = column_sum(values.astype(F32))
    left_ref[0 : 2 * WIDTH, :] = stacked(square)
    tail = jnp.concatenate([half.astype(F32) for half in halves(sums)] + [jnp.zeros((14, WIDTH), F32)], axis=0)
    left_ref[2 * WIDTH :, :] = tail.astype(BF16)

    def step(index, carry):
        at = chunk_at(index)
        weights = w_ref[at, :].T if transposed else w_ref[:, at]
        product = dot(left_ref[...], weights)
        total = column_sum(product[2 * WIDTH : 2 * WIDTH + 2])
        squares = column_sum(folded(product[: 2 * WIDTH]) * weights.astype(F32))
        stat_ref[0:1, at] = jnp.maximum(squares - total * total / count, 0.0)
        return carry

    lax.fori_loop(0, columns // CHUNK, step, 0, unroll=True)
    high = sums.astype(BF16).astype(F32)
    return fold([high, sums - high, stat_ref[0:1, :]], 16), cross


def mix_kernel(r):
    count = r.images.shape[0]
    pixels = r.images[...]
    row = lax.broadcasted_iota(jnp.int32, (ROWS, count), 0)
    column = lax.broadcasted_iota(jnp.int32, (ROWS, count), 1)
    place = lax.shift_right_logical(row, 3)
    inside = jnp.bitwise_and(row, 7)
    pair = r.mix[...].astype(F32)
    mixing = pair[:, 0:1] / (pair[:, 0:1] + pair[:, 1:2])
    for tile in range(count // ROWS):
        near = tile_images(tile)
        other = jnp.concatenate([r.partner[near, :]] * MAP, axis=0)
        weight = jnp.concatenate([mixing[near, :]] * MAP, axis=0)
        own_hot = jnp.where(column == (tile * TILE + inside) * MAP + place, 1.0, 0.0).astype(BF16)
        other_hot = jnp.where(column == other * MAP + place, 1.0, 0.0).astype(BF16)
        mixed = weight * dot(own_hot, pixels) + (1.0 - weight) * dot(other_hot, pixels)
        r.x[tile_rows(tile), :] = mixed
    r.xb[...] = r.x[...].astype(BF16)
    r.send(r.x, r.xb)
    low = r.xb[...]
    sums = column_sum(low.astype(F32))
    padded = jnp.concatenate([sums, jnp.zeros((TILE - 1, WIDTH), F32)], axis=0)
    outer = lax.dot_general(
        padded, padded, TN, preferred_element_type=F32, precision=lax.Precision.HIGHEST
    )
    square = dot_tn(low, low) - outer / count
    high = sums.astype(BF16).astype(F32)
    rows = fold([high, sums - high], 8)
    devices = r.pay.shape[0]
    part = slice_rows(devices)
    for device in range(devices):
        own = square[device * part : (device + 1) * part, :]
        block = [rows, own[:, :LANE], own[:, LANE:]]
        if 2 * part < 16:
            block.append(jnp.zeros((16 - 2 * part, LANE), F32))
        r.pay[device, :, :] = jnp.concatenate(block, axis=0).astype(BF16)
    r.send(r.pay)
    r.finish()


def mix(images, partner, mix_pair, devices):
    dims = images.shape
    return call(
        mix_kernel,
        dict(images=(images, NEAR), partner=(partner, NEAR), mix=(mix_pair, NEAR)),
        dict(
            x=(shape(dims), FAR),
            xb=(shape(dims, BF16), FAR),
            pay=(shape((devices, 24, LANE), BF16), FAR),
        ),
        {},
    )


def share_kernel(r):
    r.start()
    r.wait(r.recv)
    high, low = halves(jnp.sum(r.recv[...].astype(F32), axis=0)[8:24])
    write_alike(r.pay, jnp.concatenate([high.astype(F32), low.astype(F32)], axis=0))
    r.send(r.pay)
    r.finish()


def share(recv):
    return call(
        share_kernel,
        dict(recv=(recv, LOOSE)),
        dict(pay=(shape((recv.shape[0], 32, LANE), BF16), FAR)),
        {},
    )


def tap_terms():
    for row in range(EDGE):
        for col in range(EDGE):
            for row_shift in range(3):
                for col_shift in range(3):
                    from_row, from_col = row + row_shift - 1, col + col_shift - 1
                    if 0 <= from_row < EDGE and 0 <= from_col < EDGE:
                        yield EDGE * row + col, 3 * row_shift + col_shift, EDGE * from_row + from_col


TERMS = list(tap_terms())


def spatial_kernel(from_square, r):
    count = r.xb.shape[0]
    r.start()
    r.wait(r.recv, r.side, r.w, r.xb)
    rows = r.side[...].astype(F32)
    r.taps[0:9, :] = rows[0:9, :]
    if from_square:
        r.wait(r.square)
        mean, inverse = read_square_moments(r.recv, r.square, r.w, r.left, r.stat, count)
    else:
        mean, inverse = read_product_moments(r.recv, r.w[...], False, EXPAND, count)
    keep_norm(r.norm, mean, inverse, rows[10:11, :], rows[11:12, :])
    r.send(r.norm)
    if not from_square:
        r.cross[...] = jnp.sum(r.recv[...].astype(F32)[:, 16:32], axis=0)
        r.send(r.cross)

    def step(index, carry):
        at_chunk = chunk_at(index)
        r.h[...] = dot(r.xb[...], r.w[:, at_chunk])
        for part in range(PARTS):
            lanes = chunk_at(index * PARTS + part, LANE)
            taps = [jnp.broadcast_to(r.taps[k : k + 1, lanes], (TILE, LANE)) for k in range(9)]
            scale_row = r.norm[2:3, lanes]
            shift_row = r.norm[3:4, lanes]

            def tile_step(tile, sums):
                at = chunk_at(tile, ROWS)
                pre = r.h[at, part * LANE : (part + 1) * LANE] * scale_row + shift_row
                active = as_tile(pre * sigmoid(pre))
                result = [None] * MAP
                for target, tap, source in TERMS:
                    term = active[source] * taps[tap]
                    result[target] = term if result[target] is None else result[target] + term
                total, squares = sums
                for value in result:
                    total = total + value
                    squares = squares + value * value
                r.d[at, lanes] = jnp.concatenate(result, axis=0).astype(BF16)
                return total, squares

            zero = jnp.zeros((TILE, LANE), F32)
            total, squares = lax.fori_loop(0, count // ROWS, tile_step, (zero, zero), unroll=True)
            r.stat[0:1, lanes] = column_sum(total)
            r.stat[1:2, lanes] = column_sum(squares)
        r.part(r.d, index, at_chunk).start()
        return carry

    lax.fori_loop(0, EXPAND // CHUNK, step, 0)
    write_alike(r.pay, pack_moments(r.stat[0:1, :], r.stat[1:2, :], count))
    r.send(r.pay)
    r.finish(r.d)


def spatial(xb, mats, side, recv, square):
    count = xb.shape[0]
    devices = recv.shape[0]
    outs = dict(
        d=(shape((count, EXPAND), BF16), FAR),
        pay=(shape((devices, moment_rows(EXPAND), LANE), BF16), FAR),
        norm=(shape((8, EXPAND)), FAR),
    )
    ins = dict(
        recv=(recv, LOOSE),
        side=(side, (slice(2 * SQUEEZE, SIDE_PAD), slice(None))),
        xb=(xb, FAR),
        w=expand_rows(mats),
    )
    if square is None:
        outs["cross"] = (shape((16, LANE)), FAR)
    else:
        ins["square"] = (square, LOOSE)
    return call(
        functools.partial(spatial_kernel, square is not None),
        ins,
        outs,
        dict(
            left=vmem((2 * WIDTH, WIDTH), BF16),
            h=vmem((count, CHUNK), F32),
            taps=vmem((16, EXPAND), F32),
            stat=vmem((8, EXPAND), F32),
        ),
    )


def project_kernel(with_cross, owners, r):
    count = r.d.shape[0]
    tiles = count // ROWS
    r.start()
    r.wait(r.recv)
    mean, inverse = read_moments(r.recv, EXPAND, count)
    r.wait(r.side)
    rows = r.side[2 * SQUEEZE : SIDE_PAD, :].astype(F32)
    keep_norm(r.norm, mean, inverse, rows[12:13, :], rows[13:14, :])
    r.send(r.norm)
    width, vec_width = EXPAND // owners, VECS // owners
    vec = jnp.concatenate(
        [rows[14:15, k * width : k * width + vec_width] for k in range(owners)], axis=1
    )
    r.vec[...] = jnp.concatenate(
        [vec[:, SQUEEZE : SQUEEZE + WIDTH], vec[:, SQUEEZE + WIDTH :], jnp.zeros((6, WIDTH), F32)], axis=0
    )
    r.send(r.vec)

    def activate(index, carry):
        r.chunk(r.d, index, chunk_at(index)).wait()
        for part in range(PARTS):
            lanes = chunk_at(index * PARTS + part, LANE)
            scale_row = r.norm[2:3, lanes]
            shift_row = r.norm[3:4, lanes]
            for tile in range(tiles):
                at = tile_rows(tile)
                pre = r.d[at, lanes].astype(F32) * scale_row + shift_row
                active = pre * sigmoid(pre)
                r.a[at, lanes] = active
                r.pooled[tile_images(tile), lanes] = jnp.sum(as_tile(active), axis=0) / MAP
        return carry

    lax.fori_loop(0, EXPAND // CHUNK, activate, 0)
    r.send(r.pooled)
    before = folded(dot_nt(stacked(r.pooled[...]), r.side[0:SQUEEZE, :])) + vec[:, :SQUEEZE]
    r.squeeze[...] = before
    r.send(r.squeeze)
    opened = folded(dot(stacked(before * sigmoid(before)), r.side[SQUEEZE : 2 * SQUEEZE, :]))
    r.excite[...] = sigmoid(opened + rows[9:10, :])
    r.send(r.excite)

    def gate(index, carry):
        lanes = chunk_at(index, LANE)
        for tile in range(tiles):
            at = tile_rows(tile)
            scaled = as_tile(r.a[at, lanes]) * r.excite[tile_images(tile), lanes][None]
            r.y[at, lanes] = scaled.reshape(ROWS, LANE).astype(BF16)
        return carry

    lax.fori_loop(0, EXPAND // LANE, gate, 0)
    r.wait(r.w)
    projected = dot_nt(r.y[...], r.w[...])
    r.p[...] = projected
    r.send(r.p)
    moments = pack_moments(column_sum(projected), column_sum(projected * projected), count)
    if with_cross:
        r.wait(r.cross)
        moments = jnp.concatenate([moments, r.cross[...]], axis=0)
    write_alike(r.pay, moments)
    r.send(r.pay)
    r.finish()


def project(d, mats, side, recv, cross, owners):
    count = d.shape[0]
    images = count // MAP
    devices = recv.shape[0]
    ins = dict(
        recv=(recv, LOOSE),
        side=(side, FAR),
        d=(d, CHUNKS),
        w=project_rows(mats),
    )
    rows = moment_rows(WIDTH)
    if cross is not None:
        ins["cross"] = (cross, FAR)
        rows += 16
    return call(
        functools.partial(project_kernel, cross is not None, owners),
        ins,
        dict(
            p=(shape((count, WIDTH)), FAR),
            vec=(shape((8, WIDTH)), FAR),
            pay=(shape((devices, rows, LANE), BF16), FAR),
            norm=(shape((8, EXPAND)), FAR),
            pooled=(shape((images, EXPAND)), FAR),
            excite=(shape((images, EXPAND)), FAR),
            squeeze=(shape((images, SQUEEZE)), FAR),
        ),
        dict(a=vmem((count, EXPAND), F32), y=vmem((count, EXPAND), BF16)),
    )


def residual_kernel(transposed, with_cross, r):
    count = r.p.shape[0]
    r.start()
    r.wait(r.recv, r.vec)
    mean, inverse = read_moments(r.recv, WIDTH, count)
    keep_norm(r.norm, mean, inverse, r.vec[0:1, :], r.vec[1:2, :])
    if with_cross:
        r.cross[...] = read_matrix(r.recv, moment_rows(WIDTH))
        r.send(r.cross)
    r.wait(r.p)
    normed = (r.p[...] - mean) * inverse
    r.normed[...] = normed
    r.wait(r.before)
    result = r.before[...] + (normed * r.vec[0:1, :] + r.vec[1:2, :])
    r.x[...] = result
    r.xb[...] = result.astype(BF16)
    r.send(r.norm, r.normed, r.x, r.xb)
    r.wait(r.w)
    moments, cross = product_moments(
        r.xb, r.w, transposed, r.stat.shape[1], r.left, r.stat, normed.astype(BF16)
    )
    write_with_slices(r.pay, moments, cross)
    r.send(r.pay)
    r.finish()


def residual(x, p, vec, recv, weights, transposed):
    count = x.shape[0]
    devices = recv.shape[0]
    with_cross = recv.shape[1] > moment_rows(WIDTH)
    columns = HEAD if transposed else EXPAND
    where = (slice(0, HEAD), slice(0, WIDTH)) if transposed else (slice(0, WIDTH), slice(None))
    outs = dict(
        x=(shape((count, WIDTH)), FAR),
        xb=(shape((count, WIDTH), BF16), FAR),
        normed=(shape((count, WIDTH)), FAR),
        pay=(shape((devices, 32, LANE), BF16), FAR),
        norm=(shape((8, WIDTH)), FAR),
    )
    if with_cross:
        outs["cross"] = (shape((WIDTH, WIDTH)), FAR)
    return call(
        functools.partial(residual_kernel, transposed, with_cross),
        dict(
            recv=(recv, LOOSE), vec=(vec, FAR), p=(p, FAR), before=(x, FAR), w=(weights, where)
        ),
        outs,
        dict(left=vmem((2 * WIDTH + 16, WIDTH), BF16), stat=vmem((8, columns))),
    )


def head_rows(last_columns):
    pick_row = lax.broadcasted_iota(jnp.int32, (TILE, LANE), 0)
    pick_col = lax.broadcasted_iota(jnp.int32, (TILE, LANE), 1)
    first_col = WIDTH + CLASSES - (HEADPAD - LANE)
    pick = jnp.where((pick_col == pick_row + first_col) & (pick_row < 2), 1.0, 0.0).astype(BF16)
    return dot_nt(pick, last_columns)


def head_kernel(image_count, r):
    count = r.xb.shape[0]
    tiles = count // ROWS
    images = count // MAP
    r.start()
    r.wait(r.recv, r.xb, r.w)
    mean, inverse = read_product_moments(r.recv, r.w[...], True, HEAD, count)
    cross = jnp.sum(r.recv[...].astype(F32)[:, 16:32], axis=0)
    r.wait(r.classifier)
    gain_bias = head_rows(r.classifier[:, LOGITS - LANE :])
    keep_norm(r.norm, mean, inverse, gain_bias[0:1, :], gain_bias[1:2, :])
    r.send(r.norm)

    def features(index, carry):
        at_chunk = chunk_at(index)
        r.h[:, at_chunk] = dot_nt(r.xb[...], r.w[at_chunk, :])
        for part in range(PARTS):
            lanes = chunk_at(index * PARTS + part, LANE)
            scale_row = r.norm[2:3, lanes]
            shift_row = r.norm[3:4, lanes]
            for tile in range(tiles):
                pre = r.h[tile_rows(tile), lanes] * scale_row + shift_row
                active = as_tile(pre * sigmoid(pre))
                r.f[tile_images(tile), lanes] = jnp.sum(active, axis=0) / MAP
        return carry

    lax.fori_loop(0, HEAD // CHUNK, features, 0, unroll=True)
    features_low = r.f[...].astype(BF16)
    classifier = r.classifier[...]
    ids = lax.broadcasted_iota(jnp.int32, (images, LOGITS), 1)
    logits = dot(features_low, classifier) + r.bias[...]
    logits = jnp.where(ids < CLASSES, logits, -1e30)
    row_max = jnp.max(logits, axis=1, keepdims=True)
    log_total = row_max + jnp.log(jnp.sum(jnp.exp(logits - row_max), axis=1, keepdims=True))
    pair = r.mix[...].astype(F32)
    mixing = pair[:, 0:1] / (pair[:, 0:1] + pair[:, 1:2])
    people = lax.broadcasted_iota(jnp.int32, (images, images), 1)
    label_row = jnp.broadcast_to(r.label_row[...].astype(F32), (images, images))
    partner_label = jnp.sum(
        jnp.where(people == r.partner[...], label_row, 0.0), axis=1, keepdims=True
    ).astype(jnp.int32)
    own_hot = jnp.where(ids == r.label_col[...], 1.0, 0.0)
    other_hot = jnp.where(ids == partner_label, 1.0, 0.0)
    own_logit = jnp.sum(own_hot * logits, axis=1, keepdims=True)
    other_logit = jnp.sum(other_hot * logits, axis=1, keepdims=True)
    loss = column_sum(mixing * (log_total - own_logit) + (1.0 - mixing) * (log_total - other_logit))
    grad_logits = (
        jnp.exp(logits - log_total) - mixing * own_hot - (1.0 - mixing) * other_hot
    ) / image_count
    grad_low = grad_logits.astype(BF16)
    r.grad_fc[...] = dot_tn(features_low, grad_low).astype(BF16)
    fc_copy = pltpu.make_async_copy(r.grad_fc, r.grad_head.at[:, pl.ds(WIDTH, LOGITS)], r.part_sem.at[0])
    fc_copy.start()
    r.f[...] = dot_nt(grad_low, classifier) / MAP
    bias_sum = column_sum(grad_logits)
    bias_ids = lax.broadcasted_iota(jnp.int32, (1, LOGITS), 1)
    loss_high = loss.astype(BF16).astype(F32)
    bias_sum = jnp.where(bias_ids == CLASSES, loss_high, bias_sum)
    bias_sum = jnp.where(bias_ids == CLASSES + 1, loss - loss_high, bias_sum)

    def back(index, carry):
        lanes = chunk_at(index, LANE)
        scale_row = r.norm[2:3, lanes]
        shift_row = r.norm[3:4, lanes]
        mean_row = r.norm[0:1, lanes]
        total = jnp.zeros((TILE, LANE), F32)
        weighted = jnp.zeros((TILE, LANE), F32)
        for tile in range(tiles):
            at = tile_rows(tile)
            hidden = r.h[at, lanes]
            pre = hidden * scale_row + shift_row
            gate = sigmoid(pre)
            slope = as_tile(gate * (1.0 + pre * (1.0 - gate)))
            grad = slope * r.f[tile_images(tile), lanes][None]
            total = total + jnp.sum(grad, axis=0)
            weighted = weighted + jnp.sum(grad * as_tile(hidden), axis=0)
            flat = grad.reshape(ROWS, LANE)
            r.dz[at, lanes] = flat.astype(BF16)
            r.q[at, lanes] = (flat * scale_row).astype(BF16)
        r.stat[0:1, lanes] = column_sum(total)
        r.stat[1:2, lanes] = column_sum(weighted) - mean_row * column_sum(total)
        return carry

    lax.fori_loop(0, HEAD // LANE, back, 0)
    r.send(r.dz)
    below = dot(r.q[...], r.w[...])
    r.wait(r.normed)
    rows = fold(
        [
            r.stat[0:1, :], r.stat[1:2, :] * inverse,
            column_sum(below), column_sum(below * r.normed[...]), bias_sum,
        ],
        32,
    )
    write_alike(r.pay, jnp.concatenate([rows, cross], axis=0))
    r.send(r.pay)
    fc_copy.wait()
    r.finish()


def head(xb, head_full, bias, label_col, label_row, partner, mix_pair, normed, recv, image_count):
    count = xb.shape[0]
    images = count // MAP
    devices = recv.shape[0]
    return call(
        functools.partial(head_kernel, image_count),
        dict(
            recv=(recv, LOOSE),
            xb=(xb, FAR),
            bias=(bias, NEAR),
            label_col=(label_col, NEAR),
            label_row=(label_row, NEAR),
            partner=(partner, NEAR),
            mix=(mix_pair, NEAR),
            w=(head_full, (slice(0, HEAD), slice(0, WIDTH))),
            classifier=(head_full, (slice(0, HEAD), slice(WIDTH, HEADPAD))),
            normed=(normed, FAR),
        ),
        dict(
            dz=(shape((count, HEAD), BF16), FAR),
            pay=(shape((devices, 48, LANE), BF16), FAR),
            norm=(shape((8, HEAD)), FAR),
            grad_head=(shape((HEAD, HEADPAD), BF16), RAW),
        ),
        dict(
            h=vmem((count, HEAD), F32),
            grad_fc=vmem((HEAD, LOGITS), BF16),
            f=vmem((images, HEAD), F32),
            q=vmem((count, HEAD), BF16),
            stat=vmem((8, HEAD), F32),
        ),
    )


def product_back(is_head, row_count, sums, columns, r):
    groups = columns // LANE
    sum_bias = spread(sums, 0, groups)
    sum_gain = spread(sums, groups, groups)
    r.glob[0:1, :] = sum_gain
    r.glob[1:2, :] = sum_bias
    r.glob[2:8, :] = jnp.zeros((6, columns), F32)
    r.send(r.glob)
    r.wait(r.unorm, r.xb, r.w)
    mean = r.unorm[0:1, :]
    scale = r.unorm[2:3, :]
    slant = scale * r.unorm[1:2, :] * (sum_gain / row_count)
    r.coef[0:1, :columns] = slant
    r.coef[1:2, :columns] = mean * slant - scale * (sum_bias / row_count)
    r.xt[...] = r.xb[...].T
    count = r.xb.shape[0]

    def step(index, carry):
        at = chunk_at(index)
        r.chunk(r.dz, index, at).wait()
        if is_head:
            r.h[...] = dot_nt(r.xb[...], r.w[at, :])
        else:
            r.h[...] = dot(r.xb[...], r.w[:, at])
        grad = r.dz[:, at].astype(F32) * r.unorm[2:3, at] - r.h[...] * r.coef[0:1, at] + r.coef[1:2, at]
        low = grad.astype(BF16)
        r.dh[0:count, at] = low
        if is_head:
            r.grad_w[at, :] = dot_tn(low, r.xb[...]).astype(r.grad_w.dtype)
        else:
            r.grad_w[:, at] = dot(r.xt[...], low).astype(r.grad_w.dtype)
        return carry

    lax.fori_loop(0, columns // CHUNK, step, 0, unroll=True)
    return scale * sum_bias, slant


def owner_blocks(r, owners, row_of_owner, taps):
    rows_dev = 2 * WIDTH // owners
    width = EXPAND // owners
    vec_width = VECS // owners
    chunks = EXPAND // CHUNK
    squeeze_sums = jnp.concatenate([r.squeeze_sum[...], jnp.zeros((1, VECS - LANE), F32)], axis=1)
    for owner in range(owners):
        at = slice(owner * width, (owner + 1) * width)
        squeeze_row = squeeze_sums[:, owner * vec_width : (owner + 1) * vec_width]
        squeeze_row = jnp.concatenate([squeeze_row, jnp.zeros((1, width - vec_width), F32)], axis=1)
        pieces = [r.excite_sum[:, at], squeeze_row]
        pieces.append(taps[0:9, at] if taps is not None else jnp.zeros((9, width), F32))
        pieces.append(jnp.zeros((5, width), F32))
        first_row = chunks * rows_dev
        r.grads[owner, first_row : first_row + 2 * SQUEEZE, 0:width] = r.rx[:, at].astype(BF16)
        last_row = first_row + 2 * SQUEEZE
        r.grads[owner, last_row : last_row + 16, 0:width] = jnp.concatenate(pieces, axis=0).astype(BF16)


def gate_kernel(is_head, row_count, owners, r):
    columns = HEAD if is_head else EXPAND
    groups = columns // LANE
    count = r.xb.shape[0]
    tiles = count // ROWS
    rows_dev = 2 * WIDTH // owners
    r.start()
    r.wait(r.recv)
    sums = read_sums(r.recv)
    bias_pull, slant = product_back(is_head, row_count, sums, columns, r)
    if is_head:
        head_copy = pltpu.make_async_copy(r.grad_w, r.grad_head.at[:, pl.ds(0, WIDTH)], r.own_sem.at[0])
        head_copy.start()
        weights = r.w[...].astype(F32)
        column = lax.broadcasted_iota(jnp.int32, (1, WIDTH), 1)
        high, low = halves(jnp.broadcast_to(bias_pull, (TILE, columns)))
        pull = column_sum(dot(high, r.w[...]) + dot(low, r.w[...])) / TILE
        turned = jnp.broadcast_to(slant, (LANE, columns)).T
        slanted = (weights * jnp.concatenate([turned, turned], axis=1)).astype(BF16)
        square = dot_tn(slanted, r.w[...])
        stream = dot(r.dh[0:count, :columns], r.w[...])
        cross = read_matrix(r.recv, 32)
    else:
        r.dh[count : count + WIDTH, :] = (r.w[...].astype(F32) * slant).astype(BF16)
        high, low = halves(bias_pull)
        r.dh[count + WIDTH :, :] = jnp.concatenate(
            [high.astype(F32), low.astype(F32), jnp.zeros((14, columns), F32)], axis=0
        ).astype(BF16)
        product = dot_nt(r.dh[...], r.w[...])
        square = product[count : count + WIDTH]
        pull = column_sum(product[count + WIDTH : count + WIDTH + 2])
        r.wait(r.cross, r.stream_in)
        stream = r.stream_in[...] + product[0:count]
        cross = r.cross[...]
    r.stream[...] = stream
    r.send(r.stream)
    sum_bias = spread(sums, 2 * groups, WIDTH // LANE) - pull
    corrected = column_sum(cross.T * square)
    sum_gain = spread(sums, 2 * groups + WIDTH // LANE, WIDTH // LANE) - corrected
    r.glob3[0:1, :] = sum_gain
    r.glob3[1:2, :] = sum_bias
    if is_head:
        first_row = 2 * groups + 2 * WIDTH // LANE
        r.glob3[2:6, :] = jnp.concatenate(
            [spread(sums, first_row + PARTS * k, PARTS) for k in range(LOGITS // WIDTH)], axis=0
        )
    else:
        r.glob3[2:6, :] = jnp.zeros((4, WIDTH), F32)
    r.glob3[6:8, :] = jnp.zeros((2, WIDTH), F32)
    r.send(r.glob3)
    r.wait(r.norm3, r.normed)
    grad_p = r.norm3[2:3, :] * (
        stream - sum_bias / row_count - r.normed[...] * (sum_gain / row_count)
    )
    r.gp[...] = grad_p.astype(BF16)
    r.gt[...] = r.gp[...].T
    r.wait(r.wp, r.norm2, r.excite)
    half = owners // 2

    def first(index, carry):
        at_chunk = chunk_at(index)
        r.chunk(r.d, index, at_chunk).wait()
        r.h[...] = dot(r.gp[...], r.wp[:, at_chunk])
        for part in range(PARTS):
            lanes = chunk_at(index * PARTS + part, LANE)
            scale_row = r.norm2[2:3, lanes]
            shift_row = r.norm2[3:4, lanes]
            for tile in range(tiles):
                at = tile_rows(tile)
                near = tile_images(tile)
                pre = r.d[at, lanes].astype(F32) * scale_row + shift_row
                gate = sigmoid(pre)
                active = pre * gate
                slope = gate + active - active * gate
                grad = r.h[at, part * LANE : (part + 1) * LANE]
                factor = r.excite[near, lanes]
                r.ge[near, lanes] = jnp.sum(as_tile(grad * active), axis=0)
                r.y[at, lanes] = (as_tile(active) * factor[None]).reshape(ROWS, LANE).astype(BF16)
                r.slope[at, lanes] = slope.astype(r.slope.dtype)
                r.u[at, lanes] = (
                    (as_tile(grad * slope) * factor[None]).reshape(ROWS, LANE).astype(r.u.dtype)
                )
        grad_p_chunk = dot(r.gt[...], r.y[:, at_chunk])
        place = pl.ds(pl.multiple_of(index * rows_dev, rows_dev), rows_dev)
        for owner in range(half):
            cut = slice(owner * rows_dev, (owner + 1) * rows_dev)
            r.grads[half + owner, place, :] = grad_p_chunk[cut, :].astype(BF16)
            if is_head:
                r.grads[owner, place, :] = jnp.zeros((rows_dev, CHUNK), BF16)
            else:
                r.grads[owner, place, :] = r.grad_w[cut, at_chunk]
        return carry

    lax.fori_loop(0, EXPAND // CHUNK, first, 0)
    r.wait(r.pooled, r.squeeze, r.side)
    excite = r.excite[...]
    grad_gate = r.ge[...] * excite * (1.0 - excite)
    before = r.squeeze[...]
    opened = sigmoid(before)
    squeezed = before * opened
    reduce_mat = r.side[0:SQUEEZE, :]
    excite_mat = r.side[SQUEEZE:, :]
    gate_high, gate_low = halves(grad_gate)
    grad_squeezed = folded(dot_nt(jnp.concatenate([gate_high, gate_low], axis=0), excite_mat))
    grad_pre = grad_squeezed * (opened * (1.0 + before * (1.0 - opened)))
    r.pool[...] = folded(dot(stacked(grad_pre), reduce_mat)) / MAP

    squeezed_high, squeezed_low = halves(squeezed)
    pre_high, pre_low = halves(grad_pre)
    pooled_high, pooled_low = halves(r.pooled[...])
    r.rx[SQUEEZE:, :] = dot_tn(
        jnp.concatenate([squeezed_high, squeezed_low, squeezed_high], axis=0),
        jnp.concatenate([gate_high, gate_high, gate_low], axis=0),
    )
    r.rx[0:SQUEEZE, :] = dot_tn(
        jnp.concatenate([pre_high, pre_low, pre_high], axis=0),
        jnp.concatenate([pooled_high, pooled_high, pooled_low], axis=0),
    )
    r.excite_sum[...] = column_sum(grad_gate)
    r.squeeze_sum[...] = jnp.concatenate(
        [column_sum(grad_pre), jnp.zeros((1, LANE - SQUEEZE), F32)], axis=1
    )
    taps = None
    if not is_head:
        r.wait(r.taps)
        taps = r.taps[...]
    owner_blocks(r, owners, half, taps)
    room = r.grads.shape[1]
    place = pl.ds((r.blocks.shape[1] - room) * (not is_head), room)
    blocks_copy = pltpu.make_async_copy(r.grads, r.blocks.at[:, place, :], r.own_sem.at[1])
    blocks_copy.start()

    def second(index, carry):
        for part in range(PARTS):
            lanes = chunk_at(index * PARTS + part, LANE)
            mean_row = r.norm2[0:1, lanes]
            total = jnp.zeros((TILE, LANE), F32)
            weighted = jnp.zeros((TILE, LANE), F32)
            for tile in range(tiles):
                at = tile_rows(tile)
                pool = r.pool[tile_images(tile), lanes]
                grad = as_tile(r.u[at, lanes].astype(F32)) + as_tile(r.slope[at, lanes].astype(F32)) * pool[None]
                total = total + jnp.sum(grad, axis=0)
                weighted = weighted + jnp.sum(grad * as_tile(r.d[at, lanes].astype(F32)), axis=0)
                r.dz2[at, lanes] = grad.reshape(ROWS, LANE).astype(BF16)
            r.stat[0:1, lanes] = column_sum(total)
            r.stat[1:2, lanes] = column_sum(weighted) - mean_row * column_sum(total)
        r.part(r.dz2, index, chunk_at(index)).start()
        return carry

    lax.fori_loop(0, EXPAND // CHUNK, second, 0)
    write_alike(r.pay, fold([r.stat[0:1, :], r.stat[1:2, :] * r.norm2[1:2, :]], 24))
    r.send(r.pay)
    blocks_copy.wait()
    if is_head:
        head_copy.wait()
    r.finish(r.dz2)


def gate_back(is_head, row_count, owners, recv, upper, cross, stream, lower, blocks, extra_room):
    count = upper.xb.shape[0]
    images = count // MAP
    devices = recv.shape[0]
    columns = HEAD if is_head else EXPAND
    block = EXPAND // CHUNK * (2 * WIDTH // owners) + 2 * SQUEEZE + 16
    head_part = (slice(0, HEAD), slice(0, WIDTH))
    ins = dict(
        recv=(recv, LOOSE),
        unorm=(upper.norm, FAR),
        xb=(upper.xb, FAR),
        w=(upper.weights, head_part) if is_head else expand_rows(upper.weights),
        dz=(upper.dz, CHUNKS),
        norm3=(lower.norm3, FAR),
        normed=(lower.normed, FAR),
        norm2=(lower.norm2, FAR),
        wp=project_rows(lower.mats),
        d=(lower.d, CHUNKS),
        excite=(lower.excite, FAR),
        pooled=(lower.pooled, FAR),
        squeeze=(lower.squeeze, FAR),
        side=(lower.side, (slice(0, 2 * SQUEEZE), slice(None))),
    )
    outs = dict(
        dz2=(shape((count, EXPAND), BF16), FAR),
        pay=(shape((devices, 24, LANE), BF16), FAR),
        stream=(shape((count, WIDTH)), FAR),
        blocks=(shape((owners, block * (1 + extra_room), CHUNK), BF16), RAW),
        glob=(shape((8, columns)), FAR),
        glob3=(shape((8, WIDTH)), FAR),
    )
    scratch = dict(
        grads=vmem((owners, block, CHUNK), BF16),
        xt=vmem((WIDTH, count), BF16),
        h=vmem((count, CHUNK), F32),
        coef=vmem((8, EXPAND), F32),
        dh=vmem((count + WIDTH + 16, columns), BF16),
        u=vmem((count, EXPAND), BF16),
        slope=vmem((count, EXPAND), BF16),
        y=vmem((count, EXPAND), BF16),
        gp=vmem((count, WIDTH), BF16),
        gt=vmem((WIDTH, count), BF16),
        ge=vmem((images, EXPAND), F32),
        pool=vmem((images, EXPAND), F32),
        rx=vmem((2 * SQUEEZE, EXPAND), F32),
        excite_sum=vmem((1, EXPAND), F32),
        squeeze_sum=vmem((1, LANE), F32),
        stat=vmem((8, EXPAND), F32),
        own_sem=pltpu.SemaphoreType.DMA((2,)),
    )
    alias = []
    if is_head:
        ins["grad_head_in"] = (upper.grad_head, RAW)
        outs["grad_head"] = (shape((HEAD, HEADPAD), BF16), RAW)
        scratch["grad_w"] = vmem((HEAD, WIDTH), BF16)
        alias.append(("grad_head_in", "grad_head"))
    else:
        ins["cross"] = (cross, FAR)
        ins["stream_in"] = (stream, FAR)
        ins["taps"] = (upper.taps, FAR)
        scratch["grad_w"] = vmem((WIDTH, EXPAND), BF16)
        if blocks is not None:
            ins["blocks_in"] = (blocks, RAW)
            outs["blocks"] = (shape(blocks.shape, BF16), RAW)
            alias.append(("blocks_in", "blocks"))
    return call(functools.partial(gate_kernel, is_head, row_count, owners), ins, outs, scratch, alias)


def tap_kernel(is_first, row_count, r):
    count = r.dz2.shape[0]
    groups = EXPAND // LANE
    r.start()
    r.wait(r.recv)
    sums = read_sums(r.recv)
    sum_bias = spread(sums, 0, groups)
    sum_gain = spread(sums, groups, groups)
    r.glob[0:1, :] = sum_gain
    r.glob[1:2, :] = sum_bias
    r.glob[2:8, :] = jnp.zeros((6, EXPAND), F32)
    r.send(r.glob)
    r.wait(r.side, r.norm2)
    scale2 = r.norm2[2:3, :]
    slant2 = scale2 * r.norm2[1:2, :] * (sum_gain / row_count)
    r.coef[0:9, :] = r.side[...].astype(F32)[0:9, :]
    r.coef[9:10, :] = slant2
    r.coef[10:11, :] = r.norm2[0:1, :] * slant2 - scale2 * (sum_bias / row_count)
    r.wait(r.norm1, r.xb, r.w)

    def step(index, carry):
        at_chunk = chunk_at(index)
        r.chunk(r.dz2, index, at_chunk).wait()
        r.chunk(r.d, index, at_chunk).wait()
        r.h[...] = dot(r.xb[...], r.w[:, at_chunk])
        for part in range(PARTS):
            lanes = chunk_at(index * PARTS + part, LANE)
            near = slice(part * LANE, (part + 1) * LANE)
            taps = [jnp.broadcast_to(r.coef[k : k + 1, lanes], (TILE, LANE)) for k in range(9)]

            def tile_step(tile, sums_in):
                at = chunk_at(tile, ROWS)
                grad_d = as_tile(
                    r.dz2[at, lanes].astype(F32) * r.norm2[2:3, lanes]
                    - r.d[at, lanes].astype(F32) * r.coef[9:10, lanes]
                    + r.coef[10:11, lanes]
                )
                hidden = r.h[at, near]
                pre = hidden * r.norm1[2:3, lanes] + r.norm1[3:4, lanes]
                gate = sigmoid(pre)
                flat = pre * gate
                active = as_tile(flat)
                slope = as_tile(gate + flat - flat * gate)
                hidden = as_tile(hidden)
                grad_a = [None] * MAP
                tap_sums = [None] * 9
                for target, tap, source in TERMS:
                    term = grad_d[target] * taps[tap]
                    grad_a[source] = term if grad_a[source] is None else grad_a[source] + term
                    term = grad_d[target] * active[source]
                    tap_sums[tap] = term if tap_sums[tap] is None else tap_sums[tap] + term
                total, weighted = sums_in[9], sums_in[10]
                grads = []
                for place in range(MAP):
                    grad = grad_a[place] * slope[place]
                    total = total + grad
                    weighted = weighted + grad * hidden[place]
                    grads.append(grad)
                grad = jnp.concatenate(grads, axis=0)
                r.dz[at, lanes] = grad.astype(BF16)
                if not is_first:
                    r.q[at, lanes] = (grad * r.norm1[2:3, lanes]).astype(BF16)
                return (*[sums_in[k] + tap_sums[k] for k in range(9)], total, weighted)

            zero = jnp.zeros((TILE, LANE), F32)
            result = lax.fori_loop(0, count // ROWS, tile_step, (zero,) * 11, unroll=True)
            for k in range(9):
                r.taps[k : k + 1, lanes] = column_sum(result[k])
            total = column_sum(result[9])
            r.stat[0:1, lanes] = total
            r.stat[1:2, lanes] = column_sum(result[10]) - r.norm1[0:1, lanes] * total
        r.part(r.dz, index, at_chunk).start()
        return carry

    lax.fori_loop(0, EXPAND // CHUNK, step, 0)
    r.taps[9:16, :] = jnp.zeros((7, EXPAND), F32)
    r.send(r.taps)
    vectors = [r.stat[0:1, :], r.stat[1:2, :] * r.norm1[1:2, :]]
    if not is_first:
        r.wait(r.normed, r.stream)
        below = r.stream[...] + dot_nt(r.q[...], r.w[...])
        vectors.append(column_sum(below))
        vectors.append(column_sum(below * r.normed[...]))
    write_alike(r.pay, fold(vectors, r.pay.shape[1]))
    r.send(r.pay)
    r.finish(r.dz)


def tap_back(is_first, row_count, recv, dz2, layer, stream, below):
    count = dz2.shape[0]
    devices = recv.shape[0]
    ins = dict(
        recv=(recv, LOOSE),
        side=(layer.side, (slice(2 * SQUEEZE, SIDE_PAD), slice(None))),
        norm2=(layer.norm2, FAR),
        norm1=(layer.norm1, FAR),
        xb=(layer.xb, FAR),
        w=expand_rows(layer.mats),
        dz2=(dz2, CHUNKS),
        d=(layer.d, CHUNKS),
    )
    scratch = dict(
        h=vmem((count, CHUNK), F32),
        coef=vmem((16, EXPAND), F32),
        stat=vmem((8, EXPAND), F32),
    )
    if not is_first:
        ins["stream"] = (stream, FAR)
        ins["normed"] = (below.normed, FAR)
        scratch["q"] = vmem((count, EXPAND), BF16)
    return call(
        functools.partial(tap_kernel, is_first, row_count),
        ins,
        dict(
            dz=(shape((count, EXPAND), BF16), FAR),
            pay=(shape((devices, 24 if is_first else 32, LANE), BF16), FAR),
            taps=(shape((16, EXPAND)), FAR),
            glob=(shape((8, EXPAND)), FAR),
        ),
        scratch,
    )


def last_kernel(row_count, replicas, owners, r):
    r.start()
    r.wait(r.recv)
    product_back(False, row_count, read_sums(r.recv), EXPAND, r)
    half = owners // 2
    part = slice_rows(replicas * owners)
    rows_dev = 2 * WIDTH // owners
    chunks = EXPAND // CHUNK
    if chunks * part % 8:
        r.shares[...] = jnp.zeros(r.shares.shape, F32)
    for device in range(replicas * owners):
        replica, owner = device // owners, device % owners
        first_row = rows_dev * (owner % half) + (2 * replica + owner // half) * part
        for k in range(chunks):
            r.shares[device, k * part : (k + 1) * part, :] = r.grad_w[
                first_row : first_row + part, k * CHUNK : (k + 1) * CHUNK
            ]
    r.wait(r.taps)
    width = EXPAND // owners
    tap_rows = -(-9 * width // CHUNK)
    first_tap = -(-chunks * part // 8) * 8
    for owner in range(owners):
        pieces = [r.taps[k : k + 1, owner * width : (owner + 1) * width] for k in range(9)]
        pieces.append(jnp.zeros((1, tap_rows * CHUNK - 9 * width), F32))
        flat = jnp.concatenate(pieces, axis=1)
        lines = [flat[:, k * CHUNK : (k + 1) * CHUNK] for k in range(tap_rows)]
        lines.append(jnp.zeros((r.shares.shape[1] - first_tap - tap_rows, CHUNK), F32))
        lines = jnp.concatenate(lines, axis=0)
        for replica in range(replicas):
            r.shares[replica * owners + owner, first_tap:, :] = lines
    r.grads[...] = r.shares[...].astype(BF16)
    r.send(r.grads)
    r.finish()


def last_back(row_count, replicas, owners, recv, layer, dz, taps):
    count = dz.shape[0]
    devices = recv.shape[0]
    tap_rows = -(-9 * EXPAND // owners // CHUNK)
    block = -(-EXPAND // CHUNK * slice_rows(devices) // 8) * 8 + 8
    assert tap_rows <= 8
    return call(
        functools.partial(last_kernel, row_count, replicas, owners),
        dict(
            recv=(recv, LOOSE),
            dz=(dz, CHUNKS),
            unorm=(layer.norm1, FAR),
            xb=(layer.xb, FAR),
            w=expand_rows(layer.mats),
            taps=(taps, FAR),
        ),
        dict(
            grads=(shape((devices, block, CHUNK), BF16), FAR),
            glob=(shape((8, EXPAND)), FAR),
        ),
        dict(
            xt=vmem((WIDTH, count), BF16),
            h=vmem((count, CHUNK), F32),
            coef=vmem((8, EXPAND), F32),
            dh=vmem((count, EXPAND), BF16),
            grad_w=vmem((WIDTH, EXPAND), F32),
            shares=vmem((devices, block, CHUNK), F32),
        ),
    )


def lamb_moments(weight, moment_one, moment_two, gradient, decay_mask, step_float):
    first_new = BETA_ONE * moment_one + (1.0 - BETA_ONE) * gradient
    second_new = BETA_TWO * moment_two + (1.0 - BETA_TWO) * gradient * gradient
    corrected = (
        first_new
        / (1.0 - BETA_ONE**step_float)
        / (jnp.sqrt(second_new / (1.0 - BETA_TWO**step_float)) + EPS_ADAM)
    )
    return (first_new, second_new, corrected + DECAY_RATE * decay_mask * weight)


def group_sums(mats, side, head_shard, row_ids):
    rows = jnp.sum(mats * mats, axis=2)
    is_expand = (row_ids < WIDTH)[None, :]
    side_rows = jnp.sum(side * side, axis=2)
    head_cols = jnp.sum(head_shard * head_shard, axis=0)
    per_layer = jnp.stack(
        [
            jnp.sum(jnp.where(is_expand, rows, 0.0), axis=1),
            jnp.sum(jnp.where(is_expand, 0.0, rows), axis=1),
            jnp.sum(side_rows[:, :9], axis=1),
            jnp.sum(side_rows[:, 9 : 9 + SQUEEZE], axis=1),
            jnp.sum(side_rows[:, 9 + SQUEEZE : 9 + 2 * SQUEEZE], axis=1),
        ],
        axis=1,
    )
    tail = jnp.stack([jnp.sum(head_cols[:WIDTH]), jnp.sum(head_cols[WIDTH : WIDTH + CLASSES])])
    return jnp.concatenate([per_layer.reshape(-1), tail])


def rate_maps(trust_ratio, row_ids):
    groups = trust_ratio[: 5 * LAYERS].reshape(LAYERS, 5)
    mats_rate = RATE_MATRIX * jnp.where(row_ids[None, :] < WIDTH, groups[:, 0:1], groups[:, 1:2])
    side_ids = jnp.arange(SIDE)[None, :]
    side_rate = jnp.where(
        side_ids < 9,
        RATE_MATRIX * groups[:, 2:3],
        jnp.where(
            side_ids < 9 + SQUEEZE,
            RATE_MATRIX * groups[:, 3:4],
            jnp.where(side_ids < 9 + 2 * SQUEEZE, RATE_MATRIX * groups[:, 4:5], RATE_VECTOR),
        ),
    )
    col_ids = jnp.arange(HEADCOLS)
    head_rate = jnp.where(
        col_ids < WIDTH,
        RATE_MATRIX * trust_ratio[5 * LAYERS],
        jnp.where(
            col_ids < WIDTH + CLASSES, RATE_MATRIX * trust_ratio[5 * LAYERS + 1], RATE_VECTOR
        ),
    )
    return (mats_rate, side_rate, head_rate)


def exchange(payload):
    return lax.all_to_all(payload, BOTH, 0, 0)


def before(value, *others):
    return lax.optimization_barrier((value, *others))[0]


def spread_over(array, axis):
    copies = jnp.broadcast_to(array[None], (lax.axis_size(axis), *array.shape))
    return lax.all_to_all(copies, axis, 0, 0)


def replica_sum(array, turned=False):
    count = lax.axis_size(REPLICAS)
    steps = [1 << k for k in range(count.bit_length() - 1)]
    total = array
    for step in reversed(steps) if turned else steps:
        other = lax.ppermute(total, REPLICAS, [(k, k ^ step) for k in range(count)])
        total = (total.astype(F32) + other.astype(F32)).astype(BF16)
    return total.astype(F32)


def body(
    images, partner, mix_pair, labels, step,
    layer_mats, layer_side, layer_vecs, head_mat, fc_bias,
    mats_first, mats_second, side_first, side_second, vecs_first, vecs_second,
    head_first, head_second, bias_first, bias_second,
):
    local_images = images.shape[0]
    owners = lax.axis_size(OWNERS)
    replicas = lax.axis_size(REPLICAS)
    devices = owners * replicas
    image_count = float(local_images * devices)
    count = local_images * MAP
    row_count = float(count * devices)
    mine = lax.axis_index(OWNERS)
    side_width = layer_side.shape[2]
    vec_width = layer_vecs.shape[1]
    rows_dev = layer_mats.shape[1]
    half = owners // 2

    def side_as_sent(side, vecs):
        blank = jnp.zeros((side.shape[0], 1, side_width), F32)
        vecs = jnp.pad(vecs, ((0, 0), (0, side_width - vec_width)))[:, None, :]
        pieces = [side[:, 9 : 9 + 2 * SQUEEZE], side[:, :9], side[:, 9 + 2 * SQUEEZE :], vecs, blank]
        return jnp.concatenate(pieces, axis=1).astype(BF16)

    side_rows = -(-SIDE_PAD * side_width // EXPAND)
    side_flat = jnp.pad(side_as_sent(layer_side[:1], layer_vecs[:1]).reshape(-1), (0, side_rows * EXPAND - SIDE_PAD * side_width))
    packed = lax.all_gather(
        jnp.concatenate([layer_mats[0].astype(BF16), side_flat.reshape(side_rows, EXPAND)], axis=0),
        OWNERS, axis=0,
    )
    partner_col = partner[:, None]
    layers = []
    crosses = []
    entry = mix(images.reshape(count, WIDTH), partner_col, mix_pair, devices)
    x, xb = entry.x, entry.xb
    received = exchange(entry.pay)
    shared = share(received).pay
    later_mats, later_side, later_vecs, later_head, _ = lax.optimization_barrier(
        (layer_mats, layer_side, layer_vecs, head_mat, shared)
    )
    mats_all = [None] + [
        lax.all_gather(later_mats[k].astype(BF16), OWNERS, axis=0, tiled=True) for k in range(1, LAYERS)
    ]
    side_room = -(-side_width // CHUNK) * CHUNK
    side_rest = lax.all_gather(
        jnp.pad(side_as_sent(later_side[1:], later_vecs[1:]), ((0, 0), (0, 0), (0, side_room - side_width))), OWNERS, axis=0
    )
    side_rest = jnp.moveaxis(side_rest[..., :side_width], 0, 2).reshape(LAYERS - 1, SIDE_PAD, EXPAND)
    head_full = lax.all_gather(
        jnp.pad(later_head, ((0, 0), (0, HEADPAD - HEADCOLS))).astype(BF16), OWNERS, axis=0, tiled=True
    )

    square = exchange(shared)
    packed = before(packed, shared)
    mats_all[0] = packed
    side_flat = packed[:, rows_dev:].reshape(owners, -1)[:, : SIDE_PAD * side_width]
    side_zero = jnp.moveaxis(side_flat.reshape(owners, SIDE_PAD, side_width), 0, 1).reshape(SIDE_PAD, EXPAND)
    side_all = [side_zero, side_rest[0], side_rest[1]]
    for k in range(LAYERS):
        mats, side = mats_all[k], side_all[k]
        if k:
            received, square = exchange(pay), None
        one = spatial(xb, mats, side, received, square)
        two = project(one.d, mats, side, exchange(one.pay), getattr(one, "cross", None), owners)
        last = k == LAYERS - 1
        three = residual(
            x, two.p, two.vec, exchange(two.pay), head_full if last else mats_all[k + 1], last
        )
        if k:
            crosses.append(three.cross)
        layers.append(
            types.SimpleNamespace(
                xb=xb, d=one.d, norm1=one.norm, norm2=two.norm,
                pooled=two.pooled, excite=two.excite, squeeze=two.squeeze,
                norm3=three.norm, normed=three.normed, mats=mats, weights=mats, side=side,
            )
        )
        x, xb, pay = three.x, three.xb, three.pay
    top = head(
        xb, head_full, jnp.pad(fc_bias, (0, LOGITS - CLASSES))[None], labels[:, None], labels[None, :],
        partner_col, mix_pair, layers[-1].normed, exchange(pay), image_count,
    )

    def to_owner(blocks):
        return lax.psum_scatter(
            blocks.reshape(-1, blocks.shape[-1]), OWNERS, scatter_dimension=0, tiled=True
        )

    upper = types.SimpleNamespace(
        xb=xb, weights=head_full, dz=top.dz, norm=top.norm, grad_head=top.grad_head
    )
    pay = top.pay
    stream = None
    blocks = None
    waiting = []
    globs_one, globs_two, globs_three = [None] * LAYERS, [None] * LAYERS, [None] * LAYERS
    for k in reversed(range(LAYERS)):
        layer = layers[k]
        is_head = k == LAYERS - 1
        gate = gate_back(
            is_head, row_count, owners, exchange(pay), upper,
            None if is_head else crosses[k], stream, layer, blocks, is_head,
        )
        stream = gate.stream
        globs_three[k] = gate.glob3
        if is_head:
            head_glob, bias_loss = gate.glob, gate.glob3[2:6].reshape(LOGITS)
            shard_head = to_owner(gate.grad_head)
            blocks = gate.blocks
        else:
            globs_one[k + 1] = gate.glob
            if k:
                pair = to_owner(gate.blocks)
                blocks = None
            else:
                shard_zero = to_owner(gate.blocks)
        tap = tap_back(
            k == 0, row_count, exchange(gate.pay), gate.dz2, layer, stream, layers[max(k - 1, 0)]
        )
        globs_two[k] = tap.glob
        pay = tap.pay
        if k == 1:
            pay = before(pay, shard_head)
        upper = types.SimpleNamespace(
            xb=layer.xb, weights=layer.mats, dz=tap.dz, norm=layer.norm1, taps=tap.taps
        )
    pay = before(pay, pair)
    received = exchange(pay)
    final = last_back(row_count, replicas, owners, received, layers[0], tap.dz, tap.taps)
    globs_one[0] = final.glob
    shard_head = replica_sum(before(shard_head, received))
    pair = replica_sum(before(pair, received), True)
    room = pair.shape[0] // 2
    shards = [shard_zero, pair[room:], pair[:room]]

    part = slice_rows(devices)
    chunks = EXPAND // CHUNK
    summed = jnp.sum(exchange(final.grads).astype(F32), axis=0)
    first_tap = -(-chunks * part // 8) * 8
    late_taps = summed[first_tap:].reshape(-1)[: 9 * side_width].reshape(9, side_width)
    late = summed[: chunks * part].astype(BF16)
    shards[0] = replica_sum(before(shards[0], late))
    other = lax.ppermute(late, OWNERS, [(half + k, k) for k in range(half)])
    late = spread_over(jnp.stack([late, other]), REPLICAS)
    late = jnp.moveaxis(late.reshape(replicas, 2, chunks, part, CHUNK), 2, 3)
    late = late.reshape(rows_dev, EXPAND).astype(F32)

    def mats_of(shard):
        rows = shard[: chunks * rows_dev].reshape(chunks, rows_dev, CHUNK)
        return jnp.moveaxis(rows, 0, 1).reshape(rows_dev, EXPAND)

    from_mats = [late] + [mats_of(shard) for shard in shards]
    owns_expand = mine < half
    grad_mats = jnp.stack(
        [jnp.where(owns_expand, from_mats[k], from_mats[k + 1]) for k in range(LAYERS)]
    )

    def own_columns(vector, width):
        return lax.dynamic_slice_in_dim(vector, mine * width, width, axis=-1)

    first_row = chunks * rows_dev
    last_row = first_row + 2 * SQUEEZE
    vec_ids = mine * vec_width + jnp.arange(vec_width)
    side_list, vec_list = [], []
    for k in range(LAYERS):
        shard = shards[k][:, :side_width]
        taps = late_taps if k == 0 else shards[k - 1][last_row + 2 : last_row + 11, :side_width]
        norms_part = own_columns(
            jnp.concatenate([globs_one[k][0:2], globs_two[k][0:2]], axis=0), side_width
        )
        side_list.append(
            jnp.concatenate([taps, shard[first_row : last_row + 1], norms_part], axis=0)
        )
        outer = globs_three[k]
        outer = own_columns(
            jnp.concatenate([jnp.zeros((SQUEEZE,), F32), outer[0], outer[1]]), vec_width
        )
        vec_list.append(jnp.where(vec_ids < SQUEEZE, shard[last_row + 1, :vec_width], outer))
    grad_side = jnp.stack(side_list)
    grad_vecs = jnp.stack(vec_list)
    head_tail = own_columns(head_glob[0:2], head_mat.shape[0]).T
    grad_head = jnp.concatenate([shard_head[:, : WIDTH + CLASSES], head_tail], axis=1)
    grad_bias = bias_loss[:CLASSES]
    loss_value = (bias_loss[CLASSES] + bias_loss[CLASSES + 1]) / image_count

    step_float = step[0].astype(F32)
    side_decay = (jnp.arange(SIDE) < 9 + 2 * SQUEEZE).astype(F32)[None, :, None]
    head_decay = (jnp.arange(HEADCOLS) < WIDTH + CLASSES).astype(F32)[None, :]
    mats_moment, mats_square, mats_dir = lamb_moments(
        layer_mats, mats_first, mats_second, grad_mats, 1.0, step_float
    )
    side_moment, side_square, side_dir = lamb_moments(
        layer_side, side_first, side_second, grad_side, side_decay, step_float
    )
    vecs_moment, vecs_square, vecs_dir = lamb_moments(
        layer_vecs, vecs_first, vecs_second, grad_vecs, 0.0, step_float
    )
    head_moment, head_square, head_dir = lamb_moments(
        head_mat, head_first, head_second, grad_head, head_decay, step_float
    )
    bias_moment, bias_square, bias_dir = lamb_moments(
        fc_bias, bias_first, bias_second, grad_bias, 0.0, step_float
    )
    row_ids = mine * rows_dev + jnp.arange(rows_dev)
    squares = jnp.stack(
        [
            group_sums(layer_mats, layer_side, head_mat, row_ids),
            group_sums(mats_dir, side_dir, head_dir, row_ids),
        ]
    )
    norms = jnp.sqrt(jnp.sum(spread_over(squares, OWNERS), axis=0))
    mats_rate, side_rate, head_rate = rate_maps(norms[0] / norms[1], row_ids)
    mats_new = layer_mats - mats_rate[:, :, None] * mats_dir
    side_new = layer_side - side_rate[:, :, None] * side_dir
    vecs_new = layer_vecs - RATE_VECTOR * vecs_dir
    head_new = head_mat - head_rate[None, :] * head_dir
    bias_new = fc_bias - RATE_VECTOR * bias_dir
    return (
        loss_value,
        mats_new, mats_moment, mats_square,
        side_new, side_moment, side_square,
        vecs_new, vecs_moment, vecs_square,
        head_new, head_moment, head_square,
        bias_new, bias_moment, bias_square,
        norms,
    )


def solution(mesh):
    rows, columns = P(None, OWNERS, None), P(None, None, OWNERS)
    vecs, heads = P(None, OWNERS), P(OWNERS, None)
    return jax.shard_map(
        body,
        mesh=mesh,
        in_specs=(
            P(BOTH, None, None), P(BOTH), P(BOTH, None), P(BOTH), P(),
            rows, columns, vecs, heads, P(),
            rows, rows, columns, columns, vecs, vecs, heads, heads, P(), P(),
        ),
        out_specs=(
            P(),
            rows, rows, rows,
            columns, columns, columns,
            vecs, vecs, vecs,
            heads, heads, heads,
            P(), P(), P(), P(),
        ),
        check_vma=False,
    )
```
